32 devices in a mesh: ctx: 8 (over z, y), mp: 4 (over x, core).
Axes of the slice: x: 2, y: 2, z: 4, core: 2. Of those that a mesh axis runs over, the one named last changes fastest.
Arguments:
- features: bfloat16 [4096, 3, 8192], P('ctx', None, 'mp'), may hold values from -6 to 6
- residual: bfloat16 [4096, 8192], P('ctx', 'mp')
- short_taps: float32 [3, 7, 8192], P(None, None, 'mp'), may hold values from -2 to 2
- rates: float32 [512, 16], P('mp'), may hold values from 7.324219e-05 to 0.05, as said below
- residues: float32 [512, 16], P('mp'), may hold values from -4 to 4
- skip: float32 [8192], P('mp'), may hold values from -4 to 4
- gain: float32 [8192], P('mp'), may hold values from 0.5 to 1.5
- lengths: int32 [8], replicated, may hold values from 1 to 2048, 4096 in all
- owner: int32 [64], replicated, may hold values from 0 to 7, as said below
Outputs:
- relaid: bfloat16 [4096, 8192], P('ctx', 'mp')
The draws below stay inside these ranges and needn't reach their ends.
Inputs may be any that keep to these rules, and one draw needn't show every extreme that they name: The owner of block i of index s is (s + o_i) mod 8 for offsets o_i that depend on i alone; exactly two of the 8 offsets are equal and the others differ, so every owner receives one block of each index i and at most 2 blocks come from one index to one owner. `rates`: every rate is positive.
All inputs are finite; a program needn't handle non-finite values.
Results may differ from the reference program's by a relative error of at most 0.0065.
Values may be sent and summed in bfloat16 or wider, within the bound.
No kernel may reach another device: no remote copies, remote signals or barrier semaphores. Data moves between devices by JAX's collectives and lax.ppermute only.
A program may use at most 128 MiB of HBM per device.

```python
import math
import jax
import jax.numpy as jnp
import numpy as np
from jax import lax

D = 8192
GSIZE = 16
NMODES = 16
SHORT = 7
NDOC = 8
TOK_DEV = 512
BLOCKS = 8
TOKENS = 4096


def draw_residual(key, part):
    key = jax.random.fold_in(key, 11)
    row_key, value_key = jax.random.split(key, 2)
    columns = jnp.arange(D).astype(jnp.float32) / D
    rows = jnp.exp(jax.random.uniform(row_key, (TOKENS, 1), minval=0.0, maxval=jnp.log(10.0)))
    spread = jnp.exp(jnp.log(10.0) * columns)[None, :]
    values = jax.random.normal(value_key, (TOKENS, D))
    base = 0.15
    return (base * rows * spread * values).astype(jnp.bfloat16)


def draw_rates(key, part):
    key = jax.random.fold_in(key, 23)
    pick_key, slow_random_key, fast_key = jax.random.split(key, 3)
    shape = (D // GSIZE, NMODES)
    share = 0.5
    slow = jnp.exp(jax.random.uniform(slow_random_key, shape, minval=jnp.log(0.3 / TOKENS), maxval=jnp.log(2.0 / TOKENS)))
    fast = jnp.exp(jax.random.uniform(fast_key, shape, minval=jnp.log(1.0 / 60.0), maxval=jnp.log(1.0 / 20.0)))
    slowness = jax.random.uniform(pick_key, shape) < share
    return jnp.where(slowness, slow, fast).astype(jnp.float32)


def draw_owner(key, part):
    key = jax.random.fold_in(key, 37)
    order_key, pair_key = jax.random.split(key)
    offsets = jax.random.permutation(order_key, BLOCKS).astype(jnp.int32)
    pair = jax.random.permutation(pair_key, BLOCKS)
    offsets = offsets.at[pair[1]].set(offsets[pair[0]])
    source = jnp.arange(BLOCKS, dtype=jnp.int32)[:, None]
    return ((source + offsets[None, :]) % BLOCKS).reshape(BLOCKS * BLOCKS).astype(jnp.int32)


def levels(key, shape, shards, least, top_value):
    loudness = 1.0
    for position, blocks in shards:
        steps = jax.random.uniform(jax.random.fold_in(jax.random.fold_in(key, 6), position), (blocks,), jnp.float32, least / len(shards), top_value / len(shards))
        loudness = loudness * jnp.repeat(jnp.exp(steps), shape[position] // blocks).reshape((-1,) + (1,) * (len(shape) - 1 - position))
    return loudness


def length_profile(number_of, total, most, lean):
    loads = [(1 << 20) // math.isqrt(grade ** lean) + 1 for grade in range(2, number_of + 1)]
    rest, holding = total - most - (number_of - 1), [1] * (number_of - 1)
    while rest > 0:
        candidates = [i for i in range(number_of - 1) if holding[i] < most]
        mass, remaining = sum([loads[i] for i in candidates]), rest
        for i in candidates:
            extra = min(most - holding[i], max(1, remaining * loads[i] // mass), rest)
            holding[i] = holding[i] + extra
            rest = rest - extra
    return np.array([most] + holding)


def uneven_parts(stream_key, count, total, most, slope):
    if count == 2:
        one = jax.random.randint(stream_key, (), max(1, total - most), min(most, total - 1) + 1)
        return jnp.stack([one, total - one])
    sizes = jnp.asarray(length_profile(count, total, most, slope), jnp.int32)
    twos = (count - 1) // 2
    donor, receiver = sizes[1:1 + 2 * twos:2], sizes[2:2 + 2 * twos:2]
    margin = jnp.minimum(donor - 1, most - receiver)
    passed = jax.random.randint(jax.random.fold_in(stream_key, 1), (twos,), 0, 1 << 20) % (margin + 1)
    sizes = sizes.at[1:1 + 2 * twos:2].set(donor - passed).at[2:2 + 2 * twos:2].set(receiver + passed)
    return sizes[jax.random.permutation(jax.random.fold_in(stream_key, 2), count)]


def centred(key, shape, scale, bound, cuts=(), kind=jnp.bfloat16):
    level = levels(key, shape, cuts, -0.22, 0.18) if cuts else 1.0
    result = jax.random.normal(key, shape, jnp.float32) * scale * level
    return jnp.minimum(jnp.maximum(result, -bound), bound).astype(kind)


def setup_inputs(seed: int = 0) -> dict:
    streams_of = jax.random.split(jax.random.key(seed), 10)
    features = centred(streams_of[0], (TOKENS, 3, D), 1.0, 6.0, ((0, 8), (2, 4)))
    residual = draw_residual(jax.random.fold_in(streams_of[9], 71), 0)
    short_taps = centred(streams_of[2], (3, SHORT, D), SHORT ** -0.5, 2.0, ((2, 4),), jnp.float32)
    rates = draw_rates(jax.random.fold_in(streams_of[9], 71), 0)
    residues = centred(streams_of[4], (D // GSIZE, NMODES), 0.3, 4.0, ((0, 4),), jnp.float32)
    skip = centred(streams_of[5], (D,), 1.0, 4.0, ((0, 4),), jnp.float32)
    gain = jnp.clip(1.0 + 0.1 * jax.random.normal(streams_of[6], (D,), jnp.float32), 0.5, 1.5)
    lengths = uneven_parts(streams_of[7], NDOC, TOKENS, TOKENS // 2, 2).astype(jnp.int32)
    owner = draw_owner(jax.random.fold_in(streams_of[9], 71), 0)
    return {"features": features, "residual": residual, "short_taps": short_taps, "rates": rates, "residues": residues, "skip": skip, "gain": gain, "lengths": lengths, "owner": owner}


HIGHEST_ACCURACY = lax.Precision.HIGHEST
eps = 1e-06

def banded_operator(taps, rows):
    length = taps.shape[-1]
    lead = taps.shape[:-1]
    zeros = jnp.zeros(lead + (rows,), taps.dtype)
    line = jnp.concatenate([taps[..., ::-1], zeros], -1)
    tiled = jnp.tile(line, (1,) * len(lead) + (rows,))
    cut = tiled[..., :rows * (length + rows - 1)]
    return cut.reshape(lead + (rows, length + rows - 1))

def short_conv(window, seg_window, taps, count):
    span = taps.shape[1]
    total = jnp.zeros((count,) + window.shape[1:], jnp.float32)
    here = seg_window[span - 1:span - 1 + count]
    for lag in range(span):
        rows = window[span - 1 - lag:span - 1 - lag + count].astype(jnp.float32)
        same = (seg_window[span - 1 - lag:span - 1 - lag + count] == here).astype(jnp.float32)
        total = total + rows * taps[:, lag][None] * same[:, None, None]
    return total

def long_conv(values, seg_rows, seg_before, rates, residues, initial_state, block):
    count, width = values.shape
    groups = rates.shape[0]
    size = width // groups
    scale = residues * jnp.sqrt(1.0 - jnp.exp(-2.0 * rates))
    lags = jnp.arange(block).astype(jnp.float32)
    decay = jnp.exp(-rates[:, :, None] * lags[None, None, :])
    kernel = jnp.einsum('gr,grl->gl', scale, decay, precision=HIGHEST_ACCURACY)
    square = banded_operator(kernel, block)[:, :, block - 1:]
    entry_mask = scale[:, :, None] * decay * jnp.exp(-rates)[:, :, None]
    leave = decay[:, :, ::-1]
    whole = jnp.exp(-rates * block)
    blocks = count // block
    rows_all = values.reshape(blocks, block, width)
    segs = seg_rows.reshape(blocks, block)
    prev = jnp.concatenate([jnp.reshape(seg_before, (1,)).astype(jnp.int32), segs[:-1, -1]], 0)

    def step(running_state, inputs):
        rows, seg_blk, seg_prev = inputs
        keep_mask = (seg_blk == seg_prev).astype(jnp.float32)
        same = (seg_blk[:, None] == seg_blk[None, :]).astype(jnp.float32)
        grouped = rows.reshape(block, groups, size)
        inner = jnp.einsum('gts,sgc->tgc', square * same[None], grouped, precision=HIGHEST_ACCURACY)
        carried_state = jnp.einsum('hnx,hnm->xhm', entry_mask * keep_mask[None, None, :], running_state, precision=HIGHEST_ACCURACY)
        tail = (seg_blk == seg_blk[-1]).astype(jnp.float32)
        fresh = jnp.einsum('grs,sgc->grc', leave * tail[None, None, :], grouped, precision=HIGHEST_ACCURACY)
        running_state = (keep_mask[-1] * whole)[:, :, None] * running_state + fresh
        return (running_state, (inner + carried_state).reshape(block, width))
    final, outs = lax.scan(step, initial_state, (rows_all, segs, prev))
    return (outs.reshape(count, width), final)

def reference(features, residual, short_taps, rates, residues, skip, gain, lengths, owner):
    reach = SHORT - 1
    block = min(128, TOK_DEV)
    positions = jnp.arange(-reach, TOKENS, dtype=jnp.int32)
    ends = jnp.cumsum(lengths).astype(jnp.int32)
    seg_window = lax.optimization_barrier(jnp.sum((positions[:, None] >= ends[None, :]).astype(jnp.int32), 1)).astype(jnp.int32)
    seg_window = jnp.where(positions < 0, -1, seg_window).astype(jnp.int32)
    span_width = min(D, 1024)
    group_width = span_width // GSIZE
    sums = []
    for piece_index in range(D // span_width):
        low = piece_index * span_width
        high = low + span_width
        glow = piece_index * group_width
        ghigh = glow + group_width
        window = jnp.concatenate([jnp.zeros((reach, 3, span_width), jnp.bfloat16), features[:, :, low:high]], 0)
        short = short_conv(window, seg_window, short_taps[:, :, low:high], TOKENS)
        gate = short[:, 0]
        mixed = (short[:, 1] * short[:, 2]).astype(jnp.bfloat16)
        wide = mixed.astype(jnp.float32)
        initial_state = jnp.zeros((group_width, NMODES, GSIZE), jnp.float32)
        longer, final = long_conv(wide, seg_window[reach:], jnp.int32(-1), rates[glow:ghigh], residues[glow:ghigh], initial_state, block)
        hyena = gate * (longer + skip[low:high][None, :] * wide)
        sums.append(residual[:, low:high].astype(jnp.float32) + hyena)
    squares = jnp.zeros((TOKENS,), jnp.float32)
    for summed in sums:
        squares = squares + lax.optimization_barrier(jnp.sum(summed * summed, 1))
    inverse = lax.rsqrt(squares / D + eps)
    normed = jnp.concatenate([summed * inverse[:, None] for summed in sums], 1)
    normed = (normed * gain[None, :]).astype(jnp.bfloat16)
    rows = TOK_DEV // BLOCKS
    pieces = normed.reshape(BLOCKS, BLOCKS, rows, D)
    table = owner.reshape(BLOCKS, BLOCKS)
    ids = jnp.arange(BLOCKS, dtype=jnp.int32)
    hits = (table[None, :, :] == ids[:, None, None]).astype(jnp.int32)
    source = lax.optimization_barrier(jnp.sum(hits * ids[None, :, None], 1)).astype(jnp.int32)
    picked = pieces[source, ids[None, :]]
    return picked.reshape(TOKENS, D)
```

```python
import functools

import jax
import jax.numpy as jnp
from jax import lax
from jax.experimental import pallas as pl
from jax.experimental.pallas import tpu as pltpu
from jax.sharding import PartitionSpec as P

SHORT = 7
LANES = 128
CHUNK = 128
HALO = 8
EPS = 1e-06
PARTS = 2
F32 = jnp.float32
BF16 = jnp.bfloat16
VMEM_LIMIT = 48 * 1024 * 1024


def iota(shape, dim):
    return lax.broadcasted_iota(jnp.int32, shape, dim)


def document(ends, positions):
    total = jnp.zeros(positions.shape, jnp.int32)
    for end in ends:
        total = total + (positions >= end).astype(jnp.int32)
    return total


def scalar_document(ends, position):
    total = jnp.int32(0)
    for end in ends:
        total = total + (position >= end).astype(jnp.int32)
    return jnp.where(position < 0, -1, total)


def running_ends(meta_ref, ndoc):
    ends, total = [], jnp.int32(0)
    for j in range(ndoc):
        total = total + meta_ref[1 + j]
        ends.append(total)
    return ends


def write_lag_masks(mask_ref, ends, base):
    rows = mask_ref.shape[1]
    here = base - HALO + iota((rows, LANES), 0)
    for lag in (1, 2, 3):
        apart = jnp.zeros((rows, LANES), jnp.bool_)
        for end in ends:
            apart = apart | ((here >= end) & (here - lag < end))
        mask_ref[lag - 1] = jnp.where(apart, 0.0, 1.0).astype(F32)


def crosses(ends, first, last):
    found = jnp.bool_(False)
    for end in ends:
        found = found | ((end > first) & (end <= last))
    return found


def short_conv(ext, taps, masks):
    def back(value, lag):
        moved = pltpu.roll(value, lag, 0)
        return moved if masks is None else moved * masks[lag - 1]

    one, two = back(ext, 1), back(ext, 2)
    far = ext * taps[6]
    middle = ext * taps[3] + one * taps[4] + two * taps[5] + back(far, 3)
    near = ext * taps[0] + one * taps[1] + two * taps[2] + back(middle, 3)
    return near[HALO:]


def extended(x_ref, halo_ref, which, chunk):
    start = chunk * CHUNK
    rows = x_ref[which, start : start + CHUNK, :].astype(F32)
    if chunk == 0:
        ahead = halo_ref[which].astype(F32)
    else:
        ahead = x_ref[which, start - 16 : start, :].astype(F32)[16 - HALO :]
    return jnp.concatenate([ahead, rows], 0)


def tap_rows(taps_ref, which):
    return [taps_ref[which, j : j + 1, :] for j in range(SHORT)]


def group_mask(modes, size):
    return (iota((LANES, LANES), 0) // modes) == (iota((LANES, LANES), 1) // size)


def mix_kernel(modes, size, ndoc, meta_ref, x_ref, halo_ref, taps_ref, rate_ref, mixed_ref, state_ref, mask_ref):
    count = x_ref.shape[1]
    chunks = count // CHUNK
    base = meta_ref[0]
    ends = running_ends(meta_ref, ndoc)

    @pl.when(pl.program_id(0) == 0)
    def _():
        write_lag_masks(mask_ref, ends, base)

    key_taps, value_taps = tap_rows(taps_ref, 0), tap_rows(taps_ref, 1)
    for chunk in range(chunks):
        start = chunk * CHUNK
        split = crosses(ends, base + start - HALO, base + start + CHUNK - 1)

        def run(masks, chunk=chunk, start=start):
            key = short_conv(extended(x_ref, halo_ref, 0, chunk), key_taps, masks)
            value = short_conv(extended(x_ref, halo_ref, 1, chunk), value_taps, masks)
            mixed_ref[start : start + CHUNK, :] = (key * value).astype(BF16)

        @pl.when(split)
        def _(run=run, start=start):
            run([mask_ref[l, start : start + CHUNK + HALO, :] for l in range(3)])

        @pl.when(jnp.logical_not(split))
        def _(run=run):
            run(None)

    rate = jnp.broadcast_to(rate_ref[...], (LANES, LANES)).T
    last = scalar_document(ends, base + count - 1)
    spans = []
    for chunk in range(chunks):
        offset = chunk * CHUNK + iota((LANES, CHUNK), 1)
        decay = jnp.exp(-rate * (count - 1 - offset).astype(F32))
        tail = document(ends, base + offset) == last
        spans.append(jnp.where(tail, decay, 0.0).astype(BF16))
    full = jnp.dot(jnp.concatenate(spans, 1), mixed_ref[...], preferred_element_type=F32)
    full = jnp.where(group_mask(modes, size), full, 0.0)
    state_ref[...] = jnp.sum(full.reshape(LANES // modes, modes, LANES), 0).astype(BF16)


def conv_kernel(
    modes, size, ndoc, nblocks,
    meta_ref, slot_ref,
    x_ref, halo_ref, taps_ref, mixed_ref, states_ref, rate_ref, scale_ref, skip_ref, residual_ref,
    out_ref, spare_ref, squares_ref,
    mask_ref, same_ref, keep_ref,
):
    count = mixed_ref.shape[0]
    chunks = count // CHUNK
    rows = count // nblocks
    base = meta_ref[0]
    where = meta_ref[1 + ndoc]
    ends = running_ends(meta_ref, ndoc)
    step = pl.program_id(0)

    @pl.when(step == 0)
    def _():
        write_lag_masks(mask_ref, ends, base)
        squares_ref[...] = jnp.zeros_like(squares_ref)
        for chunk in range(chunks):
            start = base + chunk * CHUNK
            down, along = iota((CHUNK, CHUNK), 0), iota((CHUNK, CHUNK), 1)
            here = document(ends, start + down)
            linked = (here == document(ends, start + along)) & (along <= down)
            same_ref[chunk] = jnp.where(linked, 1.0, 0.0).astype(BF16)
            carried = here == scalar_document(ends, start - 1)
            keep_ref[chunk] = jnp.where(carried, 1.0, 0.0).astype(BF16)

    groups = LANES // modes
    rate_row, scale_row = rate_ref[...], scale_ref[...]
    down = iota((CHUNK, LANES), 0)
    lags = jnp.where(down == 0, 0, CHUNK - down).astype(F32)
    terms = scale_row * jnp.exp(-rate_row * lags)
    pick = (iota((groups, LANES), 1) // modes == iota((groups, LANES), 0)).astype(F32)
    line = lax.dot_general(
        pick, terms, (((1,), (1,)), ((), ())), preferred_element_type=F32, precision=lax.Precision.HIGHEST
    )
    toeplitz = []
    for g in range(groups):
        wide = jnp.broadcast_to(line[g : g + 1, :], (CHUNK, CHUNK))
        toeplitz.append(pltpu.roll(wide, 0, 1, stride=1, stride_axis=0).astype(BF16))
    entry = (scale_row * jnp.exp(-rate_row * (down + 1).astype(F32))).astype(BF16)
    rate = jnp.broadcast_to(rate_row, (LANES, LANES)).T
    along = iota((LANES, CHUNK), 1)
    leave = jnp.exp(-rate * (CHUNK - 1 - along).astype(F32))
    whole = jnp.exp(-rate * CHUNK)
    inside = group_mask(modes, size)

    before = scalar_document(ends, base - 1)

    def gather(v, total):
        wanted = scalar_document(ends, (v + 1) * count - 1) == before
        weight = jnp.exp(-rate * ((where - 1 - v) * count).astype(F32))
        piece = jnp.concatenate([states_ref[v].astype(F32)] * groups, 0)
        return total + jnp.where(inside & wanted, piece * weight, 0.0)

    state = lax.fori_loop(0, where, gather, jnp.zeros((LANES, LANES), F32))

    taps = tap_rows(taps_ref, 0)
    skip = skip_ref[...]
    lane_group = iota((CHUNK, LANES), 1) // size
    for chunk in range(chunks):
        start = chunk * CHUNK
        mixed = mixed_ref[start : start + CHUNK, :]
        same = same_ref[chunk]
        left = jnp.concatenate([t * same for t in toeplitz] + [entry * keep_ref[chunk]], 1)
        right = jnp.concatenate(
            [jnp.where(lane_group == g, mixed, jnp.zeros_like(mixed)) for g in range(groups)] + [state.astype(BF16)], 0
        )
        longer = jnp.dot(left, right, preferred_element_type=F32)
        if chunk + 1 < chunks:
            last = scalar_document(ends, base + start + CHUNK - 1)
            tail = document(ends, base + start + along) == last
            fresh = jnp.dot(jnp.where(tail, leave, 0.0).astype(BF16), mixed, preferred_element_type=F32)
            held = scalar_document(ends, base + start - 1) == last
            state = jnp.where(held, whole * state, 0.0) + jnp.where(inside, fresh, 0.0)
        body = longer + skip * mixed.astype(F32)
        split = crosses(ends, base + start - HALO, base + start + CHUNK - 1)

        def finish(masks, chunk=chunk, start=start, body=body):
            gate = short_conv(extended(x_ref, halo_ref, 0, chunk), taps, masks)
            summed = residual_ref[start : start + CHUNK, :].astype(F32) + gate * body
            squares_ref[start : start + CHUNK, :] += summed * summed
            rounded = summed.astype(BF16)
            for b in range(CHUNK // rows):
                slot = slot_ref[start // rows + b]
                block = rounded[b * rows : (b + 1) * rows]

                @pl.when(slot < nblocks)
                def _(slot=slot, block=block):
                    out_ref[slot] = block

                @pl.when(slot >= nblocks)
                def _(block=block):
                    spare_ref[...] = block

        @pl.when(split)
        def _(finish=finish, start=start):
            finish([mask_ref[l, start : start + CHUNK + HALO, :] for l in range(3)])

        @pl.when(jnp.logical_not(split))
        def _(finish=finish):
            finish(None)


def norm_kernel(parts, pick_ref, *refs):
    blocks, spares = refs[:parts], refs[parts : 2 * parts]
    scale_ref, gain_ref, out_ref = refs[2 * parts :]
    i = pl.program_id(0)
    is_spare = pick_ref[2 * pl.num_programs(0)] == i
    low = 0
    for block_ref, spare_ref in zip(blocks, spares):
        width = block_ref.shape[2]
        for tile in range(width // LANES):
            lanes = slice(tile * LANES, (tile + 1) * LANES)
            value = jnp.where(is_spare, spare_ref[0, :, lanes].astype(F32), block_ref[0, :, lanes].astype(F32))
            outs = slice(low + tile * LANES, low + (tile + 1) * LANES)
            out_ref[:, outs] = (value * scale_ref[...] * gain_ref[:, outs]).astype(BF16)
        low += width


def params():
    return pltpu.CompilerParams(dimension_semantics=("arbitrary",), vmem_limit_bytes=VMEM_LIMIT)


def mix(meta, x, halo, taps, rate, modes, size, ndoc):
    _, count, width = x.shape
    tile = lambda t, m: (0, t)
    grid_spec = pltpu.PrefetchScalarGridSpec(
        num_scalar_prefetch=1,
        grid=(width // LANES,),
        in_specs=[
            pl.BlockSpec((2, count, LANES), lambda t, m: (0, 0, t)),
            pl.BlockSpec((2, HALO, LANES), lambda t, m: (0, 0, t)),
            pl.BlockSpec((2, SHORT, LANES), lambda t, m: (0, 0, t)),
            pl.BlockSpec((1, LANES), tile),
        ],
        out_specs=[pl.BlockSpec((count, LANES), tile), pl.BlockSpec((modes, LANES), tile)],
        scratch_shapes=[pltpu.VMEM((3, count + HALO, LANES), F32)],
    )
    return pl.pallas_call(
        functools.partial(mix_kernel, modes, size, ndoc),
        grid_spec=grid_spec,
        out_shape=[jax.ShapeDtypeStruct((count, width), BF16), jax.ShapeDtypeStruct((modes, width), BF16)],
        compiler_params=params(),
        cost_estimate=pl.CostEstimate(flops=60 * count * width, bytes_accessed=8 * count * width, transcendentals=count * width),
        name="mix",
    )(meta, x, halo, taps, rate)


def conv(part, meta, slots, x, halo, taps, mixed, states, rate, scale, skip, residual, modes, size, ndoc):
    _, count, width = x.shape
    nblocks = states.shape[0]
    rows = count // nblocks
    share = width // PARTS
    first = part * (share // LANES)
    tile = lambda t, m, s: (0, first + t)
    deep = lambda t, m, s: (0, 0, first + t)
    grid_spec = pltpu.PrefetchScalarGridSpec(
        num_scalar_prefetch=2,
        grid=(share // LANES,),
        in_specs=[
            pl.BlockSpec((1, count, LANES), deep),
            pl.BlockSpec((1, HALO, LANES), deep),
            pl.BlockSpec((1, SHORT, LANES), deep),
            pl.BlockSpec((count, LANES), tile),
            pl.BlockSpec((nblocks, modes, LANES), deep),
            pl.BlockSpec((1, LANES), tile),
            pl.BlockSpec((1, LANES), tile),
            pl.BlockSpec((1, LANES), tile),
            pl.BlockSpec((count, LANES), tile),
        ],
        out_specs=[
            pl.BlockSpec((nblocks, rows, LANES), lambda t, m, s: (0, 0, t)),
            pl.BlockSpec((rows, LANES), lambda t, m, s: (0, t)),
            pl.BlockSpec((count, LANES), lambda t, m, s: (0, 0)),
        ],
        scratch_shapes=[
            pltpu.VMEM((3, count + HALO, LANES), F32),
            pltpu.VMEM((count // CHUNK, CHUNK, CHUNK), BF16),
            pltpu.VMEM((count // CHUNK, CHUNK, LANES), BF16),
        ],
    )
    return pl.pallas_call(
        functools.partial(conv_kernel, modes, size, ndoc, nblocks),
        grid_spec=grid_spec,
        out_shape=[
            jax.ShapeDtypeStruct((nblocks, rows, share), BF16),
            jax.ShapeDtypeStruct((rows, share), BF16),
            jax.ShapeDtypeStruct((count, LANES), F32),
        ],
        compiler_params=params(),
        cost_estimate=pl.CostEstimate(
            flops=2 * 1152 * count * share, bytes_accessed=8 * count * share, transcendentals=count * share
        ),
        name="conv",
    )(meta, slots, x, halo, taps, mixed, states, rate, scale, skip, residual)


def norm(pick, blocks, spares, scale, gain):
    nblocks, rows, share = blocks[0].shape
    width = share * len(blocks)
    here = lambda i, p: (p[i], 0, 0)
    spare = lambda i, p: (p[nblocks], 0, 0)
    grid_spec = pltpu.PrefetchScalarGridSpec(
        num_scalar_prefetch=1,
        grid=(nblocks,),
        in_specs=[pl.BlockSpec((1, rows, share), here) for _ in blocks]
        + [pl.BlockSpec((1, rows, share), spare) for _ in spares]
        + [pl.BlockSpec((rows, LANES), lambda i, p: (i, 0)), pl.BlockSpec((1, width), lambda i, p: (0, 0))],
        out_specs=pl.BlockSpec((rows, width), lambda i, p: (i, 0)),
    )
    return pl.pallas_call(
        functools.partial(norm_kernel, len(blocks)),
        grid_spec=grid_spec,
        out_shape=jax.ShapeDtypeStruct((nblocks * rows, width), BF16),
        compiler_params=params(),
        cost_estimate=pl.CostEstimate(flops=3 * nblocks * rows * width, bytes_accessed=4 * nblocks * rows * width, transcendentals=0),
        name="norm",
    )(pick, *blocks, *spares, scale, gain)


def on_device(features, residual, short_taps, rates, residues, skip, gain, lengths, owner):
    count, _, width = features.shape
    groups, modes = rates.shape
    size = width // groups
    ndoc = lengths.shape[0]
    nblocks = lax.axis_size("ctx")
    where = lax.axis_index("ctx")
    x = jnp.transpose(features, (1, 0, 2))
    pairs = [(i, i + 1) for i in range(nblocks - 1)]
    halo = lax.ppermute(x[:, count - HALO :], "ctx", pairs)

    meta = jnp.concatenate([(where * count)[None], lengths, where[None]]).astype(jnp.int32)
    rate = rates.reshape(1, groups * modes)
    scale = (residues * jnp.sqrt(1.0 - jnp.exp(-2.0 * rates))).reshape(1, groups * modes)

    table = owner.reshape(nblocks, nblocks)
    ids = jnp.arange(nblocks, dtype=jnp.int32)
    mine = lax.dynamic_index_in_dim(table, where, 0, keepdims=False)
    twice = jnp.any((mine[:, None] == mine[None, :]) & (ids[None, :] < ids[:, None]), 1)
    slots = jnp.where(twice, nblocks, mine).astype(jnp.int32)
    source = jnp.sum((table == where).astype(jnp.int32) * ids[:, None], 0)
    spare_block = jnp.sum(jnp.where(twice, ids, 0))
    spare_source = jnp.sum(jnp.where(twice, source, 0))
    pick = jnp.concatenate([source, jnp.broadcast_to(spare_source, (nblocks,)), spare_block[None]]).astype(jnp.int32)

    mixed, state = mix(meta, x[1:], halo[1:], short_taps[1:], rate, modes, size, ndoc)
    states = lax.all_gather(state, "ctx", axis=0)
    blocks, spares, squares = [], [], 0.0
    for part in range(PARTS):
        out, spare, part_squares = conv(
            part, meta, slots, x, halo, short_taps, mixed, states, rate, scale,
            skip.reshape(1, width), residual, modes, size, ndoc,
        )
        blocks.append(lax.all_to_all(out, "ctx", split_axis=0, concat_axis=0, tiled=True))
        spares.append(lax.all_gather(spare, "ctx", axis=0))
        squares = squares + part_squares
    squares = jnp.sum(squares, 1)
    everyone = lax.all_gather(squares, ("ctx", "mp"), axis=0)
    rows = count // nblocks
    full = jnp.sum(everyone.reshape(nblocks, -1, nblocks, rows), 1)
    chosen = jnp.sum(jnp.where((source[None, :] == ids[:, None])[:, :, None], full, 0.0), 0)
    inverse = lax.rsqrt(chosen / (width * lax.axis_size("mp")) + EPS).reshape(count, 1)
    return norm(pick, blocks, spares, jnp.broadcast_to(inverse, (count, LANES)), gain.reshape(1, width))


def solution(mesh):
    return jax.shard_map(
        on_device,
        mesh=mesh,
        in_specs=(
            P("ctx", None, "mp"),
            P("ctx", "mp"),
            P(None, None, "mp"),
            P("mp", None),
            P("mp", None),
            P("mp"),
            P("mp"),
            P(),
            P(),
        ),
        out_specs=P("ctx", "mp"),
        check_vma=False,
    )
```

```python
import functools

import jax
import jax.numpy as jnp
from jax import lax
from jax.experimental import pallas as pl
from jax.experimental.pallas import tpu as pltpu
from jax.sharding import PartitionSpec as P

SHORT = 7
LANES = 128
CHUNK = 128
HALO = 8
EPS = 1e-06
PARTS = 2
WIDE = 512
SPAN = 64
F32 = jnp.float32
BF16 = jnp.bfloat16
VMEM_LIMIT = 48 * 1024 * 1024


def iota(shape, dim):
    return lax.broadcasted_iota(jnp.int32, shape, dim)


def document(ends, positions):
    total = jnp.zeros(positions.shape, jnp.int32)
    for end in ends:
        total = total + (positions >= end).astype(jnp.int32)
    return total


def scalar_document(ends, position):
    total = jnp.int32(0)
    for end in ends:
        total = total + (position >= end).astype(jnp.int32)
    return jnp.where(position < 0, -1, total)


def running_ends(meta_ref, ndoc):
    ends, total = [], jnp.int32(0)
    for j in range(ndoc):
        total = total + meta_ref[1 + j]
        ends.append(total)
    return ends


def write_lag_masks(mask_ref, ends, base):
    rows = mask_ref.shape[1]
    here = document(ends, base - HALO + iota((rows, LANES), 0)).astype(F32)
    for lag in (1, 2, 3):
        mask_ref[lag - 1] = jnp.where(pltpu.roll(here, lag, 0) == here, 1.0, 0.0).astype(F32)


def short_conv(ext, taps, masks):
    def back(value, lag):
        return pltpu.roll(value, lag, 0) * masks[lag - 1]

    one, two = back(ext, 1), back(ext, 2)
    far = ext * taps[6]
    middle = ext * taps[3] + one * taps[4] + two * taps[5] + back(far, 3)
    near = ext * taps[0] + one * taps[1] + two * taps[2] + back(middle, 3)
    return near[HALO:]


def extended(x_ref, halo_ref, which, start, lanes):
    rows = x_ref[which, start : start + SPAN, lanes].astype(F32)
    if start == 0:
        ahead = halo_ref[which, :, lanes].astype(F32)
    else:
        ahead = x_ref[which, start - 16 : start, lanes].astype(F32)[16 - HALO :]
    return jnp.concatenate([ahead, rows], 0)


def tap_rows(taps_ref, which, lanes):
    return [taps_ref[which, j : j + 1, lanes] for j in range(SHORT)]


def lag_masks(mask_ref, start):
    return [mask_ref[l, start : start + SPAN + HALO, :] for l in range(3)]


def group_mask(modes, size):
    return (iota((LANES, LANES), 0) // modes) == (iota((LANES, LANES), 1) // size)


def each_tile(width, body):
    def step(t, carry):
        body(pl.ds(pl.multiple_of(t * LANES, LANES), LANES))
        return carry

    lax.fori_loop(0, width // LANES, step, 0)


def mix_kernel(modes, size, ndoc, meta_ref, x_ref, halo_ref, taps_ref, rate_ref, mixed_ref, state_ref, mask_ref, tail_ref):
    _, count, width = x_ref.shape
    chunks = count // CHUNK
    base = meta_ref[0]
    ends = running_ends(meta_ref, ndoc)

    @pl.when(pl.program_id(0) == 0)
    def _():
        write_lag_masks(mask_ref, ends, base)
        last = scalar_document(ends, base + count - 1)
        tail = document(ends, base + iota((8, count), 1)) == last
        tail_ref[...] = jnp.where(tail, 1.0, 0.0).astype(F32)

    def tile(lanes):
        key_taps, value_taps = tap_rows(taps_ref, 0, lanes), tap_rows(taps_ref, 1, lanes)
        for start in range(0, count, SPAN):
            masks = lag_masks(mask_ref, start)
            key = short_conv(extended(x_ref, halo_ref, 0, start, lanes), key_taps, masks)
            value = short_conv(extended(x_ref, halo_ref, 1, start, lanes), value_taps, masks)
            mixed_ref[start : start + SPAN, lanes] = (key * value).astype(BF16)
        rate = jnp.broadcast_to(rate_ref[:, lanes], (LANES, LANES)).T
        leave = jnp.exp(-rate * (CHUNK - 1 - iota((LANES, CHUNK), 1)).astype(F32))
        whole = jnp.exp(-rate * CHUNK)
        spans = []
        for chunk in reversed(range(chunks)):
            tail = tail_ref[0:1, chunk * CHUNK : (chunk + 1) * CHUNK]
            spans.append((leave * tail).astype(BF16))
            leave = leave * whole
        full = jnp.dot(jnp.concatenate(spans[::-1], 1), mixed_ref[:, lanes], preferred_element_type=F32)
        full = jnp.where(group_mask(modes, size), full, 0.0)
        state_ref[:, lanes] = jnp.sum(full.reshape(LANES // modes, modes, LANES), 0).astype(BF16)

    each_tile(width, tile)


def conv_kernel(
    modes, size, ndoc, nblocks,
    meta_ref, slot_ref,
    x_ref, halo_ref, taps_ref, mixed_ref, states_ref, rate_ref, scale_ref, skip_ref, residual_ref,
    out_ref, spare_ref, squares_ref,
    mask_ref, same_ref, keep_ref, tail_ref,
):
    count, width = mixed_ref.shape
    chunks = count // CHUNK
    rows = count // nblocks
    base = meta_ref[0]
    where = meta_ref[1 + ndoc]
    ends = running_ends(meta_ref, ndoc)

    @pl.when(pl.program_id(0) == 0)
    def _():
        write_lag_masks(mask_ref, ends, base)
        squares_ref[...] = jnp.zeros_like(squares_ref)
        for chunk in range(chunks):
            start = base + chunk * CHUNK
            down, along = iota((CHUNK, CHUNK), 0), iota((CHUNK, CHUNK), 1)
            here, there = document(ends, start + down), document(ends, start + along)
            linked = (here == there) & (along <= down)
            same_ref[chunk] = jnp.where(linked, 1.0, 0.0).astype(BF16)
            carried = here == scalar_document(ends, start - 1)
            keep_ref[chunk] = jnp.where(carried, 1.0, 0.0).astype(BF16)
            last = scalar_document(ends, start + CHUNK - 1)
            tail_ref[chunk] = jnp.where(there == last, 1.0, 0.0).astype(F32)

    groups = LANES // modes
    before = scalar_document(ends, base - 1)
    first = jnp.int32(0)
    for v in range(nblocks):
        first = first + (scalar_document(ends, (v + 1) * count - 1) < before).astype(jnp.int32)

    def tile(lanes):
        rate_row, scale_row = rate_ref[:, lanes], scale_ref[:, lanes]
        down = iota((CHUNK, LANES), 0)
        along = iota((LANES, CHUNK), 1)
        lags = jnp.where(down == 0, 0, CHUNK - down).astype(F32)
        terms = scale_row * jnp.exp(-rate_row * lags)
        pick = (iota((groups, LANES), 1) // modes == iota((groups, LANES), 0)).astype(F32)
        line = lax.dot_general(
            pick, terms, (((1,), (1,)), ((), ())), preferred_element_type=F32, precision=lax.Precision.HIGHEST
        )
        toeplitz = []
        for g in range(groups):
            top = pltpu.roll(jnp.broadcast_to(line[g : g + 1, :], (8, CHUNK)), 0, 1, stride=1, stride_axis=0)
            parts = [top] + [pltpu.roll(top, 8 * k, 1) for k in range(1, CHUNK // 8)]
            toeplitz.append(jnp.concatenate(parts, 0).astype(BF16))
        entry = (scale_row * jnp.exp(-rate_row * (down + 1).astype(F32))).astype(BF16)
        rate = jnp.broadcast_to(rate_row, (LANES, LANES)).T
        leave = jnp.exp(-rate * (CHUNK - 1 - along).astype(F32))
        whole = jnp.exp(-rate * CHUNK)
        inside = group_mask(modes, size)

        def gather(v, total):
            weight = jnp.exp(-rate * ((where - 1 - v) * count).astype(F32))
            piece = jnp.concatenate([states_ref[v, :, lanes].astype(F32)] * groups, 0)
            return total + jnp.where(inside, piece * weight, 0.0)

        state = lax.fori_loop(first, where, gather, jnp.zeros((LANES, LANES), F32))

        taps = tap_rows(taps_ref, 0, lanes)
        skip = skip_ref[:, lanes]
        lane_group = iota((CHUNK, LANES), 1) // size
        for chunk in range(chunks):
            start = chunk * CHUNK
            mixed = mixed_ref[start : start + CHUNK, lanes]
            same = same_ref[chunk]
            left = jnp.concatenate([t * same for t in toeplitz] + [entry * keep_ref[chunk]], 1)
            right = jnp.concatenate(
                [jnp.where(lane_group == g, mixed, jnp.zeros_like(mixed)) for g in range(groups)]
                + [state.astype(BF16)],
                0,
            )
            longer = jnp.dot(left, right, preferred_element_type=F32)
            if chunk + 1 < chunks:
                fresh = jnp.dot((leave * tail_ref[chunk]).astype(BF16), mixed, preferred_element_type=F32)
                last = scalar_document(ends, base + start + CHUNK - 1)
                held = scalar_document(ends, base + start - 1) == last
                state = jnp.where(held, whole * state, 0.0) + jnp.where(inside, fresh, 0.0)
            body = longer + skip * mixed.astype(F32)
            for half in range(start, start + CHUNK, SPAN):
                gate = short_conv(extended(x_ref, halo_ref, 0, half, lanes), taps, lag_masks(mask_ref, half))
                inner = body[half - start : half - start + SPAN]
                summed = residual_ref[half : half + SPAN, lanes].astype(F32) + gate * inner
                squares_ref[half : half + SPAN, :] += summed * summed
                rounded = summed.astype(BF16)
                for b in range(SPAN // rows):
                    out_ref[slot_ref[half // rows + b], :, lanes] = rounded[b * rows : (b + 1) * rows]

    each_tile(width, tile)
    spare_ref[...] = out_ref[slot_ref[nblocks]]


def norm_kernel(parts, pick_ref, *refs):
    blocks = refs[:parts]
    spare_ref, sums_ref, lane_source_ref, gain_ref, out_ref, scale_ref = refs[parts:]
    nblocks, rows, share = blocks[0].shape
    count, width = out_ref.shape
    total = jnp.zeros((1, count), F32)
    for s in range(nblocks):
        total = total + jnp.where(lane_source_ref[...] == s, sums_ref[s : s + 1, :], 0.0)
    inverse = lax.rsqrt(total / pick_ref[2 * nblocks + 1].astype(F32) + EPS)
    for start in range(0, count, LANES):
        scale_ref[start : start + LANES, :] = jnp.broadcast_to(inverse[:, start : start + LANES], (LANES, LANES)).T

    def block(i, carry):
        rows_out = pl.ds(pl.multiple_of(i * rows, rows), rows)
        scale = scale_ref[rows_out, :]
        is_spare = pick_ref[2 * nblocks] == i
        for part in range(parts):
            for low in range(0, share, LANES):
                outs = slice(part * share + low, part * share + low + LANES)
                value = blocks[part][pick_ref[i], :, low : low + LANES].astype(F32)
                value = jnp.where(is_spare, spare_ref[:, outs].astype(F32), value)
                out_ref[rows_out, outs] = (value * scale * gain_ref[:, outs]).astype(BF16)
        return carry

    lax.fori_loop(0, nblocks, block, 0)


def params():
    return pltpu.CompilerParams(dimension_semantics=("arbitrary",), vmem_limit_bytes=VMEM_LIMIT)


def mix(meta, x, halo, taps, rate, modes, size, ndoc):
    _, count, width = x.shape
    wide = min(WIDE, width)
    tile = lambda t, m: (0, t)
    deep = lambda t, m: (0, 0, t)
    grid_spec = pltpu.PrefetchScalarGridSpec(
        num_scalar_prefetch=1,
        grid=(width // wide,),
        in_specs=[
            pl.BlockSpec((2, count, wide), deep),
            pl.BlockSpec((2, HALO, wide), deep),
            pl.BlockSpec((2, SHORT, wide), deep),
            pl.BlockSpec((1, wide), tile),
        ],
        out_specs=[pl.BlockSpec((count, wide), tile), pl.BlockSpec((modes, wide), tile)],
        scratch_shapes=[pltpu.VMEM((3, count + HALO, LANES), F32), pltpu.VMEM((8, count), F32)],
    )
    return pl.pallas_call(
        functools.partial(mix_kernel, modes, size, ndoc),
        grid_spec=grid_spec,
        out_shape=[jax.ShapeDtypeStruct((count, width), BF16), jax.ShapeDtypeStruct((modes, width), BF16)],
        compiler_params=params(),
        cost_estimate=pl.CostEstimate(flops=60 * count * width, bytes_accessed=8 * count * width, transcendentals=count * width),
        name="mix",
    )(meta, x, halo, taps, rate)


def conv(part, meta, slots, x, halo, taps, mixed, states, rate, scale, skip, residual, modes, size, ndoc):
    _, count, width = x.shape
    nblocks = states.shape[0]
    rows = count // nblocks
    share = width // PARTS
    wide = min(WIDE, share)
    first = part * (share // wide)
    tile = lambda t, m, s: (0, first + t)
    deep = lambda t, m, s: (0, 0, first + t)
    grid_spec = pltpu.PrefetchScalarGridSpec(
        num_scalar_prefetch=2,
        grid=(share // wide,),
        in_specs=[
            pl.BlockSpec((1, count, wide), deep),
            pl.BlockSpec((1, HALO, wide), deep),
            pl.BlockSpec((1, SHORT, wide), deep),
            pl.BlockSpec((count, wide), tile),
            pl.BlockSpec((nblocks, modes, wide), deep),
            pl.BlockSpec((1, wide), tile),
            pl.BlockSpec((1, wide), tile),
            pl.BlockSpec((1, wide), tile),
            pl.BlockSpec((count, wide), tile),
        ],
        out_specs=[
            pl.BlockSpec((nblocks, rows, wide), lambda t, m, s: (0, 0, t)),
            pl.BlockSpec((rows, wide), lambda t, m, s: (0, t)),
            pl.BlockSpec((count, LANES), lambda t, m, s: (0, 0)),
        ],
        scratch_shapes=[
            pltpu.VMEM((3, count + HALO, LANES), F32),
            pltpu.VMEM((count // CHUNK, CHUNK, CHUNK), BF16),
            pltpu.VMEM((count // CHUNK, CHUNK, LANES), BF16),
            pltpu.VMEM((count // CHUNK, LANES, CHUNK), F32),
        ],
    )
    return pl.pallas_call(
        functools.partial(conv_kernel, modes, size, ndoc, nblocks),
        grid_spec=grid_spec,
        out_shape=[
            jax.ShapeDtypeStruct((nblocks, rows, share), BF16),
            jax.ShapeDtypeStruct((rows, share), BF16),
            jax.ShapeDtypeStruct((count, LANES), F32),
        ],
        compiler_params=params(),
        cost_estimate=pl.CostEstimate(
            flops=2 * 1152 * count * share, bytes_accessed=8 * count * share, transcendentals=count * share
        ),
        name="conv",
    )(meta, slots, x, halo, taps, mixed, states, rate, scale, skip, residual)


def norm(pick, blocks, spare, sums, lane_source, gain):
    nblocks, rows, share = blocks[0].shape
    count, width = nblocks * rows, share * len(blocks)
    vmem = pl.BlockSpec(memory_space=pltpu.VMEM)
    return pl.pallas_call(
        functools.partial(norm_kernel, len(blocks)),
        in_specs=[pl.BlockSpec(memory_space=pltpu.SMEM)] + [vmem] * (len(blocks) + 4),
        out_specs=vmem,
        out_shape=jax.ShapeDtypeStruct((count, width), BF16),
        scratch_shapes=[pltpu.VMEM((count, LANES), F32)],
        compiler_params=pltpu.CompilerParams(vmem_limit_bytes=VMEM_LIMIT),
        cost_estimate=pl.CostEstimate(flops=3 * count * width, bytes_accessed=4 * count * width, transcendentals=0),
        name="norm",
    )(pick, *blocks, spare, sums, lane_source, gain)


def to_everyone(value, axis):
    copies = jnp.broadcast_to(value[None], (lax.axis_size(axis),) + value.shape)
    return lax.all_to_all(copies, axis, split_axis=0, concat_axis=0, tiled=True)


def on_device(features, residual, short_taps, rates, residues, skip, gain, lengths, owner):
    count, _, width = features.shape
    groups, modes = rates.shape
    size = width // groups
    ndoc = lengths.shape[0]
    nblocks = lax.axis_size("ctx")
    rows = count // nblocks
    where = lax.axis_index("ctx")
    x = jnp.transpose(features, (1, 0, 2))
    pairs = [(i, i + 1) for i in range(nblocks - 1)]
    halo = lax.ppermute(x[:, count - HALO :], "ctx", pairs)

    meta = jnp.concatenate([(where * count)[None], lengths, where[None]]).astype(jnp.int32)
    rate = rates.reshape(1, groups * modes)
    scale = (residues * jnp.sqrt(1.0 - jnp.exp(-2.0 * rates))).reshape(1, groups * modes)

    table = owner.reshape(nblocks, nblocks)
    ids = jnp.arange(nblocks, dtype=jnp.int32)
    mine = lax.dynamic_index_in_dim(table, where, 0, keepdims=False)
    twice = jnp.any((mine[:, None] == mine[None, :]) & (ids[None, :] < ids[:, None]), 1)
    unused = nblocks * (nblocks - 1) // 2 - jnp.sum(jnp.where(twice, 0, mine))
    slots = jnp.concatenate([jnp.where(twice, unused, mine), unused[None]]).astype(jnp.int32)
    source = jnp.sum((table == where).astype(jnp.int32) * ids[:, None], 0)
    spare_block = jnp.sum(jnp.where(twice, ids, 0))
    spare_shift = jnp.sum(jnp.where(twice, table[0], 0))
    whole_width = jnp.full((1,), width * lax.axis_size("mp"), jnp.int32)
    pick = jnp.concatenate([source, source, spare_block[None], whole_width]).astype(jnp.int32)

    mixed, state = mix(meta, x[1:], halo[1:], short_taps[1:], rate, modes, size, ndoc)
    states = to_everyone(state, "ctx")
    blocks, spares, squares = [], [], 0.0
    for part in range(PARTS):
        out, spare, part_squares = conv(
            part, meta, slots, x, halo, short_taps, mixed, states, rate, scale,
            skip.reshape(1, width), residual, modes, size, ndoc,
        )
        blocks.append(lax.all_to_all(out, "ctx", split_axis=0, concat_axis=0, tiled=True))
        spares.append(spare)
        squares = squares + part_squares
    sums = to_everyone(lax.psum(jnp.sum(squares, 1), "mp"), "ctx")

    def moved(by):
        return lambda value: lax.ppermute(value, "ctx", [(s, (s + by) % nblocks) for s in range(nblocks)])

    spare = lax.switch(spare_shift, [lambda value: value] + [moved(d) for d in range(1, nblocks)], jnp.concatenate(spares, 1))
    lane_source = jnp.repeat(source, rows).reshape(1, count)
    return norm(pick, blocks, spare, sums, lane_source, gain.reshape(1, width))


def solution(mesh):
    return jax.shard_map(
        on_device,
        mesh=mesh,
        in_specs=(
            P("ctx", None, "mp"),
            P("ctx", "mp"),
            P(None, None, "mp"),
            P("mp", None),
            P("mp", None),
            P("mp"),
            P("mp"),
            P(),
            P(),
        ),
        out_specs=P("ctx", "mp"),
        check_vma=False,
    )
```

```python
import functools
import math

import jax
import jax.numpy as jnp
from jax import lax
from jax.experimental import pallas as pl
from jax.experimental.pallas import tpu as pltpu
from jax.sharding import PartitionSpec as P

SHORT = 7
LANES = 128
CHUNK = 128
HALO = 8
EPS = 1e-06
SPLIT = (2, 3, 3)
WIDE = 512
SPAN = 64
F32 = jnp.float32
BF16 = jnp.bfloat16
VMEM_LIMIT = 48 * 1024 * 1024


def iota(shape, dim):
    return lax.broadcasted_iota(jnp.int32, shape, dim)


def document(ends, positions):
    total = jnp.zeros(positions.shape, jnp.int32)
    for end in ends:
        total = total + (positions >= end).astype(jnp.int32)
    return total


def scalar_document(ends, position):
    total = jnp.int32(0)
    for end in ends:
        total = total + (position >= end).astype(jnp.int32)
    return jnp.where(position < 0, -1, total)


def running_ends(meta_ref, ndoc):
    ends, total = [], jnp.int32(0)
    for j in range(ndoc):
        total = total + meta_ref[1 + j]
        ends.append(total)
    return ends


def write_lag_masks(mask_ref, ends, base):
    rows = mask_ref.shape[1]
    here = document(ends, base - HALO + iota((rows, LANES), 0)).astype(F32)
    for lag in (1, 2, 3):
        mask_ref[lag - 1] = jnp.where(pltpu.roll(here, lag, 0) == here, 1.0, 0.0).astype(F32)


def short_conv(ext, taps, masks):
    def back(value, lag):
        return pltpu.roll(value, lag, 0) * masks[lag - 1]

    one, two = back(ext, 1), back(ext, 2)
    far = ext * taps[6]
    middle = ext * taps[3] + one * taps[4] + two * taps[5] + back(far, 3)
    near = ext * taps[0] + one * taps[1] + two * taps[2] + back(middle, 3)
    return near[HALO:]


def extended(x_ref, halo_ref, which, start, lanes):
    rows = x_ref[0, start : start + SPAN, lanes].astype(F32)
    if start == 0:
        ahead = halo_ref[which, :, lanes].astype(F32)
    else:
        ahead = x_ref[0, start - 16 : start, lanes].astype(F32)[16 - HALO :]
    return jnp.concatenate([ahead, rows], 0)


def tap_rows(taps_ref, which, lanes):
    return [taps_ref[which, j : j + 1, lanes] for j in range(SHORT)]


def lag_masks(mask_ref, start):
    return [mask_ref[l, start : start + SPAN + HALO, :] for l in range(3)]


def group_mask(modes, size):
    return (iota((LANES, LANES), 0) // modes) == (iota((LANES, LANES), 1) // size)


def each_tile(width, body):
    def step(t, carry):
        body(pl.ds(pl.multiple_of(t * LANES, LANES), LANES))
        return carry

    lax.fori_loop(0, width // LANES, step, 0)


def mix_kernel(
    modes, size, ndoc,
    meta_ref, key_ref, value_ref, halo_ref, taps_ref, rate_ref,
    mixed_ref, state_ref,
    mask_ref, tail_ref,
):
    _, count, width = key_ref.shape
    chunks = count // CHUNK
    base = meta_ref[0]
    ends = running_ends(meta_ref, ndoc)

    @pl.when(pl.program_id(0) == 0)
    def _():
        write_lag_masks(mask_ref, ends, base)
        last = scalar_document(ends, base + count - 1)
        tail = document(ends, base + iota((8, count), 1)) == last
        tail_ref[...] = jnp.where(tail, 1.0, 0.0).astype(F32)

    def tile(lanes):
        key_taps, value_taps = tap_rows(taps_ref, 1, lanes), tap_rows(taps_ref, 2, lanes)
        for start in range(0, count, SPAN):
            masks = lag_masks(mask_ref, start)
            key = short_conv(extended(key_ref, halo_ref, 1, start, lanes), key_taps, masks)
            value = short_conv(extended(value_ref, halo_ref, 2, start, lanes), value_taps, masks)
            mixed_ref[start : start + SPAN, lanes] = (key * value).astype(BF16)
        rate = jnp.broadcast_to(rate_ref[:, lanes], (LANES, LANES)).T
        leave = jnp.exp(-rate * (CHUNK - 1 - iota((LANES, CHUNK), 1)).astype(F32))
        whole = jnp.exp(-rate * CHUNK)
        spans = []
        for chunk in reversed(range(chunks)):
            tail = tail_ref[0:1, chunk * CHUNK : (chunk + 1) * CHUNK]
            spans.append((leave * tail).astype(BF16))
            leave = leave * whole
        full = jnp.dot(jnp.concatenate(spans[::-1], 1), mixed_ref[:, lanes], preferred_element_type=F32)
        full = jnp.where(group_mask(modes, size), full, 0.0)
        state_ref[:, lanes] = jnp.sum(full.reshape(LANES // modes, modes, LANES), 0).astype(BF16)

    each_tile(width, tile)


def conv_kernel(
    modes, size, ndoc, nblocks,
    meta_ref, slot_ref,
    x_ref, halo_ref, taps_ref, mixed_ref, states_ref, rate_ref, scale_ref, skip_ref, residual_ref,
    out_ref, spare_ref, squares_ref,
    mask_ref, same_ref, keep_ref, tail_ref,
):
    count, width = mixed_ref.shape
    chunks = count // CHUNK
    rows = count // nblocks
    base = meta_ref[0]
    where = meta_ref[1 + ndoc]
    ends = running_ends(meta_ref, ndoc)

    @pl.when(pl.program_id(0) == 0)
    def _():
        write_lag_masks(mask_ref, ends, base)
        squares_ref[...] = jnp.zeros_like(squares_ref)
        for chunk in range(chunks):
            start = base + chunk * CHUNK
            down, along = iota((CHUNK, CHUNK), 0), iota((CHUNK, CHUNK), 1)
            here, there = document(ends, start + down), document(ends, start + along)
            linked = (here == there) & (along <= down)
            same_ref[chunk] = jnp.where(linked, 1.0, 0.0).astype(BF16)
            carried = here == scalar_document(ends, start - 1)
            keep_ref[chunk] = jnp.where(carried, 1.0, 0.0).astype(BF16)
            last = scalar_document(ends, start + CHUNK - 1)
            tail_ref[chunk] = jnp.where(there == last, 1.0, 0.0).astype(F32)

    groups = LANES // modes
    before = scalar_document(ends, base - 1)
    first = jnp.int32(0)
    for v in range(nblocks):
        first = first + (scalar_document(ends, (v + 1) * count - 1) < before).astype(jnp.int32)

    def tile(lanes):
        rate_row, scale_row = rate_ref[:, lanes], scale_ref[:, lanes]
        down = iota((CHUNK, LANES), 0)
        along = iota((LANES, CHUNK), 1)
        lags = jnp.where(down == 0, 0, CHUNK - down).astype(F32)
        terms = scale_row * jnp.exp(-rate_row * lags)
        pick = (iota((groups, LANES), 1) // modes == iota((groups, LANES), 0)).astype(F32)
        line = lax.dot_general(
            pick, terms, (((1,), (1,)), ((), ())), preferred_element_type=F32, precision=lax.Precision.HIGHEST
        )
        toeplitz = []
        for g in range(groups):
            top = pltpu.roll(jnp.broadcast_to(line[g : g + 1, :], (8, CHUNK)), 0, 1, stride=1, stride_axis=0)
            parts = [top] + [pltpu.roll(top, 8 * k, 1) for k in range(1, CHUNK // 8)]
            toeplitz.append(jnp.concatenate(parts, 0).astype(BF16))
        entry = (scale_row * jnp.exp(-rate_row * (down + 1).astype(F32))).astype(BF16)
        rate = jnp.broadcast_to(rate_row, (LANES, LANES)).T
        leave = jnp.exp(-rate * (CHUNK - 1 - along).astype(F32))
        whole = jnp.exp(-rate * CHUNK)
        inside = group_mask(modes, size)

        def gather(v, total):
            weight = jnp.exp(-rate * ((where - 1 - v) * count).astype(F32))
            piece = jnp.concatenate([states_ref[v, :, lanes].astype(F32)] * groups, 0)
            return total + jnp.where(inside, piece * weight, 0.0)

        state = lax.fori_loop(first, where, gather, jnp.zeros((LANES, LANES), F32))

        taps = tap_rows(taps_ref, 0, lanes)
        skip = skip_ref[:, lanes]
        lane_group = iota((CHUNK, LANES), 1) // size
        for chunk in range(chunks):
            start = chunk * CHUNK
            mixed = mixed_ref[start : start + CHUNK, lanes]
            same = same_ref[chunk]
            left = jnp.concatenate([t * same for t in toeplitz] + [entry * keep_ref[chunk]], 1)
            right = jnp.concatenate(
                [jnp.where(lane_group == g, mixed, jnp.zeros_like(mixed)) for g in range(groups)]
                + [state.astype(BF16)],
                0,
            )
            longer = jnp.dot(left, right, preferred_element_type=F32)
            if chunk + 1 < chunks:
                fresh = jnp.dot((leave * tail_ref[chunk]).astype(BF16), mixed, preferred_element_type=F32)
                last = scalar_document(ends, base + start + CHUNK - 1)
                held = scalar_document(ends, base + start - 1) == last
                state = jnp.where(held, whole * state, 0.0) + jnp.where(inside, fresh, 0.0)
            body = longer + skip * mixed.astype(F32)
            for half in range(start, start + CHUNK, SPAN):
                gate = short_conv(extended(x_ref, halo_ref, 0, half, lanes), taps, lag_masks(mask_ref, half))
                inner = body[half - start : half - start + SPAN]
                summed = residual_ref[half : half + SPAN, lanes].astype(F32) + gate * inner
                squares_ref[half : half + SPAN, :] += summed * summed
                rounded = summed.astype(BF16)
                for b in range(SPAN // rows):
                    out_ref[slot_ref[half // rows + b], :, lanes] = rounded[b * rows : (b + 1) * rows]

    each_tile(width, tile)
    spare_ref[...] = out_ref[slot_ref[nblocks]]


def norm_kernel(parts, pick_ref, *refs):
    blocks = refs[:parts]
    spare_ref, gain_ref, out_ref = refs[parts:]
    nblocks, rows, _ = blocks[0].shape
    count, width = out_ref.shape

    def block(i, carry):
        rows_out = pl.ds(pl.multiple_of(i * rows, rows), rows)
        is_spare = pick_ref[nblocks] == i
        source = pick_ref[i]
        halves = jnp.where(is_spare, spare_ref[:, width:].astype(F32), blocks[-1][source, :, -LANES:].astype(F32))
        scale = halves[:, 0:1] + halves[:, 1:2]
        low = 0
        for part in range(parts):
            share = min(blocks[part].shape[2], width - low)
            for lane in range(0, share, LANES):
                outs = slice(low + lane, low + lane + LANES)
                value = blocks[part][source, :, lane : lane + LANES].astype(F32)
                value = jnp.where(is_spare, spare_ref[:, outs].astype(F32), value)
                out_ref[rows_out, outs] = (value * scale * gain_ref[:, outs]).astype(BF16)
            low += share
        return carry

    lax.fori_loop(0, nblocks, block, 0)


def params():
    return pltpu.CompilerParams(dimension_semantics=("arbitrary",), vmem_limit_bytes=VMEM_LIMIT)


def mix(meta, x, halo, taps, rate, modes, size, ndoc):
    _, count, width = x.shape
    wide = min(WIDE, width)
    tile = lambda t, m: (0, t)
    deep = lambda t, m: (0, 0, t)
    grid_spec = pltpu.PrefetchScalarGridSpec(
        num_scalar_prefetch=1,
        grid=(width // wide,),
        in_specs=[
            pl.BlockSpec((1, count, wide), lambda t, m: (1, 0, t)),
            pl.BlockSpec((1, count, wide), lambda t, m: (2, 0, t)),
            pl.BlockSpec((3, HALO, wide), deep),
            pl.BlockSpec((3, SHORT, wide), deep),
            pl.BlockSpec((1, wide), tile),
        ],
        out_specs=[pl.BlockSpec((count, wide), tile), pl.BlockSpec((modes, wide), tile)],
        scratch_shapes=[pltpu.VMEM((3, count + HALO, LANES), F32), pltpu.VMEM((8, count), F32)],
    )
    return pl.pallas_call(
        functools.partial(mix_kernel, modes, size, ndoc),
        grid_spec=grid_spec,
        out_shape=[jax.ShapeDtypeStruct((count, width), BF16), jax.ShapeDtypeStruct((modes, width), BF16)],
        compiler_params=params(),
        cost_estimate=pl.CostEstimate(flops=60 * count * width, bytes_accessed=8 * count * width, transcendentals=count * width),
        name="mix",
    )(meta, x, x, halo, taps, rate)


def conv(low, share, meta, slots, x, halo, taps, mixed, states, rate, scale, skip, residual, modes, size, ndoc):
    _, count, width = x.shape
    nblocks = states.shape[0]
    rows = count // nblocks
    wide = math.gcd(math.gcd(low, share), WIDE)
    first = low // wide
    tile = lambda t, m, s: (0, first + t)
    deep = lambda t, m, s: (0, 0, first + t)
    grid_spec = pltpu.PrefetchScalarGridSpec(
        num_scalar_prefetch=2,
        grid=(share // wide,),
        in_specs=[
            pl.BlockSpec((1, count, wide), deep),
            pl.BlockSpec((1, HALO, wide), deep),
            pl.BlockSpec((1, SHORT, wide), deep),
            pl.BlockSpec((count, wide), tile),
            pl.BlockSpec((nblocks, modes, wide), deep),
            pl.BlockSpec((1, wide), tile),
            pl.BlockSpec((1, wide), tile),
            pl.BlockSpec((1, wide), tile),
            pl.BlockSpec((count, wide), tile),
        ],
        out_specs=[
            pl.BlockSpec((nblocks, rows, wide), lambda t, m, s: (0, 0, t)),
            pl.BlockSpec((rows, wide), lambda t, m, s: (0, t)),
            pl.BlockSpec((count, LANES), lambda t, m, s: (0, 0)),
        ],
        scratch_shapes=[
            pltpu.VMEM((3, count + HALO, LANES), F32),
            pltpu.VMEM((count // CHUNK, CHUNK, CHUNK), BF16),
            pltpu.VMEM((count // CHUNK, CHUNK, LANES), BF16),
            pltpu.VMEM((count // CHUNK, LANES, CHUNK), F32),
        ],
    )
    return pl.pallas_call(
        functools.partial(conv_kernel, modes, size, ndoc, nblocks),
        grid_spec=grid_spec,
        out_shape=[
            jax.ShapeDtypeStruct((nblocks, rows, share), BF16),
            jax.ShapeDtypeStruct((rows, share), BF16),
            jax.ShapeDtypeStruct((count, LANES), F32),
        ],
        compiler_params=params(),
        cost_estimate=pl.CostEstimate(
            flops=2 * 1152 * count * share, bytes_accessed=8 * count * share, transcendentals=count * share
        ),
        name="conv",
    )(meta, slots, x, halo, taps, mixed, states, rate, scale, skip, residual)


def norm(pick, blocks, spare, gain):
    nblocks, rows, _ = blocks[0].shape
    count, width = nblocks * rows, gain.shape[1]
    vmem = pl.BlockSpec(memory_space=pltpu.VMEM)
    return pl.pallas_call(
        functools.partial(norm_kernel, len(blocks)),
        in_specs=[pl.BlockSpec(memory_space=pltpu.SMEM)] + [vmem] * (len(blocks) + 2),
        out_specs=vmem,
        out_shape=jax.ShapeDtypeStruct((count, width), BF16),
        compiler_params=pltpu.CompilerParams(vmem_limit_bytes=VMEM_LIMIT),
        cost_estimate=pl.CostEstimate(flops=3 * count * width, bytes_accessed=4 * count * width, transcendentals=0),
        name="norm",
    )(pick, *blocks, spare, gain)


def to_everyone(value, axis):
    copies = jnp.broadcast_to(value[None], (lax.axis_size(axis),) + value.shape)
    return lax.all_to_all(copies, axis, split_axis=0, concat_axis=0, tiled=True)


def on_device(features, residual, short_taps, rates, residues, skip, gain, lengths, owner):
    count, _, width = features.shape
    groups, modes = rates.shape
    size = width // groups
    ndoc = lengths.shape[0]
    nblocks = lax.axis_size("ctx")
    rows = count // nblocks
    where = lax.axis_index("ctx")
    x = jnp.transpose(features, (1, 0, 2))
    pairs = [(i, i + 1) for i in range(nblocks - 1)]
    halo = lax.ppermute(x[:, count - HALO :], "ctx", pairs)

    meta = jnp.concatenate([(where * count)[None], lengths, where[None]]).astype(jnp.int32)
    rate = rates.reshape(1, groups * modes)
    scale = (residues * jnp.sqrt(1.0 - jnp.exp(-2.0 * rates))).reshape(1, groups * modes)

    table = owner.reshape(nblocks, nblocks)
    ids = jnp.arange(nblocks, dtype=jnp.int32)
    mine = lax.dynamic_index_in_dim(table, where, 0, keepdims=False)
    twice = jnp.any((mine[:, None] == mine[None, :]) & (ids[None, :] < ids[:, None]), 1)
    unused = nblocks * (nblocks - 1) // 2 - jnp.sum(jnp.where(twice, 0, mine))
    slots = jnp.concatenate([jnp.where(twice, unused, mine), unused[None]]).astype(jnp.int32)
    source = jnp.sum((table == where).astype(jnp.int32) * ids[:, None], 0)
    spare_block = jnp.sum(jnp.where(twice, ids, 0))
    spare_shift = jnp.sum(jnp.where(twice, table[0], 0))
    pick = jnp.concatenate([source, spare_block[None]]).astype(jnp.int32)

    mixed, state = mix(meta, x, halo, short_taps, rate, modes, size, ndoc)
    states = to_everyone(state, "ctx")
    blocks, spares, squares, low = [], [], 0.0, 0
    for part, eighths in enumerate(SPLIT):
        share = width * eighths // sum(SPLIT)
        out, spare, part_squares = conv(
            low, share, meta, slots, x, halo, short_taps, mixed, states, rate, scale,
            skip.reshape(1, width), residual, modes, size, ndoc,
        )
        spares.append(spare)
        squares = squares + part_squares
        low += share
        if part + 1 == len(SPLIT):
            mean = lax.psum(jnp.sum(squares, 1), "mp") / (width * lax.axis_size("mp"))
            inverse = lax.rsqrt(mean + EPS)
            high = lax.reduce_precision(inverse, 8, 7)
            column = iota((count, LANES), 1)
            halves = jnp.where(column == 0, high[:, None], jnp.where(column == 1, (inverse - high)[:, None], 0.0))
            halves = halves.reshape(nblocks, rows, LANES)
            in_slot = slots[None, :nblocks] == ids[:, None]
            by_slot = jnp.sum(jnp.where(in_slot[:, :, None, None], halves[None], 0.0), 1).astype(BF16)
            spare_halves = jnp.sum(jnp.where(twice[:, None, None], halves, 0.0), 0).astype(BF16)
            out = jnp.concatenate([out, by_slot], 2)
            spares.append(spare_halves)
        if blocks:
            out, blocks[-1] = lax.optimization_barrier((out, blocks[-1]))
        blocks.append(lax.all_to_all(out, "ctx", split_axis=0, concat_axis=0, tiled=True))

    def moved(by):
        return lambda value: lax.ppermute(value, "ctx", [(s, (s + by) % nblocks) for s in range(nblocks)])

    spare = lax.switch(spare_shift, [lambda value: value] + [moved(d) for d in range(1, nblocks)], jnp.concatenate(spares, 1))
    return norm(pick, blocks, spare, gain.reshape(1, width))


def solution(mesh):
    return jax.shard_map(
        on_device,
        mesh=mesh,
        in_specs=(
            P("ctx", None, "mp"),
            P("ctx", "mp"),
            P(None, None, "mp"),
            P("mp", None),
            P("mp", None),
            P("mp"),
            P("mp"),
            P(),
            P(),
        ),
        out_specs=P("ctx", "mp"),
        check_vma=False,
    )
```

```python
import functools
import math

import jax
import jax.numpy as jnp
from jax import lax
from jax.experimental import pallas as pl
from jax.experimental.pallas import tpu as pltpu
from jax.sharding import PartitionSpec as P

SHORT = 7
LANES = 128
CHUNK = 128
HALO = 8
EPS = 1e-06
SPLIT = (3, 5)
WIDE = 512
SPAN = 64
F32 = jnp.float32
BF16 = jnp.bfloat16
VMEM_LIMIT = 60 * 1024 * 1024


def iota(shape, dim):
    return lax.broadcasted_iota(jnp.int32, shape, dim)


def document(ends, positions):
    total = jnp.zeros(positions.shape, jnp.int32)
    for end in ends:
        total = total + (positions >= end).astype(jnp.int32)
    return total


def scalar_document(ends, position):
    total = jnp.int32(0)
    for end in ends:
        total = total + (position >= end).astype(jnp.int32)
    return jnp.where(position < 0, -1, total)


def running_ends(meta_ref, ndoc):
    ends, total = [], jnp.int32(0)
    for j in range(ndoc):
        total = total + meta_ref[1 + j]
        ends.append(total)
    return ends


def write_lag_masks(mask_ref, ends, base):
    rows = mask_ref.shape[1]
    here = document(ends, base - HALO + iota((rows, LANES), 0)).astype(F32)
    for lag in (1, 2, 3):
        mask_ref[lag - 1] = jnp.where(pltpu.roll(here, lag, 0) == here, 1.0, 0.0).astype(F32)


def short_conv(ext, taps, masks):
    def back(value, lag):
        return pltpu.roll(value, lag, 0) * masks[lag - 1]

    one, two = back(ext, 1), back(ext, 2)
    far = ext * taps[6]
    middle = ext * taps[3] + one * taps[4] + two * taps[5] + back(far, 3)
    near = ext * taps[0] + one * taps[1] + two * taps[2] + back(middle, 3)
    return near[HALO:]


def extended(x_ref, halo_ref, which, start, lanes):
    rows = x_ref[0, start : start + SPAN, lanes].astype(F32)
    if start == 0:
        ahead = halo_ref[which, :, lanes].astype(F32)
    else:
        ahead = x_ref[0, start - 16 : start, lanes].astype(F32)[16 - HALO :]
    return jnp.concatenate([ahead, rows], 0)


def tap_rows(taps_ref, which, lanes):
    return [taps_ref[which, j : j + 1, lanes] for j in range(SHORT)]


def lag_masks(mask_ref, start):
    return [mask_ref[l, start : start + SPAN + HALO, :] for l in range(3)]


def group_mask(modes, size):
    return (iota((LANES, LANES), 0) // modes) == (iota((LANES, LANES), 1) // size)


def each_tile(width, body):
    for low in range(0, width, LANES):
        body(slice(low, low + LANES))


def mix_kernel(
    modes, size, ndoc,
    meta_ref, key_ref, value_ref, halo_ref, taps_ref, rate_ref,
    mixed_ref, state_ref,
    mask_ref, tail_ref,
):
    _, count, width = key_ref.shape
    chunks = count // CHUNK
    base = meta_ref[0]
    ends = running_ends(meta_ref, ndoc)

    @pl.when(pl.program_id(0) == 0)
    def _():
        write_lag_masks(mask_ref, ends, base)
        last = scalar_document(ends, base + count - 1)
        tail = document(ends, base + iota((8, count), 1)) == last
        tail_ref[...] = jnp.where(tail, 1.0, 0.0).astype(F32)

    def tile(lanes):
        key_taps, value_taps = tap_rows(taps_ref, 1, lanes), tap_rows(taps_ref, 2, lanes)
        for start in range(0, count, SPAN):
            masks = lag_masks(mask_ref, start)
            key = short_conv(extended(key_ref, halo_ref, 1, start, lanes), key_taps, masks)
            value = short_conv(extended(value_ref, halo_ref, 2, start, lanes), value_taps, masks)
            mixed_ref[start : start + SPAN, lanes] = (key * value).astype(BF16)
        rate = jnp.broadcast_to(rate_ref[:, lanes], (LANES, LANES)).T
        leave = jnp.exp(-rate * (CHUNK - 1 - iota((LANES, CHUNK), 1)).astype(F32))
        whole = jnp.exp(-rate * CHUNK)
        spans = []
        for chunk in reversed(range(chunks)):
            tail = tail_ref[0:1, chunk * CHUNK : (chunk + 1) * CHUNK]
            spans.append((leave * tail).astype(BF16))
            leave = leave * whole
        full = jnp.dot(jnp.concatenate(spans[::-1], 1), mixed_ref[:, lanes], preferred_element_type=F32)
        full = jnp.where(group_mask(modes, size), full, 0.0)
        state = jnp.sum(full.reshape(LANES // modes, modes, LANES), 0).astype(BF16)
        for owner in range(state_ref.shape[0]):
            state_ref[owner, :, lanes] = state

    each_tile(width, tile)


def conv_kernel(
    modes, size, ndoc, nblocks,
    meta_ref, slot_ref,
    x_ref, halo_ref, taps_ref, mixed_ref, states_ref, rate_ref, scale_ref, skip_ref, residual_ref,
    out_ref, spare_ref, squares_ref,
    mask_ref, same_ref, keep_ref, tail_ref,
):
    count, width = mixed_ref.shape
    chunks = count // CHUNK
    rows = count // nblocks
    base = meta_ref[0]
    where = meta_ref[1 + ndoc]
    ends = running_ends(meta_ref, ndoc)

    @pl.when(pl.program_id(0) == 0)
    def _():
        write_lag_masks(mask_ref, ends, base)
        squares_ref[...] = jnp.zeros_like(squares_ref)
        for chunk in range(chunks):
            start = base + chunk * CHUNK
            down, along = iota((CHUNK, CHUNK), 0), iota((CHUNK, CHUNK), 1)
            here, there = document(ends, start + down), document(ends, start + along)
            linked = (here == there) & (along <= down)
            same_ref[chunk] = jnp.where(linked, 1.0, 0.0).astype(BF16)
            carried = here == scalar_document(ends, start - 1)
            keep_ref[chunk] = jnp.where(carried, 1.0, 0.0).astype(BF16)
            last = scalar_document(ends, start + CHUNK - 1)
            tail_ref[chunk] = jnp.where(there == last, 1.0, 0.0).astype(F32)

    groups = LANES // modes
    before = scalar_document(ends, base - 1)
    first = jnp.int32(0)
    for v in range(nblocks):
        first = first + (scalar_document(ends, (v + 1) * count - 1) < before).astype(jnp.int32)

    def tile(lanes):
        rate_row, scale_row = rate_ref[:, lanes], scale_ref[:, lanes]
        rate = jnp.broadcast_to(rate_row, (LANES, LANES)).T
        scale = jnp.broadcast_to(scale_row, (LANES, LANES)).T
        down = iota((CHUNK, LANES), 0)
        along = iota((LANES, CHUNK), 1)
        entry = (scale_row * jnp.exp(-rate_row * (down + 1).astype(F32))).astype(BF16)
        leave = jnp.exp(-rate * (CHUNK - 1 - along).astype(F32))
        whole = jnp.exp(-rate * CHUNK)
        terms = scale * jnp.where(along == 0, 1.0, leave * jnp.exp(-rate))
        toeplitz = []
        for g in range(groups):
            line = jnp.sum(terms[g * modes : (g + 1) * modes], 0, keepdims=True)
            top = pltpu.roll(jnp.broadcast_to(line, (8, CHUNK)), 0, 1, stride=1, stride_axis=0)
            parts = [top] + [pltpu.roll(top, 8 * k, 1) for k in range(1, CHUNK // 8)]
            toeplitz.append(jnp.concatenate(parts, 0).astype(BF16))
        inside = group_mask(modes, size)

        def gather(v, total):
            weight = jnp.exp(-rate * ((where - 1 - v) * count).astype(F32))
            piece = jnp.concatenate([states_ref[v, :, lanes].astype(F32)] * groups, 0)
            return total + jnp.where(inside, piece * weight, 0.0)

        state = lax.fori_loop(first, where, gather, jnp.zeros((LANES, LANES), F32))

        taps = tap_rows(taps_ref, 0, lanes)
        skip = skip_ref[:, lanes]
        lane_group = iota((CHUNK, LANES), 1) // size
        for chunk in range(chunks):
            start = chunk * CHUNK
            mixed = mixed_ref[start : start + CHUNK, lanes]
            same = same_ref[chunk]
            left = jnp.concatenate([t * same for t in toeplitz] + [entry * keep_ref[chunk]], 1)
            right = jnp.concatenate(
                [jnp.where(lane_group == g, mixed, jnp.zeros_like(mixed)) for g in range(groups)]
                + [state.astype(BF16)],
                0,
            )
            longer = jnp.dot(left, right, preferred_element_type=F32)
            if chunk + 1 < chunks:
                fresh = jnp.dot((leave * tail_ref[chunk]).astype(BF16), mixed, preferred_element_type=F32)
                last = scalar_document(ends, base + start + CHUNK - 1)
                held = scalar_document(ends, base + start - 1) == last
                state = jnp.where(held, whole * state, 0.0) + jnp.where(inside, fresh, 0.0)
            body = longer + skip * mixed.astype(F32)
            for half in range(start, start + CHUNK, SPAN):
                gate = short_conv(extended(x_ref, halo_ref, 0, half, lanes), taps, lag_masks(mask_ref, half))
                inner = body[half - start : half - start + SPAN]
                summed = residual_ref[half : half + SPAN, lanes].astype(F32) + gate * inner
                squares_ref[half : half + SPAN, :] += summed * summed
                rounded = summed.astype(BF16)
                for b in range(SPAN // rows):
                    out_ref[slot_ref[half // rows + b], :, lanes] = rounded[b * rows : (b + 1) * rows]

    each_tile(width, tile)
    spare_ref[...] = out_ref[slot_ref[nblocks]]


def norm_kernel(parts, pick_ref, *refs):
    blocks = refs[:parts]
    spare_ref, gain_ref, out_ref = refs[parts:]
    nblocks, rows, _ = blocks[0].shape
    count, width = out_ref.shape

    def block(i, carry):
        rows_out = pl.ds(pl.multiple_of(i * rows, rows), rows)
        is_spare = pick_ref[nblocks] == i
        source = pick_ref[i]
        halves = jnp.where(is_spare, spare_ref[:, width:].astype(F32), blocks[-1][source, :, -LANES:].astype(F32))
        scale = halves[:, 0:1] + halves[:, 1:2]
        low = 0
        for part in range(parts):
            share = min(blocks[part].shape[2], width - low)
            for lane in range(0, share, LANES):
                outs = slice(low + lane, low + lane + LANES)
                value = blocks[part][source, :, lane : lane + LANES].astype(F32)
                value = jnp.where(is_spare, spare_ref[:, outs].astype(F32), value)
                out_ref[rows_out, outs] = (value * scale * gain_ref[:, outs]).astype(BF16)
            low += share
        return carry

    lax.fori_loop(0, nblocks, block, 0)


def params():
    return pltpu.CompilerParams(dimension_semantics=("arbitrary",), vmem_limit_bytes=VMEM_LIMIT)


def mix(low, share, meta, x, halo, taps, rate, modes, size, ndoc, copies):
    _, count, _ = x.shape
    wide = math.gcd(math.gcd(low, share), WIDE)
    first = low // wide
    deep = lambda t, m: (0, 0, first + t)
    grid_spec = pltpu.PrefetchScalarGridSpec(
        num_scalar_prefetch=1,
        grid=(share // wide,),
        in_specs=[
            pl.BlockSpec((1, count, wide), lambda t, m: (1, 0, first + t)),
            pl.BlockSpec((1, count, wide), lambda t, m: (2, 0, first + t)),
            pl.BlockSpec((3, HALO, wide), deep),
            pl.BlockSpec((3, SHORT, wide), deep),
            pl.BlockSpec((1, wide), lambda t, m: (0, first + t)),
        ],
        out_specs=[
            pl.BlockSpec((count, wide), lambda t, m: (0, t)),
            pl.BlockSpec((copies, modes, wide), lambda t, m: (0, 0, t)),
        ],
        scratch_shapes=[pltpu.VMEM((3, count + HALO, LANES), F32), pltpu.VMEM((8, count), F32)],
    )
    return pl.pallas_call(
        functools.partial(mix_kernel, modes, size, ndoc),
        grid_spec=grid_spec,
        out_shape=[
            jax.ShapeDtypeStruct((count, share), BF16),
            jax.ShapeDtypeStruct((copies, modes, share), BF16),
        ],
        compiler_params=params(),
        cost_estimate=pl.CostEstimate(flops=60 * count * share, bytes_accessed=8 * count * share, transcendentals=count * share),
        name="mix",
    )(meta, x, x, halo, taps, rate)


def conv(low, share, room, meta, slots, x, halo, taps, mixed, states, rate, scale, skip, residual, modes, size, ndoc):
    _, count, width = x.shape
    nblocks = states.shape[0]
    rows = count // nblocks
    wide = math.gcd(math.gcd(low, share), WIDE)
    first = low // wide
    tile = lambda t, m, s: (0, first + t)
    deep = lambda t, m, s: (0, 0, first + t)
    grid_spec = pltpu.PrefetchScalarGridSpec(
        num_scalar_prefetch=2,
        grid=(share // wide,),
        in_specs=[
            pl.BlockSpec((1, count, wide), deep),
            pl.BlockSpec((1, HALO, wide), deep),
            pl.BlockSpec((1, SHORT, wide), deep),
            pl.BlockSpec((count, wide), lambda t, m, s: (0, t)),
            pl.BlockSpec((nblocks, modes, wide), lambda t, m, s: (0, 0, t)),
            pl.BlockSpec((1, wide), tile),
            pl.BlockSpec((1, wide), tile),
            pl.BlockSpec((1, wide), tile),
            pl.BlockSpec((count, wide), tile),
        ],
        out_specs=[
            pl.BlockSpec((nblocks, rows, wide), lambda t, m, s: (0, 0, t)),
            pl.BlockSpec((rows, wide), lambda t, m, s: (0, t)),
            pl.BlockSpec((count, LANES), lambda t, m, s: (0, 0)),
        ],
        scratch_shapes=[
            pltpu.VMEM((3, count + HALO, LANES), F32),
            pltpu.VMEM((count // CHUNK, CHUNK, CHUNK), BF16),
            pltpu.VMEM((count // CHUNK, CHUNK, LANES), BF16),
            pltpu.VMEM((count // CHUNK, LANES, CHUNK), F32),
        ],
    )
    return pl.pallas_call(
        functools.partial(conv_kernel, modes, size, ndoc, nblocks),
        grid_spec=grid_spec,
        out_shape=[
            jax.ShapeDtypeStruct((nblocks, rows, share + room), BF16),
            jax.ShapeDtypeStruct((rows, share), BF16),
            jax.ShapeDtypeStruct((count, LANES), F32),
        ],
        compiler_params=params(),
        cost_estimate=pl.CostEstimate(
            flops=2 * 1152 * count * share, bytes_accessed=8 * count * share, transcendentals=count * share
        ),
        name="conv",
    )(meta, slots, x, halo, taps, mixed, states, rate, scale, skip, residual)


def norm(pick, blocks, spare, gain):
    nblocks, rows, _ = blocks[0].shape
    count, width = nblocks * rows, gain.shape[1]
    vmem = pl.BlockSpec(memory_space=pltpu.VMEM)
    return pl.pallas_call(
        functools.partial(norm_kernel, len(blocks)),
        in_specs=[pl.BlockSpec(memory_space=pltpu.SMEM)] + [vmem] * (len(blocks) + 2),
        out_specs=vmem,
        out_shape=jax.ShapeDtypeStruct((count, width), BF16),
        compiler_params=pltpu.CompilerParams(vmem_limit_bytes=VMEM_LIMIT),
        cost_estimate=pl.CostEstimate(flops=3 * count * width, bytes_accessed=4 * count * width, transcendentals=0),
        name="norm",
    )(pick, *blocks, spare, gain)


def on_device(features, residual, short_taps, rates, residues, skip, gain, lengths, owner):
    count, _, width = features.shape
    groups, modes = rates.shape
    size = width // groups
    ndoc = lengths.shape[0]
    nblocks = lax.axis_size("ctx")
    rows = count // nblocks
    where = lax.axis_index("ctx")
    x = jnp.transpose(features, (1, 0, 2))
    pairs = [(i, i + 1) for i in range(nblocks - 1)]
    halo = lax.ppermute(x[:, count - HALO :], "ctx", pairs)

    meta = jnp.concatenate([(where * count)[None], lengths, where[None]]).astype(jnp.int32)
    rate = rates.reshape(1, groups * modes)
    scale = (residues * jnp.sqrt(1.0 - jnp.exp(-2.0 * rates))).reshape(1, groups * modes)

    table = owner.reshape(nblocks, nblocks)
    ids = jnp.arange(nblocks, dtype=jnp.int32)
    mine = lax.dynamic_index_in_dim(table, where, 0, keepdims=False)
    twice = jnp.any((mine[:, None] == mine[None, :]) & (ids[None, :] < ids[:, None]), 1)
    unused = nblocks * (nblocks - 1) // 2 - jnp.sum(jnp.where(twice, 0, mine))
    slots = jnp.concatenate([jnp.where(twice, unused, mine), unused[None]]).astype(jnp.int32)
    source = jnp.sum((table == where).astype(jnp.int32) * ids[:, None], 0)
    spare_block = jnp.sum(jnp.where(twice, ids, 0))
    spare_shift = jnp.sum(jnp.where(twice, table[0], 0))
    pick = jnp.concatenate([source, spare_block[None]]).astype(jnp.int32)

    def exchanged(value):
        return lax.all_to_all(value, "ctx", split_axis=0, concat_axis=0, tiled=True)

    shares = [width * eighths // sum(SPLIT) for eighths in SPLIT]
    lows = [sum(shares[:part]) for part in range(len(shares))]
    mixes = [
        mix(low, share, meta, x, halo, short_taps, rate, modes, size, ndoc, nblocks) for low, share in zip(lows, shares)
    ]
    states = [exchanged(copies) for _, copies in mixes]
    mixed = list(lax.optimization_barrier(tuple(m for m, _ in mixes)))
    blocks, spares, squares = [], [], 0.0
    for part, (low, share) in enumerate(zip(lows, shares)):
        is_last = part + 1 == len(shares)
        out, spare, part_squares = conv(
            low, share, LANES if is_last else 0, meta, slots, x, halo, short_taps, mixed[part], states[part],
            rate, scale, skip.reshape(1, width), residual, modes, size, ndoc,
        )
        spares.append(spare)
        squares = squares + part_squares
        if is_last:
            mean = lax.psum(jnp.sum(squares, 1), "mp") / (width * lax.axis_size("mp"))
            inverse = lax.rsqrt(mean + EPS)
            high = lax.reduce_precision(inverse, 8, 7)
            column = iota((count, LANES), 1)
            halves = jnp.where(column == 0, high[:, None], jnp.where(column == 1, (inverse - high)[:, None], 0.0))
            halves = halves.reshape(nblocks, rows, LANES)
            in_slot = slots[None, :nblocks] == ids[:, None]
            by_slot = jnp.sum(jnp.where(in_slot[:, :, None, None], halves[None], 0.0), 1).astype(BF16)
            spare_halves = jnp.sum(jnp.where(twice[:, None, None], halves, 0.0), 0).astype(BF16)
            out = lax.dynamic_update_slice(out, by_slot, (0, 0, share))
            spares.append(spare_halves)
        if blocks:
            out, blocks[-1] = lax.optimization_barrier((out, blocks[-1]))
        blocks.append(exchanged(out))

    def moved(by):
        return lambda value: lax.ppermute(value, "ctx", [(s, (s + by) % nblocks) for s in range(nblocks)])

    spare = lax.switch(spare_shift, [lambda value: value] + [moved(d) for d in range(1, nblocks)], jnp.concatenate(spares, 1))
    return norm(pick, blocks, spare, gain.reshape(1, width))


def solution(mesh):
    return jax.shard_map(
        on_device,
        mesh=mesh,
        in_specs=(
            P("ctx", None, "mp"),
            P("ctx", "mp"),
            P(None, None, "mp"),
            P("mp", None),
            P("mp", None),
            P("mp"),
            P("mp"),
            P(),
            P(),
        ),
        out_specs=P("ctx", "mp"),
        check_vma=False,
    )
```

```python
import functools
import math

import jax
import jax.numpy as jnp
from jax import lax
from jax.experimental import pallas as pl
from jax.experimental.pallas import tpu as pltpu
from jax.sharding import PartitionSpec as P

SHORT = 7
LANES = 128
CHUNK = 128
HALO = 8
EPS = 1e-06
SPLIT = (3, 5)
WIDE = 512
SPAN = 64
F32 = jnp.float32
BF16 = jnp.bfloat16
VMEM_LIMIT = 60 * 1024 * 1024


def iota(shape, dim):
    return lax.broadcasted_iota(jnp.int32, shape, dim)


def document(ends, positions):
    total = jnp.zeros(positions.shape, jnp.int32)
    for end in ends:
        total = total + (positions >= end).astype(jnp.int32)
    return total


def scalar_document(ends, position):
    total = jnp.int32(0)
    for end in ends:
        total = total + (position >= end).astype(jnp.int32)
    return jnp.where(position < 0, -1, total)


def running_ends(meta_ref, ndoc):
    ends, total = [], jnp.int32(0)
    for j in range(ndoc):
        total = total + meta_ref[1 + j]
        ends.append(total)
    return ends


def write_lag_masks(mask_ref, ends, base):
    rows = mask_ref.shape[1]
    here = document(ends, base - HALO + iota((rows, LANES), 0)).astype(F32)
    for lag in (1, 2, 3):
        mask_ref[lag - 1] = jnp.where(pltpu.roll(here, lag, 0) == here, 1.0, 0.0).astype(F32)


def short_conv(ext, taps, masks):
    def back(value, lag):
        return pltpu.roll(value, lag, 0) * masks[lag - 1]

    one, two = back(ext, 1), back(ext, 2)
    far = ext * taps[6]
    middle = ext * taps[3] + one * taps[4] + two * taps[5] + back(far, 3)
    near = ext * taps[0] + one * taps[1] + two * taps[2] + back(middle, 3)
    return near[HALO:]


def extended(x_ref, halo_ref, which, start, lanes):
    rows = x_ref[0, start : start + SPAN, lanes].astype(F32)
    if start == 0:
        ahead = halo_ref[which, :, lanes].astype(F32)
    else:
        ahead = x_ref[0, start - 16 : start, lanes].astype(F32)[16 - HALO :]
    return jnp.concatenate([ahead, rows], 0)


def tap_rows(taps_ref, which, lanes):
    return [taps_ref[which, j : j + 1, lanes] for j in range(SHORT)]


def lag_masks(mask_ref, start):
    return [mask_ref[l, start : start + SPAN + HALO, :] for l in range(3)]


def group_mask(modes, size):
    return (iota((LANES, LANES), 0) // modes) == (iota((LANES, LANES), 1) // size)


def each_tile(width, body):
    for low in range(0, width, LANES):
        body(slice(low, low + LANES))


def mix_kernel(
    modes, size, ndoc,
    meta_ref, key_ref, value_ref, halo_ref, taps_ref, rate_ref,
    mixed_ref, state_ref,
    mask_ref, tail_ref,
):
    _, count, width = key_ref.shape
    chunks = count // CHUNK
    base = meta_ref[0]
    ends = running_ends(meta_ref, ndoc)

    @pl.when(pl.program_id(0) == 0)
    def _():
        write_lag_masks(mask_ref, ends, base)
        last = scalar_document(ends, base + count - 1)
        tail = document(ends, base + iota((8, count), 1)) == last
        tail_ref[...] = jnp.where(tail, 1.0, 0.0).astype(F32)

    def tile(lanes):
        key_taps, value_taps = tap_rows(taps_ref, 1, lanes), tap_rows(taps_ref, 2, lanes)
        for start in range(0, count, SPAN):
            masks = lag_masks(mask_ref, start)
            key = short_conv(extended(key_ref, halo_ref, 1, start, lanes), key_taps, masks)
            value = short_conv(extended(value_ref, halo_ref, 2, start, lanes), value_taps, masks)
            mixed_ref[start : start + SPAN, lanes] = (key * value).astype(BF16)
        rate = jnp.broadcast_to(rate_ref[:, lanes], (LANES, LANES)).T
        leave = jnp.exp(-rate * (CHUNK - 1 - iota((LANES, CHUNK), 1)).astype(F32))
        whole = jnp.exp(-rate * CHUNK)
        spans = []
        for chunk in reversed(range(chunks)):
            tail = tail_ref[0:1, chunk * CHUNK : (chunk + 1) * CHUNK]
            spans.append((leave * tail).astype(BF16))
            leave = leave * whole
        full = jnp.dot(jnp.concatenate(spans[::-1], 1), mixed_ref[:, lanes], preferred_element_type=F32)
        full = jnp.where(group_mask(modes, size), full, 0.0)
        state = jnp.sum(full.reshape(LANES // modes, modes, LANES), 0).astype(BF16)
        for owner in range(state_ref.shape[0]):
            state_ref[owner, :, lanes] = state

    each_tile(width, tile)


def conv_kernel(
    modes, size, ndoc, nblocks,
    meta_ref, slot_ref,
    x_ref, halo_ref, taps_ref, mixed_ref, states_ref, rate_ref, scale_ref, skip_ref, residual_ref,
    out_ref, spare_ref, squares_ref,
    mask_ref, same_ref, keep_ref, tail_ref,
):
    count, width = mixed_ref.shape
    chunks = count // CHUNK
    rows = count // nblocks
    base = meta_ref[0]
    where = meta_ref[1 + ndoc]
    ends = running_ends(meta_ref, ndoc)

    @pl.when(pl.program_id(0) == 0)
    def _():
        write_lag_masks(mask_ref, ends, base)
        squares_ref[...] = jnp.zeros_like(squares_ref)
        for chunk in range(chunks):
            start = base + chunk * CHUNK
            down, along = iota((CHUNK, CHUNK), 0), iota((CHUNK, CHUNK), 1)
            here, there = document(ends, start + down), document(ends, start + along)
            linked = (here == there) & (along <= down)
            same_ref[chunk] = jnp.where(linked, 1.0, 0.0).astype(BF16)
            carried = here == scalar_document(ends, start - 1)
            keep_ref[chunk] = jnp.where(carried, 1.0, 0.0).astype(BF16)
            last = scalar_document(ends, start + CHUNK - 1)
            tail_ref[chunk] = jnp.where(there == last, 1.0, 0.0).astype(F32)

    groups = LANES // modes
    before = scalar_document(ends, base - 1)
    first = jnp.int32(0)
    for v in range(nblocks):
        first = first + (scalar_document(ends, (v + 1) * count - 1) < before).astype(jnp.int32)

    def tile(lanes):
        rate_row, scale_row = rate_ref[:, lanes], scale_ref[:, lanes]
        rate = jnp.broadcast_to(rate_row, (LANES, LANES)).T
        scale = jnp.broadcast_to(scale_row, (LANES, LANES)).T
        down = iota((CHUNK, LANES), 0)
        along = iota((LANES, CHUNK), 1)
        entry = (scale_row * jnp.exp(-rate_row * (down + 1).astype(F32))).astype(BF16)
        leave = jnp.exp(-rate * (CHUNK - 1 - along).astype(F32))
        whole = jnp.exp(-rate * CHUNK)
        terms = scale * jnp.where(along == 0, 1.0, leave * jnp.exp(-rate))
        toeplitz = []
        for g in range(groups):
            line = jnp.sum(terms[g * modes : (g + 1) * modes], 0, keepdims=True)
            top = pltpu.roll(jnp.broadcast_to(line, (8, CHUNK)), 0, 1, stride=1, stride_axis=0)
            parts = [top] + [pltpu.roll(top, 8 * k, 1) for k in range(1, CHUNK // 8)]
            toeplitz.append(jnp.concatenate(parts, 0).astype(BF16))
        inside = group_mask(modes, size)

        def gather(v, total):
            weight = jnp.exp(-rate * ((where - 1 - v) * count).astype(F32))
            piece = jnp.concatenate([states_ref[v, :, lanes].astype(F32)] * groups, 0)
            return total + jnp.where(inside, piece * weight, 0.0)

        state = lax.fori_loop(first, where, gather, jnp.zeros((LANES, LANES), F32))

        taps = tap_rows(taps_ref, 0, lanes)
        skip = skip_ref[:, lanes]
        lane_group = iota((CHUNK, LANES), 1) // size
        for chunk in range(chunks):
            start = chunk * CHUNK
            mixed = mixed_ref[start : start + CHUNK, lanes]
            same = same_ref[chunk]
            left = jnp.concatenate([t * same for t in toeplitz] + [entry * keep_ref[chunk]], 1)
            right = jnp.concatenate(
                [jnp.where(lane_group == g, mixed, jnp.zeros_like(mixed)) for g in range(groups)]
                + [state.astype(BF16)],
                0,
            )
            longer = jnp.dot(left, right, preferred_element_type=F32)
            if chunk + 1 < chunks:
                fresh = jnp.dot((leave * tail_ref[chunk]).astype(BF16), mixed, preferred_element_type=F32)
                last = scalar_document(ends, base + start + CHUNK - 1)
                held = scalar_document(ends, base + start - 1) == last
                state = jnp.where(held, whole * state, 0.0) + jnp.where(inside, fresh, 0.0)
            body = longer + skip * mixed.astype(F32)
            for half in range(start, start + CHUNK, SPAN):
                gate = short_conv(extended(x_ref, halo_ref, 0, half, lanes), taps, lag_masks(mask_ref, half))
                inner = body[half - start : half - start + SPAN]
                summed = residual_ref[half : half + SPAN, lanes].astype(F32) + gate * inner
                squares_ref[half : half + SPAN, :] += summed * summed
                rounded = summed.astype(BF16)
                for b in range(SPAN // rows):
                    out_ref[slot_ref[half // rows + b], :, lanes] = rounded[b * rows : (b + 1) * rows]

    each_tile(width, tile)
    spare_ref[...] = out_ref[slot_ref[nblocks]]


def norm_kernel(parts, pick_ref, *refs):
    blocks = refs[:parts]
    spare_ref, gain_ref, out_ref = refs[parts:]
    nblocks, rows, _ = blocks[0].shape
    count, width = out_ref.shape

    def block(i, carry):
        rows_out = pl.ds(pl.multiple_of(i * rows, rows), rows)
        is_spare = pick_ref[nblocks] == i
        source = pick_ref[i]
        halves = jnp.where(is_spare, spare_ref[:, width:].astype(F32), blocks[-1][source, :, -LANES:].astype(F32))
        scale = halves[:, 0:1] + halves[:, 1:2]
        low = 0
        for part in range(parts):
            share = min(blocks[part].shape[2], width - low)
            for lane in range(0, share, LANES):
                outs = slice(low + lane, low + lane + LANES)
                value = blocks[part][source, :, lane : lane + LANES].astype(F32)
                value = jnp.where(is_spare, spare_ref[:, outs].astype(F32), value)
                out_ref[rows_out, outs] = (value * scale * gain_ref[:, outs]).astype(BF16)
            low += share
        return carry

    lax.fori_loop(0, nblocks, block, 0)


def params():
    return pltpu.CompilerParams(dimension_semantics=("arbitrary",), vmem_limit_bytes=VMEM_LIMIT)


def mix(low, share, meta, x, halo, taps, rate, modes, size, ndoc, copies):
    _, count, _ = x.shape
    wide = math.gcd(math.gcd(low, share), WIDE)
    first = low // wide
    deep = lambda t, m: (0, 0, first + t)
    grid_spec = pltpu.PrefetchScalarGridSpec(
        num_scalar_prefetch=1,
        grid=(share // wide,),
        in_specs=[
            pl.BlockSpec((1, count, wide), lambda t, m: (1, 0, first + t)),
            pl.BlockSpec((1, count, wide), lambda t, m: (2, 0, first + t)),
            pl.BlockSpec((3, HALO, wide), deep),
            pl.BlockSpec((3, SHORT, wide), deep),
            pl.BlockSpec((1, wide), lambda t, m: (0, first + t)),
        ],
        out_specs=[
            pl.BlockSpec((count, wide), lambda t, m: (0, t)),
            pl.BlockSpec((copies, modes, wide), lambda t, m: (0, 0, t)),
        ],
        scratch_shapes=[pltpu.VMEM((3, count + HALO, LANES), F32), pltpu.VMEM((8, count), F32)],
    )
    return pl.pallas_call(
        functools.partial(mix_kernel, modes, size, ndoc),
        grid_spec=grid_spec,
        out_shape=[
            jax.ShapeDtypeStruct((count, share), BF16),
            jax.ShapeDtypeStruct((copies, modes, share), BF16),
        ],
        compiler_params=params(),
        cost_estimate=pl.CostEstimate(flops=60 * count * share, bytes_accessed=8 * count * share, transcendentals=count * share),
        name="mix",
    )(meta, x, x, halo, taps, rate)


def conv(low, share, room, meta, slots, x, halo, taps, mixed, states, rate, scale, skip, residual, modes, size, ndoc):
    _, count, width = x.shape
    nblocks = states.shape[0]
    rows = count // nblocks
    wide = math.gcd(math.gcd(low, share), WIDE)
    first = low // wide
    tile = lambda t, m, s: (0, first + t)
    deep = lambda t, m, s: (0, 0, first + t)
    grid_spec = pltpu.PrefetchScalarGridSpec(
        num_scalar_prefetch=2,
        grid=(share // wide,),
        in_specs=[
            pl.BlockSpec((1, count, wide), deep),
            pl.BlockSpec((1, HALO, wide), deep),
            pl.BlockSpec((1, SHORT, wide), deep),
            pl.BlockSpec((count, wide), lambda t, m, s: (0, t)),
            pl.BlockSpec((nblocks, modes, wide), lambda t, m, s: (0, 0, t)),
            pl.BlockSpec((1, wide), tile),
            pl.BlockSpec((1, wide), tile),
            pl.BlockSpec((1, wide), tile),
            pl.BlockSpec((count, wide), tile),
        ],
        out_specs=[
            pl.BlockSpec((nblocks, rows, wide), lambda t, m, s: (0, 0, t)),
            pl.BlockSpec((rows, wide), lambda t, m, s: (0, t)),
            pl.BlockSpec((count, LANES), lambda t, m, s: (0, 0)),
        ],
        scratch_shapes=[
            pltpu.VMEM((3, count + HALO, LANES), F32),
            pltpu.VMEM((count // CHUNK, CHUNK, CHUNK), BF16),
            pltpu.VMEM((count // CHUNK, CHUNK, LANES), BF16),
            pltpu.VMEM((count // CHUNK, LANES, CHUNK), F32),
        ],
    )
    return pl.pallas_call(
        functools.partial(conv_kernel, modes, size, ndoc, nblocks),
        grid_spec=grid_spec,
        out_shape=[
            jax.ShapeDtypeStruct((nblocks, rows, share + room), BF16),
            jax.ShapeDtypeStruct((rows, share), BF16),
            jax.ShapeDtypeStruct((count, LANES), F32),
        ],
        compiler_params=params(),
        cost_estimate=pl.CostEstimate(
            flops=2 * 1152 * count * share, bytes_accessed=8 * count * share, transcendentals=count * share
        ),
        name="conv",
    )(meta, slots, x, halo, taps, mixed, states, rate, scale, skip, residual)


def norm(pick, blocks, spare, gain):
    nblocks, rows, _ = blocks[0].shape
    count, width = nblocks * rows, gain.shape[1]
    vmem = pl.BlockSpec(memory_space=pltpu.VMEM)
    return pl.pallas_call(
        functools.partial(norm_kernel, len(blocks)),
        in_specs=[pl.BlockSpec(memory_space=pltpu.SMEM)] + [vmem] * (len(blocks) + 2),
        out_specs=vmem,
        out_shape=jax.ShapeDtypeStruct((count, width), BF16),
        compiler_params=pltpu.CompilerParams(vmem_limit_bytes=VMEM_LIMIT),
        cost_estimate=pl.CostEstimate(flops=3 * count * width, bytes_accessed=4 * count * width, transcendentals=0),
        name="norm",
    )(pick, *blocks, spare, gain)


def on_device(features, residual, short_taps, rates, residues, skip, gain, lengths, owner):
    count, _, width = features.shape
    groups, modes = rates.shape
    size = width // groups
    ndoc = lengths.shape[0]
    nblocks = lax.axis_size("ctx")
    rows = count // nblocks
    where = lax.axis_index("ctx")
    x = jnp.transpose(features, (1, 0, 2))
    pairs = [(i, i + 1) for i in range(nblocks - 1)]
    halo = lax.ppermute(x[:, count - HALO :], "ctx", pairs)

    meta = jnp.concatenate([(where * count)[None], lengths, where[None]]).astype(jnp.int32)
    rate = rates.reshape(1, groups * modes)
    scale = (residues * jnp.sqrt(1.0 - jnp.exp(-2.0 * rates))).reshape(1, groups * modes)

    table = owner.reshape(nblocks, nblocks)
    ids = jnp.arange(nblocks, dtype=jnp.int32)
    mine = lax.dynamic_index_in_dim(table, where, 0, keepdims=False)
    twice = jnp.any((mine[:, None] == mine[None, :]) & (ids[None, :] < ids[:, None]), 1)
    unused = nblocks * (nblocks - 1) // 2 - jnp.sum(jnp.where(twice, 0, mine))
    slots = jnp.concatenate([jnp.where(twice, unused, mine), unused[None]]).astype(jnp.int32)
    source = jnp.sum((table == where).astype(jnp.int32) * ids[:, None], 0)
    spare_block = jnp.sum(jnp.where(twice, ids, 0))
    spare_shift = jnp.sum(jnp.where(twice, table[0], 0))
    pick = jnp.concatenate([source, spare_block[None]]).astype(jnp.int32)

    def exchanged(value):
        return lax.all_to_all(value, "ctx", split_axis=0, concat_axis=0, tiled=True)

    shares = [width * eighths // sum(SPLIT) for eighths in SPLIT]
    lows = [sum(shares[:part]) for part in range(len(shares))]
    mixes = [
        mix(low, share, meta, x, halo, short_taps, rate, modes, size, ndoc, nblocks) for low, share in zip(lows, shares)
    ]
    states = [exchanged(copies) for _, copies in mixes]
    mixed = list(lax.optimization_barrier(tuple(m for m, _ in mixes)))
    blocks, spares, squares = [], [], 0.0
    for part, (low, share) in enumerate(zip(lows, shares)):
        is_last = part + 1 == len(shares)
        out, spare, part_squares = conv(
            low, share, LANES if is_last else 0, meta, slots, x, halo, short_taps, mixed[part], states[part],
            rate, scale, skip.reshape(1, width), residual, modes, size, ndoc,
        )
        spares.append(spare)
        squares = squares + part_squares
        if is_last:
            mean = lax.psum(jnp.sum(squares, 1), "mp") / (width * lax.axis_size("mp"))
            inverse = lax.rsqrt(mean + EPS)
            high = lax.reduce_precision(inverse, 8, 7)
            column = iota((count, LANES), 1)
            halves = jnp.where(column == 0, high[:, None], jnp.where(column == 1, (inverse - high)[:, None], 0.0))
            halves = halves.reshape(nblocks, rows, LANES)
            in_slot = slots[None, :nblocks] == ids[:, None]
            by_slot = jnp.sum(jnp.where(in_slot[:, :, None, None], halves[None], 0.0), 1).astype(BF16)
            spare_halves = jnp.sum(jnp.where(twice[:, None, None], halves, 0.0), 0).astype(BF16)
            out = lax.dynamic_update_slice(out, by_slot, (0, 0, share))
            spares.append(spare_halves)
        blocks.append(exchanged(out))

    def moved(by):
        return lambda value: lax.ppermute(value, "ctx", [(s, (s + by) % nblocks) for s in range(nblocks)])

    spare = lax.switch(spare_shift, [lambda value: value] + [moved(d) for d in range(1, nblocks)], jnp.concatenate(spares, 1))
    return norm(pick, blocks, spare, gain.reshape(1, width))


def solution(mesh):
    return jax.shard_map(
        on_device,
        mesh=mesh,
        in_specs=(
            P("ctx", None, "mp"),
            P("ctx", "mp"),
            P(None, None, "mp"),
            P("mp", None),
            P("mp", None),
            P("mp"),
            P("mp"),
            P(),
            P(),
        ),
        out_specs=P("ctx", "mp"),
        check_vma=False,
    )
```

```python
import functools
import math

import jax
import jax.numpy as jnp
from jax import lax
from jax.experimental import pallas as pl
from jax.experimental.pallas import tpu as pltpu
from jax.sharding import PartitionSpec as P

SHORT = 7
LANES = 128
CHUNK = 128
HALO = 8
EPS = 1e-06
SPLIT = (3, 5)
WIDE = 512
SPAN = 64
F32 = jnp.float32
BF16 = jnp.bfloat16
VMEM_LIMIT = 60 * 1024 * 1024


def iota(shape, dim):
    return lax.broadcasted_iota(jnp.int32, shape, dim)


def document(ends, positions):
    total = jnp.zeros(positions.shape, jnp.int32)
    for end in ends:
        total = total + (positions >= end).astype(jnp.int32)
    return total


def scalar_document(ends, position):
    total = jnp.int32(0)
    for end in ends:
        total = total + (position >= end).astype(jnp.int32)
    return jnp.where(position < 0, -1, total)


def running_ends(lengths_ref, ndoc):
    ends, total = [], jnp.int32(0)
    for j in range(ndoc):
        total = total + lengths_ref[j]
        ends.append(total)
    return ends


def write_lag_masks(mask_ref, ends, base, count):
    mask_ref[...] = jnp.ones_like(mask_ref)
    gap = jnp.zeros((1, LANES), F32)
    for end in ends:
        row = end - base + HALO

        @pl.when((row >= 0) & (row < count + HALO))
        def _(row=row):
            for lag in (1, 2, 3):
                for past in range(lag):
                    mask_ref[lag - 1, pl.ds(row + past, 1), :] = gap


def row_documents(ends, base, count):
    return document(ends, base + iota((8, count), 1)).astype(F32)


def is_second(owner_ref, nblocks, i):
    found = jnp.bool_(False)
    for j in range(i):
        found = found | (owner_ref[j] == owner_ref[i])
    return found


def write_slots(slot_ref, owner_ref, where, nblocks):
    unused = jnp.int32(nblocks * (nblocks - 1) // 2)
    seconds = [is_second(owner_ref, nblocks, i) for i in range(nblocks)]
    mine = [owner_ref[where * nblocks + i] for i in range(nblocks)]
    for i in range(nblocks):
        unused = unused - jnp.where(seconds[i], 0, mine[i])
    for i in range(nblocks):
        slot_ref[i] = jnp.where(seconds[i], unused, mine[i])
    slot_ref[nblocks] = unused


def tile_rates(rates_ref, low, size):
    first = low // size
    columns = [rates_ref[:, first + g : first + g + 1] for g in range(LANES // size)]
    return jnp.concatenate([jnp.broadcast_to(column, (column.shape[0], LANES)) for column in columns], 0)


def short_conv(ext, taps, masks):
    def back(value, lag):
        return pltpu.roll(value, lag, 0) * masks[lag - 1]

    one, two = back(ext, 1), back(ext, 2)
    far = ext * taps[6]
    middle = ext * taps[3] + one * taps[4] + two * taps[5] + back(far, 3)
    near = ext * taps[0] + one * taps[1] + two * taps[2] + back(middle, 3)
    return near[HALO:]


def extended(x_ref, halo_ref, which, start, lanes):
    rows = x_ref[0, start : start + SPAN, lanes].astype(F32)
    if start == 0:
        ahead = halo_ref[which, :, lanes].astype(F32)
    else:
        ahead = x_ref[0, start - 16 : start, lanes].astype(F32)[16 - HALO :]
    return jnp.concatenate([ahead, rows], 0)


def tap_rows(taps_ref, which, lanes):
    return [taps_ref[which, j : j + 1, lanes] for j in range(SHORT)]


def lag_masks(mask_ref, start):
    return [mask_ref[l, start : start + SPAN + HALO, :] for l in range(3)]


def group_mask(modes, size):
    return (iota((LANES, LANES), 0) // modes) == (iota((LANES, LANES), 1) // size)


def each_tile(width, body):
    for low in range(0, width, LANES):
        body(slice(low, low + LANES))


def mix_kernel(
    modes, size, ndoc,
    where_ref, lengths_ref,
    key_ref, value_ref, halo_ref, taps_ref, rates_ref,
    mixed_ref, state_ref,
    mask_ref, tail_ref,
):
    _, count, width = key_ref.shape
    chunks = count // CHUNK

    @pl.when(pl.program_id(0) == 0)
    def _():
        base = where_ref[0] * count
        ends = running_ends(lengths_ref, ndoc)
        write_lag_masks(mask_ref, ends, base, count)
        last = scalar_document(ends, base + count - 1).astype(F32)
        tail_ref[...] = jnp.where(row_documents(ends, base, count) == last, 1.0, 0.0).astype(F32)

    def tile(lanes):
        key_taps, value_taps = tap_rows(taps_ref, 1, lanes), tap_rows(taps_ref, 2, lanes)
        for start in range(0, count, SPAN):
            masks = lag_masks(mask_ref, start)
            key = short_conv(extended(key_ref, halo_ref, 1, start, lanes), key_taps, masks)
            value = short_conv(extended(value_ref, halo_ref, 2, start, lanes), value_taps, masks)
            mixed_ref[start : start + SPAN, lanes] = (key * value).astype(BF16)
        rate = tile_rates(rates_ref.at[0], lanes.start, size)
        leave = jnp.exp(-rate * (CHUNK - 1 - iota((LANES, CHUNK), 1)).astype(F32))
        whole = jnp.exp(-rate * CHUNK)
        spans = []
        for chunk in reversed(range(chunks)):
            tail = tail_ref[0:1, chunk * CHUNK : (chunk + 1) * CHUNK]
            spans.append((leave * tail).astype(BF16))
            leave = leave * whole
        full = jnp.dot(jnp.concatenate(spans[::-1], 1), mixed_ref[:, lanes], preferred_element_type=F32)
        full = jnp.where(group_mask(modes, size), full, 0.0)
        state = jnp.sum(full.reshape(LANES // modes, modes, LANES), 0).astype(BF16)
        for owner in range(state_ref.shape[0]):
            state_ref[owner, :, lanes] = state

    each_tile(width, tile)


def left_state(states_ref, flags_ref, rate, lanes, modes, size, count):
    inside = group_mask(modes, size)
    where = flags_ref[1]

    def gather(v, total):
        weight = jnp.exp(-rate * ((where - 1 - v) * count).astype(F32))
        piece = jnp.concatenate([states_ref[v, :, lanes].astype(F32)] * (LANES // modes), 0)
        return total + jnp.where(inside, piece * weight, 0.0)

    return lax.fori_loop(flags_ref[0], where, gather, jnp.zeros((LANES, LANES), F32))


def write_flags(flags_ref, ends, where, count, nblocks):
    before = scalar_document(ends, where * count - 1)
    first = jnp.int32(0)
    for v in range(nblocks):
        first = first + (scalar_document(ends, (v + 1) * count - 1) < before).astype(jnp.int32)
    flags_ref[0] = first
    flags_ref[1] = where
    for chunk in range(count // CHUNK):
        start = where * count + chunk * CHUNK
        held = scalar_document(ends, start - 1) == scalar_document(ends, start + CHUNK - 1)
        flags_ref[2 + chunk] = held.astype(jnp.int32)


def hand_over(out_ref, squares_ref, slot_ref, summed, start, rows, lanes):
    squares_ref[start : start + SPAN, :] += summed * summed
    rounded = summed.astype(BF16)
    for b in range(SPAN // rows):
        out_ref[slot_ref[start // rows + b], :, lanes] = rounded[b * rows : (b + 1) * rows]


def conv_kernel(modes, size, ndoc, nblocks, carried, where_ref, lengths_ref, owner_ref, *refs):
    x_ref, halo_ref, taps_ref, mixed_ref, rates_ref, residues_ref, skip_ref, residual_ref = refs[:8]
    refs = refs[8:]
    if carried:
        states_ref, out_ref, spare_ref, squares_ref = refs[:4]
        refs = refs[4:]
    else:
        base_ref, gate_ref = refs[:2]
        refs = refs[2:]
    mask_ref, same_ref, keep_ref, tail_ref, flags_ref = refs[:5]
    count, width = mixed_ref.shape
    chunks = count // CHUNK

    @pl.when(pl.program_id(0) == 0)
    def _():
        where = where_ref[0]
        base = where * count
        ends = running_ends(lengths_ref, ndoc)
        write_lag_masks(mask_ref, ends, base, count)
        write_flags(flags_ref, ends, where, count, nblocks)
        if carried:
            write_slots(refs[5], owner_ref, where, nblocks)
            squares_ref[...] = jnp.zeros_like(squares_ref)
        documents = row_documents(ends, base, count)
        causal = iota((CHUNK, CHUNK), 1) <= iota((CHUNK, CHUNK), 0)
        for chunk in range(chunks):
            start = base + chunk * CHUNK
            there = jnp.broadcast_to(documents[0:1, chunk * CHUNK : (chunk + 1) * CHUNK], (CHUNK, CHUNK))
            here = there.T
            same_ref[chunk] = jnp.where((here == there) & causal, 1.0, 0.0).astype(BF16)
            before = scalar_document(ends, start - 1).astype(F32)
            keep_ref[chunk] = jnp.where(here == before, 1.0, 0.0).astype(BF16)
            last = scalar_document(ends, start + CHUNK - 1).astype(F32)
            tail_ref[chunk] = jnp.where(there == last, 1.0, 0.0).astype(F32)

    groups = LANES // modes

    def tile(lanes):
        rate = tile_rates(rates_ref.at[0], lanes.start, size)
        scale = tile_rates(residues_ref.at[0], lanes.start, size) * jnp.sqrt(1.0 - jnp.exp(-2.0 * rate))
        down = iota((CHUNK, LANES), 0)
        along = iota((LANES, CHUNK), 1)
        entry = (scale.T * jnp.exp(-rate.T * (down + 1).astype(F32))).astype(BF16)
        leave = jnp.exp(-rate * (CHUNK - 1 - along).astype(F32))
        whole = jnp.exp(-rate * CHUNK)
        terms = scale * jnp.where(along == 0, 1.0, leave * jnp.exp(-rate))
        toeplitz = []
        for g in range(groups):
            line = jnp.sum(terms[g * modes : (g + 1) * modes], 0, keepdims=True)
            top = pltpu.roll(jnp.broadcast_to(line, (8, CHUNK)), 0, 1, stride=1, stride_axis=0)
            parts = [top] + [pltpu.roll(top, 8 * k, 1) for k in range(1, CHUNK // 8)]
            toeplitz.append(jnp.concatenate(parts, 0).astype(BF16))
        inside = group_mask(modes, size)
        state = left_state(states_ref, flags_ref, rate, lanes, modes, size, count) if carried else None
        taps = tap_rows(taps_ref, 0, lanes)
        skip = skip_ref[:, lanes]
        lane_group = iota((CHUNK, LANES), 1) // size
        for chunk in range(chunks):
            start = chunk * CHUNK
            mixed = mixed_ref[start : start + CHUNK, lanes]
            same = same_ref[chunk]
            left = [t * same for t in toeplitz]
            right = [jnp.where(lane_group == g, mixed, jnp.zeros_like(mixed)) for g in range(groups)]
            if state is not None:
                left.append(entry * keep_ref[chunk])
                right.append(state.astype(BF16))
            longer = jnp.dot(jnp.concatenate(left, 1), jnp.concatenate(right, 0), preferred_element_type=F32)
            if chunk + 1 < chunks:
                fresh = jnp.dot((leave * tail_ref[chunk]).astype(BF16), mixed, preferred_element_type=F32)
                held = flags_ref[2 + chunk] == 1
                fresh = jnp.where(inside, fresh, 0.0)
                state = fresh if state is None else jnp.where(held, whole * state, 0.0) + fresh
            body = longer + skip * mixed.astype(F32)
            for half in range(start, start + CHUNK, SPAN):
                gate = short_conv(extended(x_ref, halo_ref, 0, half, lanes), taps, lag_masks(mask_ref, half))
                inner = body[half - start : half - start + SPAN]
                summed = residual_ref[half : half + SPAN, lanes].astype(F32) + gate * inner
                if carried:
                    hand_over(out_ref, squares_ref, refs[5], summed, half, count // nblocks, lanes)
                else:
                    base_ref[half : half + SPAN, lanes] = summed
                    gate_ref[half : half + SPAN, lanes] = gate.astype(BF16)

    each_tile(width, tile)
    if carried:
        spare_ref[...] = out_ref[refs[5][nblocks], :, :width]


def add_kernel(
    modes, size, ndoc, nblocks,
    where_ref, lengths_ref, owner_ref,
    base_ref, gate_ref, rates_ref, residues_ref, states_ref,
    out_ref, spare_ref, squares_ref,
    keep_ref, flags_ref, slot_ref,
):
    count, width = base_ref.shape
    chunks = count // CHUNK

    @pl.when(pl.program_id(0) == 0)
    def _():
        where = where_ref[0]
        ends = running_ends(lengths_ref, ndoc)
        write_flags(flags_ref, ends, where, count, nblocks)
        write_slots(slot_ref, owner_ref, where, nblocks)
        squares_ref[...] = jnp.zeros_like(squares_ref)
        before = scalar_document(ends, where * count - 1)
        kept = jnp.int32(0)
        for end in reversed(ends):
            kept = jnp.where(end >= where * count, end - where * count, kept)
        kept = jnp.where(before < 0, 0, kept)
        keep_ref[...] = jnp.where(iota((count, LANES), 0) < kept, 1.0, 0.0).astype(F32)

    def tile(lanes):
        rate = tile_rates(rates_ref.at[0], lanes.start, size)
        scale = tile_rates(residues_ref.at[0], lanes.start, size) * jnp.sqrt(1.0 - jnp.exp(-2.0 * rate))
        down = iota((CHUNK, LANES), 0)
        entry = (scale.T * jnp.exp(-rate.T * (down + 1).astype(F32))).astype(BF16)
        whole = jnp.exp(-rate * CHUNK)
        state = left_state(states_ref, flags_ref, rate, lanes, modes, size, count)
        held = []
        for _ in range(chunks):
            held.append(state.astype(BF16))
            state = state * whole
        left = jnp.dot(entry, jnp.concatenate(held, 1), preferred_element_type=F32)
        for start in range(0, count, SPAN):
            low = start % CHUNK
            chunk = start // CHUNK
            carried = left[low : low + SPAN, chunk * LANES : (chunk + 1) * LANES] * keep_ref[start : start + SPAN, :]
            gate = gate_ref[start : start + SPAN, lanes].astype(F32)
            summed = base_ref[start : start + SPAN, lanes] + gate * carried
            hand_over(out_ref, squares_ref, slot_ref, summed, start, count // nblocks, lanes)

    each_tile(width, tile)
    spare_ref[...] = out_ref[slot_ref[nblocks], :, :width]


def norm_kernel(parts, where_ref, owner_ref, *refs):
    blocks = refs[:parts]
    spare_ref, gain_ref, out_ref = refs[parts:]
    nblocks, rows, _ = blocks[0].shape
    count, width = out_ref.shape
    spare_block = jnp.int32(0)
    for i in range(nblocks):
        spare_block = jnp.where(is_second(owner_ref, nblocks, i), i, spare_block)

    def block(i, carry):
        rows_out = pl.ds(pl.multiple_of(i * rows, rows), rows)
        is_spare = spare_block == i
        ahead = where_ref[0] - owner_ref[i]
        source = jnp.where(ahead < 0, ahead + nblocks, ahead)
        halves = jnp.where(is_spare, spare_ref[:, width:].astype(F32), blocks[-1][source, :, -LANES:].astype(F32))
        scale = halves[:, 0:1] + halves[:, 1:2]
        low = 0
        for part in range(parts):
            share = min(blocks[part].shape[2], width - low)
            for lane in range(0, share, LANES):
                outs = slice(low + lane, low + lane + LANES)
                value = blocks[part][source, :, lane : lane + LANES].astype(F32)
                value = jnp.where(is_spare, spare_ref[:, outs].astype(F32), value)
                out_ref[rows_out, outs] = (value * scale * gain_ref[:, outs]).astype(BF16)
            low += share
        return carry

    lax.fori_loop(0, nblocks, block, 0)


def params():
    return pltpu.CompilerParams(dimension_semantics=("arbitrary",), vmem_limit_bytes=VMEM_LIMIT)


def whole_array(rank):
    return lambda *_: (0,) * rank


def by_step(rates, wide, size):
    modes, groups = rates.shape
    held = wide // size
    return jnp.transpose(rates.reshape(modes, groups // held, held), (1, 0, 2))


def mix(scalars, x, halo, taps, rates, size, ndoc, copies):
    _, count, width = x.shape
    modes = rates.shape[0]
    wide = min(WIDE, width)
    deep = lambda t, *_: (0, 0, t)
    grid_spec = pltpu.PrefetchScalarGridSpec(
        num_scalar_prefetch=2,
        grid=(width // wide,),
        in_specs=[
            pl.BlockSpec((1, count, wide), lambda t, *_: (1, 0, t)),
            pl.BlockSpec((1, count, wide), lambda t, *_: (2, 0, t)),
            pl.BlockSpec((3, HALO, wide), deep),
            pl.BlockSpec((3, SHORT, wide), deep),
            pl.BlockSpec((1, modes, wide // size), lambda t, *_: (t, 0, 0)),
        ],
        out_specs=[
            pl.BlockSpec((count, wide), lambda t, *_: (0, t)),
            pl.BlockSpec((copies, modes, wide), deep),
        ],
        scratch_shapes=[pltpu.VMEM((3, count + 2 * HALO, LANES), F32), pltpu.VMEM((8, count), F32)],
    )
    return pl.pallas_call(
        functools.partial(mix_kernel, modes, size, ndoc),
        grid_spec=grid_spec,
        out_shape=[
            jax.ShapeDtypeStruct((count, width), BF16),
            jax.ShapeDtypeStruct((copies, modes, width), BF16),
        ],
        compiler_params=params(),
        cost_estimate=pl.CostEstimate(flops=60 * count * width, bytes_accessed=8 * count * width, transcendentals=count * width),
        name="mix",
    )(*scalars[:2], x, x, halo, taps, by_step(rates, wide, size))


def conv(low, share, room, scalars, x, halo, taps, mixed, rates, residues, skip, residual, states, size, ndoc, nblocks):
    _, count, width = x.shape
    modes = rates.shape[0]
    rows = count // nblocks
    wide = math.gcd(math.gcd(low, share), WIDE)
    first = low // wide
    carried = states is not None
    tile = lambda t, *_: (0, first + t)
    deep = lambda t, *_: (0, 0, first + t)
    step = pl.BlockSpec((1, modes, wide // size), lambda t, *_: (first + t, 0, 0))
    in_specs = [
        pl.BlockSpec((1, count, wide), deep),
        pl.BlockSpec((1, HALO, wide), deep),
        pl.BlockSpec((1, SHORT, wide), deep),
        pl.BlockSpec((count, wide), tile),
        step,
        step,
        pl.BlockSpec((1, wide), tile),
        pl.BlockSpec((count, wide), tile),
    ]
    operands = [x, halo, taps, mixed, by_step(rates, wide, size), by_step(residues, wide, size), skip, residual]
    scratch = [
        pltpu.VMEM((3, count + 2 * HALO, LANES), F32),
        pltpu.VMEM((count // CHUNK, CHUNK, CHUNK), BF16),
        pltpu.VMEM((count // CHUNK, CHUNK, LANES), BF16),
        pltpu.VMEM((count // CHUNK, LANES, CHUNK), F32),
        pltpu.SMEM((2 + count // CHUNK,), jnp.int32),
    ]
    if carried:
        in_specs.append(pl.BlockSpec((nblocks, modes, wide), deep))
        operands.append(states)
        scratch.append(pltpu.SMEM((nblocks + 1,), jnp.int32))
        out_specs, out_shape = handed(share, room, wide, count, nblocks)
    else:
        out_specs = [pl.BlockSpec((count, wide), lambda t, *_: (0, t))] * 2
        out_shape = [jax.ShapeDtypeStruct((count, share), F32), jax.ShapeDtypeStruct((count, share), BF16)]
    grid_spec = pltpu.PrefetchScalarGridSpec(
        num_scalar_prefetch=3, grid=(share // wide,), in_specs=in_specs, out_specs=out_specs, scratch_shapes=scratch
    )
    return pl.pallas_call(
        functools.partial(conv_kernel, modes, size, ndoc, nblocks, carried),
        grid_spec=grid_spec,
        out_shape=out_shape,
        compiler_params=params(),
        cost_estimate=pl.CostEstimate(
            flops=2 * 1152 * count * share, bytes_accessed=8 * count * share, transcendentals=count * share
        ),
        name="conv",
    )(*scalars, *operands)


def handed(share, room, wide, count, nblocks):
    rows = count // nblocks
    specs = [
        pl.BlockSpec((nblocks, rows, wide), lambda t, *_: (0, 0, t)),
        pl.BlockSpec((rows, wide), lambda t, *_: (0, t)),
        pl.BlockSpec((count, LANES), whole_array(2)),
    ]
    shapes = [
        jax.ShapeDtypeStruct((nblocks, rows, share + room), BF16),
        jax.ShapeDtypeStruct((rows, share), BF16),
        jax.ShapeDtypeStruct((count, LANES), F32),
    ]
    return specs, shapes


def add(scalars, base, gate, rates, residues, states, size, ndoc, nblocks):
    count, share = base.shape
    modes = rates.shape[0]
    wide = math.gcd(share, WIDE)
    tile = lambda t, *_: (0, t)
    step = pl.BlockSpec((1, modes, wide // size), lambda t, *_: (t, 0, 0))
    out_specs, out_shape = handed(share, 0, wide, count, nblocks)
    grid_spec = pltpu.PrefetchScalarGridSpec(
        num_scalar_prefetch=3,
        grid=(share // wide,),
        in_specs=[
            pl.BlockSpec((count, wide), tile),
            pl.BlockSpec((count, wide), tile),
            step,
            step,
            pl.BlockSpec((nblocks, modes, wide), lambda t, *_: (0, 0, t)),
        ],
        out_specs=out_specs,
        scratch_shapes=[
            pltpu.VMEM((count, LANES), F32),
            pltpu.SMEM((2 + count // CHUNK,), jnp.int32),
            pltpu.SMEM((nblocks + 1,), jnp.int32),
        ],
    )
    return pl.pallas_call(
        functools.partial(add_kernel, modes, size, ndoc, nblocks),
        grid_spec=grid_spec,
        out_shape=out_shape,
        compiler_params=params(),
        cost_estimate=pl.CostEstimate(flops=300 * count * share, bytes_accessed=8 * count * share, transcendentals=count * share),
        name="add",
    )(*scalars, base, gate, by_step(rates, wide, size), by_step(residues, wide, size), states)


def norm(where, owner, blocks, spare, gain):
    nblocks, rows, _ = blocks[0].shape
    count, width = nblocks * rows, gain.shape[1]
    vmem = pl.BlockSpec(memory_space=pltpu.VMEM)
    smem = pl.BlockSpec(memory_space=pltpu.SMEM)
    return pl.pallas_call(
        functools.partial(norm_kernel, len(blocks)),
        in_specs=[smem, smem] + [vmem] * (len(blocks) + 2),
        out_specs=vmem,
        out_shape=jax.ShapeDtypeStruct((count, width), BF16),
        compiler_params=pltpu.CompilerParams(vmem_limit_bytes=16 * 1024 * 1024),
        cost_estimate=pl.CostEstimate(flops=3 * count * width, bytes_accessed=4 * count * width, transcendentals=0),
        name="norm",
    )(where, owner, *blocks, spare, gain)


def on_device(features, residual, short_taps, rates, residues, skip, gain, lengths, owner):
    count, _, width = features.shape
    size = width // rates.shape[0]
    ndoc = lengths.shape[0]
    nblocks = lax.axis_size("ctx")
    rows = count // nblocks
    where = lax.axis_index("ctx")
    x = jnp.transpose(features, (1, 0, 2))
    pairs = [(i, i + 1) for i in range(nblocks - 1)]
    halo = lax.ppermute(x[:, count - HALO :], "ctx", pairs)

    scalars = (where.reshape(1).astype(jnp.int32), lengths, owner)
    rates, residues = rates.T, residues.T

    table = owner.reshape(nblocks, nblocks)
    ids = jnp.arange(nblocks, dtype=jnp.int32)
    mine = lax.dynamic_index_in_dim(table, where, 0, keepdims=False)
    twice = jnp.any((mine[:, None] == mine[None, :]) & (ids[None, :] < ids[:, None]), 1)
    unused = nblocks * (nblocks - 1) // 2 - jnp.sum(jnp.where(twice, 0, mine))
    slots = jnp.where(twice, unused, mine).astype(jnp.int32)
    spare_shift = jnp.sum(jnp.where(twice, table[0], 0))

    def exchanged(value):
        return lax.all_to_all(value, "ctx", split_axis=0, concat_axis=0, tiled=True)

    first = width * SPLIT[0] // sum(SPLIT)
    second = width - first
    mixed, copies = mix(scalars, x, halo, short_taps, rates, size, ndoc, nblocks)
    states = exchanged(copies)
    shared = (scalars, x, halo, short_taps, mixed, rates, residues, skip.reshape(1, width), residual)
    base, gate = conv(0, first, 0, *shared, None, size, ndoc, nblocks)
    out, spare, squares = add(scalars, base, gate, rates, residues, states, size, ndoc, nblocks)
    block = exchanged(out)
    out, last_spare, last_squares = conv(first, second, LANES, *shared, states, size, ndoc, nblocks)
    mean = lax.psum(jnp.sum(squares + last_squares, 1), "mp") / (width * lax.axis_size("mp"))
    inverse = lax.rsqrt(mean + EPS)
    high = lax.reduce_precision(inverse, 8, 7)
    column = iota((count, LANES), 1)
    halves = jnp.where(column == 0, high[:, None], jnp.where(column == 1, (inverse - high)[:, None], 0.0))
    halves = halves.reshape(nblocks, rows, LANES)
    in_slot = slots[None, :] == ids[:, None]
    by_slot = jnp.sum(jnp.where(in_slot[:, :, None, None], halves[None], 0.0), 1).astype(BF16)
    spare_halves = jnp.sum(jnp.where(twice[:, None, None], halves, 0.0), 0).astype(BF16)
    out = lax.dynamic_update_slice(out, by_slot, (0, 0, second))
    out, block = lax.optimization_barrier((out, block))
    blocks = [block, exchanged(out)]
    spares = jnp.concatenate([spare, last_spare, spare_halves], 1)

    def moved(by):
        return lambda value: lax.ppermute(value, "ctx", [(s, (s + by) % nblocks) for s in range(nblocks)])

    spare = lax.switch(spare_shift, [lambda value: value] + [moved(d) for d in range(1, nblocks)], spares)
    return norm(scalars[0], owner, blocks, spare, gain.reshape(1, width))


def solution(mesh):
    return jax.shard_map(
        on_device,
        mesh=mesh,
        in_specs=(
            P("ctx", None, "mp"),
            P("ctx", "mp"),
            P(None, None, "mp"),
            P("mp", None),
            P("mp", None),
            P("mp"),
            P("mp"),
            P(),
            P(),
        ),
        out_specs=P("ctx", "mp"),
        check_vma=False,
    )
```

```python
import functools
import math

import jax
import jax.numpy as jnp
from jax import lax
from jax.experimental import pallas as pl
from jax.experimental.pallas import tpu as pltpu
from jax.sharding import PartitionSpec as P

SHORT = 7
LANES = 128
CHUNK = 128
HALO = 8
EPS = 1e-06
SPLIT = (4, 4)
WIDE = 512
SPAN = 64
F32 = jnp.float32
BF16 = jnp.bfloat16
VMEM_LIMIT = 60 * 1024 * 1024


def iota(shape, dim):
    return lax.broadcasted_iota(jnp.int32, shape, dim)


def document(ends, positions):
    total = jnp.zeros(positions.shape, jnp.int32)
    for end in ends:
        total = total + (positions >= end).astype(jnp.int32)
    return total


def scalar_document(ends, position):
    total = jnp.int32(0)
    for end in ends:
        total = total + (position >= end).astype(jnp.int32)
    return jnp.where(position < 0, -1, total)


def running_ends(lengths_ref, ndoc):
    ends, total = [], jnp.int32(0)
    for j in range(ndoc):
        total = total + lengths_ref[j]
        ends.append(total)
    return ends


def write_lag_masks(mask_ref, ends, base, count):
    mask_ref[...] = jnp.ones_like(mask_ref)
    gap = jnp.zeros((1, LANES), F32)
    for end in ends:
        row = end - base + HALO

        @pl.when((row >= 0) & (row < count + HALO))
        def _(row=row):
            for lag in (1, 2, 3):
                for past in range(lag):
                    mask_ref[lag - 1, pl.ds(row + past, 1), :] = gap


def row_documents(ends, base, count):
    return document(ends, base + iota((8, count), 1)).astype(F32)


def is_second(owner_ref, nblocks, i):
    found = jnp.bool_(False)
    for j in range(i):
        found = found | (owner_ref[j] == owner_ref[i])
    return found


def write_slots(slot_ref, owner_ref, where, nblocks):
    unused = jnp.int32(nblocks * (nblocks - 1) // 2)
    seconds = [is_second(owner_ref, nblocks, i) for i in range(nblocks)]
    mine = [owner_ref[where * nblocks + i] for i in range(nblocks)]
    for i in range(nblocks):
        unused = unused - jnp.where(seconds[i], 0, mine[i])
    for i in range(nblocks):
        slot_ref[i] = jnp.where(seconds[i], unused, mine[i])
    slot_ref[nblocks] = unused


def tile_rates(rates_ref, low, size):
    first = low // size
    columns = [rates_ref[:, first + g : first + g + 1] for g in range(LANES // size)]
    return jnp.concatenate([jnp.broadcast_to(column, (column.shape[0], LANES)) for column in columns], 0)


def short_conv(ext, taps, masks):
    def back(value, lag):
        return pltpu.roll(value, lag, 0) * masks[lag - 1]

    one, two = back(ext, 1), back(ext, 2)
    far = ext * taps[6]
    middle = ext * taps[3] + one * taps[4] + two * taps[5] + back(far, 3)
    near = ext * taps[0] + one * taps[1] + two * taps[2] + back(middle, 3)
    return near[HALO:]


def extended(x_ref, halo_ref, which, start, lanes):
    rows = x_ref[0, start : start + SPAN, lanes].astype(F32)
    if start == 0:
        ahead = halo_ref[which, :, lanes].astype(F32)
    else:
        ahead = x_ref[0, start - 16 : start, lanes].astype(F32)[16 - HALO :]
    return jnp.concatenate([ahead, rows], 0)


def tap_rows(taps_ref, which, lanes):
    return [taps_ref[which, j : j + 1, lanes] for j in range(SHORT)]


def lag_masks(mask_ref, start):
    return [mask_ref[l, start : start + SPAN + HALO, :] for l in range(3)]


def group_mask(modes, size):
    return (iota((LANES, LANES), 0) // modes) == (iota((LANES, LANES), 1) // size)


def each_tile(width, body):
    for low in range(0, width, LANES):
        body(slice(low, low + LANES))


def mix_kernel(
    modes, size, ndoc,
    where_ref, lengths_ref,
    key_ref, value_ref, halo_ref, taps_ref, rates_ref,
    mixed_ref, state_ref,
    mask_ref, tail_ref,
):
    _, count, width = key_ref.shape
    chunks = count // CHUNK

    @pl.when(pl.program_id(0) == 0)
    def _():
        base = where_ref[0] * count
        ends = running_ends(lengths_ref, ndoc)
        write_lag_masks(mask_ref, ends, base, count)
        last = scalar_document(ends, base + count - 1).astype(F32)
        tail_ref[...] = jnp.where(row_documents(ends, base, count) == last, 1.0, 0.0).astype(F32)

    def tile(lanes):
        key_taps, value_taps = tap_rows(taps_ref, 1, lanes), tap_rows(taps_ref, 2, lanes)
        for start in range(0, count, SPAN):
            masks = lag_masks(mask_ref, start)
            key = short_conv(extended(key_ref, halo_ref, 1, start, lanes), key_taps, masks)
            value = short_conv(extended(value_ref, halo_ref, 2, start, lanes), value_taps, masks)
            mixed_ref[start : start + SPAN, lanes] = (key * value).astype(BF16)
        rate = tile_rates(rates_ref.at[0], lanes.start, size)
        leave = jnp.exp(-rate * (CHUNK - 1 - iota((LANES, CHUNK), 1)).astype(F32))
        whole = jnp.exp(-rate * CHUNK)
        spans = []
        for chunk in reversed(range(chunks)):
            tail = tail_ref[0:1, chunk * CHUNK : (chunk + 1) * CHUNK]
            spans.append((leave * tail).astype(BF16))
            leave = leave * whole
        full = jnp.dot(jnp.concatenate(spans[::-1], 1), mixed_ref[:, lanes], preferred_element_type=F32)
        full = jnp.where(group_mask(modes, size), full, 0.0)
        state = jnp.sum(full.reshape(LANES // modes, modes, LANES), 0).astype(BF16)
        for owner in range(state_ref.shape[0]):
            state_ref[owner, :, lanes] = state

    each_tile(width, tile)


def left_state(states_ref, flags_ref, rate, lanes, modes, size, count):
    inside = group_mask(modes, size)
    where = flags_ref[1]

    def gather(v, total):
        weight = jnp.exp(-rate * ((where - 1 - v) * count).astype(F32))
        piece = jnp.concatenate([states_ref[v, :, lanes].astype(F32)] * (LANES // modes), 0)
        return total + jnp.where(inside, piece * weight, 0.0)

    return lax.fori_loop(flags_ref[0], where, gather, jnp.zeros((LANES, LANES), F32))


def write_flags(flags_ref, ends, where, count, nblocks):
    before = scalar_document(ends, where * count - 1)
    first = jnp.int32(0)
    for v in range(nblocks):
        first = first + (scalar_document(ends, (v + 1) * count - 1) < before).astype(jnp.int32)
    flags_ref[0] = first
    flags_ref[1] = where
    for chunk in range(count // CHUNK):
        start = where * count + chunk * CHUNK
        held = scalar_document(ends, start - 1) == scalar_document(ends, start + CHUNK - 1)
        flags_ref[2 + chunk] = held.astype(jnp.int32)


def hand_over(out_ref, squares_ref, slot_ref, summed, start, rows, lanes):
    squares_ref[start : start + SPAN, :] += summed * summed
    rounded = summed.astype(BF16)
    for b in range(SPAN // rows):
        out_ref[slot_ref[start // rows + b], :, lanes] = rounded[b * rows : (b + 1) * rows]


def conv_kernel(modes, size, ndoc, nblocks, carried, where_ref, lengths_ref, owner_ref, *refs):
    x_ref, halo_ref, taps_ref, mixed_ref, rates_ref, residues_ref, skip_ref, residual_ref = refs[:8]
    refs = refs[8:]
    if carried:
        states_ref, out_ref, spare_ref, squares_ref = refs[:4]
        refs = refs[4:]
    else:
        base_ref, gate_ref = refs[:2]
        refs = refs[2:]
    mask_ref, same_ref, keep_ref, tail_ref, flags_ref = refs[:5]
    count, width = mixed_ref.shape
    chunks = count // CHUNK

    @pl.when(pl.program_id(0) == 0)
    def _():
        where = where_ref[0]
        base = where * count
        ends = running_ends(lengths_ref, ndoc)
        write_lag_masks(mask_ref, ends, base, count)
        write_flags(flags_ref, ends, where, count, nblocks)
        if carried:
            write_slots(refs[5], owner_ref, where, nblocks)
            squares_ref[...] = jnp.zeros_like(squares_ref)
        documents = row_documents(ends, base, count)
        causal = iota((CHUNK, CHUNK), 1) <= iota((CHUNK, CHUNK), 0)
        for chunk in range(chunks):
            start = base + chunk * CHUNK
            there = jnp.broadcast_to(documents[0:1, chunk * CHUNK : (chunk + 1) * CHUNK], (CHUNK, CHUNK))
            here = there.T
            same_ref[chunk] = jnp.where((here == there) & causal, 1.0, 0.0).astype(BF16)
            before = scalar_document(ends, start - 1).astype(F32)
            keep_ref[chunk] = jnp.where(here == before, 1.0, 0.0).astype(BF16)
            last = scalar_document(ends, start + CHUNK - 1).astype(F32)
            tail_ref[chunk] = jnp.where(there == last, 1.0, 0.0).astype(F32)

    groups = LANES // modes

    def tile(lanes):
        rate = tile_rates(rates_ref.at[0], lanes.start, size)
        scale = tile_rates(residues_ref.at[0], lanes.start, size) * jnp.sqrt(1.0 - jnp.exp(-2.0 * rate))
        down = iota((CHUNK, LANES), 0)
        along = iota((LANES, CHUNK), 1)
        entry = (scale.T * jnp.exp(-rate.T * (down + 1).astype(F32))).astype(BF16)
        leave = jnp.exp(-rate * (CHUNK - 1 - along).astype(F32))
        whole = jnp.exp(-rate * CHUNK)
        terms = scale * jnp.where(along == 0, 1.0, leave * jnp.exp(-rate))
        toeplitz = []
        for g in range(groups):
            line = jnp.sum(terms[g * modes : (g + 1) * modes], 0, keepdims=True)
            top = pltpu.roll(jnp.broadcast_to(line, (8, CHUNK)), 0, 1, stride=1, stride_axis=0)
            parts = [top] + [pltpu.roll(top, 8 * k, 1) for k in range(1, CHUNK // 8)]
            toeplitz.append(jnp.concatenate(parts, 0).astype(BF16))
        inside = group_mask(modes, size)
        state = left_state(states_ref, flags_ref, rate, lanes, modes, size, count) if carried else None
        taps = tap_rows(taps_ref, 0, lanes)
        skip = skip_ref[:, lanes]
        lane_group = iota((CHUNK, LANES), 1) // size
        for chunk in range(chunks):
            start = chunk * CHUNK
            mixed = mixed_ref[start : start + CHUNK, lanes]
            same = same_ref[chunk]
            left = [t * same for t in toeplitz]
            right = [jnp.where(lane_group == g, mixed, jnp.zeros_like(mixed)) for g in range(groups)]
            if state is not None:
                left.append(entry * keep_ref[chunk])
                right.append(state.astype(BF16))
            longer = jnp.dot(jnp.concatenate(left, 1), jnp.concatenate(right, 0), preferred_element_type=F32)
            if chunk + 1 < chunks:
                fresh = jnp.dot((leave * tail_ref[chunk]).astype(BF16), mixed, preferred_element_type=F32)
                held = flags_ref[2 + chunk] == 1
                fresh = jnp.where(inside, fresh, 0.0)
                state = fresh if state is None else jnp.where(held, whole * state, 0.0) + fresh
            body = longer + skip * mixed.astype(F32)
            for half in range(start, start + CHUNK, SPAN):
                gate = short_conv(extended(x_ref, halo_ref, 0, half, lanes), taps, lag_masks(mask_ref, half))
                inner = body[half - start : half - start + SPAN]
                summed = residual_ref[half : half + SPAN, lanes].astype(F32) + gate * inner
                if carried:
                    hand_over(out_ref, squares_ref, refs[5], summed, half, count // nblocks, lanes)
                else:
                    base_ref[half : half + SPAN, lanes] = summed
                    gate_ref[half : half + SPAN, lanes] = gate.astype(BF16)

    each_tile(width, tile)
    if carried:
        spare_ref[...] = out_ref[refs[5][nblocks], :, :width]


def add_kernel(
    modes, size, ndoc, nblocks,
    where_ref, lengths_ref, owner_ref,
    base_ref, gate_ref, rates_ref, residues_ref, states_ref,
    out_ref, spare_ref, squares_ref,
    keep_ref, flags_ref, slot_ref,
):
    count, width = base_ref.shape
    chunks = count // CHUNK

    @pl.when(pl.program_id(0) == 0)
    def _():
        where = where_ref[0]
        ends = running_ends(lengths_ref, ndoc)
        write_flags(flags_ref, ends, where, count, nblocks)
        write_slots(slot_ref, owner_ref, where, nblocks)
        squares_ref[...] = jnp.zeros_like(squares_ref)
        before = scalar_document(ends, where * count - 1)
        kept = jnp.int32(0)
        for end in reversed(ends):
            kept = jnp.where(end >= where * count, end - where * count, kept)
        kept = jnp.where(before < 0, 0, kept)
        keep_ref[...] = jnp.where(iota((count, LANES), 0) < kept, 1.0, 0.0).astype(F32)

    def tile(lanes):
        rate = tile_rates(rates_ref.at[0], lanes.start, size)
        scale = tile_rates(residues_ref.at[0], lanes.start, size) * jnp.sqrt(1.0 - jnp.exp(-2.0 * rate))
        down = iota((CHUNK, LANES), 0)
        entry = (scale.T * jnp.exp(-rate.T * (down + 1).astype(F32))).astype(BF16)
        whole = jnp.exp(-rate * CHUNK)
        state = left_state(states_ref, flags_ref, rate, lanes, modes, size, count)
        held = []
        for _ in range(chunks):
            held.append(state.astype(BF16))
            state = state * whole
        left = jnp.dot(entry, jnp.concatenate(held, 1), preferred_element_type=F32)
        for start in range(0, count, SPAN):
            low = start % CHUNK
            chunk = start // CHUNK
            carried = left[low : low + SPAN, chunk * LANES : (chunk + 1) * LANES] * keep_ref[start : start + SPAN, :]
            gate = gate_ref[start : start + SPAN, lanes].astype(F32)
            summed = base_ref[start : start + SPAN, lanes] + gate * carried
            hand_over(out_ref, squares_ref, slot_ref, summed, start, count // nblocks, lanes)

    each_tile(width, tile)
    spare_ref[...] = out_ref[slot_ref[nblocks], :, :width]


def norm_kernel(parts, where_ref, owner_ref, *refs):
    blocks = refs[:parts]
    spare_ref, gain_ref, out_ref = refs[parts:]
    nblocks, rows, _ = blocks[0].shape
    count, width = out_ref.shape
    spare_block = jnp.int32(0)
    for i in range(nblocks):
        spare_block = jnp.where(is_second(owner_ref, nblocks, i), i, spare_block)

    def block(i, carry):
        rows_out = pl.ds(pl.multiple_of(i * rows, rows), rows)
        is_spare = spare_block == i
        ahead = where_ref[0] - owner_ref[i]
        source = jnp.where(ahead < 0, ahead + nblocks, ahead)
        halves = jnp.where(is_spare, spare_ref[:, width:].astype(F32), blocks[-1][source, :, -LANES:].astype(F32))
        scale = halves[:, 0:1] + halves[:, 1:2]
        low = 0
        for part in range(parts):
            share = min(blocks[part].shape[2], width - low)
            for lane in range(0, share, LANES):
                outs = slice(low + lane, low + lane + LANES)
                value = blocks[part][source, :, lane : lane + LANES].astype(F32)
                value = jnp.where(is_spare, spare_ref[:, outs].astype(F32), value)
                out_ref[rows_out, outs] = (value * scale * gain_ref[:, outs]).astype(BF16)
            low += share
        return carry

    lax.fori_loop(0, nblocks, block, 0)


def params():
    return pltpu.CompilerParams(dimension_semantics=("arbitrary",), vmem_limit_bytes=VMEM_LIMIT)


def whole_array(rank):
    return lambda *_: (0,) * rank


def by_step(rates, wide, size):
    modes, groups = rates.shape
    held = wide // size
    return jnp.transpose(rates.reshape(modes, groups // held, held), (1, 0, 2))


def mix(scalars, x, halo, taps, rates, size, ndoc, copies):
    _, count, width = x.shape
    modes = rates.shape[0]
    wide = min(WIDE, width)
    deep = lambda t, *_: (0, 0, t)
    grid_spec = pltpu.PrefetchScalarGridSpec(
        num_scalar_prefetch=2,
        grid=(width // wide,),
        in_specs=[
            pl.BlockSpec((1, count, wide), lambda t, *_: (1, 0, t)),
            pl.BlockSpec((1, count, wide), lambda t, *_: (2, 0, t)),
            pl.BlockSpec((3, HALO, wide), deep),
            pl.BlockSpec((3, SHORT, wide), deep),
            pl.BlockSpec((1, modes, wide // size), lambda t, *_: (t, 0, 0)),
        ],
        out_specs=[
            pl.BlockSpec((count, wide), lambda t, *_: (0, t)),
            pl.BlockSpec((copies, modes, wide), deep),
        ],
        scratch_shapes=[pltpu.VMEM((3, count + 2 * HALO, LANES), F32), pltpu.VMEM((8, count), F32)],
    )
    return pl.pallas_call(
        functools.partial(mix_kernel, modes, size, ndoc),
        grid_spec=grid_spec,
        out_shape=[
            jax.ShapeDtypeStruct((count, width), BF16),
            jax.ShapeDtypeStruct((copies, modes, width), BF16),
        ],
        compiler_params=params(),
        cost_estimate=pl.CostEstimate(flops=60 * count * width, bytes_accessed=8 * count * width, transcendentals=count * width),
        name="mix",
    )(*scalars[:2], x, x, halo, taps, by_step(rates, wide, size))


def conv(low, share, room, scalars, x, halo, taps, mixed, rates, residues, skip, residual, states, size, ndoc, nblocks):
    _, count, width = x.shape
    modes = rates.shape[0]
    rows = count // nblocks
    wide = math.gcd(math.gcd(low, share), WIDE)
    first = low // wide
    carried = states is not None
    tile = lambda t, *_: (0, first + t)
    deep = lambda t, *_: (0, 0, first + t)
    step = pl.BlockSpec((1, modes, wide // size), lambda t, *_: (first + t, 0, 0))
    in_specs = [
        pl.BlockSpec((1, count, wide), deep),
        pl.BlockSpec((1, HALO, wide), deep),
        pl.BlockSpec((1, SHORT, wide), deep),
        pl.BlockSpec((count, wide), tile),
        step,
        step,
        pl.BlockSpec((1, wide), tile),
        pl.BlockSpec((count, wide), tile),
    ]
    operands = [x, halo, taps, mixed, by_step(rates, wide, size), by_step(residues, wide, size), skip, residual]
    scratch = [
        pltpu.VMEM((3, count + 2 * HALO, LANES), F32),
        pltpu.VMEM((count // CHUNK, CHUNK, CHUNK), BF16),
        pltpu.VMEM((count // CHUNK, CHUNK, LANES), BF16),
        pltpu.VMEM((count // CHUNK, LANES, CHUNK), F32),
        pltpu.SMEM((2 + count // CHUNK,), jnp.int32),
    ]
    if carried:
        in_specs.append(pl.BlockSpec((nblocks, modes, wide), deep))
        operands.append(states)
        scratch.append(pltpu.SMEM((nblocks + 1,), jnp.int32))
        out_specs, out_shape = handed(share, room, wide, count, nblocks)
    else:
        out_specs = [pl.BlockSpec((count, wide), lambda t, *_: (0, t))] * 2
        out_shape = [jax.ShapeDtypeStruct((count, share), F32), jax.ShapeDtypeStruct((count, share), BF16)]
    grid_spec = pltpu.PrefetchScalarGridSpec(
        num_scalar_prefetch=3, grid=(share // wide,), in_specs=in_specs, out_specs=out_specs, scratch_shapes=scratch
    )
    return pl.pallas_call(
        functools.partial(conv_kernel, modes, size, ndoc, nblocks, carried),
        grid_spec=grid_spec,
        out_shape=out_shape,
        compiler_params=params(),
        cost_estimate=pl.CostEstimate(
            flops=2 * 1152 * count * share, bytes_accessed=8 * count * share, transcendentals=count * share
        ),
        name="conv",
    )(*scalars, *operands)


def handed(share, room, wide, count, nblocks):
    rows = count // nblocks
    specs = [
        pl.BlockSpec((nblocks, rows, wide), lambda t, *_: (0, 0, t)),
        pl.BlockSpec((rows, wide), lambda t, *_: (0, t)),
        pl.BlockSpec((count, LANES), whole_array(2)),
    ]
    shapes = [
        jax.ShapeDtypeStruct((nblocks, rows, share + room), BF16),
        jax.ShapeDtypeStruct((rows, share), BF16),
        jax.ShapeDtypeStruct((count, LANES), F32),
    ]
    return specs, shapes


def add(scalars, base, gate, rates, residues, states, size, ndoc, nblocks):
    count, share = base.shape
    modes = rates.shape[0]
    wide = math.gcd(share, WIDE)
    tile = lambda t, *_: (0, t)
    step = pl.BlockSpec((1, modes, wide // size), lambda t, *_: (t, 0, 0))
    out_specs, out_shape = handed(share, 0, wide, count, nblocks)
    grid_spec = pltpu.PrefetchScalarGridSpec(
        num_scalar_prefetch=3,
        grid=(share // wide,),
        in_specs=[
            pl.BlockSpec((count, wide), tile),
            pl.BlockSpec((count, wide), tile),
            step,
            step,
            pl.BlockSpec((nblocks, modes, wide), lambda t, *_: (0, 0, t)),
        ],
        out_specs=out_specs,
        scratch_shapes=[
            pltpu.VMEM((count, LANES), F32),
            pltpu.SMEM((2 + count // CHUNK,), jnp.int32),
            pltpu.SMEM((nblocks + 1,), jnp.int32),
        ],
    )
    return pl.pallas_call(
        functools.partial(add_kernel, modes, size, ndoc, nblocks),
        grid_spec=grid_spec,
        out_shape=out_shape,
        compiler_params=params(),
        cost_estimate=pl.CostEstimate(flops=300 * count * share, bytes_accessed=8 * count * share, transcendentals=count * share),
        name="add",
    )(*scalars, base, gate, by_step(rates, wide, size), by_step(residues, wide, size), states)


def norm(where, owner, blocks, spare, gain):
    nblocks, rows, _ = blocks[0].shape
    count, width = nblocks * rows, gain.shape[1]
    vmem = pl.BlockSpec(memory_space=pltpu.VMEM)
    smem = pl.BlockSpec(memory_space=pltpu.SMEM)
    return pl.pallas_call(
        functools.partial(norm_kernel, len(blocks)),
        in_specs=[smem, smem] + [vmem] * (len(blocks) + 2),
        out_specs=vmem,
        out_shape=jax.ShapeDtypeStruct((count, width), BF16),
        compiler_params=pltpu.CompilerParams(vmem_limit_bytes=16 * 1024 * 1024),
        cost_estimate=pl.CostEstimate(flops=3 * count * width, bytes_accessed=4 * count * width, transcendentals=0),
        name="norm",
    )(where, owner, *blocks, spare, gain)


def on_device(features, residual, short_taps, rates, residues, skip, gain, lengths, owner):
    count, _, width = features.shape
    size = width // rates.shape[0]
    ndoc = lengths.shape[0]
    nblocks = lax.axis_size("ctx")
    rows = count // nblocks
    where = lax.axis_index("ctx")
    x = jnp.transpose(features, (1, 0, 2))
    pairs = [(i, i + 1) for i in range(nblocks - 1)]
    halo = lax.ppermute(x[:, count - HALO :], "ctx", pairs)

    scalars = (where.reshape(1).astype(jnp.int32), lengths, owner)
    rates, residues = rates.T, residues.T

    table = owner.reshape(nblocks, nblocks)
    ids = jnp.arange(nblocks, dtype=jnp.int32)
    mine = lax.dynamic_index_in_dim(table, where, 0, keepdims=False)
    twice = jnp.any((mine[:, None] == mine[None, :]) & (ids[None, :] < ids[:, None]), 1)
    unused = nblocks * (nblocks - 1) // 2 - jnp.sum(jnp.where(twice, 0, mine))
    slots = jnp.where(twice, unused, mine).astype(jnp.int32)
    spare_shift = jnp.sum(jnp.where(twice, table[0], 0))

    def exchanged(value):
        return lax.all_to_all(value, "ctx", split_axis=0, concat_axis=0, tiled=True)

    first = width * SPLIT[0] // sum(SPLIT)
    second = width - first
    mixed, copies = mix(scalars, x, halo, short_taps, rates, size, ndoc, nblocks)
    states = exchanged(copies)
    shared = (scalars, x, halo, short_taps, mixed, rates, residues, skip.reshape(1, width), residual)
    base, gate = conv(0, first, 0, *shared, None, size, ndoc, nblocks)
    out, spare, squares = add(scalars, base, gate, rates, residues, states, size, ndoc, nblocks)
    block = exchanged(out)
    out, last_spare, last_squares = conv(first, second, LANES, *shared, states, size, ndoc, nblocks)
    mean = lax.psum(jnp.sum(squares + last_squares, 1), "mp") / (width * lax.axis_size("mp"))
    inverse = lax.rsqrt(mean + EPS)
    high = lax.reduce_precision(inverse, 8, 7)
    column = iota((count, LANES), 1)
    halves = jnp.where(column == 0, high[:, None], jnp.where(column == 1, (inverse - high)[:, None], 0.0))
    halves = halves.reshape(nblocks, rows, LANES)
    in_slot = slots[None, :] == ids[:, None]
    by_slot = jnp.sum(jnp.where(in_slot[:, :, None, None], halves[None], 0.0), 1).astype(BF16)
    spare_halves = jnp.sum(jnp.where(twice[:, None, None], halves, 0.0), 0).astype(BF16)
    out = lax.dynamic_update_slice(out, by_slot, (0, 0, second))
    blocks = [block, exchanged(out)]
    spares = jnp.concatenate([spare, last_spare, spare_halves], 1)

    def moved(by):
        return lambda value: lax.ppermute(value, "ctx", [(s, (s + by) % nblocks) for s in range(nblocks)])

    spare = lax.switch(spare_shift, [lambda value: value] + [moved(d) for d in range(1, nblocks)], spares)
    return norm(scalars[0], owner, blocks, spare, gain.reshape(1, width))


def solution(mesh):
    return jax.shard_map(
        on_device,
        mesh=mesh,
        in_specs=(
            P("ctx", None, "mp"),
            P("ctx", "mp"),
            P(None, None, "mp"),
            P("mp", None),
            P("mp", None),
            P("mp"),
            P("mp"),
            P(),
            P(),
        ),
        out_specs=P("ctx", "mp"),
        check_vma=False,
    )
```

```python
import functools
import math

import jax
import jax.numpy as jnp
from jax import lax
from jax.experimental import pallas as pl
from jax.experimental.pallas import tpu as pltpu
from jax.sharding import PartitionSpec as P

SHORT = 7
LANES = 128
CHUNK = 128
HALO = 8
EPS = 1e-06
SPLIT = (4, 4)
WIDE = 512
SPAN = 64
F32 = jnp.float32
BF16 = jnp.bfloat16
VMEM_LIMIT = 60 * 1024 * 1024


def iota(shape, dim):
    return lax.broadcasted_iota(jnp.int32, shape, dim)


def document(ends, positions):
    total = jnp.zeros(positions.shape, jnp.int32)
    for end in ends:
        total = total + (positions >= end).astype(jnp.int32)
    return total


def scalar_document(ends, position):
    total = jnp.int32(0)
    for end in ends:
        total = total + (position >= end).astype(jnp.int32)
    return jnp.where(position < 0, -1, total)


def running_ends(lengths_ref, ndoc):
    ends, total = [], jnp.int32(0)
    for j in range(ndoc):
        total = total + lengths_ref[j]
        ends.append(total)
    return ends


def write_lag_masks(mask_ref, ends, base, count):
    mask_ref[...] = jnp.ones_like(mask_ref)
    gap = jnp.zeros((1, LANES), F32)
    for end in ends:
        row = end - base + HALO

        @pl.when((row >= 0) & (row < count + HALO))
        def _(row=row):
            for lag in (1, 2, 3):
                for past in range(lag):
                    mask_ref[lag - 1, pl.ds(row + past, 1), :] = gap


def row_documents(ends, base, count):
    return document(ends, base + iota((8, count), 1)).astype(F32)


def is_second(owner_ref, nblocks, i):
    found = jnp.bool_(False)
    for j in range(i):
        found = found | (owner_ref[j] == owner_ref[i])
    return found


def write_slots(slot_ref, owner_ref, where, nblocks):
    unused = jnp.int32(nblocks * (nblocks - 1) // 2)
    seconds = [is_second(owner_ref, nblocks, i) for i in range(nblocks)]
    mine = [owner_ref[where * nblocks + i] for i in range(nblocks)]
    for i in range(nblocks):
        unused = unused - jnp.where(seconds[i], 0, mine[i])
    for i in range(nblocks):
        slot_ref[i] = jnp.where(seconds[i], unused, mine[i])
    slot_ref[nblocks] = unused


def tile_rates(rates_ref, low, size):
    first = low // size
    columns = [rates_ref[:, first + g : first + g + 1] for g in range(LANES // size)]
    return jnp.concatenate([jnp.broadcast_to(column, (column.shape[0], LANES)) for column in columns], 0)


def short_conv(ext, taps, masks):
    def back(value, lag):
        return pltpu.roll(value, lag, 0) * masks[lag - 1]

    one, two = back(ext, 1), back(ext, 2)
    far = ext * taps[6]
    middle = ext * taps[3] + one * taps[4] + two * taps[5] + back(far, 3)
    near = ext * taps[0] + one * taps[1] + two * taps[2] + back(middle, 3)
    return near[HALO:]


def extended(x_ref, halo_ref, which, start, lanes):
    rows = x_ref[0, start : start + SPAN, lanes].astype(F32)
    if start == 0:
        ahead = halo_ref[which, :, lanes].astype(F32)
    else:
        ahead = x_ref[0, start - 16 : start, lanes].astype(F32)[16 - HALO :]
    return jnp.concatenate([ahead, rows], 0)


def tap_rows(taps_ref, which, lanes):
    return [taps_ref[which, j : j + 1, lanes] for j in range(SHORT)]


def lag_masks(mask_ref, start):
    return [mask_ref[l, start : start + SPAN + HALO, :] for l in range(3)]


def group_mask(modes, size):
    return (iota((LANES, LANES), 0) // modes) == (iota((LANES, LANES), 1) // size)


def each_tile(width, body):
    for low in range(0, width, LANES):
        body(slice(low, low + LANES))


def write_shifts(shift_ref, mask_ref, ends, base, count):
    mask_ref[...] = jnp.ones_like(mask_ref)
    gap = jnp.zeros((1, LANES), F32)
    for end in ends:
        row = end - base + HALO

        @pl.when((row >= 0) & (row < count + HALO))
        def _(row=row):
            for lag in range(1, SHORT):
                for past in range(lag):
                    mask_ref[lag - 1, pl.ds(row + past, 1), :] = gap

    back = iota((CHUNK, LANES), 0) + 16 - iota((CHUNK, LANES), 1)
    late = iota((CHUNK, 16), 0) + 16 - LANES - iota((CHUNK, 16), 1)
    for lag in range(1, SHORT):
        rows = slice((lag - 1) * CHUNK, lag * CHUNK)
        for chunk in range(count // CHUNK):
            mask = mask_ref[lag - 1, HALO + chunk * CHUNK : HALO + (chunk + 1) * CHUNK, :]
            shift_ref[chunk, rows, :LANES] = jnp.where(back == lag, mask, 0.0).astype(BF16)
            shift_ref[chunk, rows, LANES:] = jnp.where(late == lag, mask[:, :16], 0.0).astype(BF16)


def mix_kernel(
    modes, size, ndoc,
    where_ref, lengths_ref,
    key_ref, value_ref, halo_ref, taps_ref, rates_ref,
    mixed_ref, state_ref,
    shift_ref, mask_ref, tail_ref,
):
    _, count, width = key_ref.shape
    chunks = count // CHUNK

    @pl.when(pl.program_id(0) == 0)
    def _():
        base = where_ref[0] * count
        ends = running_ends(lengths_ref, ndoc)
        write_shifts(shift_ref, mask_ref, ends, base, count)
        last = scalar_document(ends, base + count - 1).astype(F32)
        tail_ref[...] = jnp.where(row_documents(ends, base, count) == last, 1.0, 0.0).astype(F32)

    def window(x_ref, which, start, lanes):
        if start == 0:
            halo = halo_ref[which, :, lanes].astype(F32)
            ahead = jnp.concatenate([jnp.zeros((16 - HALO, LANES), F32), halo], 0).astype(BF16)
        else:
            ahead = x_ref[0, start - 16 : start, lanes]
        return jnp.concatenate([ahead, x_ref[0, start : start + CHUNK, lanes]], 0)

    def tile(lanes):
        key_taps, value_taps = tap_rows(taps_ref, 1, lanes), tap_rows(taps_ref, 2, lanes)
        for chunk in range(chunks):
            start = chunk * CHUNK
            both = jnp.concatenate(
                [window(key_ref, 1, start, lanes), window(value_ref, 2, start, lanes)], 1
            )
            moved = jnp.dot(shift_ref[chunk], both, preferred_element_type=F32)
            key = key_ref[0, start : start + CHUNK, lanes].astype(F32) * key_taps[0]
            value = value_ref[0, start : start + CHUNK, lanes].astype(F32) * value_taps[0]
            for lag in range(1, SHORT):
                rows = moved[(lag - 1) * CHUNK : lag * CHUNK]
                key = key + rows[:, :LANES] * key_taps[lag]
                value = value + rows[:, LANES:] * value_taps[lag]
            mixed_ref[start : start + CHUNK, lanes] = (key * value).astype(BF16)
        rate = tile_rates(rates_ref.at[0], lanes.start, size)
        leave = jnp.exp(-rate * (CHUNK - 1 - iota((LANES, CHUNK), 1)).astype(F32))
        whole = jnp.exp(-rate * CHUNK)
        spans = []
        for chunk in reversed(range(chunks)):
            tail = tail_ref[0:1, chunk * CHUNK : (chunk + 1) * CHUNK]
            spans.append((leave * tail).astype(BF16))
            leave = leave * whole
        full = jnp.dot(jnp.concatenate(spans[::-1], 1), mixed_ref[:, lanes], preferred_element_type=F32)
        full = jnp.where(group_mask(modes, size), full, 0.0)
        state = jnp.sum(full.reshape(LANES // modes, modes, LANES), 0).astype(BF16)
        for owner in range(state_ref.shape[0]):
            state_ref[owner, :, lanes] = state

    each_tile(width, tile)


def left_state(states_ref, flags_ref, rate, lanes, modes, size, count):
    inside = group_mask(modes, size)
    where = flags_ref[1]

    def gather(v, total):
        weight = jnp.exp(-rate * ((where - 1 - v) * count).astype(F32))
        piece = jnp.concatenate([states_ref[v, :, lanes].astype(F32)] * (LANES // modes), 0)
        return total + jnp.where(inside, piece * weight, 0.0)

    return lax.fori_loop(flags_ref[0], where, gather, jnp.zeros((LANES, LANES), F32))


def write_flags(flags_ref, ends, where, count, nblocks):
    before = scalar_document(ends, where * count - 1)
    first = jnp.int32(0)
    for v in range(nblocks):
        first = first + (scalar_document(ends, (v + 1) * count - 1) < before).astype(jnp.int32)
    flags_ref[0] = first
    flags_ref[1] = where
    for chunk in range(count // CHUNK):
        start = where * count + chunk * CHUNK
        held = scalar_document(ends, start - 1) == scalar_document(ends, start + CHUNK - 1)
        flags_ref[2 + chunk] = held.astype(jnp.int32)


def hand_over(out_ref, squares_ref, slot_ref, summed, start, rows, lanes):
    squares_ref[start : start + SPAN, :] += summed * summed
    rounded = summed.astype(BF16)
    for b in range(SPAN // rows):
        out_ref[slot_ref[start // rows + b], :, lanes] = rounded[b * rows : (b + 1) * rows]


def conv_kernel(modes, size, ndoc, nblocks, carried, where_ref, lengths_ref, owner_ref, *refs):
    x_ref, halo_ref, taps_ref, mixed_ref, rates_ref, residues_ref, skip_ref, residual_ref = refs[:8]
    refs = refs[8:]
    if carried:
        states_ref, out_ref, spare_ref, squares_ref = refs[:4]
        refs = refs[4:]
    else:
        base_ref, gate_ref = refs[:2]
        refs = refs[2:]
    mask_ref, same_ref, keep_ref, tail_ref, flags_ref = refs[:5]
    count, width = mixed_ref.shape
    chunks = count // CHUNK

    @pl.when(pl.program_id(0) == 0)
    def _():
        where = where_ref[0]
        base = where * count
        ends = running_ends(lengths_ref, ndoc)
        write_lag_masks(mask_ref, ends, base, count)
        write_flags(flags_ref, ends, where, count, nblocks)
        if carried:
            write_slots(refs[5], owner_ref, where, nblocks)
            squares_ref[...] = jnp.zeros_like(squares_ref)
        documents = row_documents(ends, base, count)
        causal = iota((CHUNK, CHUNK), 1) <= iota((CHUNK, CHUNK), 0)
        for chunk in range(chunks):
            start = base + chunk * CHUNK
            there = jnp.broadcast_to(documents[0:1, chunk * CHUNK : (chunk + 1) * CHUNK], (CHUNK, CHUNK))
            here = there.T
            same_ref[chunk] = jnp.where((here == there) & causal, 1.0, 0.0).astype(BF16)
            before = scalar_document(ends, start - 1).astype(F32)
            keep_ref[chunk] = jnp.where(here == before, 1.0, 0.0).astype(BF16)
            last = scalar_document(ends, start + CHUNK - 1).astype(F32)
            tail_ref[chunk] = jnp.where(there == last, 1.0, 0.0).astype(F32)

    groups = LANES // modes

    def tile(lanes):
        rate = tile_rates(rates_ref.at[0], lanes.start, size)
        scale = tile_rates(residues_ref.at[0], lanes.start, size) * jnp.sqrt(1.0 - jnp.exp(-2.0 * rate))
        down = iota((CHUNK, LANES), 0)
        along = iota((LANES, CHUNK), 1)
        entry = (scale.T * jnp.exp(-rate.T * (down + 1).astype(F32))).astype(BF16)
        leave = jnp.exp(-rate * (CHUNK - 1 - along).astype(F32))
        whole = jnp.exp(-rate * CHUNK)
        terms = scale * jnp.where(along == 0, 1.0, leave * jnp.exp(-rate))
        toeplitz = []
        for g in range(groups):
            line = jnp.sum(terms[g * modes : (g + 1) * modes], 0, keepdims=True)
            top = pltpu.roll(jnp.broadcast_to(line, (8, CHUNK)), 0, 1, stride=1, stride_axis=0)
            parts = [top] + [pltpu.roll(top, 8 * k, 1) for k in range(1, CHUNK // 8)]
            toeplitz.append(jnp.concatenate(parts, 0).astype(BF16))
        inside = group_mask(modes, size)
        state = left_state(states_ref, flags_ref, rate, lanes, modes, size, count) if carried else None
        taps = tap_rows(taps_ref, 0, lanes)
        skip = skip_ref[:, lanes]
        lane_group = iota((CHUNK, LANES), 1) // size
        for chunk in range(chunks):
            start = chunk * CHUNK
            mixed = mixed_ref[start : start + CHUNK, lanes]
            same = same_ref[chunk]
            left = [t * same for t in toeplitz]
            right = [jnp.where(lane_group == g, mixed, jnp.zeros_like(mixed)) for g in range(groups)]
            if state is not None:
                left.append(entry * keep_ref[chunk])
                right.append(state.astype(BF16))
            longer = jnp.dot(jnp.concatenate(left, 1), jnp.concatenate(right, 0), preferred_element_type=F32)
            if chunk + 1 < chunks:
                fresh = jnp.dot((leave * tail_ref[chunk]).astype(BF16), mixed, preferred_element_type=F32)
                held = flags_ref[2 + chunk] == 1
                fresh = jnp.where(inside, fresh, 0.0)
                state = fresh if state is None else jnp.where(held, whole * state, 0.0) + fresh
            body = longer + skip * mixed.astype(F32)
            for half in range(start, start + CHUNK, SPAN):
                gate = short_conv(extended(x_ref, halo_ref, 0, half, lanes), taps, lag_masks(mask_ref, half))
                inner = body[half - start : half - start + SPAN]
                summed = residual_ref[half : half + SPAN, lanes].astype(F32) + gate * inner
                if carried:
                    hand_over(out_ref, squares_ref, refs[5], summed, half, count // nblocks, lanes)
                else:
                    base_ref[half : half + SPAN, lanes] = summed
                    gate_ref[half : half + SPAN, lanes] = gate.astype(BF16)

    each_tile(width, tile)
    if carried:
        spare_ref[...] = out_ref[refs[5][nblocks], :, :width]


def add_kernel(
    modes, size, ndoc, nblocks,
    where_ref, lengths_ref, owner_ref,
    base_ref, gate_ref, rates_ref, residues_ref, states_ref,
    out_ref, spare_ref, squares_ref,
    keep_ref, flags_ref, slot_ref,
):
    count, width = base_ref.shape
    chunks = count // CHUNK

    @pl.when(pl.program_id(0) == 0)
    def _():
        where = where_ref[0]
        ends = running_ends(lengths_ref, ndoc)
        write_flags(flags_ref, ends, where, count, nblocks)
        write_slots(slot_ref, owner_ref, where, nblocks)
        squares_ref[...] = jnp.zeros_like(squares_ref)
        before = scalar_document(ends, where * count - 1)
        kept = jnp.int32(0)
        for end in reversed(ends):
            kept = jnp.where(end >= where * count, end - where * count, kept)
        kept = jnp.where(before < 0, 0, kept)
        keep_ref[...] = jnp.where(iota((count, LANES), 0) < kept, 1.0, 0.0).astype(F32)

    def tile(lanes):
        rate = tile_rates(rates_ref.at[0], lanes.start, size)
        scale = tile_rates(residues_ref.at[0], lanes.start, size) * jnp.sqrt(1.0 - jnp.exp(-2.0 * rate))
        down = iota((CHUNK, LANES), 0)
        entry = (scale.T * jnp.exp(-rate.T * (down + 1).astype(F32))).astype(BF16)
        whole = jnp.exp(-rate * CHUNK)
        state = left_state(states_ref, flags_ref, rate, lanes, modes, size, count)
        held = []
        for _ in range(chunks):
            held.append(state.astype(BF16))
            state = state * whole
        left = jnp.dot(entry, jnp.concatenate(held, 1), preferred_element_type=F32)
        for start in range(0, count, SPAN):
            low = start % CHUNK
            chunk = start // CHUNK
            carried = left[low : low + SPAN, chunk * LANES : (chunk + 1) * LANES] * keep_ref[start : start + SPAN, :]
            gate = gate_ref[start : start + SPAN, lanes].astype(F32)
            summed = base_ref[start : start + SPAN, lanes] + gate * carried
            hand_over(out_ref, squares_ref, slot_ref, summed, start, count // nblocks, lanes)

    each_tile(width, tile)
    spare_ref[...] = out_ref[slot_ref[nblocks], :, :width]


def norm_kernel(parts, where_ref, owner_ref, *refs):
    blocks = refs[:parts]
    spare_ref, gain_ref, out_ref = refs[parts:]
    nblocks, rows, _ = blocks[0].shape
    count, width = out_ref.shape
    spare_block = jnp.int32(0)
    for i in range(nblocks):
        spare_block = jnp.where(is_second(owner_ref, nblocks, i), i, spare_block)

    def block(i, carry):
        rows_out = pl.ds(pl.multiple_of(i * rows, rows), rows)
        is_spare = spare_block == i
        ahead = where_ref[0] - owner_ref[i]
        source = jnp.where(ahead < 0, ahead + nblocks, ahead)
        halves = jnp.where(is_spare, spare_ref[:, width:].astype(F32), blocks[-1][source, :, -LANES:].astype(F32))
        scale = halves[:, 0:1] + halves[:, 1:2]
        low = 0
        for part in range(parts):
            share = min(blocks[part].shape[2], width - low)
            for lane in range(0, share, LANES):
                outs = slice(low + lane, low + lane + LANES)
                value = blocks[part][source, :, lane : lane + LANES].astype(F32)
                value = jnp.where(is_spare, spare_ref[:, outs].astype(F32), value)
                out_ref[rows_out, outs] = (value * scale * gain_ref[:, outs]).astype(BF16)
            low += share
        return carry

    lax.fori_loop(0, nblocks, block, 0)


def params():
    return pltpu.CompilerParams(dimension_semantics=("arbitrary",), vmem_limit_bytes=VMEM_LIMIT)


def whole_array(rank):
    return lambda *_: (0,) * rank


def by_step(rates, wide, size):
    modes, groups = rates.shape
    held = wide // size
    return jnp.transpose(rates.reshape(modes, groups // held, held), (1, 0, 2))


def mix(scalars, x, halo, taps, rates, size, ndoc, copies):
    _, count, width = x.shape
    modes = rates.shape[0]
    wide = min(WIDE, width)
    deep = lambda t, *_: (0, 0, t)
    grid_spec = pltpu.PrefetchScalarGridSpec(
        num_scalar_prefetch=2,
        grid=(width // wide,),
        in_specs=[
            pl.BlockSpec((1, count, wide), lambda t, *_: (1, 0, t)),
            pl.BlockSpec((1, count, wide), lambda t, *_: (2, 0, t)),
            pl.BlockSpec((3, HALO, wide), deep),
            pl.BlockSpec((3, SHORT, wide), deep),
            pl.BlockSpec((1, modes, wide // size), lambda t, *_: (t, 0, 0)),
        ],
        out_specs=[
            pl.BlockSpec((count, wide), lambda t, *_: (0, t)),
            pl.BlockSpec((copies, modes, wide), deep),
        ],
        scratch_shapes=[
            pltpu.VMEM((count // CHUNK, (SHORT - 1) * CHUNK, CHUNK + 16), BF16),
            pltpu.VMEM((SHORT - 1, count + 2 * HALO, LANES), F32),
            pltpu.VMEM((8, count), F32),
        ],
    )
    return pl.pallas_call(
        functools.partial(mix_kernel, modes, size, ndoc),
        grid_spec=grid_spec,
        out_shape=[
            jax.ShapeDtypeStruct((count, width), BF16),
            jax.ShapeDtypeStruct((copies, modes, width), BF16),
        ],
        compiler_params=params(),
        cost_estimate=pl.CostEstimate(flops=60 * count * width, bytes_accessed=8 * count * width, transcendentals=count * width),
        name="mix",
    )(*scalars[:2], x, x, halo, taps, by_step(rates, wide, size))


def conv(low, share, room, scalars, x, halo, taps, mixed, rates, residues, skip, residual, states, size, ndoc, nblocks):
    _, count, width = x.shape
    modes = rates.shape[0]
    rows = count // nblocks
    wide = math.gcd(math.gcd(low, share), WIDE)
    first = low // wide
    carried = states is not None
    tile = lambda t, *_: (0, first + t)
    deep = lambda t, *_: (0, 0, first + t)
    step = pl.BlockSpec((1, modes, wide // size), lambda t, *_: (first + t, 0, 0))
    in_specs = [
        pl.BlockSpec((1, count, wide), deep),
        pl.BlockSpec((1, HALO, wide), deep),
        pl.BlockSpec((1, SHORT, wide), deep),
        pl.BlockSpec((count, wide), tile),
        step,
        step,
        pl.BlockSpec((1, wide), tile),
        pl.BlockSpec((count, wide), tile),
    ]
    operands = [x, halo, taps, mixed, by_step(rates, wide, size), by_step(residues, wide, size), skip, residual]
    scratch = [
        pltpu.VMEM((3, count + 2 * HALO, LANES), F32),
        pltpu.VMEM((count // CHUNK, CHUNK, CHUNK), BF16),
        pltpu.VMEM((count // CHUNK, CHUNK, LANES), BF16),
        pltpu.VMEM((count // CHUNK, LANES, CHUNK), F32),
        pltpu.SMEM((2 + count // CHUNK,), jnp.int32),
    ]
    if carried:
        in_specs.append(pl.BlockSpec((nblocks, modes, wide), deep))
        operands.append(states)
        scratch.append(pltpu.SMEM((nblocks + 1,), jnp.int32))
        out_specs, out_shape = handed(share, room, wide, count, nblocks)
    else:
        out_specs = [pl.BlockSpec((count, wide), lambda t, *_: (0, t))] * 2
        out_shape = [jax.ShapeDtypeStruct((count, share), F32), jax.ShapeDtypeStruct((count, share), BF16)]
    grid_spec = pltpu.PrefetchScalarGridSpec(
        num_scalar_prefetch=3, grid=(share // wide,), in_specs=in_specs, out_specs=out_specs, scratch_shapes=scratch
    )
    return pl.pallas_call(
        functools.partial(conv_kernel, modes, size, ndoc, nblocks, carried),
        grid_spec=grid_spec,
        out_shape=out_shape,
        compiler_params=params(),
        cost_estimate=pl.CostEstimate(
            flops=2 * 1152 * count * share, bytes_accessed=8 * count * share, transcendentals=count * share
        ),
        name="conv",
    )(*scalars, *operands)


def handed(share, room, wide, count, nblocks):
    rows = count // nblocks
    specs = [
        pl.BlockSpec((nblocks, rows, wide), lambda t, *_: (0, 0, t)),
        pl.BlockSpec((rows, wide), lambda t, *_: (0, t)),
        pl.BlockSpec((count, LANES), whole_array(2)),
    ]
    shapes = [
        jax.ShapeDtypeStruct((nblocks, rows, share + room), BF16),
        jax.ShapeDtypeStruct((rows, share), BF16),
        jax.ShapeDtypeStruct((count, LANES), F32),
    ]
    return specs, shapes


def add(scalars, base, gate, rates, residues, states, size, ndoc, nblocks):
    count, share = base.shape
    modes = rates.shape[0]
    wide = math.gcd(share, WIDE)
    tile = lambda t, *_: (0, t)
    step = pl.BlockSpec((1, modes, wide // size), lambda t, *_: (t, 0, 0))
    out_specs, out_shape = handed(share, 0, wide, count, nblocks)
    grid_spec = pltpu.PrefetchScalarGridSpec(
        num_scalar_prefetch=3,
        grid=(share // wide,),
        in_specs=[
            pl.BlockSpec((count, wide), tile),
            pl.BlockSpec((count, wide), tile),
            step,
            step,
            pl.BlockSpec((nblocks, modes, wide), lambda t, *_: (0, 0, t)),
        ],
        out_specs=out_specs,
        scratch_shapes=[
            pltpu.VMEM((count, LANES), F32),
            pltpu.SMEM((2 + count // CHUNK,), jnp.int32),
            pltpu.SMEM((nblocks + 1,), jnp.int32),
        ],
    )
    return pl.pallas_call(
        functools.partial(add_kernel, modes, size, ndoc, nblocks),
        grid_spec=grid_spec,
        out_shape=out_shape,
        compiler_params=params(),
        cost_estimate=pl.CostEstimate(flops=300 * count * share, bytes_accessed=8 * count * share, transcendentals=count * share),
        name="add",
    )(*scalars, base, gate, by_step(rates, wide, size), by_step(residues, wide, size), states)


def norm(where, owner, blocks, spare, gain):
    nblocks, rows, _ = blocks[0].shape
    count, width = nblocks * rows, gain.shape[1]
    vmem = pl.BlockSpec(memory_space=pltpu.VMEM)
    smem = pl.BlockSpec(memory_space=pltpu.SMEM)
    return pl.pallas_call(
        functools.partial(norm_kernel, len(blocks)),
        in_specs=[smem, smem] + [vmem] * (len(blocks) + 2),
        out_specs=vmem,
        out_shape=jax.ShapeDtypeStruct((count, width), BF16),
        compiler_params=pltpu.CompilerParams(vmem_limit_bytes=16 * 1024 * 1024),
        cost_estimate=pl.CostEstimate(flops=3 * count * width, bytes_accessed=4 * count * width, transcendentals=0),
        name="norm",
    )(where, owner, *blocks, spare, gain)


def on_device(features, residual, short_taps, rates, residues, skip, gain, lengths, owner):
    count, _, width = features.shape
    size = width // rates.shape[0]
    ndoc = lengths.shape[0]
    nblocks = lax.axis_size("ctx")
    rows = count // nblocks
    where = lax.axis_index("ctx")
    x = jnp.transpose(features, (1, 0, 2))
    pairs = [(i, i + 1) for i in range(nblocks - 1)]
    halo = lax.ppermute(x[:, count - HALO :], "ctx", pairs)

    scalars = (where.reshape(1).astype(jnp.int32), lengths, owner)
    rates, residues = rates.T, residues.T

    table = owner.reshape(nblocks, nblocks)
    ids = jnp.arange(nblocks, dtype=jnp.int32)
    mine = lax.dynamic_index_in_dim(table, where, 0, keepdims=False)
    twice = jnp.any((mine[:, None] == mine[None, :]) & (ids[None, :] < ids[:, None]), 1)
    unused = nblocks * (nblocks - 1) // 2 - jnp.sum(jnp.where(twice, 0, mine))
    slots = jnp.where(twice, unused, mine).astype(jnp.int32)
    spare_shift = jnp.sum(jnp.where(twice, table[0], 0))

    def exchanged(value):
        return lax.all_to_all(value, "ctx", split_axis=0, concat_axis=0, tiled=True)

    first = width * SPLIT[0] // sum(SPLIT)
    second = width - first
    mixed, copies = mix(scalars, x, halo, short_taps, rates, size, ndoc, nblocks)
    states = exchanged(copies)
    shared = (scalars, x, halo, short_taps, mixed, rates, residues, skip.reshape(1, width), residual)
    base, gate = conv(0, first, 0, *shared, None, size, ndoc, nblocks)
    out, spare, squares = add(scalars, base, gate, rates, residues, states, size, ndoc, nblocks)
    block = exchanged(out)
    out, last_spare, last_squares = conv(first, second, LANES, *shared, states, size, ndoc, nblocks)
    mean = lax.psum(jnp.sum(squares + last_squares, 1), "mp") / (width * lax.axis_size("mp"))
    inverse = lax.rsqrt(mean + EPS)
    high = lax.reduce_precision(inverse, 8, 7)
    column = iota((count, LANES), 1)
    halves = jnp.where(column == 0, high[:, None], jnp.where(column == 1, (inverse - high)[:, None], 0.0))
    halves = halves.reshape(nblocks, rows, LANES)
    in_slot = slots[None, :] == ids[:, None]
    by_slot = jnp.sum(jnp.where(in_slot[:, :, None, None], halves[None], 0.0), 1).astype(BF16)
    spare_halves = jnp.sum(jnp.where(twice[:, None, None], halves, 0.0), 0).astype(BF16)
    out = lax.dynamic_update_slice(out, by_slot, (0, 0, second))
    blocks = [block, exchanged(out)]
    spares = jnp.concatenate([spare, last_spare, spare_halves], 1)

    def moved(by):
        return lambda value: lax.ppermute(value, "ctx", [(s, (s + by) % nblocks) for s in range(nblocks)])

    spare = lax.switch(spare_shift, [lambda value: value] + [moved(d) for d in range(1, nblocks)], spares)
    return norm(scalars[0], owner, blocks, spare, gain.reshape(1, width))


def solution(mesh):
    return jax.shard_map(
        on_device,
        mesh=mesh,
        in_specs=(
            P("ctx", None, "mp"),
            P("ctx", "mp"),
            P(None, None, "mp"),
            P("mp", None),
            P("mp", None),
            P("mp"),
            P("mp"),
            P(),
            P(),
        ),
        out_specs=P("ctx", "mp"),
        check_vma=False,
    )
```

```python
import functools
import math

import jax
import jax.numpy as jnp
from jax import lax
from jax.experimental import pallas as pl
from jax.experimental.pallas import tpu as pltpu
from jax.sharding import PartitionSpec as P

SHORT = 7
LANES = 128
CHUNK = 128
HALO = 8
EPS = 1e-06
SPLIT = (4, 4)
NEAR = 4
ROOM = 16
WIDE = 512
SPAN = 64
F32 = jnp.float32
BF16 = jnp.bfloat16
VMEM_LIMIT = 64 * 1024 * 1024 - 256 * 1024


def iota(shape, dim):
    return lax.broadcasted_iota(jnp.int32, shape, dim)


def document(ends, positions):
    total = jnp.zeros(positions.shape, jnp.int32)
    for end in ends:
        total = total + (positions >= end).astype(jnp.int32)
    return total


def scalar_document(ends, position):
    total = jnp.int32(0)
    for end in ends:
        total = total + (position >= end).astype(jnp.int32)
    return jnp.where(position < 0, -1, total)


def running_ends(lengths_ref, ndoc):
    ends, total = [], jnp.int32(0)
    for j in range(ndoc):
        total = total + lengths_ref[j]
        ends.append(total)
    return ends


def write_lag_masks(mask_ref, ends, base, count):
    mask_ref[...] = jnp.ones_like(mask_ref)
    gap = jnp.zeros((1, LANES), F32)
    for end in ends:
        row = end - base + HALO

        @pl.when((row >= 0) & (row < count + HALO))
        def _(row=row):
            for lag in (1, 2, 3):
                for past in range(lag):
                    mask_ref[lag - 1, pl.ds(row + past, 1), :] = gap


def row_documents(ends, base, count):
    return document(ends, base + iota((8, count), 1)).astype(F32)


def is_second(owner_ref, nblocks, i):
    found = jnp.bool_(False)
    for j in range(i):
        found = found | (owner_ref[j] == owner_ref[i])
    return found


def write_slots(slot_ref, owner_ref, where, nblocks):
    unused = jnp.int32(nblocks * (nblocks - 1) // 2)
    seconds = [is_second(owner_ref, nblocks, i) for i in range(nblocks)]
    mine = [owner_ref[where * nblocks + i] for i in range(nblocks)]
    for i in range(nblocks):
        unused = unused - jnp.where(seconds[i], 0, mine[i])
    for i in range(nblocks):
        slot_ref[i] = jnp.where(seconds[i], unused, mine[i])
    slot_ref[nblocks] = unused


def tile_rates(rates_ref, low, size):
    first = low // size
    columns = [rates_ref[:, first + g : first + g + 1] for g in range(LANES // size)]
    return jnp.concatenate([jnp.broadcast_to(column, (column.shape[0], LANES)) for column in columns], 0)


def short_conv(ext, taps, masks):
    def back(value, lag):
        return pltpu.roll(value, lag, 0) * masks[lag - 1]

    one, two = back(ext, 1), back(ext, 2)
    far = ext * taps[6]
    middle = ext * taps[3] + one * taps[4] + two * taps[5] + back(far, 3)
    near = ext * taps[0] + one * taps[1] + two * taps[2] + back(middle, 3)
    return near[HALO:]


def extended(x_ref, halo_ref, which, start, lanes):
    rows = x_ref[0, start : start + SPAN, lanes].astype(F32)
    if start == 0:
        ahead = halo_ref[which, :, lanes].astype(F32)
    else:
        ahead = x_ref[0, start - 16 : start, lanes].astype(F32)[16 - HALO :]
    return jnp.concatenate([ahead, rows], 0)


def tap_rows(taps_ref, which, lanes):
    return [taps_ref[which, j : j + 1, lanes] for j in range(SHORT)]


def lag_masks(mask_ref, start):
    return [mask_ref[l, start : start + SPAN + HALO, :] for l in range(3)]


def group_mask(modes, size):
    return (iota((LANES, LANES), 0) // modes) == (iota((LANES, LANES), 1) // size)


def each_tile(width, body):
    for low in range(0, width, LANES):
        body(slice(low, low + LANES))


def write_shifts(shift_ref, mask_ref, ends, base, count):
    mask_ref[...] = jnp.ones_like(mask_ref)
    gap = jnp.zeros((1, LANES), F32)
    for end in ends:
        row = end - base + HALO

        @pl.when((row >= 0) & (row < count + HALO))
        def _(row=row):
            for lag in range(1, NEAR + 1):
                for past in range(lag):
                    mask_ref[lag - 1, pl.ds(row + past, 1), :] = gap

    reach = CHUNK + HALO
    back = iota((reach, LANES), 0) + HALO - iota((reach, LANES), 1)
    late = iota((reach, 16), 0) + HALO - LANES - iota((reach, 16), 1)
    for chunk in range(count // CHUNK):
        first, second = [], []
        for lag in range(1, NEAR):
            mask = mask_ref[lag - 1, chunk * CHUNK : chunk * CHUNK + reach, :]
            first.append(jnp.where(back == lag, mask, 0.0))
            second.append(jnp.where(late == lag, mask[:, :16], 0.0))
        shift_ref[chunk, :, :LANES] = jnp.concatenate(first, 0).astype(BF16)
        shift_ref[chunk, :, LANES:] = jnp.concatenate(second, 0).astype(BF16)


def mix_kernel(
    modes, size, ndoc,
    where_ref, lengths_ref,
    key_ref, value_ref, halo_ref, taps_ref, rates_ref,
    mixed_ref, state_ref,
    shift_ref, mask_ref, tail_ref,
):
    _, count, width = key_ref.shape
    chunks = count // CHUNK
    reach = CHUNK + HALO

    @pl.when(pl.program_id(0) == 0)
    def _():
        base = where_ref[0] * count
        ends = running_ends(lengths_ref, ndoc)
        write_shifts(shift_ref, mask_ref, ends, base, count)
        last = scalar_document(ends, base + count - 1).astype(F32)
        tail_ref[...] = jnp.where(row_documents(ends, base, count) == last, 1.0, 0.0).astype(F32)

    def window(x_ref, which, start, lanes):
        if start == 0:
            halo = halo_ref[which, :, lanes].astype(F32)
            ahead = jnp.concatenate([jnp.zeros((16 - HALO, LANES), F32), halo], 0).astype(BF16)
        else:
            ahead = x_ref[0, start - 16 : start, lanes]
        return jnp.concatenate([ahead, x_ref[0, start : start + CHUNK, lanes]], 0)

    def finish(here, moved, taps, apart):
        rows = [here] + [moved[lag * reach : (lag + 1) * reach] for lag in range(NEAR - 1)]
        far = sum(rows[lag] * taps[NEAR + lag] for lag in range(SHORT - NEAR))
        far = pltpu.roll(far, NEAR, 0)[HALO:] * apart
        return far + sum(row[HALO:] * taps[lag] for lag, row in enumerate(rows))

    def tile(lanes):
        key_taps, value_taps = tap_rows(taps_ref, 1, lanes), tap_rows(taps_ref, 2, lanes)
        for chunk in range(chunks):
            start = chunk * CHUNK
            keys, values = window(key_ref, 1, start, lanes), window(value_ref, 2, start, lanes)
            moved = jnp.dot(shift_ref[chunk], jnp.concatenate([keys, values], 1), preferred_element_type=F32)
            apart = mask_ref[NEAR - 1, HALO + start : HALO + start + CHUNK, :]
            key = finish(keys.astype(F32)[16 - HALO :], moved[:, :LANES], key_taps, apart)
            value = finish(values.astype(F32)[16 - HALO :], moved[:, LANES:], value_taps, apart)
            mixed_ref[start : start + CHUNK, lanes] = (key * value).astype(BF16)
        rate = tile_rates(rates_ref.at[0], lanes.start, size)
        leave = jnp.exp(-rate * (CHUNK - 1 - iota((LANES, CHUNK), 1)).astype(F32))
        whole = jnp.exp(-rate * CHUNK)
        spans = []
        for chunk in reversed(range(chunks)):
            tail = tail_ref[0:1, chunk * CHUNK : (chunk + 1) * CHUNK]
            spans.append((leave * tail).astype(BF16))
            leave = leave * whole
        full = jnp.dot(jnp.concatenate(spans[::-1], 1), mixed_ref[:, lanes], preferred_element_type=F32)
        full = jnp.where(group_mask(modes, size), full, 0.0)
        state = jnp.sum(full.reshape(LANES // modes, modes, LANES), 0).astype(BF16)
        for owner in range(state_ref.shape[0]):
            state_ref[owner, :, lanes] = state

    each_tile(width, tile)


def left_state(states_ref, flags_ref, rate, lanes, modes, size, count):
    inside = group_mask(modes, size)
    where = flags_ref[1]

    def gather(v, total):
        weight = jnp.exp(-rate * ((where - 1 - v) * count).astype(F32))
        piece = jnp.concatenate([states_ref[v, :, lanes].astype(F32)] * (LANES // modes), 0)
        return total + jnp.where(inside, piece * weight, 0.0)

    return lax.fori_loop(flags_ref[0], where, gather, jnp.zeros((LANES, LANES), F32))


def write_flags(flags_ref, ends, where, count, nblocks):
    before = scalar_document(ends, where * count - 1)
    first = jnp.int32(0)
    for v in range(nblocks):
        first = first + (scalar_document(ends, (v + 1) * count - 1) < before).astype(jnp.int32)
    flags_ref[0] = first
    flags_ref[1] = where
    for chunk in range(count // CHUNK):
        start = where * count + chunk * CHUNK
        held = scalar_document(ends, start - 1) == scalar_document(ends, start + CHUNK - 1)
        flags_ref[2 + chunk] = held.astype(jnp.int32)


def hand_over(out_ref, squares_ref, slot_ref, summed, start, rows, lanes):
    squares_ref[start : start + SPAN, :] += summed * summed
    rounded = summed.astype(BF16)
    for b in range(SPAN // rows):
        tile = lanes.start // LANES * rows
        out_ref[slot_ref[start // rows + b], tile : tile + rows, :] = rounded[b * rows : (b + 1) * rows]


def conv_kernel(modes, size, ndoc, nblocks, carried, where_ref, lengths_ref, owner_ref, *refs):
    x_ref, halo_ref, taps_ref, mixed_ref, rates_ref, residues_ref, skip_ref, residual_ref = refs[:8]
    refs = refs[8:]
    if carried:
        states_ref, out_ref, spare_ref, squares_ref = refs[:4]
        refs = refs[4:]
    else:
        base_ref, gate_ref = refs[:2]
        refs = refs[2:]
    mask_ref, same_ref, keep_ref, tail_ref, flags_ref = refs[:5]
    count, width = mixed_ref.shape
    chunks = count // CHUNK

    @pl.when(pl.program_id(0) == 0)
    def _():
        where = where_ref[0]
        base = where * count
        ends = running_ends(lengths_ref, ndoc)
        write_lag_masks(mask_ref, ends, base, count)
        write_flags(flags_ref, ends, where, count, nblocks)
        if carried:
            write_slots(refs[5], owner_ref, where, nblocks)
            squares_ref[...] = jnp.zeros_like(squares_ref)
        documents = row_documents(ends, base, count)
        causal = iota((CHUNK, CHUNK), 1) <= iota((CHUNK, CHUNK), 0)
        for chunk in range(chunks):
            start = base + chunk * CHUNK
            there = jnp.broadcast_to(documents[0:1, chunk * CHUNK : (chunk + 1) * CHUNK], (CHUNK, CHUNK))
            here = there.T
            same_ref[chunk] = jnp.where((here == there) & causal, 1.0, 0.0).astype(BF16)
            before = scalar_document(ends, start - 1).astype(F32)
            keep_ref[chunk] = jnp.where(here == before, 1.0, 0.0).astype(BF16)
            last = scalar_document(ends, start + CHUNK - 1).astype(F32)
            tail_ref[chunk] = jnp.where(there == last, 1.0, 0.0).astype(F32)

    groups = LANES // modes

    def tile(lanes):
        rate = tile_rates(rates_ref.at[0], lanes.start, size)
        scale = tile_rates(residues_ref.at[0], lanes.start, size) * jnp.sqrt(1.0 - jnp.exp(-2.0 * rate))
        down = iota((CHUNK, LANES), 0)
        along = iota((LANES, CHUNK), 1)
        entry = (scale.T * jnp.exp(-rate.T * (down + 1).astype(F32))).astype(BF16)
        leave = jnp.exp(-rate * (CHUNK - 1 - along).astype(F32))
        whole = jnp.exp(-rate * CHUNK)
        terms = scale * jnp.where(along == 0, 1.0, leave * jnp.exp(-rate))
        toeplitz = []
        for g in range(groups):
            line = jnp.sum(terms[g * modes : (g + 1) * modes], 0, keepdims=True)
            top = pltpu.roll(jnp.broadcast_to(line, (8, CHUNK)), 0, 1, stride=1, stride_axis=0)
            parts = [top] + [pltpu.roll(top, 8 * k, 1) for k in range(1, CHUNK // 8)]
            toeplitz.append(jnp.concatenate(parts, 0).astype(BF16))
        inside = group_mask(modes, size)
        state = left_state(states_ref, flags_ref, rate, lanes, modes, size, count) if carried else None
        taps = tap_rows(taps_ref, 0, lanes)
        skip = skip_ref[:, lanes]
        lane_group = iota((CHUNK, LANES), 1) // size
        for chunk in range(chunks):
            start = chunk * CHUNK
            mixed = mixed_ref[start : start + CHUNK, lanes]
            same = same_ref[chunk]
            left = [t * same for t in toeplitz]
            right = [jnp.where(lane_group == g, mixed, jnp.zeros_like(mixed)) for g in range(groups)]
            if state is not None:
                left.append(entry * keep_ref[chunk])
                right.append(state.astype(BF16))
            longer = jnp.dot(jnp.concatenate(left, 1), jnp.concatenate(right, 0), preferred_element_type=F32)
            if chunk + 1 < chunks:
                fresh = jnp.dot((leave * tail_ref[chunk]).astype(BF16), mixed, preferred_element_type=F32)
                held = flags_ref[2 + chunk] == 1
                fresh = jnp.where(inside, fresh, 0.0)
                state = fresh if state is None else jnp.where(held, whole * state, 0.0) + fresh
            body = longer + skip * mixed.astype(F32)
            for half in range(start, start + CHUNK, SPAN):
                gate = short_conv(extended(x_ref, halo_ref, 0, half, lanes), taps, lag_masks(mask_ref, half))
                inner = body[half - start : half - start + SPAN]
                summed = residual_ref[half : half + SPAN, lanes].astype(F32) + gate * inner
                if carried:
                    hand_over(out_ref, squares_ref, refs[5], summed, half, count // nblocks, lanes)
                else:
                    base_ref[half : half + SPAN, lanes] = summed
                    gate_ref[half : half + SPAN, lanes] = gate.astype(BF16)

    each_tile(width, tile)
    if carried:
        spare_ref[...] = out_ref[refs[5][nblocks]]


def add_kernel(
    modes, size, ndoc, nblocks,
    where_ref, lengths_ref, owner_ref,
    base_ref, gate_ref, rates_ref, residues_ref, states_ref,
    out_ref, spare_ref, squares_ref,
    keep_ref, flags_ref, slot_ref,
):
    count, width = base_ref.shape
    chunks = count // CHUNK

    @pl.when(pl.program_id(0) == 0)
    def _():
        where = where_ref[0]
        ends = running_ends(lengths_ref, ndoc)
        write_flags(flags_ref, ends, where, count, nblocks)
        write_slots(slot_ref, owner_ref, where, nblocks)
        squares_ref[...] = jnp.zeros_like(squares_ref)
        before = scalar_document(ends, where * count - 1)
        kept = jnp.int32(0)
        for end in reversed(ends):
            kept = jnp.where(end >= where * count, end - where * count, kept)
        kept = jnp.where(before < 0, 0, kept)
        keep_ref[...] = jnp.where(iota((count, LANES), 0) < kept, 1.0, 0.0).astype(F32)

    def tile(lanes):
        rate = tile_rates(rates_ref.at[0], lanes.start, size)
        scale = tile_rates(residues_ref.at[0], lanes.start, size) * jnp.sqrt(1.0 - jnp.exp(-2.0 * rate))
        down = iota((CHUNK, LANES), 0)
        entry = (scale.T * jnp.exp(-rate.T * (down + 1).astype(F32))).astype(BF16)
        whole = jnp.exp(-rate * CHUNK)
        state = left_state(states_ref, flags_ref, rate, lanes, modes, size, count)
        held = []
        for _ in range(chunks):
            held.append(state.astype(BF16))
            state = state * whole
        left = jnp.dot(entry, jnp.concatenate(held, 1), preferred_element_type=F32)
        for start in range(0, count, SPAN):
            low = start % CHUNK
            chunk = start // CHUNK
            carried = left[low : low + SPAN, chunk * LANES : (chunk + 1) * LANES] * keep_ref[start : start + SPAN, :]
            gate = gate_ref[start : start + SPAN, lanes].astype(F32)
            summed = base_ref[start : start + SPAN, lanes] + gate * carried
            hand_over(out_ref, squares_ref, slot_ref, summed, start, count // nblocks, lanes)

    each_tile(width, tile)
    spare_ref[...] = out_ref[slot_ref[nblocks]]


def norm_kernel(parts, where_ref, owner_ref, *refs):
    blocks = refs[:parts]
    spare_ref, gain_ref, out_ref = refs[parts:]
    count, width = out_ref.shape
    nblocks = blocks[0].shape[0]
    rows = count // nblocks
    spare_block = jnp.int32(0)
    for i in range(nblocks):
        spare_block = jnp.where(is_second(owner_ref, nblocks, i), i, spare_block)

    def block(i, carry):
        rows_out = pl.ds(pl.multiple_of(i * rows, rows), rows)
        is_spare = spare_block == i
        ahead = where_ref[0] - owner_ref[i]
        source = jnp.where(ahead < 0, ahead + nblocks, ahead)
        halves = jnp.where(is_spare, spare_ref[-ROOM:, :].astype(F32), blocks[-1][source, -ROOM:, :].astype(F32))[0:1]
        scale = halves + pltpu.roll(jnp.broadcast_to(halves, (8, LANES)), LANES - rows, 1)[0:1]
        scale = jnp.broadcast_to(scale, (LANES, LANES)).T[:rows]
        tile = 0
        for part in range(parts):
            for low in range(0, min(blocks[part].shape[1] // rows * rows, width // LANES * rows - tile * rows), rows):
                outs = slice(tile * LANES, (tile + 1) * LANES)
                value = blocks[part][source, low : low + rows, :].astype(F32)
                value = jnp.where(is_spare, spare_ref[tile * rows : (tile + 1) * rows, :].astype(F32), value)
                out_ref[rows_out, outs] = (value * scale * gain_ref[:, outs]).astype(BF16)
                tile += 1
        return carry

    lax.fori_loop(0, nblocks, block, 0)


def params():
    return pltpu.CompilerParams(dimension_semantics=("arbitrary",), vmem_limit_bytes=VMEM_LIMIT)


def whole_array(rank):
    return lambda *_: (0,) * rank


def by_step(rates, wide, size):
    modes, groups = rates.shape
    held = wide // size
    return jnp.transpose(rates.reshape(modes, groups // held, held), (1, 0, 2))


def mix(scalars, x, halo, taps, rates, size, ndoc, copies):
    _, count, width = x.shape
    modes = rates.shape[0]
    wide = min(WIDE, width)
    deep = lambda t, *_: (0, 0, t)
    grid_spec = pltpu.PrefetchScalarGridSpec(
        num_scalar_prefetch=2,
        grid=(width // wide,),
        in_specs=[
            pl.BlockSpec((1, count, wide), lambda t, *_: (1, 0, t)),
            pl.BlockSpec((1, count, wide), lambda t, *_: (2, 0, t)),
            pl.BlockSpec((3, HALO, wide), deep),
            pl.BlockSpec((3, SHORT, wide), deep),
            pl.BlockSpec((1, modes, wide // size), lambda t, *_: (t, 0, 0)),
        ],
        out_specs=[
            pl.BlockSpec((count, wide), lambda t, *_: (0, t)),
            pl.BlockSpec((copies, modes, wide), deep),
        ],
        scratch_shapes=[
            pltpu.VMEM((count // CHUNK, (NEAR - 1) * (CHUNK + HALO), CHUNK + 16), BF16),
            pltpu.VMEM((NEAR, count + 2 * HALO, LANES), F32),
            pltpu.VMEM((8, count), F32),
        ],
    )
    return pl.pallas_call(
        functools.partial(mix_kernel, modes, size, ndoc),
        grid_spec=grid_spec,
        out_shape=[
            jax.ShapeDtypeStruct((count, width), BF16),
            jax.ShapeDtypeStruct((copies, modes, width), BF16),
        ],
        compiler_params=params(),
        cost_estimate=pl.CostEstimate(flops=60 * count * width, bytes_accessed=8 * count * width, transcendentals=count * width),
        name="mix",
    )(*scalars[:2], x, x, halo, taps, by_step(rates, wide, size))


def conv(low, share, room, scalars, x, halo, taps, mixed, rates, residues, skip, residual, states, size, ndoc, nblocks):
    _, count, width = x.shape
    modes = rates.shape[0]
    rows = count // nblocks
    wide = math.gcd(math.gcd(low, share), WIDE)
    first = low // wide
    carried = states is not None
    tile = lambda t, *_: (0, first + t)
    deep = lambda t, *_: (0, 0, first + t)
    step = pl.BlockSpec((1, modes, wide // size), lambda t, *_: (first + t, 0, 0))
    in_specs = [
        pl.BlockSpec((1, count, wide), deep),
        pl.BlockSpec((1, HALO, wide), deep),
        pl.BlockSpec((1, SHORT, wide), deep),
        pl.BlockSpec((count, wide), tile),
        step,
        step,
        pl.BlockSpec((1, wide), tile),
        pl.BlockSpec((count, wide), tile),
    ]
    operands = [x, halo, taps, mixed, by_step(rates, wide, size), by_step(residues, wide, size), skip, residual]
    scratch = [
        pltpu.VMEM((3, count + 2 * HALO, LANES), F32),
        pltpu.VMEM((count // CHUNK, CHUNK, CHUNK), BF16),
        pltpu.VMEM((count // CHUNK, CHUNK, LANES), BF16),
        pltpu.VMEM((count // CHUNK, LANES, CHUNK), F32),
        pltpu.SMEM((2 + count // CHUNK,), jnp.int32),
    ]
    if carried:
        in_specs.append(pl.BlockSpec((nblocks, modes, wide), deep))
        operands.append(states)
        scratch.append(pltpu.SMEM((nblocks + 1,), jnp.int32))
        out_specs, out_shape = handed(share, room, wide, count, nblocks)
    else:
        out_specs = [pl.BlockSpec((count, wide), lambda t, *_: (0, t))] * 2
        out_shape = [jax.ShapeDtypeStruct((count, share), F32), jax.ShapeDtypeStruct((count, share), BF16)]
    grid_spec = pltpu.PrefetchScalarGridSpec(
        num_scalar_prefetch=3, grid=(share // wide,), in_specs=in_specs, out_specs=out_specs, scratch_shapes=scratch
    )
    return pl.pallas_call(
        functools.partial(conv_kernel, modes, size, ndoc, nblocks, carried),
        grid_spec=grid_spec,
        out_shape=out_shape,
        compiler_params=params(),
        cost_estimate=pl.CostEstimate(
            flops=2 * 1152 * count * share, bytes_accessed=8 * count * share, transcendentals=count * share
        ),
        name="conv",
    )(*scalars, *operands)


def handed(share, room, wide, count, nblocks):
    rows = count // nblocks
    specs = [
        pl.BlockSpec((nblocks, wide // LANES * rows, LANES), lambda t, *_: (0, t, 0)),
        pl.BlockSpec((wide // LANES * rows, LANES), lambda t, *_: (t, 0)),
        pl.BlockSpec((count, LANES), whole_array(2)),
    ]
    shapes = [
        jax.ShapeDtypeStruct((nblocks, share // LANES * rows + room, LANES), BF16),
        jax.ShapeDtypeStruct((share // LANES * rows, LANES), BF16),
        jax.ShapeDtypeStruct((count, LANES), F32),
    ]
    return specs, shapes


def add(scalars, base, gate, rates, residues, states, size, ndoc, nblocks):
    count, share = base.shape
    modes = rates.shape[0]
    wide = math.gcd(share, WIDE)
    tile = lambda t, *_: (0, t)
    step = pl.BlockSpec((1, modes, wide // size), lambda t, *_: (t, 0, 0))
    out_specs, out_shape = handed(share, 0, wide, count, nblocks)
    grid_spec = pltpu.PrefetchScalarGridSpec(
        num_scalar_prefetch=3,
        grid=(share // wide,),
        in_specs=[
            pl.BlockSpec((count, wide), tile),
            pl.BlockSpec((count, wide), tile),
            step,
            step,
            pl.BlockSpec((nblocks, modes, wide), lambda t, *_: (0, 0, t)),
        ],
        out_specs=out_specs,
        scratch_shapes=[
            pltpu.VMEM((count, LANES), F32),
            pltpu.SMEM((2 + count // CHUNK,), jnp.int32),
            pltpu.SMEM((nblocks + 1,), jnp.int32),
        ],
    )
    return pl.pallas_call(
        functools.partial(add_kernel, modes, size, ndoc, nblocks),
        grid_spec=grid_spec,
        out_shape=out_shape,
        compiler_params=params(),
        cost_estimate=pl.CostEstimate(flops=300 * count * share, bytes_accessed=8 * count * share, transcendentals=count * share),
        name="add",
    )(*scalars, base, gate, by_step(rates, wide, size), by_step(residues, wide, size), states)


def norm(where, owner, blocks, spare, gain, count):
    width = gain.shape[1]
    vmem = pl.BlockSpec(memory_space=pltpu.VMEM)
    smem = pl.BlockSpec(memory_space=pltpu.SMEM)
    return pl.pallas_call(
        functools.partial(norm_kernel, len(blocks)),
        in_specs=[smem, smem] + [vmem] * (len(blocks) + 2),
        out_specs=vmem,
        out_shape=jax.ShapeDtypeStruct((count, width), BF16),
        compiler_params=pltpu.CompilerParams(vmem_limit_bytes=16 * 1024 * 1024),
        cost_estimate=pl.CostEstimate(flops=3 * count * width, bytes_accessed=4 * count * width, transcendentals=0),
        name="norm",
    )(where, owner, *blocks, spare, gain)


def on_device(features, residual, short_taps, rates, residues, skip, gain, lengths, owner):
    count, _, width = features.shape
    size = width // rates.shape[0]
    ndoc = lengths.shape[0]
    nblocks = lax.axis_size("ctx")
    rows = count // nblocks
    where = lax.axis_index("ctx")
    x = jnp.transpose(features, (1, 0, 2))
    pairs = [(i, i + 1) for i in range(nblocks - 1)]
    halo = lax.ppermute(x[:, count - HALO :], "ctx", pairs)

    scalars = (where.reshape(1).astype(jnp.int32), lengths, owner)
    rates, residues = rates.T, residues.T

    table = owner.reshape(nblocks, nblocks)
    ids = jnp.arange(nblocks, dtype=jnp.int32)
    mine = lax.dynamic_index_in_dim(table, where, 0, keepdims=False)
    twice = jnp.any((mine[:, None] == mine[None, :]) & (ids[None, :] < ids[:, None]), 1)
    unused = nblocks * (nblocks - 1) // 2 - jnp.sum(jnp.where(twice, 0, mine))
    slots = jnp.where(twice, unused, mine).astype(jnp.int32)
    spare_shift = jnp.sum(jnp.where(twice, table[0], 0))

    def exchanged(value):
        return lax.all_to_all(value, "ctx", split_axis=0, concat_axis=0, tiled=True)

    first = width * SPLIT[0] // sum(SPLIT)
    second = width - first
    mixed, copies = mix(scalars, x, halo, short_taps, rates, size, ndoc, nblocks)
    states = exchanged(copies)
    shared = (scalars, x, halo, short_taps, mixed, rates, residues, skip.reshape(1, width), residual)
    base, gate = conv(0, first, 0, *shared, None, size, ndoc, nblocks)
    out, spare, squares = add(scalars, base, gate, rates, residues, states, size, ndoc, nblocks)
    block = exchanged(out)
    out, last_spare, last_squares = conv(first, second, ROOM, *shared, states, size, ndoc, nblocks)
    mean = lax.psum(jnp.sum(squares + last_squares, 1), "mp") / (width * lax.axis_size("mp"))
    inverse = lax.rsqrt(mean + EPS)
    high = lax.reduce_precision(inverse, 8, 7)
    halves = jnp.concatenate([high.reshape(nblocks, rows), (inverse - high).reshape(nblocks, rows)], 1)
    halves = jnp.pad(halves, ((0, 0), (0, LANES - 2 * rows)))
    in_slot = slots[None, :] == ids[:, None]
    by_slot = jnp.sum(jnp.where(in_slot[:, :, None], halves[None], 0.0), 1)
    by_slot = jnp.broadcast_to(by_slot.astype(BF16)[:, None], (nblocks, ROOM, LANES))
    spare_halves = jnp.sum(jnp.where(twice[:, None], halves, 0.0), 0).astype(BF16)
    out = lax.dynamic_update_slice(out, by_slot, (0, second // LANES * rows, 0))
    blocks = [block, exchanged(out)]
    spares = jnp.concatenate([spare, last_spare, jnp.broadcast_to(spare_halves[None], (ROOM, LANES))], 0)

    def moved(by):
        return lambda value: lax.ppermute(value, "ctx", [(s, (s + by) % nblocks) for s in range(nblocks)])

    spare = lax.switch(spare_shift, [lambda value: value] + [moved(d) for d in range(1, nblocks)], spares)
    return norm(scalars[0], owner, blocks, spare, gain.reshape(1, width), count)


def solution(mesh):
    return jax.shard_map(
        on_device,
        mesh=mesh,
        in_specs=(
            P("ctx", None, "mp"),
            P("ctx", "mp"),
            P(None, None, "mp"),
            P("mp", None),
            P("mp", None),
            P("mp"),
            P("mp"),
            P(),
            P(),
        ),
        out_specs=P("ctx", "mp"),
        check_vma=False,
    )
```

```python
import functools
import math

import jax
import jax.numpy as jnp
from jax import lax
from jax.experimental import pallas as pl
from jax.experimental.pallas import tpu as pltpu
from jax.sharding import PartitionSpec as P

SHORT = 7
LANES = 128
CHUNK = 128
HALO = 8
EPS = 1e-06
SPLIT = (4, 4)
NEAR = 4
ROOM = 16
WIDE = 512
NARROW = 256
SPAN = 64
F32 = jnp.float32
BF16 = jnp.bfloat16
VMEM_LIMIT = 64 * 1024 * 1024


def iota(shape, dim):
    return lax.broadcasted_iota(jnp.int32, shape, dim)


def document(ends, positions):
    total = jnp.zeros(positions.shape, jnp.int32)
    for end in ends:
        total = total + (positions >= end).astype(jnp.int32)
    return total


def scalar_document(ends, position):
    total = jnp.int32(0)
    for end in ends:
        total = total + (position >= end).astype(jnp.int32)
    return jnp.where(position < 0, -1, total)


def running_ends(lengths_ref, ndoc):
    ends, total = [], jnp.int32(0)
    for j in range(ndoc):
        total = total + lengths_ref[j]
        ends.append(total)
    return ends


def write_lag_masks(mask_ref, ends, base, count):
    mask_ref[...] = jnp.ones_like(mask_ref)
    gap = jnp.zeros((1, LANES), F32)
    for end in ends:
        row = end - base + HALO

        @pl.when((row >= 0) & (row < count + HALO))
        def _(row=row):
            for lag in (1, 2, 3):
                for past in range(lag):
                    mask_ref[lag - 1, pl.ds(row + past, 1), :] = gap


def row_documents(ends, base, count):
    return document(ends, base + iota((8, count), 1)).astype(F32)


def is_second(owner_ref, nblocks, i):
    found = jnp.bool_(False)
    for j in range(i):
        found = found | (owner_ref[j] == owner_ref[i])
    return found


def write_slots(slot_ref, owner_ref, where, nblocks):
    unused = jnp.int32(nblocks * (nblocks - 1) // 2)
    seconds = [is_second(owner_ref, nblocks, i) for i in range(nblocks)]
    mine = [owner_ref[where * nblocks + i] for i in range(nblocks)]
    for i in range(nblocks):
        unused = unused - jnp.where(seconds[i], 0, mine[i])
    for i in range(nblocks):
        slot_ref[i] = jnp.where(seconds[i], unused, mine[i])
    slot_ref[nblocks] = unused


def tile_rates(rates_ref, low, size):
    first = low // size
    columns = [rates_ref[:, first + g : first + g + 1] for g in range(LANES // size)]
    return jnp.concatenate([jnp.broadcast_to(column, (column.shape[0], LANES)) for column in columns], 0)


def short_conv(ext, taps, masks):
    def back(value, lag):
        return pltpu.roll(value, lag, 0) * masks[lag - 1]

    one, two = back(ext, 1), back(ext, 2)
    far = ext * taps[6]
    middle = ext * taps[3] + one * taps[4] + two * taps[5] + back(far, 3)
    near = ext * taps[0] + one * taps[1] + two * taps[2] + back(middle, 3)
    return near[HALO:]


def extended(x_ref, halo_ref, which, start, lanes):
    rows = x_ref[0, start : start + SPAN, lanes].astype(F32)
    if start == 0:
        ahead = halo_ref[which, :, lanes].astype(F32)
    else:
        ahead = x_ref[0, start - 16 : start, lanes].astype(F32)[16 - HALO :]
    return jnp.concatenate([ahead, rows], 0)


def tap_rows(taps_ref, which, lanes):
    return [taps_ref[which, j : j + 1, lanes] for j in range(SHORT)]


def lag_masks(mask_ref, start):
    return [mask_ref[l, start : start + SPAN + HALO, :] for l in range(3)]


def group_mask(modes, size):
    return (iota((LANES, LANES), 0) // modes) == (iota((LANES, LANES), 1) // size)


def each_tile(width, body):
    for low in range(0, width, LANES):
        body(slice(low, low + LANES))


def write_shifts(shift_ref, mask_ref, ends, base, count):
    mask_ref[...] = jnp.ones_like(mask_ref)
    gap = jnp.zeros((1, LANES), F32)
    for end in ends:
        row = end - base + HALO

        @pl.when((row >= 0) & (row < count + HALO))
        def _(row=row):
            for lag in range(1, NEAR + 1):
                for past in range(lag):
                    mask_ref[lag - 1, pl.ds(row + past, 1), :] = gap

    reach = SPAN + HALO
    back = iota((reach, SPAN + 16), 0) + HALO - iota((reach, SPAN + 16), 1)
    for span in range(count // SPAN):
        moves = []
        for lag in range(1, NEAR):
            mask = mask_ref[lag - 1, span * SPAN : span * SPAN + reach, : SPAN + 16]
            moves.append(jnp.where(back == lag, mask, 0.0))
        shift_ref[span] = jnp.concatenate(moves, 0).astype(BF16)


def mix_kernel(
    modes, size, ndoc,
    where_ref, lengths_ref,
    key_ref, value_ref, halo_ref, taps_ref, rates_ref,
    mixed_ref, state_ref,
    shift_ref, mask_ref, tail_ref,
):
    _, count, width = key_ref.shape
    chunks = count // CHUNK
    reach = SPAN + HALO

    @pl.when(pl.program_id(0) == 0)
    def _():
        base = where_ref[0] * count
        ends = running_ends(lengths_ref, ndoc)
        write_shifts(shift_ref, mask_ref, ends, base, count)
        last = scalar_document(ends, base + count - 1).astype(F32)
        tail_ref[...] = jnp.where(row_documents(ends, base, count) == last, 1.0, 0.0).astype(F32)

    def window(x_ref, which, start, lanes):
        if start == 0:
            halo = halo_ref[which, :, lanes].astype(F32)
            ahead = jnp.concatenate([jnp.zeros((16 - HALO, LANES), F32), halo], 0).astype(BF16)
        else:
            ahead = x_ref[0, start - 16 : start, lanes]
        return jnp.concatenate([ahead, x_ref[0, start : start + SPAN, lanes]], 0)

    def finish(here, moved, taps, apart):
        rows = [here] + [moved[lag * reach : (lag + 1) * reach] for lag in range(NEAR - 1)]
        far = sum(rows[lag] * taps[NEAR + lag] for lag in range(SHORT - NEAR))
        far = pltpu.roll(far, NEAR, 0)[HALO:] * apart
        return far + sum(row[HALO:] * taps[lag] for lag, row in enumerate(rows))

    def tile(lanes):
        key_taps, value_taps = tap_rows(taps_ref, 1, lanes), tap_rows(taps_ref, 2, lanes)
        for start in range(0, count, SPAN):
            keys, values = window(key_ref, 1, start, lanes), window(value_ref, 2, start, lanes)
            moved = jnp.dot(shift_ref[start // SPAN], jnp.concatenate([keys, values], 1), preferred_element_type=F32)
            apart = mask_ref[NEAR - 1, HALO + start : HALO + start + SPAN, :]
            key = finish(keys.astype(F32)[16 - HALO :], moved[:, :LANES], key_taps, apart)
            value = finish(values.astype(F32)[16 - HALO :], moved[:, LANES:], value_taps, apart)
            mixed_ref[start : start + SPAN, lanes] = (key * value).astype(BF16)
        rate = tile_rates(rates_ref.at[0], lanes.start, size)
        leave = jnp.exp(-rate * (CHUNK - 1 - iota((LANES, CHUNK), 1)).astype(F32))
        whole = jnp.exp(-rate * CHUNK)
        spans = []
        for chunk in reversed(range(chunks)):
            tail = tail_ref[0:1, chunk * CHUNK : (chunk + 1) * CHUNK]
            spans.append((leave * tail).astype(BF16))
            leave = leave * whole
        full = jnp.dot(jnp.concatenate(spans[::-1], 1), mixed_ref[:, lanes], preferred_element_type=F32)
        full = jnp.where(group_mask(modes, size), full, 0.0)
        state = jnp.sum(full.reshape(LANES // modes, modes, LANES), 0).astype(BF16)
        for owner in range(state_ref.shape[0]):
            state_ref[owner, :, lanes] = state

    each_tile(width, tile)


def left_state(states_ref, flags_ref, rate, lanes, modes, size, count):
    inside = group_mask(modes, size)
    where = flags_ref[1]

    def gather(v, total):
        weight = jnp.exp(-rate * ((where - 1 - v) * count).astype(F32))
        piece = jnp.concatenate([states_ref[v, :, lanes].astype(F32)] * (LANES // modes), 0)
        return total + jnp.where(inside, piece * weight, 0.0)

    return lax.fori_loop(flags_ref[0], where, gather, jnp.zeros((LANES, LANES), F32))


def write_flags(flags_ref, ends, where, count, nblocks):
    before = scalar_document(ends, where * count - 1)
    first = jnp.int32(0)
    for v in range(nblocks):
        first = first + (scalar_document(ends, (v + 1) * count - 1) < before).astype(jnp.int32)
    flags_ref[0] = first
    flags_ref[1] = where
    for chunk in range(count // CHUNK):
        start = where * count + chunk * CHUNK
        held = scalar_document(ends, start - 1) == scalar_document(ends, start + CHUNK - 1)
        flags_ref[2 + chunk] = held.astype(jnp.int32)


def hand_over(out_ref, squares_ref, slot_ref, summed, start, rows, lanes):
    squares_ref[start : start + SPAN, :] += summed * summed
    rounded = summed.astype(BF16)
    for b in range(SPAN // rows):
        tile = lanes.start // LANES * rows
        out_ref[slot_ref[start // rows + b], tile : tile + rows, :] = rounded[b * rows : (b + 1) * rows]


def conv_kernel(modes, size, ndoc, nblocks, carried, where_ref, lengths_ref, owner_ref, *refs):
    x_ref, halo_ref, taps_ref, mixed_ref, rates_ref, residues_ref, skip_ref, residual_ref = refs[:8]
    refs = refs[8:]
    if carried:
        states_ref, out_ref, spare_ref, squares_ref = refs[:4]
        refs = refs[4:]
    else:
        base_ref, gate_ref = refs[:2]
        refs = refs[2:]
    mask_ref, same_ref, keep_ref, tail_ref, flags_ref = refs[:5]
    count, width = mixed_ref.shape
    chunks = count // CHUNK

    @pl.when(pl.program_id(0) == 0)
    def _():
        where = where_ref[0]
        base = where * count
        ends = running_ends(lengths_ref, ndoc)
        write_lag_masks(mask_ref, ends, base, count)
        write_flags(flags_ref, ends, where, count, nblocks)
        if carried:
            write_slots(refs[5], owner_ref, where, nblocks)
            squares_ref[...] = jnp.zeros_like(squares_ref)
        documents = row_documents(ends, base, count)
        causal = iota((CHUNK, CHUNK), 1) <= iota((CHUNK, CHUNK), 0)
        for chunk in range(chunks):
            start = base + chunk * CHUNK
            there = jnp.broadcast_to(documents[0:1, chunk * CHUNK : (chunk + 1) * CHUNK], (CHUNK, CHUNK))
            here = there.T
            same_ref[chunk] = jnp.where((here == there) & causal, 1.0, 0.0).astype(BF16)
            before = scalar_document(ends, start - 1).astype(F32)
            keep_ref[chunk] = jnp.where(here == before, 1.0, 0.0).astype(BF16)
            last = scalar_document(ends, start + CHUNK - 1).astype(F32)
            tail_ref[chunk] = jnp.where(there == last, 1.0, 0.0).astype(F32)

    groups = LANES // modes

    def tile(lanes):
        rate = tile_rates(rates_ref.at[0], lanes.start, size)
        scale = tile_rates(residues_ref.at[0], lanes.start, size) * jnp.sqrt(1.0 - jnp.exp(-2.0 * rate))
        down = iota((CHUNK, LANES), 0)
        along = iota((LANES, CHUNK), 1)
        entry = (scale.T * jnp.exp(-rate.T * (down + 1).astype(F32))).astype(BF16)
        leave = jnp.exp(-rate * (CHUNK - 1 - along).astype(F32))
        whole = jnp.exp(-rate * CHUNK)
        terms = scale * jnp.where(along == 0, 1.0, leave * jnp.exp(-rate))
        toeplitz = []
        for g in range(groups):
            line = jnp.sum(terms[g * modes : (g + 1) * modes], 0, keepdims=True)
            top = pltpu.roll(jnp.broadcast_to(line, (8, CHUNK)), 0, 1, stride=1, stride_axis=0)
            parts = [top] + [pltpu.roll(top, 8 * k, 1) for k in range(1, CHUNK // 8)]
            toeplitz.append(jnp.concatenate(parts, 0).astype(BF16))
        inside = group_mask(modes, size)
        state = left_state(states_ref, flags_ref, rate, lanes, modes, size, count) if carried else None
        taps = tap_rows(taps_ref, 0, lanes)
        skip = skip_ref[:, lanes]
        lane_group = iota((CHUNK, LANES), 1) // size
        for chunk in range(chunks):
            start = chunk * CHUNK
            mixed = mixed_ref[start : start + CHUNK, lanes]
            same = same_ref[chunk]
            left = [t * same for t in toeplitz]
            right = [jnp.where(lane_group == g, mixed, jnp.zeros_like(mixed)) for g in range(groups)]
            if state is not None:
                left.append(entry * keep_ref[chunk])
                right.append(state.astype(BF16))
            longer = jnp.dot(jnp.concatenate(left, 1), jnp.concatenate(right, 0), preferred_element_type=F32)
            if chunk + 1 < chunks:
                fresh = jnp.dot((leave * tail_ref[chunk]).astype(BF16), mixed, preferred_element_type=F32)
                held = flags_ref[2 + chunk] == 1
                fresh = jnp.where(inside, fresh, 0.0)
                state = fresh if state is None else jnp.where(held, whole * state, 0.0) + fresh
            body = longer + skip * mixed.astype(F32)
            for half in range(start, start + CHUNK, SPAN):
                gate = short_conv(extended(x_ref, halo_ref, 0, half, lanes), taps, lag_masks(mask_ref, half))
                inner = body[half - start : half - start + SPAN]
                summed = residual_ref[half : half + SPAN, lanes].astype(F32) + gate * inner
                if carried:
                    hand_over(out_ref, squares_ref, refs[5], summed, half, count // nblocks, lanes)
                else:
                    base_ref[half : half + SPAN, lanes] = summed
                    gate_ref[half : half + SPAN, lanes] = gate.astype(BF16)

    each_tile(width, tile)
    if carried:
        spare_ref[...] = out_ref[refs[5][nblocks]]


def add_kernel(
    modes, size, ndoc, nblocks,
    where_ref, lengths_ref, owner_ref,
    base_ref, gate_ref, rates_ref, residues_ref, states_ref,
    out_ref, spare_ref, squares_ref,
    keep_ref, flags_ref, slot_ref,
):
    count, width = base_ref.shape
    chunks = count // CHUNK

    @pl.when(pl.program_id(0) == 0)
    def _():
        where = where_ref[0]
        ends = running_ends(lengths_ref, ndoc)
        write_flags(flags_ref, ends, where, count, nblocks)
        write_slots(slot_ref, owner_ref, where, nblocks)
        squares_ref[...] = jnp.zeros_like(squares_ref)
        before = scalar_document(ends, where * count - 1)
        kept = jnp.int32(0)
        for end in reversed(ends):
            kept = jnp.where(end >= where * count, end - where * count, kept)
        kept = jnp.where(before < 0, 0, kept)
        keep_ref[...] = jnp.where(iota((count, LANES), 0) < kept, 1.0, 0.0).astype(F32)

    def tile(lanes):
        rate = tile_rates(rates_ref.at[0], lanes.start, size)
        scale = tile_rates(residues_ref.at[0], lanes.start, size) * jnp.sqrt(1.0 - jnp.exp(-2.0 * rate))
        down = iota((CHUNK, LANES), 0)
        entry = (scale.T * jnp.exp(-rate.T * (down + 1).astype(F32))).astype(BF16)
        whole = jnp.exp(-rate * CHUNK)
        state = left_state(states_ref, flags_ref, rate, lanes, modes, size, count)
        held = []
        for _ in range(chunks):
            held.append(state.astype(BF16))
            state = state * whole
        left = jnp.dot(entry, jnp.concatenate(held, 1), preferred_element_type=F32)
        for start in range(0, count, SPAN):
            low = start % CHUNK
            chunk = start // CHUNK
            carried = left[low : low + SPAN, chunk * LANES : (chunk + 1) * LANES] * keep_ref[start : start + SPAN, :]
            gate = gate_ref[start : start + SPAN, lanes].astype(F32)
            summed = base_ref[start : start + SPAN, lanes] + gate * carried
            hand_over(out_ref, squares_ref, slot_ref, summed, start, count // nblocks, lanes)

    each_tile(width, tile)
    spare_ref[...] = out_ref[slot_ref[nblocks]]


def norm_kernel(parts, where_ref, owner_ref, *refs):
    blocks, refs = refs[:parts], refs[parts:]
    spare_ref, gain_ref, out_ref = refs[:3]
    held, (done_ref, in_sems, out_sems) = refs[3 : 3 + parts], refs[3 + parts :]
    nblocks = blocks[0].shape[0]
    rows = out_ref.shape[0] // nblocks

    def fetch(part, i, source):
        return pltpu.make_async_copy(source, held[part].at[i], in_sems.at[part, i])

    for i in range(nblocks):
        ahead = where_ref[0] - owner_ref[i]
        source = jnp.where(ahead < 0, ahead + nblocks, ahead)
        second = is_second(owner_ref, nblocks, i)
        low = 0
        for part in range(parts):
            size = blocks[part].shape[1]

            @pl.when(second)
            def _(part=part, i=i, low=low, size=size):
                fetch(part, i, spare_ref.at[pl.ds(low, size)]).start()

            @pl.when(jnp.logical_not(second))
            def _(part=part, i=i, source=source):
                fetch(part, i, blocks[part].at[source]).start()

            low += size

    def store(i):
        here = pl.ds(i * rows, rows)
        return pltpu.make_async_copy(done_ref.at[here], out_ref.at[here], out_sems.at[i])

    for i in range(nblocks):
        for part in range(parts):
            fetch(part, i, blocks[part].at[0]).wait()
        halves = jnp.broadcast_to(held[-1][i, -ROOM:, :].astype(F32)[0:1], (8, LANES))
        scale = halves + pltpu.roll(halves, LANES - rows, 1)
        scale = jnp.broadcast_to(scale[0:1], (LANES, LANES)).T[:rows]
        tile = 0
        for part in range(parts):
            for low in range(0, held[part].shape[1] - (ROOM if part + 1 == parts else 0), rows):
                outs = slice(tile * LANES, (tile + 1) * LANES)
                value = held[part][i, low : low + rows, :].astype(F32)
                done_ref[i * rows : (i + 1) * rows, outs] = (value * scale * gain_ref[:, outs]).astype(BF16)
                tile += 1
        store(i).start()
    for i in range(nblocks):
        store(i).wait()


def params():
    return pltpu.CompilerParams(dimension_semantics=("arbitrary",), vmem_limit_bytes=VMEM_LIMIT)


def whole_array(rank):
    return lambda *_: (0,) * rank


def by_step(rates, wide, size):
    modes, groups = rates.shape
    held = wide // size
    return jnp.transpose(rates.reshape(modes, groups // held, held), (1, 0, 2))


def mix(scalars, x, halo, taps, rates, size, ndoc, copies):
    _, count, width = x.shape
    modes = rates.shape[0]
    wide = min(NARROW, width)
    deep = lambda t, *_: (0, 0, t)
    grid_spec = pltpu.PrefetchScalarGridSpec(
        num_scalar_prefetch=2,
        grid=(width // wide,),
        in_specs=[
            pl.BlockSpec((1, count, wide), lambda t, *_: (1, 0, t)),
            pl.BlockSpec((1, count, wide), lambda t, *_: (2, 0, t)),
            pl.BlockSpec((3, HALO, wide), deep),
            pl.BlockSpec((3, SHORT, wide), deep),
            pl.BlockSpec((1, modes, wide // size), lambda t, *_: (t, 0, 0)),
        ],
        out_specs=[
            pl.BlockSpec((count, wide), lambda t, *_: (0, t)),
            pl.BlockSpec((copies, modes, wide), deep),
        ],
        scratch_shapes=[
            pltpu.VMEM((count // SPAN, (NEAR - 1) * (SPAN + HALO), SPAN + 16), BF16),
            pltpu.VMEM((NEAR, count + 2 * HALO, LANES), F32),
            pltpu.VMEM((8, count), F32),
        ],
    )
    return pl.pallas_call(
        functools.partial(mix_kernel, modes, size, ndoc),
        grid_spec=grid_spec,
        out_shape=[
            jax.ShapeDtypeStruct((count, width), BF16),
            jax.ShapeDtypeStruct((copies, modes, width), BF16),
        ],
        compiler_params=params(),
        cost_estimate=pl.CostEstimate(flops=60 * count * width, bytes_accessed=8 * count * width, transcendentals=count * width),
        name="mix",
    )(*scalars[:2], x, x, halo, taps, by_step(rates, wide, size))


def conv(low, share, room, scalars, x, halo, taps, mixed, rates, residues, skip, residual, states, size, ndoc, nblocks):
    _, count, width = x.shape
    modes = rates.shape[0]
    rows = count // nblocks
    wide = math.gcd(math.gcd(low, share), WIDE)
    first = low // wide
    carried = states is not None
    tile = lambda t, *_: (0, first + t)
    deep = lambda t, *_: (0, 0, first + t)
    step = pl.BlockSpec((1, modes, wide // size), lambda t, *_: (first + t, 0, 0))
    in_specs = [
        pl.BlockSpec((1, count, wide), deep),
        pl.BlockSpec((1, HALO, wide), deep),
        pl.BlockSpec((1, SHORT, wide), deep),
        pl.BlockSpec((count, wide), tile),
        step,
        step,
        pl.BlockSpec((1, wide), tile),
        pl.BlockSpec((count, wide), tile),
    ]
    operands = [x, halo, taps, mixed, by_step(rates, wide, size), by_step(residues, wide, size), skip, residual]
    scratch = [
        pltpu.VMEM((3, count + 2 * HALO, LANES), F32),
        pltpu.VMEM((count // CHUNK, CHUNK, CHUNK), BF16),
        pltpu.VMEM((count // CHUNK, CHUNK, LANES), BF16),
        pltpu.VMEM((count // CHUNK, LANES, CHUNK), F32),
        pltpu.SMEM((2 + count // CHUNK,), jnp.int32),
    ]
    if carried:
        in_specs.append(pl.BlockSpec((nblocks, modes, wide), deep))
        operands.append(states)
        scratch.append(pltpu.SMEM((nblocks + 1,), jnp.int32))
        out_specs, out_shape = handed(share, room, wide, count, nblocks)
    else:
        out_specs = [pl.BlockSpec((count, wide), lambda t, *_: (0, t))] * 2
        out_shape = [jax.ShapeDtypeStruct((count, share), F32), jax.ShapeDtypeStruct((count, share), BF16)]
    grid_spec = pltpu.PrefetchScalarGridSpec(
        num_scalar_prefetch=3, grid=(share // wide,), in_specs=in_specs, out_specs=out_specs, scratch_shapes=scratch
    )
    return pl.pallas_call(
        functools.partial(conv_kernel, modes, size, ndoc, nblocks, carried),
        grid_spec=grid_spec,
        out_shape=out_shape,
        compiler_params=params(),
        cost_estimate=pl.CostEstimate(
            flops=2 * 1152 * count * share, bytes_accessed=8 * count * share, transcendentals=count * share
        ),
        name="conv",
    )(*scalars, *operands)


def handed(share, room, wide, count, nblocks):
    rows = count // nblocks
    specs = [
        pl.BlockSpec((nblocks, wide // LANES * rows, LANES), lambda t, *_: (0, t, 0)),
        pl.BlockSpec((wide // LANES * rows, LANES), lambda t, *_: (t, 0)),
        pl.BlockSpec((count, LANES), whole_array(2)),
    ]
    shapes = [
        jax.ShapeDtypeStruct((nblocks, share // LANES * rows + room, LANES), BF16),
        jax.ShapeDtypeStruct((share // LANES * rows, LANES), BF16),
        jax.ShapeDtypeStruct((count, LANES), F32),
    ]
    return specs, shapes


def add(scalars, base, gate, rates, residues, states, size, ndoc, nblocks):
    count, share = base.shape
    modes = rates.shape[0]
    wide = math.gcd(share, NARROW)
    tile = lambda t, *_: (0, t)
    step = pl.BlockSpec((1, modes, wide // size), lambda t, *_: (t, 0, 0))
    out_specs, out_shape = handed(share, 0, wide, count, nblocks)
    grid_spec = pltpu.PrefetchScalarGridSpec(
        num_scalar_prefetch=3,
        grid=(share // wide,),
        in_specs=[
            pl.BlockSpec((count, wide), tile),
            pl.BlockSpec((count, wide), tile),
            step,
            step,
            pl.BlockSpec((nblocks, modes, wide), lambda t, *_: (0, 0, t)),
        ],
        out_specs=out_specs,
        scratch_shapes=[
            pltpu.VMEM((count, LANES), F32),
            pltpu.SMEM((2 + count // CHUNK,), jnp.int32),
            pltpu.SMEM((nblocks + 1,), jnp.int32),
        ],
    )
    return pl.pallas_call(
        functools.partial(add_kernel, modes, size, ndoc, nblocks),
        grid_spec=grid_spec,
        out_shape=out_shape,
        compiler_params=params(),
        cost_estimate=pl.CostEstimate(flops=300 * count * share, bytes_accessed=8 * count * share, transcendentals=count * share),
        name="add",
    )(*scalars, base, gate, by_step(rates, wide, size), by_step(residues, wide, size), states)


def norm(where, owner, blocks, spare, gain, count):
    width = gain.shape[1]
    nblocks = blocks[0].shape[0]
    smem, vmem, anywhere = (pl.BlockSpec(memory_space=space) for space in (pltpu.SMEM, pltpu.VMEM, pl.ANY))
    return pl.pallas_call(
        functools.partial(norm_kernel, len(blocks)),
        in_specs=[smem, smem] + [anywhere] * (len(blocks) + 1) + [vmem],
        out_specs=anywhere,
        out_shape=jax.ShapeDtypeStruct((count, width), BF16),
        scratch_shapes=[pltpu.VMEM(block.shape, BF16) for block in blocks]
        + [
            pltpu.VMEM((count, width), BF16),
            pltpu.SemaphoreType.DMA((len(blocks), nblocks)),
            pltpu.SemaphoreType.DMA((nblocks,)),
        ],
        compiler_params=pltpu.CompilerParams(vmem_limit_bytes=VMEM_LIMIT),
        cost_estimate=pl.CostEstimate(flops=3 * count * width, bytes_accessed=4 * count * width, transcendentals=0),
        name="norm",
    )(where, owner, *blocks, spare, gain)


def on_device(features, residual, short_taps, rates, residues, skip, gain, lengths, owner):
    count, _, width = features.shape
    size = width // rates.shape[0]
    ndoc = lengths.shape[0]
    nblocks = lax.axis_size("ctx")
    rows = count // nblocks
    where = lax.axis_index("ctx")
    x = jnp.transpose(features, (1, 0, 2))
    pairs = [(i, i + 1) for i in range(nblocks - 1)]
    halo = lax.ppermute(x[:, count - HALO :], "ctx", pairs)

    scalars = (where.reshape(1).astype(jnp.int32), lengths, owner)
    rates, residues = rates.T, residues.T

    table = owner.reshape(nblocks, nblocks)
    ids = jnp.arange(nblocks, dtype=jnp.int32)
    mine = lax.dynamic_index_in_dim(table, where, 0, keepdims=False)
    twice = jnp.any((mine[:, None] == mine[None, :]) & (ids[None, :] < ids[:, None]), 1)
    unused = nblocks * (nblocks - 1) // 2 - jnp.sum(jnp.where(twice, 0, mine))
    slots = jnp.where(twice, unused, mine).astype(jnp.int32)
    spare_shift = jnp.sum(jnp.where(twice, table[0], 0))

    def exchanged(value):
        return lax.all_to_all(value, "ctx", split_axis=0, concat_axis=0, tiled=True)

    first = width * SPLIT[0] // sum(SPLIT)
    second = width - first
    mixed, copies = mix(scalars, x, halo, short_taps, rates, size, ndoc, nblocks)
    states = exchanged(copies)
    shared = (scalars, x, halo, short_taps, mixed, rates, residues, skip.reshape(1, width), residual)
    base, gate = conv(0, first, 0, *shared, None, size, ndoc, nblocks)
    out, spare, squares = add(scalars, base, gate, rates, residues, states, size, ndoc, nblocks)
    block = exchanged(out)
    out, last_spare, last_squares = conv(first, second, ROOM, *shared, states, size, ndoc, nblocks)
    mean = lax.psum(jnp.sum(squares + last_squares, 1), "mp") / (width * lax.axis_size("mp"))
    inverse = lax.rsqrt(mean + EPS)
    high = lax.reduce_precision(inverse, 8, 7)
    halves = jnp.concatenate([high.reshape(nblocks, rows), (inverse - high).reshape(nblocks, rows)], 1)
    halves = jnp.pad(halves, ((0, 0), (0, LANES - 2 * rows)))
    in_slot = slots[None, :] == ids[:, None]
    by_slot = jnp.sum(jnp.where(in_slot[:, :, None], halves[None], 0.0), 1)
    by_slot = jnp.broadcast_to(by_slot.astype(BF16)[:, None], (nblocks, ROOM, LANES))
    spare_halves = jnp.sum(jnp.where(twice[:, None], halves, 0.0), 0).astype(BF16)
    out = lax.dynamic_update_slice(out, by_slot, (0, second // LANES * rows, 0))
    blocks = [block, exchanged(out)]
    spares = jnp.concatenate([spare, last_spare, jnp.broadcast_to(spare_halves[None], (ROOM, LANES))], 0)

    def moved(by):
        return lambda value: lax.ppermute(value, "ctx", [(s, (s + by) % nblocks) for s in range(nblocks)])

    spare = lax.switch(spare_shift, [lambda value: value] + [moved(d) for d in range(1, nblocks)], spares)
    return norm(scalars[0], owner, blocks, spare, gain.reshape(1, width), count)


def solution(mesh):
    return jax.shard_map(
        on_device,
        mesh=mesh,
        in_specs=(
            P("ctx", None, "mp"),
            P("ctx", "mp"),
            P(None, None, "mp"),
            P("mp", None),
            P("mp", None),
            P("mp"),
            P("mp"),
            P(),
            P(),
        ),
        out_specs=P("ctx", "mp"),
        check_vma=False,
    )
```

```python
import functools
import math

import jax
import jax.numpy as jnp
from jax import lax
from jax.experimental import pallas as pl
from jax.experimental.pallas import tpu as pltpu
from jax.sharding import PartitionSpec as P

SHORT = 7
LANES = 128
CHUNK = 128
HALO = 8
EPS = 1e-06
SPLIT = (4, 4)
NEAR = 4
ROOM = 16
WIDE = 512
SPAN = 64
F32 = jnp.float32
BF16 = jnp.bfloat16
VMEM_LIMIT = 24 * 1024 * 1024


def iota(shape, dim):
    return lax.broadcasted_iota(jnp.int32, shape, dim)


def document(ends, positions):
    total = jnp.zeros(positions.shape, jnp.int32)
    for end in ends:
        total = total + (positions >= end).astype(jnp.int32)
    return total


def scalar_document(ends, position):
    total = jnp.int32(0)
    for end in ends:
        total = total + (position >= end).astype(jnp.int32)
    return jnp.where(position < 0, -1, total)


def running_ends(lengths_ref, ndoc):
    ends, total = [], jnp.int32(0)
    for j in range(ndoc):
        total = total + lengths_ref[j]
        ends.append(total)
    return ends


def write_lag_masks(mask_ref, ends, base, count):
    mask_ref[...] = jnp.ones_like(mask_ref)
    gap = jnp.zeros((1, LANES), F32)
    for end in ends:
        row = end - base + HALO

        @pl.when((row >= 0) & (row < count + HALO))
        def _(row=row):
            for lag in (1, 2, 3):
                for past in range(lag):
                    mask_ref[lag - 1, pl.ds(row + past, 1), :] = gap


def row_documents(ends, base, count):
    return document(ends, base + iota((8, count), 1)).astype(F32)


def is_second(owner_ref, nblocks, i):
    found = jnp.bool_(False)
    for j in range(i):
        found = found | (owner_ref[j] == owner_ref[i])
    return found


def write_slots(slot_ref, owner_ref, where, nblocks):
    unused = jnp.int32(nblocks * (nblocks - 1) // 2)
    seconds = [is_second(owner_ref, nblocks, i) for i in range(nblocks)]
    mine = [owner_ref[where * nblocks + i] for i in range(nblocks)]
    for i in range(nblocks):
        unused = unused - jnp.where(seconds[i], 0, mine[i])
    for i in range(nblocks):
        slot_ref[i] = jnp.where(seconds[i], unused, mine[i])
    slot_ref[nblocks] = unused


def tile_rates(rates_ref, low, size):
    first = low // size
    columns = [rates_ref[:, first + g : first + g + 1] for g in range(LANES // size)]
    return jnp.concatenate([jnp.broadcast_to(column, (column.shape[0], LANES)) for column in columns], 0)


def short_conv(ext, taps, masks):
    def back(value, lag):
        return pltpu.roll(value, lag, 0) * masks[lag - 1]

    one, two = back(ext, 1), back(ext, 2)
    far = ext * taps[6]
    middle = ext * taps[3] + one * taps[4] + two * taps[5] + back(far, 3)
    near = ext * taps[0] + one * taps[1] + two * taps[2] + back(middle, 3)
    return near[HALO:]


def extended(x_ref, halo_ref, which, start, lanes):
    rows = x_ref[0, start : start + SPAN, lanes].astype(F32)
    if start == 0:
        ahead = halo_ref[which, :, lanes].astype(F32)
    else:
        ahead = x_ref[0, start - 16 : start, lanes].astype(F32)[16 - HALO :]
    return jnp.concatenate([ahead, rows], 0)


def tap_rows(taps_ref, which, lanes):
    return [taps_ref[which, j : j + 1, lanes] for j in range(SHORT)]


def lag_masks(mask_ref, start):
    return [mask_ref[l, start : start + SPAN + HALO, :] for l in range(3)]


def group_mask(modes, size):
    return (iota((LANES, LANES), 0) // modes) == (iota((LANES, LANES), 1) // size)


def each_tile(width, body):
    for low in range(0, width, LANES):
        body(slice(low, low + LANES))


def write_shifts(shift_ref, mask_ref, ends, base, count):
    mask_ref[...] = jnp.ones_like(mask_ref)
    gap = jnp.zeros((1, LANES), F32)
    for end in ends:
        row = end - base + HALO

        @pl.when((row >= 0) & (row < count + HALO))
        def _(row=row):
            for lag in range(1, NEAR + 1):
                for past in range(lag):
                    mask_ref[lag - 1, pl.ds(row + past, 1), :] = gap

    reach = SPAN + HALO
    back = iota((reach, SPAN + 16), 0) + HALO - iota((reach, SPAN + 16), 1)
    for span in range(count // SPAN):
        moves = []
        for lag in range(1, NEAR):
            mask = mask_ref[lag - 1, span * SPAN : span * SPAN + reach, : SPAN + 16]
            moves.append(jnp.where(back == lag, mask, 0.0))
        shift_ref[span] = jnp.concatenate(moves, 0).astype(BF16)


def mix_kernel(
    modes, size, ndoc,
    where_ref, lengths_ref,
    key_ref, value_ref, halo_ref, taps_ref, rates_ref,
    mixed_ref, state_ref,
    shift_ref, mask_ref, tail_ref,
):
    _, count, width = key_ref.shape
    chunks = count // CHUNK
    reach = SPAN + HALO

    @pl.when(pl.program_id(0) == 0)
    def _():
        base = where_ref[0] * count
        ends = running_ends(lengths_ref, ndoc)
        write_shifts(shift_ref, mask_ref, ends, base, count)
        last = scalar_document(ends, base + count - 1).astype(F32)
        tail_ref[...] = jnp.where(row_documents(ends, base, count) == last, 1.0, 0.0).astype(F32)

    def window(x_ref, which, start, lanes):
        if start == 0:
            halo = halo_ref[which, :, lanes].astype(F32)
            ahead = jnp.concatenate([jnp.zeros((16 - HALO, LANES), F32), halo], 0).astype(BF16)
        else:
            ahead = x_ref[0, start - 16 : start, lanes]
        return jnp.concatenate([ahead, x_ref[0, start : start + SPAN, lanes]], 0)

    def finish(here, moved, taps, apart):
        rows = [here] + [moved[lag * reach : (lag + 1) * reach] for lag in range(NEAR - 1)]
        far = sum(rows[lag] * taps[NEAR + lag] for lag in range(SHORT - NEAR))
        far = pltpu.roll(far, NEAR, 0)[HALO:] * apart
        return far + sum(row[HALO:] * taps[lag] for lag, row in enumerate(rows))

    def tile(lanes):
        key_taps, value_taps = tap_rows(taps_ref, 1, lanes), tap_rows(taps_ref, 2, lanes)
        for start in range(0, count, SPAN):
            keys, values = window(key_ref, 1, start, lanes), window(value_ref, 2, start, lanes)
            moved = jnp.dot(shift_ref[start // SPAN], jnp.concatenate([keys, values], 1), preferred_element_type=F32)
            apart = mask_ref[NEAR - 1, HALO + start : HALO + start + SPAN, :]
            key = finish(keys.astype(F32)[16 - HALO :], moved[:, :LANES], key_taps, apart)
            value = finish(values.astype(F32)[16 - HALO :], moved[:, LANES:], value_taps, apart)
            mixed_ref[start : start + SPAN, lanes] = (key * value).astype(BF16)
        rate = tile_rates(rates_ref.at[0], lanes.start, size)
        leave = jnp.exp(-rate * (CHUNK - 1 - iota((LANES, CHUNK), 1)).astype(F32))
        whole = jnp.exp(-rate * CHUNK)
        spans = []
        for chunk in reversed(range(chunks)):
            tail = tail_ref[0:1, chunk * CHUNK : (chunk + 1) * CHUNK]
            spans.append((leave * tail).astype(BF16))
            leave = leave * whole
        full = jnp.dot(jnp.concatenate(spans[::-1], 1), mixed_ref[:, lanes], preferred_element_type=F32)
        full = jnp.where(group_mask(modes, size), full, 0.0)
        state = jnp.sum(full.reshape(LANES // modes, modes, LANES), 0).astype(BF16)
        for owner in range(state_ref.shape[0]):
            state_ref[owner, :, lanes] = state

    each_tile(width, tile)


def left_state(states_ref, flags_ref, rate, lanes, modes, size, count):
    inside = group_mask(modes, size)
    where = flags_ref[1]

    def gather(v, total):
        weight = jnp.exp(-rate * ((where - 1 - v) * count).astype(F32))
        piece = jnp.concatenate([states_ref[v, :, lanes].astype(F32)] * (LANES // modes), 0)
        return total + jnp.where(inside, piece * weight, 0.0)

    return lax.fori_loop(flags_ref[0], where, gather, jnp.zeros((LANES, LANES), F32))


def write_flags(flags_ref, ends, where, count, nblocks):
    before = scalar_document(ends, where * count - 1)
    first = jnp.int32(0)
    for v in range(nblocks):
        first = first + (scalar_document(ends, (v + 1) * count - 1) < before).astype(jnp.int32)
    flags_ref[0] = first
    flags_ref[1] = where
    for chunk in range(count // CHUNK):
        start = where * count + chunk * CHUNK
        held = scalar_document(ends, start - 1) == scalar_document(ends, start + CHUNK - 1)
        flags_ref[2 + chunk] = held.astype(jnp.int32)


def hand_over(out_ref, squares_ref, slot_ref, summed, start, rows, lanes):
    squares_ref[start : start + SPAN, :] += summed * summed
    rounded = summed.astype(BF16)
    for b in range(SPAN // rows):
        tile = lanes.start // LANES * rows
        out_ref[slot_ref[start // rows + b], tile : tile + rows, :] = rounded[b * rows : (b + 1) * rows]


def conv_kernel(modes, size, ndoc, nblocks, carried, where_ref, lengths_ref, owner_ref, *refs):
    x_ref, halo_ref, taps_ref, mixed_ref, rates_ref, residues_ref, skip_ref, residual_ref = refs[:8]
    refs = refs[8:]
    if carried:
        states_ref, out_ref, spare_ref, squares_ref = refs[:4]
        refs = refs[4:]
    else:
        base_ref, gate_ref = refs[:2]
        refs = refs[2:]
    mask_ref, same_ref, keep_ref, tail_ref, flags_ref = refs[:5]
    count, width = mixed_ref.shape
    chunks = count // CHUNK

    @pl.when(pl.program_id(0) == 0)
    def _():
        where = where_ref[0]
        base = where * count
        ends = running_ends(lengths_ref, ndoc)
        write_lag_masks(mask_ref, ends, base, count)
        write_flags(flags_ref, ends, where, count, nblocks)
        if carried:
            write_slots(refs[5], owner_ref, where, nblocks)
            squares_ref[...] = jnp.zeros_like(squares_ref)
        documents = row_documents(ends, base, count)
        causal = iota((CHUNK, CHUNK), 1) <= iota((CHUNK, CHUNK), 0)
        for chunk in range(chunks):
            start = base + chunk * CHUNK
            there = jnp.broadcast_to(documents[0:1, chunk * CHUNK : (chunk + 1) * CHUNK], (CHUNK, CHUNK))
            here = there.T
            same_ref[chunk] = jnp.where((here == there) & causal, 1.0, 0.0).astype(BF16)
            before = scalar_document(ends, start - 1).astype(F32)
            keep_ref[chunk] = jnp.where(here == before, 1.0, 0.0).astype(BF16)
            last = scalar_document(ends, start + CHUNK - 1).astype(F32)
            tail_ref[chunk] = jnp.where(there == last, 1.0, 0.0).astype(F32)

    groups = LANES // modes

    def tile(lanes):
        rate = tile_rates(rates_ref.at[0], lanes.start, size)
        scale = tile_rates(residues_ref.at[0], lanes.start, size) * jnp.sqrt(1.0 - jnp.exp(-2.0 * rate))
        down = iota((CHUNK, LANES), 0)
        along = iota((LANES, CHUNK), 1)
        entry = (scale.T * jnp.exp(-rate.T * (down + 1).astype(F32))).astype(BF16)
        leave = jnp.exp(-rate * (CHUNK - 1 - along).astype(F32))
        whole = jnp.exp(-rate * CHUNK)
        terms = scale * jnp.where(along == 0, 1.0, leave * jnp.exp(-rate))
        toeplitz = []
        for g in range(groups):
            line = jnp.sum(terms[g * modes : (g + 1) * modes], 0, keepdims=True)
            top = pltpu.roll(jnp.broadcast_to(line, (8, CHUNK)), 0, 1, stride=1, stride_axis=0)
            parts = [top] + [pltpu.roll(top, 8 * k, 1) for k in range(1, CHUNK // 8)]
            toeplitz.append(jnp.concatenate(parts, 0).astype(BF16))
        inside = group_mask(modes, size)
        state = left_state(states_ref, flags_ref, rate, lanes, modes, size, count) if carried else None
        taps = tap_rows(taps_ref, 0, lanes)
        skip = skip_ref[:, lanes]
        lane_group = iota((CHUNK, LANES), 1) // size
        for chunk in range(chunks):
            start = chunk * CHUNK
            mixed = mixed_ref[start : start + CHUNK, lanes]
            same = same_ref[chunk]
            left = [t * same for t in toeplitz]
            right = [jnp.where(lane_group == g, mixed, jnp.zeros_like(mixed)) for g in range(groups)]
            if state is not None:
                left.append(entry * keep_ref[chunk])
                right.append(state.astype(BF16))
            longer = jnp.dot(jnp.concatenate(left, 1), jnp.concatenate(right, 0), preferred_element_type=F32)
            if chunk + 1 < chunks:
                fresh = jnp.dot((leave * tail_ref[chunk]).astype(BF16), mixed, preferred_element_type=F32)
                held = flags_ref[2 + chunk] == 1
                fresh = jnp.where(inside, fresh, 0.0)
                state = fresh if state is None else jnp.where(held, whole * state, 0.0) + fresh
            body = longer + skip * mixed.astype(F32)
            for half in range(start, start + CHUNK, SPAN):
                gate = short_conv(extended(x_ref, halo_ref, 0, half, lanes), taps, lag_masks(mask_ref, half))
                inner = body[half - start : half - start + SPAN]
                summed = residual_ref[half : half + SPAN, lanes].astype(F32) + gate * inner
                if carried:
                    hand_over(out_ref, squares_ref, refs[5], summed, half, count // nblocks, lanes)
                else:
                    base_ref[half : half + SPAN, lanes] = summed
                    gate_ref[half : half + SPAN, lanes] = gate.astype(BF16)

    each_tile(width, tile)
    if carried:
        spare_ref[...] = out_ref[refs[5][nblocks]]


def add_kernel(
    modes, size, ndoc, nblocks,
    where_ref, lengths_ref, owner_ref,
    base_ref, gate_ref, rates_ref, residues_ref, states_ref,
    out_ref, spare_ref, squares_ref,
    keep_ref, flags_ref, slot_ref,
):
    count, width = base_ref.shape
    chunks = count // CHUNK

    @pl.when(pl.program_id(0) == 0)
    def _():
        where = where_ref[0]
        ends = running_ends(lengths_ref, ndoc)
        write_flags(flags_ref, ends, where, count, nblocks)
        write_slots(slot_ref, owner_ref, where, nblocks)
        squares_ref[...] = jnp.zeros_like(squares_ref)
        before = scalar_document(ends, where * count - 1)
        kept = jnp.int32(0)
        for end in reversed(ends):
            kept = jnp.where(end >= where * count, end - where * count, kept)
        kept = jnp.where(before < 0, 0, kept)
        keep_ref[...] = jnp.where(iota((count, LANES), 0) < kept, 1.0, 0.0).astype(F32)

    def tile(lanes):
        rate = tile_rates(rates_ref.at[0], lanes.start, size)
        scale = tile_rates(residues_ref.at[0], lanes.start, size) * jnp.sqrt(1.0 - jnp.exp(-2.0 * rate))
        down = iota((CHUNK, LANES), 0)
        entry = (scale.T * jnp.exp(-rate.T * (down + 1).astype(F32))).astype(BF16)
        whole = jnp.exp(-rate * CHUNK)
        state = left_state(states_ref, flags_ref, rate, lanes, modes, size, count)
        held = []
        for _ in range(chunks):
            held.append(state.astype(BF16))
            state = state * whole
        left = jnp.dot(entry, jnp.concatenate(held, 1), preferred_element_type=F32)
        for start in range(0, count, SPAN):
            low = start % CHUNK
            chunk = start // CHUNK
            carried = left[low : low + SPAN, chunk * LANES : (chunk + 1) * LANES] * keep_ref[start : start + SPAN, :]
            gate = gate_ref[start : start + SPAN, lanes].astype(F32)
            summed = base_ref[start : start + SPAN, lanes] + gate * carried
            hand_over(out_ref, squares_ref, slot_ref, summed, start, count // nblocks, lanes)

    each_tile(width, tile)
    spare_ref[...] = out_ref[slot_ref[nblocks]]


def norm_kernel(parts, where_ref, owner_ref, *refs):
    blocks, refs = refs[:parts], refs[parts:]
    spare_ref, gain_ref, out_ref = refs[:3]
    held, (done_ref, in_sems, out_sems) = refs[3 : 3 + parts], refs[3 + parts :]
    nblocks = blocks[0].shape[0]
    rows = out_ref.shape[0] // nblocks

    def fetch(part, i, source):
        return pltpu.make_async_copy(source, held[part].at[i], in_sems.at[part, i])

    for i in range(nblocks):
        ahead = where_ref[0] - owner_ref[i]
        source = jnp.where(ahead < 0, ahead + nblocks, ahead)
        second = is_second(owner_ref, nblocks, i)
        low = 0
        for part in range(parts):
            size = blocks[part].shape[1]

            @pl.when(second)
            def _(part=part, i=i, low=low, size=size):
                fetch(part, i, spare_ref.at[pl.ds(low, size)]).start()

            @pl.when(jnp.logical_not(second))
            def _(part=part, i=i, source=source):
                fetch(part, i, blocks[part].at[source]).start()

            low += size

    def store(i):
        here = pl.ds(i * rows, rows)
        return pltpu.make_async_copy(done_ref.at[here], out_ref.at[here], out_sems.at[i])

    for i in range(nblocks):
        for part in range(parts):
            fetch(part, i, blocks[part].at[0]).wait()
        halves = jnp.broadcast_to(held[-1][i, -ROOM:, :].astype(F32)[0:1], (8, LANES))
        scale = halves + pltpu.roll(halves, LANES - rows, 1)
        scale = jnp.broadcast_to(scale[0:1], (LANES, LANES)).T[:rows]
        tile = 0
        for part in range(parts):
            for low in range(0, held[part].shape[1] - (ROOM if part + 1 == parts else 0), rows):
                outs = slice(tile * LANES, (tile + 1) * LANES)
                value = held[part][i, low : low + rows, :].astype(F32)
                done_ref[i * rows : (i + 1) * rows, outs] = (value * scale * gain_ref[:, outs]).astype(BF16)
                tile += 1
        store(i).start()
    for i in range(nblocks):
        store(i).wait()


def params():
    return pltpu.CompilerParams(dimension_semantics=("arbitrary",), vmem_limit_bytes=VMEM_LIMIT)


def whole_array(rank):
    return lambda *_: (0,) * rank


def by_step(rates, wide, size):
    modes, groups = rates.shape
    held = wide // size
    return jnp.transpose(rates.reshape(modes, groups // held, held), (1, 0, 2))


def mix(scalars, x, halo, taps, rates, size, ndoc, copies):
    _, count, width = x.shape
    modes = rates.shape[0]
    wide = min(WIDE, width)
    deep = lambda t, *_: (0, 0, t)
    grid_spec = pltpu.PrefetchScalarGridSpec(
        num_scalar_prefetch=2,
        grid=(width // wide,),
        in_specs=[
            pl.BlockSpec((1, count, wide), lambda t, *_: (1, 0, t)),
            pl.BlockSpec((1, count, wide), lambda t, *_: (2, 0, t)),
            pl.BlockSpec((3, HALO, wide), deep),
            pl.BlockSpec((3, SHORT, wide), deep),
            pl.BlockSpec((1, modes, wide // size), lambda t, *_: (t, 0, 0)),
        ],
        out_specs=[
            pl.BlockSpec((count, wide), lambda t, *_: (0, t)),
            pl.BlockSpec((copies, modes, wide), deep),
        ],
        scratch_shapes=[
            pltpu.VMEM((count // SPAN, (NEAR - 1) * (SPAN + HALO), SPAN + 16), BF16),
            pltpu.VMEM((NEAR, count + 2 * HALO, LANES), F32),
            pltpu.VMEM((8, count), F32),
        ],
    )
    return pl.pallas_call(
        functools.partial(mix_kernel, modes, size, ndoc),
        grid_spec=grid_spec,
        out_shape=[
            jax.ShapeDtypeStruct((count, width), BF16),
            jax.ShapeDtypeStruct((copies, modes, width), BF16),
        ],
        compiler_params=params(),
        cost_estimate=pl.CostEstimate(flops=60 * count * width, bytes_accessed=8 * count * width, transcendentals=count * width),
        name="mix",
    )(*scalars[:2], x, x, halo, taps, by_step(rates, wide, size))


def conv(low, share, room, scalars, x, halo, taps, mixed, rates, residues, skip, residual, states, size, ndoc, nblocks):
    _, count, width = x.shape
    modes = rates.shape[0]
    rows = count // nblocks
    wide = math.gcd(math.gcd(low, share), WIDE)
    first = low // wide
    carried = states is not None
    tile = lambda t, *_: (0, first + t)
    deep = lambda t, *_: (0, 0, first + t)
    step = pl.BlockSpec((1, modes, wide // size), lambda t, *_: (first + t, 0, 0))
    in_specs = [
        pl.BlockSpec((1, count, wide), deep),
        pl.BlockSpec((1, HALO, wide), deep),
        pl.BlockSpec((1, SHORT, wide), deep),
        pl.BlockSpec((count, wide), tile),
        step,
        step,
        pl.BlockSpec((1, wide), tile),
        pl.BlockSpec((count, wide), tile),
    ]
    operands = [x, halo, taps, mixed, by_step(rates, wide, size), by_step(residues, wide, size), skip, residual]
    scratch = [
        pltpu.VMEM((3, count + 2 * HALO, LANES), F32),
        pltpu.VMEM((count // CHUNK, CHUNK, CHUNK), BF16),
        pltpu.VMEM((count // CHUNK, CHUNK, LANES), BF16),
        pltpu.VMEM((count // CHUNK, LANES, CHUNK), F32),
        pltpu.SMEM((2 + count // CHUNK,), jnp.int32),
    ]
    if carried:
        in_specs.append(pl.BlockSpec((nblocks, modes, wide), deep))
        operands.append(states)
        scratch.append(pltpu.SMEM((nblocks + 1,), jnp.int32))
        out_specs, out_shape = handed(share, room, wide, count, nblocks)
    else:
        out_specs = [pl.BlockSpec((count, wide), lambda t, *_: (0, t))] * 2
        out_shape = [jax.ShapeDtypeStruct((count, share), F32), jax.ShapeDtypeStruct((count, share), BF16)]
    grid_spec = pltpu.PrefetchScalarGridSpec(
        num_scalar_prefetch=3, grid=(share // wide,), in_specs=in_specs, out_specs=out_specs, scratch_shapes=scratch
    )
    return pl.pallas_call(
        functools.partial(conv_kernel, modes, size, ndoc, nblocks, carried),
        grid_spec=grid_spec,
        out_shape=out_shape,
        compiler_params=params(),
        cost_estimate=pl.CostEstimate(
            flops=2 * 1152 * count * share, bytes_accessed=8 * count * share, transcendentals=count * share
        ),
        name="conv",
    )(*scalars, *operands)


def handed(share, room, wide, count, nblocks):
    rows = count // nblocks
    specs = [
        pl.BlockSpec((nblocks, wide // LANES * rows, LANES), lambda t, *_: (0, t, 0)),
        pl.BlockSpec((wide // LANES * rows, LANES), lambda t, *_: (t, 0)),
        pl.BlockSpec((count, LANES), whole_array(2)),
    ]
    shapes = [
        jax.ShapeDtypeStruct((nblocks, share // LANES * rows + room, LANES), BF16),
        jax.ShapeDtypeStruct((share // LANES * rows, LANES), BF16),
        jax.ShapeDtypeStruct((count, LANES), F32),
    ]
    return specs, shapes


def add(scalars, base, gate, rates, residues, states, size, ndoc, nblocks):
    count, share = base.shape
    modes = rates.shape[0]
    wide = math.gcd(share, WIDE)
    tile = lambda t, *_: (0, t)
    step = pl.BlockSpec((1, modes, wide // size), lambda t, *_: (t, 0, 0))
    out_specs, out_shape = handed(share, 0, wide, count, nblocks)
    grid_spec = pltpu.PrefetchScalarGridSpec(
        num_scalar_prefetch=3,
        grid=(share // wide,),
        in_specs=[
            pl.BlockSpec((count, wide), tile),
            pl.BlockSpec((count, wide), tile),
            step,
            step,
            pl.BlockSpec((nblocks, modes, wide), lambda t, *_: (0, 0, t)),
        ],
        out_specs=out_specs,
        scratch_shapes=[
            pltpu.VMEM((count, LANES), F32),
            pltpu.SMEM((2 + count // CHUNK,), jnp.int32),
            pltpu.SMEM((nblocks + 1,), jnp.int32),
        ],
    )
    return pl.pallas_call(
        functools.partial(add_kernel, modes, size, ndoc, nblocks),
        grid_spec=grid_spec,
        out_shape=out_shape,
        compiler_params=params(),
        cost_estimate=pl.CostEstimate(flops=300 * count * share, bytes_accessed=8 * count * share, transcendentals=count * share),
        name="add",
    )(*scalars, base, gate, by_step(rates, wide, size), by_step(residues, wide, size), states)


def norm(where, owner, blocks, spare, gain, count):
    width = gain.shape[1]
    nblocks = blocks[0].shape[0]
    smem, vmem, anywhere = (pl.BlockSpec(memory_space=space) for space in (pltpu.SMEM, pltpu.VMEM, pl.ANY))
    return pl.pallas_call(
        functools.partial(norm_kernel, len(blocks)),
        in_specs=[smem, smem] + [anywhere] * (len(blocks) + 1) + [vmem],
        out_specs=anywhere,
        out_shape=jax.ShapeDtypeStruct((count, width), BF16),
        scratch_shapes=[pltpu.VMEM(block.shape, BF16) for block in blocks]
        + [
            pltpu.VMEM((count, width), BF16),
            pltpu.SemaphoreType.DMA((len(blocks), nblocks)),
            pltpu.SemaphoreType.DMA((nblocks,)),
        ],
        compiler_params=pltpu.CompilerParams(vmem_limit_bytes=VMEM_LIMIT),
        cost_estimate=pl.CostEstimate(flops=3 * count * width, bytes_accessed=4 * count * width, transcendentals=0),
        name="norm",
    )(where, owner, *blocks, spare, gain)


def on_device(features, residual, short_taps, rates, residues, skip, gain, lengths, owner):
    count, _, width = features.shape
    size = width // rates.shape[0]
    ndoc = lengths.shape[0]
    nblocks = lax.axis_size("ctx")
    rows = count // nblocks
    where = lax.axis_index("ctx")
    x = jnp.transpose(features, (1, 0, 2))
    pairs = [(i, i + 1) for i in range(nblocks - 1)]
    halo = lax.ppermute(x[:, count - HALO :], "ctx", pairs)

    scalars = (where.reshape(1).astype(jnp.int32), lengths, owner)
    rates, residues = rates.T, residues.T

    table = owner.reshape(nblocks, nblocks)
    ids = jnp.arange(nblocks, dtype=jnp.int32)
    mine = lax.dynamic_index_in_dim(table, where, 0, keepdims=False)
    twice = jnp.any((mine[:, None] == mine[None, :]) & (ids[None, :] < ids[:, None]), 1)
    unused = nblocks * (nblocks - 1) // 2 - jnp.sum(jnp.where(twice, 0, mine))
    slots = jnp.where(twice, unused, mine).astype(jnp.int32)
    spare_shift = jnp.sum(jnp.where(twice, table[0], 0))

    def exchanged(value):
        return lax.all_to_all(value, "ctx", split_axis=0, concat_axis=0, tiled=True)

    first = width * SPLIT[0] // sum(SPLIT)
    second = width - first
    mixed, copies = mix(scalars, x, halo, short_taps, rates, size, ndoc, nblocks)
    states = exchanged(copies)
    shared = (scalars, x, halo, short_taps, mixed, rates, residues, skip.reshape(1, width), residual)
    base, gate = conv(0, first, 0, *shared, None, size, ndoc, nblocks)
    out, spare, squares = add(scalars, base, gate, rates, residues, states, size, ndoc, nblocks)
    block = exchanged(out)
    out, last_spare, last_squares = conv(first, second, ROOM, *shared, states, size, ndoc, nblocks)
    mean = lax.psum(jnp.sum(squares + last_squares, 1), "mp") / (width * lax.axis_size("mp"))
    inverse = lax.rsqrt(mean + EPS)
    high = lax.reduce_precision(inverse, 8, 7)
    halves = jnp.concatenate([high.reshape(nblocks, rows), (inverse - high).reshape(nblocks, rows)], 1)
    halves = jnp.pad(halves, ((0, 0), (0, LANES - 2 * rows)))
    in_slot = slots[None, :] == ids[:, None]
    by_slot = jnp.sum(jnp.where(in_slot[:, :, None], halves[None], 0.0), 1)
    by_slot = jnp.broadcast_to(by_slot.astype(BF16)[:, None], (nblocks, ROOM, LANES))
    spare_halves = jnp.sum(jnp.where(twice[:, None], halves, 0.0), 0).astype(BF16)
    out = lax.dynamic_update_slice(out, by_slot, (0, second // LANES * rows, 0))
    blocks = [block, exchanged(out)]
    spares = jnp.concatenate([spare, last_spare, jnp.broadcast_to(spare_halves[None], (ROOM, LANES))], 0)

    def moved(by):
        return lambda value: lax.ppermute(value, "ctx", [(s, (s + by) % nblocks) for s in range(nblocks)])

    spare = lax.switch(spare_shift, [lambda value: value] + [moved(d) for d in range(1, nblocks)], spares)
    return norm(scalars[0], owner, blocks, spare, gain.reshape(1, width), count)


def solution(mesh):
    return jax.shard_map(
        on_device,
        mesh=mesh,
        in_specs=(
            P("ctx", None, "mp"),
            P("ctx", "mp"),
            P(None, None, "mp"),
            P("mp", None),
            P("mp", None),
            P("mp"),
            P("mp"),
            P(),
            P(),
        ),
        out_specs=P("ctx", "mp"),
        check_vma=False,
    )
```

```python
import functools
import math

import jax
import jax.numpy as jnp
from jax import lax
from jax.experimental import pallas as pl
from jax.experimental.pallas import tpu as pltpu
from jax.sharding import PartitionSpec as P

SHORT = 7
LANES = 128
CHUNK = 128
HALO = 8
EPS = 1e-06
SPLIT = (4, 4)
NEAR = 4
ROOM = 16
WIDE = 512
SPAN = 64
F32 = jnp.float32
BF16 = jnp.bfloat16
VMEM_LIMIT = 40 * 1024 * 1024


def iota(shape, dim):
    return lax.broadcasted_iota(jnp.int32, shape, dim)


def document(ends, positions):
    total = jnp.zeros(positions.shape, jnp.int32)
    for end in ends:
        total = total + (positions >= end).astype(jnp.int32)
    return total


def scalar_document(ends, position):
    total = jnp.int32(0)
    for end in ends:
        total = total + (position >= end).astype(jnp.int32)
    return jnp.where(position < 0, -1, total)


def running_ends(lengths_ref, ndoc):
    ends, total = [], jnp.int32(0)
    for j in range(ndoc):
        total = total + lengths_ref[j]
        ends.append(total)
    return ends


def write_lag_masks(mask_ref, ends, base, count):
    mask_ref[...] = jnp.ones_like(mask_ref)
    gap = jnp.zeros((1, LANES), F32)
    for end in ends:
        row = end - base + HALO

        @pl.when((row >= 0) & (row < count + HALO))
        def _(row=row):
            for lag in (1, 2, 3):
                for past in range(lag):
                    mask_ref[lag - 1, pl.ds(row + past, 1), :] = gap


def row_documents(ends, base, count):
    return document(ends, base + iota((8, count), 1)).astype(F32)


def is_second(owner_ref, nblocks, i):
    found = jnp.bool_(False)
    for j in range(i):
        found = found | (owner_ref[j] == owner_ref[i])
    return found


def write_slots(slot_ref, owner_ref, where, nblocks):
    unused = jnp.int32(nblocks * (nblocks - 1) // 2)
    seconds = [is_second(owner_ref, nblocks, i) for i in range(nblocks)]
    mine = [owner_ref[where * nblocks + i] for i in range(nblocks)]
    for i in range(nblocks):
        unused = unused - jnp.where(seconds[i], 0, mine[i])
    for i in range(nblocks):
        slot_ref[i] = jnp.where(seconds[i], unused, mine[i])
    slot_ref[nblocks] = unused


def tile_rates(rates_ref, low, size):
    first = low // size
    columns = [rates_ref[:, first + g : first + g + 1] for g in range(LANES // size)]
    return jnp.concatenate([jnp.broadcast_to(column, (column.shape[0], LANES)) for column in columns], 0)


def short_conv(ext, taps, masks):
    def back(value, lag):
        return pltpu.roll(value, lag, 0) * masks[lag - 1]

    one, two = back(ext, 1), back(ext, 2)
    far = ext * taps[6]
    middle = ext * taps[3] + one * taps[4] + two * taps[5] + back(far, 3)
    near = ext * taps[0] + one * taps[1] + two * taps[2] + back(middle, 3)
    return near[HALO:]


def extended(x_ref, halo_ref, which, start, lanes):
    rows = x_ref[0, start : start + SPAN, lanes].astype(F32)
    if start == 0:
        ahead = halo_ref[which, :, lanes].astype(F32)
    else:
        ahead = x_ref[0, start - 16 : start, lanes].astype(F32)[16 - HALO :]
    return jnp.concatenate([ahead, rows], 0)


def tap_rows(taps_ref, which, lanes):
    return [taps_ref[which, j : j + 1, lanes] for j in range(SHORT)]


def lag_masks(mask_ref, start):
    return [mask_ref[l, start : start + SPAN + HALO, :] for l in range(3)]


def group_mask(modes, size):
    return (iota((LANES, LANES), 0) // modes) == (iota((LANES, LANES), 1) // size)


def each_tile(width, body):
    for low in range(0, width, LANES):
        body(slice(low, low + LANES))


def write_shifts(shift_ref, mask_ref, ends, base, count):
    mask_ref[...] = jnp.ones_like(mask_ref)
    gap = jnp.zeros((1, LANES), F32)
    for end in ends:
        row = end - base + HALO

        @pl.when((row >= 0) & (row < count + HALO))
        def _(row=row):
            for lag in range(1, NEAR + 1):
                for past in range(lag):
                    mask_ref[lag - 1, pl.ds(row + past, 1), :] = gap

    reach = SPAN + HALO
    back = iota((reach, SPAN + 16), 0) + HALO - iota((reach, SPAN + 16), 1)
    for span in range(count // SPAN):
        moves = []
        for lag in range(1, NEAR):
            mask = mask_ref[lag - 1, span * SPAN : span * SPAN + reach, : SPAN + 16]
            moves.append(jnp.where(back == lag, mask, 0.0))
        shift_ref[span] = jnp.concatenate(moves, 0).astype(BF16)


def mix_kernel(
    modes, size, ndoc,
    where_ref, lengths_ref,
    x_ref, halo_ref, taps_ref, rates_ref,
    mixed_ref, state_ref,
    shift_ref, mask_ref, tail_ref, held_ref, sems,
):
    count, width = mixed_ref.shape
    chunks = count // CHUNK
    reach = SPAN + HALO

    def fetch(which, t):
        lanes = pl.ds(pl.multiple_of(t * LANES, LANES), LANES)
        return pltpu.make_async_copy(x_ref.at[which, :, lanes], held_ref.at[which - 1, t], sems.at[which - 1, t])

    @pl.when(pl.program_id(0) == 0)
    def _():
        for t in range(held_ref.shape[1]):
            for which in (1, 2):
                fetch(which, t).start()
        base = where_ref[0] * count
        ends = running_ends(lengths_ref, ndoc)
        write_shifts(shift_ref, mask_ref, ends, base, count)
        last = scalar_document(ends, base + count - 1).astype(F32)
        tail_ref[...] = jnp.where(row_documents(ends, base, count) == last, 1.0, 0.0).astype(F32)

    def window(which, t, start, lanes):
        if start == 0:
            halo = halo_ref[which, :, lanes].astype(F32)
            ahead = jnp.concatenate([jnp.zeros((16 - HALO, LANES), F32), halo], 0).astype(BF16)
        else:
            ahead = held_ref[which - 1, t, start - 16 : start, :]
        return jnp.concatenate([ahead, held_ref[which - 1, t, start : start + SPAN, :]], 0)

    def finish(here, moved, taps, apart):
        rows = [here] + [moved[lag * reach : (lag + 1) * reach] for lag in range(NEAR - 1)]
        far = sum(rows[lag] * taps[NEAR + lag] for lag in range(SHORT - NEAR))
        far = pltpu.roll(far, NEAR, 0)[HALO:] * apart
        return far + sum(row[HALO:] * taps[lag] for lag, row in enumerate(rows))

    def tile(lanes):
        key_taps, value_taps = tap_rows(taps_ref, 1, lanes), tap_rows(taps_ref, 2, lanes)
        t = pl.program_id(0) * (width // LANES) + lanes.start // LANES
        fetch(1, t).wait()
        fetch(2, t).wait()
        for start in range(0, count, SPAN):
            keys, values = window(1, t, start, lanes), window(2, t, start, lanes)
            moved = jnp.dot(shift_ref[start // SPAN], jnp.concatenate([keys, values], 1), preferred_element_type=F32)
            apart = mask_ref[NEAR - 1, HALO + start : HALO + start + SPAN, :]
            key = finish(keys.astype(F32)[16 - HALO :], moved[:, :LANES], key_taps, apart)
            value = finish(values.astype(F32)[16 - HALO :], moved[:, LANES:], value_taps, apart)
            mixed_ref[start : start + SPAN, lanes] = (key * value).astype(BF16)
        rate = tile_rates(rates_ref.at[0], lanes.start, size)
        leave = jnp.exp(-rate * (CHUNK - 1 - iota((LANES, CHUNK), 1)).astype(F32))
        whole = jnp.exp(-rate * CHUNK)
        spans = []
        for chunk in reversed(range(chunks)):
            tail = tail_ref[0:1, chunk * CHUNK : (chunk + 1) * CHUNK]
            spans.append((leave * tail).astype(BF16))
            leave = leave * whole
        full = jnp.dot(jnp.concatenate(spans[::-1], 1), mixed_ref[:, lanes], preferred_element_type=F32)
        full = jnp.where(group_mask(modes, size), full, 0.0)
        state = jnp.sum(full.reshape(LANES // modes, modes, LANES), 0).astype(BF16)
        for owner in range(state_ref.shape[0]):
            state_ref[owner, :, lanes] = state

    each_tile(width, tile)


def left_state(states_ref, flags_ref, rate, lanes, modes, size, count):
    inside = group_mask(modes, size)
    where = flags_ref[1]

    def gather(v, total):
        weight = jnp.exp(-rate * ((where - 1 - v) * count).astype(F32))
        piece = jnp.concatenate([states_ref[v, :, lanes].astype(F32)] * (LANES // modes), 0)
        return total + jnp.where(inside, piece * weight, 0.0)

    return lax.fori_loop(flags_ref[0], where, gather, jnp.zeros((LANES, LANES), F32))


def write_flags(flags_ref, ends, where, count, nblocks):
    before = scalar_document(ends, where * count - 1)
    first = jnp.int32(0)
    for v in range(nblocks):
        first = first + (scalar_document(ends, (v + 1) * count - 1) < before).astype(jnp.int32)
    flags_ref[0] = first
    flags_ref[1] = where
    for chunk in range(count // CHUNK):
        start = where * count + chunk * CHUNK
        held = scalar_document(ends, start - 1) == scalar_document(ends, start + CHUNK - 1)
        flags_ref[2 + chunk] = held.astype(jnp.int32)


def hand_over(out_ref, squares_ref, slot_ref, summed, start, rows, lanes):
    squares_ref[start : start + SPAN, :] += summed * summed
    rounded = summed.astype(BF16)
    for b in range(SPAN // rows):
        tile = lanes.start // LANES * rows
        out_ref[slot_ref[start // rows + b], tile : tile + rows, :] = rounded[b * rows : (b + 1) * rows]


def conv_kernel(modes, size, ndoc, nblocks, carried, where_ref, lengths_ref, owner_ref, *refs):
    x_ref, halo_ref, taps_ref, mixed_ref, rates_ref, residues_ref, skip_ref, residual_ref = refs[:8]
    refs = refs[8:]
    if carried:
        states_ref, out_ref, spare_ref, squares_ref = refs[:4]
        refs = refs[4:]
    else:
        base_ref, gate_ref = refs[:2]
        refs = refs[2:]
    mask_ref, same_ref, keep_ref, tail_ref, flags_ref = refs[:5]
    count, width = mixed_ref.shape
    chunks = count // CHUNK

    @pl.when(pl.program_id(0) == 0)
    def _():
        where = where_ref[0]
        base = where * count
        ends = running_ends(lengths_ref, ndoc)
        write_lag_masks(mask_ref, ends, base, count)
        write_flags(flags_ref, ends, where, count, nblocks)
        if carried:
            write_slots(refs[5], owner_ref, where, nblocks)
            squares_ref[...] = jnp.zeros_like(squares_ref)
        documents = row_documents(ends, base, count)
        causal = iota((CHUNK, CHUNK), 1) <= iota((CHUNK, CHUNK), 0)
        for chunk in range(chunks):
            start = base + chunk * CHUNK
            there = jnp.broadcast_to(documents[0:1, chunk * CHUNK : (chunk + 1) * CHUNK], (CHUNK, CHUNK))
            here = there.T
            same_ref[chunk] = jnp.where((here == there) & causal, 1.0, 0.0).astype(BF16)
            before = scalar_document(ends, start - 1).astype(F32)
            keep_ref[chunk] = jnp.where(here == before, 1.0, 0.0).astype(BF16)
            last = scalar_document(ends, start + CHUNK - 1).astype(F32)
            tail_ref[chunk] = jnp.where(there == last, 1.0, 0.0).astype(F32)

    groups = LANES // modes

    def tile(lanes):
        rate = tile_rates(rates_ref.at[0], lanes.start, size)
        scale = tile_rates(residues_ref.at[0], lanes.start, size) * jnp.sqrt(1.0 - jnp.exp(-2.0 * rate))
        down = iota((CHUNK, LANES), 0)
        along = iota((LANES, CHUNK), 1)
        entry = (scale.T * jnp.exp(-rate.T * (down + 1).astype(F32))).astype(BF16)
        leave = jnp.exp(-rate * (CHUNK - 1 - along).astype(F32))
        whole = jnp.exp(-rate * CHUNK)
        terms = scale * jnp.where(along == 0, 1.0, leave * jnp.exp(-rate))
        toeplitz = []
        for g in range(groups):
            line = jnp.sum(terms[g * modes : (g + 1) * modes], 0, keepdims=True)
            top = pltpu.roll(jnp.broadcast_to(line, (8, CHUNK)), 0, 1, stride=1, stride_axis=0)
            parts = [top] + [pltpu.roll(top, 8 * k, 1) for k in range(1, CHUNK // 8)]
            toeplitz.append(jnp.concatenate(parts, 0).astype(BF16))
        inside = group_mask(modes, size)
        state = left_state(states_ref, flags_ref, rate, lanes, modes, size, count) if carried else None
        taps = tap_rows(taps_ref, 0, lanes)
        skip = skip_ref[:, lanes]
        lane_group = iota((CHUNK, LANES), 1) // size
        for chunk in range(chunks):
            start = chunk * CHUNK
            mixed = mixed_ref[start : start + CHUNK, lanes]
            same = same_ref[chunk]
            left = [t * same for t in toeplitz]
            right = [jnp.where(lane_group == g, mixed, jnp.zeros_like(mixed)) for g in range(groups)]
            if state is not None:
                left.append(entry * keep_ref[chunk])
                right.append(state.astype(BF16))
            longer = jnp.dot(jnp.concatenate(left, 1), jnp.concatenate(right, 0), preferred_element_type=F32)
            if chunk + 1 < chunks:
                fresh = jnp.dot((leave * tail_ref[chunk]).astype(BF16), mixed, preferred_element_type=F32)
                held = flags_ref[2 + chunk] == 1
                fresh = jnp.where(inside, fresh, 0.0)
                state = fresh if state is None else jnp.where(held, whole * state, 0.0) + fresh
            body = longer + skip * mixed.astype(F32)
            for half in range(start, start + CHUNK, SPAN):
                gate = short_conv(extended(x_ref, halo_ref, 0, half, lanes), taps, lag_masks(mask_ref, half))
                inner = body[half - start : half - start + SPAN]
                summed = residual_ref[half : half + SPAN, lanes].astype(F32) + gate * inner
                if carried:
                    hand_over(out_ref, squares_ref, refs[5], summed, half, count // nblocks, lanes)
                else:
                    base_ref[half : half + SPAN, lanes] = summed
                    gate_ref[half : half + SPAN, lanes] = gate.astype(BF16)

    each_tile(width, tile)
    if carried:
        spare_ref[...] = out_ref[refs[5][nblocks]]


def add_kernel(
    modes, size, ndoc, nblocks,
    where_ref, lengths_ref, owner_ref,
    base_ref, gate_ref, rates_ref, residues_ref, states_ref,
    out_ref, spare_ref, squares_ref,
    keep_ref, flags_ref, slot_ref,
):
    count, width = base_ref.shape
    chunks = count // CHUNK

    @pl.when(pl.program_id(0) == 0)
    def _():
        where = where_ref[0]
        ends = running_ends(lengths_ref, ndoc)
        write_flags(flags_ref, ends, where, count, nblocks)
        write_slots(slot_ref, owner_ref, where, nblocks)
        squares_ref[...] = jnp.zeros_like(squares_ref)
        before = scalar_document(ends, where * count - 1)
        kept = jnp.int32(0)
        for end in reversed(ends):
            kept = jnp.where(end >= where * count, end - where * count, kept)
        kept = jnp.where(before < 0, 0, kept)
        keep_ref[...] = jnp.where(iota((count, LANES), 0) < kept, 1.0, 0.0).astype(F32)

    def tile(lanes):
        rate = tile_rates(rates_ref.at[0], lanes.start, size)
        scale = tile_rates(residues_ref.at[0], lanes.start, size) * jnp.sqrt(1.0 - jnp.exp(-2.0 * rate))
        down = iota((CHUNK, LANES), 0)
        entry = (scale.T * jnp.exp(-rate.T * (down + 1).astype(F32))).astype(BF16)
        whole = jnp.exp(-rate * CHUNK)
        state = left_state(states_ref, flags_ref, rate, lanes, modes, size, count)
        held = []
        for _ in range(chunks):
            held.append(state.astype(BF16))
            state = state * whole
        left = jnp.dot(entry, jnp.concatenate(held, 1), preferred_element_type=F32)
        for start in range(0, count, SPAN):
            low = start % CHUNK
            chunk = start // CHUNK
            carried = left[low : low + SPAN, chunk * LANES : (chunk + 1) * LANES] * keep_ref[start : start + SPAN, :]
            gate = gate_ref[start : start + SPAN, lanes].astype(F32)
            summed = base_ref[start : start + SPAN, lanes] + gate * carried
            hand_over(out_ref, squares_ref, slot_ref, summed, start, count // nblocks, lanes)

    each_tile(width, tile)
    spare_ref[...] = out_ref[slot_ref[nblocks]]


def norm_kernel(where_ref, owner_ref, first_ref, spare_ref, gain_ref, second_ref, out_ref, held_ref, done_ref, in_sems, out_sems):
    nblocks, front, _ = first_ref.shape
    rows = out_ref.shape[0] // nblocks
    sources, spares = [], []
    for i in range(nblocks):
        ahead = where_ref[0] - owner_ref[i]
        sources.append(jnp.where(ahead < 0, ahead + nblocks, ahead))
        spares.append(is_second(owner_ref, nblocks, i))

    def fetch(i):
        return pltpu.make_async_copy(second_ref.at[sources[i]], held_ref.at[i], in_sems.at[i])

    def store(i):
        here = pl.ds(i * rows, rows)
        return pltpu.make_async_copy(done_ref.at[here], out_ref.at[here], out_sems.at[i])

    for i in range(nblocks):
        fetch(i).start()
    for i in range(nblocks):
        fetch(i).wait()

        def block(low):
            usual = first_ref[sources[i], low : low + rows, :] if low < front else held_ref[i, low - front : low - front + rows, :]
            return jnp.where(spares[i], spare_ref[low : low + rows, :].astype(F32), usual.astype(F32))

        last = spare_ref.shape[0] - ROOM
        halves = jnp.where(spares[i], spare_ref[last:, :].astype(F32), held_ref[i, last - front :, :].astype(F32))
        halves = jnp.broadcast_to(halves[0:1], (8, LANES))
        scale = halves + pltpu.roll(halves, LANES - rows, 1)
        scale = jnp.broadcast_to(scale[0:1], (LANES, LANES)).T[:rows]
        for low in range(0, last, rows):
            outs = slice(low // rows * LANES, (low // rows + 1) * LANES)
            done_ref[i * rows : (i + 1) * rows, outs] = (block(low) * scale * gain_ref[:, outs]).astype(BF16)
        store(i).start()
    for i in range(nblocks):
        store(i).wait()


def params():
    return pltpu.CompilerParams(dimension_semantics=("arbitrary",), vmem_limit_bytes=VMEM_LIMIT)


def in_hbm(*arrays):
    return [pltpu.with_memory_space_constraint(array, pltpu.HBM) for array in arrays]


def in_vmem(array):
    return pltpu.with_memory_space_constraint(array, pltpu.VMEM)


def whole_array(rank):
    return lambda *_: (0,) * rank


def by_step(rates, wide, size):
    modes, groups = rates.shape
    held = wide // size
    return jnp.transpose(rates.reshape(modes, groups // held, held), (1, 0, 2))


def mix(scalars, x, halo, taps, rates, size, ndoc, copies):
    _, count, width = x.shape
    modes = rates.shape[0]
    wide = min(WIDE, width)
    deep = lambda t, *_: (0, 0, t)
    grid_spec = pltpu.PrefetchScalarGridSpec(
        num_scalar_prefetch=2,
        grid=(width // wide,),
        in_specs=[
            pl.BlockSpec(memory_space=pl.ANY),
            pl.BlockSpec((3, HALO, wide), deep),
            pl.BlockSpec((3, SHORT, wide), deep),
            pl.BlockSpec((1, modes, wide // size), lambda t, *_: (t, 0, 0)),
        ],
        out_specs=[
            pl.BlockSpec((count, wide), lambda t, *_: (0, t)),
            pl.BlockSpec((copies, modes, wide), deep),
        ],
        scratch_shapes=[
            pltpu.VMEM((count // SPAN, (NEAR - 1) * (SPAN + HALO), SPAN + 16), BF16),
            pltpu.VMEM((NEAR, count + 2 * HALO, LANES), F32),
            pltpu.VMEM((8, count), F32),
            pltpu.VMEM((2, width // LANES, count, LANES), BF16),
            pltpu.SemaphoreType.DMA((2, width // LANES)),
        ],
    )
    return pl.pallas_call(
        functools.partial(mix_kernel, modes, size, ndoc),
        grid_spec=grid_spec,
        out_shape=[pltpu.HBM((count, width), BF16), pltpu.HBM((copies, modes, width), BF16)],
        compiler_params=params(),
        cost_estimate=pl.CostEstimate(flops=60 * count * width, bytes_accessed=8 * count * width, transcendentals=count * width),
        name="mix",
    )(*scalars[:2], *in_hbm(x, halo, taps, by_step(rates, wide, size)))


def conv(low, share, room, scalars, x, halo, taps, mixed, rates, residues, skip, residual, states, size, ndoc, nblocks):
    _, count, width = x.shape
    modes = rates.shape[0]
    rows = count // nblocks
    wide = math.gcd(math.gcd(low, share), WIDE)
    first = low // wide
    carried = states is not None
    tile = lambda t, *_: (0, first + t)
    deep = lambda t, *_: (0, 0, first + t)
    step = pl.BlockSpec((1, modes, wide // size), lambda t, *_: (first + t, 0, 0))
    in_specs = [
        pl.BlockSpec((1, count, wide), deep),
        pl.BlockSpec((1, HALO, wide), deep),
        pl.BlockSpec((1, SHORT, wide), deep),
        pl.BlockSpec((count, wide), tile),
        step,
        step,
        pl.BlockSpec((1, wide), tile),
        pl.BlockSpec((count, wide), tile),
    ]
    operands = [x, halo, taps, mixed, by_step(rates, wide, size), by_step(residues, wide, size), skip, residual]
    scratch = [
        pltpu.VMEM((3, count + 2 * HALO, LANES), F32),
        pltpu.VMEM((count // CHUNK, CHUNK, CHUNK), BF16),
        pltpu.VMEM((count // CHUNK, CHUNK, LANES), BF16),
        pltpu.VMEM((count // CHUNK, LANES, CHUNK), F32),
        pltpu.SMEM((2 + count // CHUNK,), jnp.int32),
    ]
    if carried:
        in_specs.append(pl.BlockSpec((nblocks, modes, wide), deep))
        operands.append(states)
        scratch.append(pltpu.SMEM((nblocks + 1,), jnp.int32))
        out_specs, out_shape = handed(share, room, wide, count, nblocks)
    else:
        out_specs = [pl.BlockSpec((count, wide), lambda t, *_: (0, t))] * 2
        out_shape = [pltpu.VMEM((count, share), F32), pltpu.VMEM((count, share), BF16)]
    grid_spec = pltpu.PrefetchScalarGridSpec(
        num_scalar_prefetch=3, grid=(share // wide,), in_specs=in_specs, out_specs=out_specs, scratch_shapes=scratch
    )
    return pl.pallas_call(
        functools.partial(conv_kernel, modes, size, ndoc, nblocks, carried),
        grid_spec=grid_spec,
        out_shape=out_shape,
        compiler_params=params(),
        cost_estimate=pl.CostEstimate(
            flops=2 * 1152 * count * share, bytes_accessed=8 * count * share, transcendentals=count * share
        ),
        name="conv",
    )(*scalars, *in_hbm(*operands))


def handed(share, room, wide, count, nblocks):
    rows = count // nblocks
    specs = [
        pl.BlockSpec((nblocks, wide // LANES * rows, LANES), lambda t, *_: (0, t, 0)),
        pl.BlockSpec((wide // LANES * rows, LANES), lambda t, *_: (t, 0)),
        pl.BlockSpec((count, LANES), whole_array(2)),
    ]
    shapes = [
        pltpu.HBM((nblocks, share // LANES * rows + room, LANES), BF16),
        pltpu.HBM((share // LANES * rows, LANES), BF16),
        pltpu.HBM((count, LANES), F32),
    ]
    return specs, shapes


def add(scalars, base, gate, rates, residues, states, size, ndoc, nblocks):
    count, share = base.shape
    modes = rates.shape[0]
    wide = math.gcd(share, WIDE)
    tile = lambda t, *_: (0, t)
    step = pl.BlockSpec((1, modes, wide // size), lambda t, *_: (t, 0, 0))
    out_specs, out_shape = handed(share, 0, wide, count, nblocks)
    grid_spec = pltpu.PrefetchScalarGridSpec(
        num_scalar_prefetch=3,
        grid=(share // wide,),
        in_specs=[
            pl.BlockSpec((count, wide), tile),
            pl.BlockSpec((count, wide), tile),
            step,
            step,
            pl.BlockSpec((nblocks, modes, wide), lambda t, *_: (0, 0, t)),
        ],
        out_specs=out_specs,
        scratch_shapes=[
            pltpu.VMEM((count, LANES), F32),
            pltpu.SMEM((2 + count // CHUNK,), jnp.int32),
            pltpu.SMEM((nblocks + 1,), jnp.int32),
        ],
    )
    return pl.pallas_call(
        functools.partial(add_kernel, modes, size, ndoc, nblocks),
        grid_spec=grid_spec,
        out_shape=out_shape,
        compiler_params=params(),
        cost_estimate=pl.CostEstimate(flops=300 * count * share, bytes_accessed=8 * count * share, transcendentals=count * share),
        name="add",
    )(*scalars, in_vmem(base), in_vmem(gate), *in_hbm(by_step(rates, wide, size), by_step(residues, wide, size), states))


def norm(where, owner, first, second, spare, gain, count):
    width = gain.shape[1]
    nblocks = first.shape[0]
    smem, vmem, anywhere = (pl.BlockSpec(memory_space=space) for space in (pltpu.SMEM, pltpu.VMEM, pl.ANY))
    return pl.pallas_call(
        norm_kernel,
        in_specs=[smem, smem, vmem, vmem, vmem, anywhere],
        out_specs=anywhere,
        out_shape=jax.ShapeDtypeStruct((count, width), BF16),
        scratch_shapes=[
            pltpu.VMEM(second.shape, BF16),
            pltpu.VMEM((count, width), BF16),
            pltpu.SemaphoreType.DMA((nblocks,)),
            pltpu.SemaphoreType.DMA((nblocks,)),
        ],
        compiler_params=pltpu.CompilerParams(vmem_limit_bytes=VMEM_LIMIT),
        cost_estimate=pl.CostEstimate(flops=3 * count * width, bytes_accessed=4 * count * width, transcendentals=0),
        name="norm",
    )(where, owner, in_vmem(first), in_vmem(spare), gain, *in_hbm(second))


def on_device(features, residual, short_taps, rates, residues, skip, gain, lengths, owner):
    count, _, width = features.shape
    size = width // rates.shape[0]
    ndoc = lengths.shape[0]
    nblocks = lax.axis_size("ctx")
    rows = count // nblocks
    where = lax.axis_index("ctx")
    x = jnp.transpose(features, (1, 0, 2))
    pairs = [(i, i + 1) for i in range(nblocks - 1)]
    halo = lax.ppermute(x[:, count - HALO :], "ctx", pairs)

    scalars = (where.reshape(1).astype(jnp.int32), lengths, owner)
    rates, residues = rates.T, residues.T

    table = owner.reshape(nblocks, nblocks)
    ids = jnp.arange(nblocks, dtype=jnp.int32)
    mine = lax.dynamic_index_in_dim(table, where, 0, keepdims=False)
    twice = jnp.any((mine[:, None] == mine[None, :]) & (ids[None, :] < ids[:, None]), 1)
    unused = nblocks * (nblocks - 1) // 2 - jnp.sum(jnp.where(twice, 0, mine))
    slots = jnp.where(twice, unused, mine).astype(jnp.int32)
    spare_shift = jnp.sum(jnp.where(twice, table[0], 0))

    def exchanged(value):
        return lax.all_to_all(value, "ctx", split_axis=0, concat_axis=0, tiled=True)

    first = width * SPLIT[0] // sum(SPLIT)
    second = width - first
    mixed, copies = mix(scalars, x, halo, short_taps, rates, size, ndoc, nblocks)
    states = exchanged(copies)
    shared = (scalars, x, halo, short_taps, mixed, rates, residues, skip.reshape(1, width), residual)
    base, gate = conv(0, first, 0, *shared, None, size, ndoc, nblocks)
    out, spare, squares = add(scalars, base, gate, rates, residues, states, size, ndoc, nblocks)
    block = exchanged(out)
    out, last_spare, last_squares = conv(first, second, ROOM, *shared, states, size, ndoc, nblocks)
    mean = lax.psum(jnp.sum(squares + last_squares, 1), "mp") / (width * lax.axis_size("mp"))
    inverse = lax.rsqrt(mean + EPS)
    high = lax.reduce_precision(inverse, 8, 7)
    halves = jnp.concatenate([high.reshape(nblocks, rows), (inverse - high).reshape(nblocks, rows)], 1)
    halves = jnp.pad(halves, ((0, 0), (0, LANES - 2 * rows)))
    in_slot = slots[None, :] == ids[:, None]
    by_slot = jnp.sum(jnp.where(in_slot[:, :, None], halves[None], 0.0), 1)
    by_slot = jnp.broadcast_to(by_slot.astype(BF16)[:, None], (nblocks, ROOM, LANES))
    spare_halves = jnp.sum(jnp.where(twice[:, None], halves, 0.0), 0).astype(BF16)
    out = lax.dynamic_update_slice(out, by_slot, (0, second // LANES * rows, 0))
    last_block = exchanged(out)
    spares = jnp.concatenate([spare, last_spare, jnp.broadcast_to(spare_halves[None], (ROOM, LANES))], 0)

    def moved(by):
        return lambda value: lax.ppermute(value, "ctx", [(s, (s + by) % nblocks) for s in range(nblocks)])

    spare = lax.switch(spare_shift, [lambda value: value] + [moved(d) for d in range(1, nblocks)], spares)
    return norm(scalars[0], owner, block, last_block, spare, gain.reshape(1, width), count)


def solution(mesh):
    return jax.shard_map(
        on_device,
        mesh=mesh,
        in_specs=(
            P("ctx", None, "mp"),
            P("ctx", "mp"),
            P(None, None, "mp"),
            P("mp", None),
            P("mp", None),
            P("mp"),
            P("mp"),
            P(),
            P(),
        ),
        out_specs=P("ctx", "mp"),
        check_vma=False,
    )
```

```python
import functools
import math

import jax
import jax.numpy as jnp
from jax import lax
from jax.experimental import pallas as pl
from jax.experimental.pallas import tpu as pltpu
from jax.sharding import PartitionSpec as P

SHORT = 7
LANES = 128
CHUNK = 128
HALO = 8
EPS = 1e-06
SPLIT = (4, 4)
NEAR = 4
ROOM = 16
WIDE = 512
SPAN = 64
F32 = jnp.float32
BF16 = jnp.bfloat16
VMEM_LIMIT = 64 * 1024 * 1024
VMEM_LIMIT_BESIDE = 56 * 1024 * 1024


def iota(shape, dim):
    return lax.broadcasted_iota(jnp.int32, shape, dim)


def document(ends, positions):
    total = jnp.zeros(positions.shape, jnp.int32)
    for end in ends:
        total = total + (positions >= end).astype(jnp.int32)
    return total


def scalar_document(ends, position):
    total = jnp.int32(0)
    for end in ends:
        total = total + (position >= end).astype(jnp.int32)
    return jnp.where(position < 0, -1, total)


def running_ends(lengths_ref, ndoc):
    ends, total = [], jnp.int32(0)
    for j in range(ndoc):
        total = total + lengths_ref[j]
        ends.append(total)
    return ends


def write_lag_masks(mask_ref, ends, base, count):
    mask_ref[...] = jnp.ones_like(mask_ref)
    gap = jnp.zeros((1, LANES), F32)
    for end in ends:
        row = end - base + HALO

        @pl.when((row >= 0) & (row < count + HALO))
        def _(row=row):
            for lag in (1, 2, 3):
                for past in range(lag):
                    mask_ref[lag - 1, pl.ds(row + past, 1), :] = gap


def row_documents(ends, base, count):
    return document(ends, base + iota((8, count), 1)).astype(F32)


def is_second(owner_ref, nblocks, i):
    found = jnp.bool_(False)
    for j in range(i):
        found = found | (owner_ref[j] == owner_ref[i])
    return found


def write_slots(slot_ref, owner_ref, where, nblocks):
    unused = jnp.int32(nblocks * (nblocks - 1) // 2)
    seconds = [is_second(owner_ref, nblocks, i) for i in range(nblocks)]
    mine = [owner_ref[where * nblocks + i] for i in range(nblocks)]
    for i in range(nblocks):
        unused = unused - jnp.where(seconds[i], 0, mine[i])
    for i in range(nblocks):
        slot_ref[i] = jnp.where(seconds[i], unused, mine[i])
    slot_ref[nblocks] = unused


def tile_rates(rates_ref, low, size):
    first = low // size
    columns = [rates_ref[:, first + g : first + g + 1] for g in range(LANES // size)]
    return jnp.concatenate([jnp.broadcast_to(column, (column.shape[0], LANES)) for column in columns], 0)


def short_conv(ext, taps, masks):
    def back(value, lag):
        return pltpu.roll(value, lag, 0) * masks[lag - 1]

    one, two = back(ext, 1), back(ext, 2)
    far = ext * taps[6]
    middle = ext * taps[3] + one * taps[4] + two * taps[5] + back(far, 3)
    near = ext * taps[0] + one * taps[1] + two * taps[2] + back(middle, 3)
    return near[HALO:]


def extended(x_ref, halo_ref, which, start, lanes):
    rows = x_ref[0, start : start + SPAN, lanes].astype(F32)
    if start == 0:
        ahead = halo_ref[which, :, lanes].astype(F32)
    else:
        ahead = x_ref[0, start - 16 : start, lanes].astype(F32)[16 - HALO :]
    return jnp.concatenate([ahead, rows], 0)


def tap_rows(taps_ref, which, lanes):
    return [taps_ref[which, j : j + 1, lanes] for j in range(SHORT)]


def lag_masks(mask_ref, start):
    return [mask_ref[l, start : start + SPAN + HALO, :] for l in range(3)]


def group_mask(modes, size):
    return (iota((LANES, LANES), 0) // modes) == (iota((LANES, LANES), 1) // size)


def each_tile(width, body):
    for low in range(0, width, LANES):
        body(slice(low, low + LANES))


def write_shifts(shift_ref, mask_ref, ends, base, count):
    mask_ref[...] = jnp.ones_like(mask_ref)
    gap = jnp.zeros((1, LANES), F32)
    for end in ends:
        row = end - base + HALO

        @pl.when((row >= 0) & (row < count + HALO))
        def _(row=row):
            for lag in range(1, NEAR + 1):
                for past in range(lag):
                    mask_ref[lag - 1, pl.ds(row + past, 1), :] = gap

    reach = SPAN + HALO
    back = iota((reach, SPAN + 16), 0) + HALO - iota((reach, SPAN + 16), 1)
    for span in range(count // SPAN):
        moves = []
        for lag in range(1, NEAR):
            mask = mask_ref[lag - 1, span * SPAN : span * SPAN + reach, : SPAN + 16]
            moves.append(jnp.where(back == lag, mask, 0.0))
        shift_ref[span] = jnp.concatenate(moves, 0).astype(BF16)


def mix_kernel(
    modes, size, ndoc,
    where_ref, lengths_ref,
    key_ref, value_ref, halo_ref, taps_ref, rates_ref,
    mixed_ref, state_ref,
    shift_ref, mask_ref, tail_ref,
):
    _, count, width = key_ref.shape
    chunks = count // CHUNK
    reach = SPAN + HALO

    @pl.when(pl.program_id(0) == 0)
    def _():
        base = where_ref[0] * count
        ends = running_ends(lengths_ref, ndoc)
        write_shifts(shift_ref, mask_ref, ends, base, count)
        last = scalar_document(ends, base + count - 1).astype(F32)
        tail_ref[...] = jnp.where(row_documents(ends, base, count) == last, 1.0, 0.0).astype(F32)

    def window(x_ref, which, start, lanes):
        if start == 0:
            halo = halo_ref[which, :, lanes].astype(F32)
            ahead = jnp.concatenate([jnp.zeros((16 - HALO, LANES), F32), halo], 0).astype(BF16)
        else:
            ahead = x_ref[0, start - 16 : start, lanes]
        return jnp.concatenate([ahead, x_ref[0, start : start + SPAN, lanes]], 0)

    def finish(here, moved, taps, apart):
        rows = [here] + [moved[lag * reach : (lag + 1) * reach] for lag in range(NEAR - 1)]
        far = sum(rows[lag] * taps[NEAR + lag] for lag in range(SHORT - NEAR))
        far = pltpu.roll(far, NEAR, 0)[HALO:] * apart
        return far + sum(row[HALO:] * taps[lag] for lag, row in enumerate(rows))

    def tile(lanes):
        key_taps, value_taps = tap_rows(taps_ref, 1, lanes), tap_rows(taps_ref, 2, lanes)
        for start in range(0, count, SPAN):
            keys, values = window(key_ref, 1, start, lanes), window(value_ref, 2, start, lanes)
            moved = jnp.dot(shift_ref[start // SPAN], jnp.concatenate([keys, values], 1), preferred_element_type=F32)
            apart = mask_ref[NEAR - 1, HALO + start : HALO + start + SPAN, :]
            key = finish(keys.astype(F32)[16 - HALO :], moved[:, :LANES], key_taps, apart)
            value = finish(values.astype(F32)[16 - HALO :], moved[:, LANES:], value_taps, apart)
            mixed_ref[start : start + SPAN, lanes] = (key * value).astype(BF16)
        rate = tile_rates(rates_ref.at[0], lanes.start, size)
        leave = jnp.exp(-rate * (CHUNK - 1 - iota((LANES, CHUNK), 1)).astype(F32))
        whole = jnp.exp(-rate * CHUNK)
        spans = []
        for chunk in reversed(range(chunks)):
            tail = tail_ref[0:1, chunk * CHUNK : (chunk + 1) * CHUNK]
            spans.append((leave * tail).astype(BF16))
            leave = leave * whole
        full = jnp.dot(jnp.concatenate(spans[::-1], 1), mixed_ref[:, lanes], preferred_element_type=F32)
        full = jnp.where(group_mask(modes, size), full, 0.0)
        state = jnp.sum(full.reshape(LANES // modes, modes, LANES), 0).astype(BF16)
        for owner in range(state_ref.shape[0]):
            state_ref[owner, :, lanes] = state

    each_tile(width, tile)


def left_state(states_ref, flags_ref, rate, lanes, modes, size, count):
    inside = group_mask(modes, size)
    where = flags_ref[1]

    def gather(v, total):
        weight = jnp.exp(-rate * ((where - 1 - v) * count).astype(F32))
        piece = jnp.concatenate([states_ref[v, :, lanes].astype(F32)] * (LANES // modes), 0)
        return total + jnp.where(inside, piece * weight, 0.0)

    return lax.fori_loop(flags_ref[0], where, gather, jnp.zeros((LANES, LANES), F32))


def write_flags(flags_ref, ends, where, count, nblocks):
    before = scalar_document(ends, where * count - 1)
    first = jnp.int32(0)
    for v in range(nblocks):
        first = first + (scalar_document(ends, (v + 1) * count - 1) < before).astype(jnp.int32)
    flags_ref[0] = first
    flags_ref[1] = where
    for chunk in range(count // CHUNK):
        start = where * count + chunk * CHUNK
        held = scalar_document(ends, start - 1) == scalar_document(ends, start + CHUNK - 1)
        flags_ref[2 + chunk] = held.astype(jnp.int32)


def hand_over(out_ref, squares_ref, slot_ref, summed, start, rows, lanes):
    squares_ref[start : start + SPAN, :] += summed * summed
    rounded = summed.astype(BF16)
    for b in range(SPAN // rows):
        tile = lanes.start // LANES * rows
        out_ref[slot_ref[start // rows + b], tile : tile + rows, :] = rounded[b * rows : (b + 1) * rows]


def conv_kernel(modes, size, ndoc, nblocks, carried, where_ref, lengths_ref, owner_ref, *refs):
    x_ref, halo_ref, taps_ref, mixed_ref, rates_ref, residues_ref, skip_ref, residual_ref = refs[:8]
    refs = refs[8:]
    if carried:
        states_ref, out_ref, spare_ref, squares_ref = refs[:4]
        refs = refs[4:]
    else:
        base_ref, gate_ref = refs[:2]
        refs = refs[2:]
    mask_ref, same_ref, keep_ref, tail_ref, flags_ref = refs[:5]
    count, width = mixed_ref.shape
    chunks = count // CHUNK

    @pl.when(pl.program_id(0) == 0)
    def _():
        where = where_ref[0]
        base = where * count
        ends = running_ends(lengths_ref, ndoc)
        write_lag_masks(mask_ref, ends, base, count)
        write_flags(flags_ref, ends, where, count, nblocks)
        if carried:
            write_slots(refs[5], owner_ref, where, nblocks)
            squares_ref[...] = jnp.zeros_like(squares_ref)
        documents = row_documents(ends, base, count)
        causal = iota((CHUNK, CHUNK), 1) <= iota((CHUNK, CHUNK), 0)
        for chunk in range(chunks):
            start = base + chunk * CHUNK
            there = jnp.broadcast_to(documents[0:1, chunk * CHUNK : (chunk + 1) * CHUNK], (CHUNK, CHUNK))
            here = there.T
            same_ref[chunk] = jnp.where((here == there) & causal, 1.0, 0.0).astype(BF16)
            before = scalar_document(ends, start - 1).astype(F32)
            keep_ref[chunk] = jnp.where(here == before, 1.0, 0.0).astype(BF16)
            last = scalar_document(ends, start + CHUNK - 1).astype(F32)
            tail_ref[chunk] = jnp.where(there == last, 1.0, 0.0).astype(F32)

    groups = LANES // modes

    def tile(lanes):
        rate = tile_rates(rates_ref.at[0], lanes.start, size)
        scale = tile_rates(residues_ref.at[0], lanes.start, size) * jnp.sqrt(1.0 - jnp.exp(-2.0 * rate))
        down = iota((CHUNK, LANES), 0)
        along = iota((LANES, CHUNK), 1)
        entry = (scale.T * jnp.exp(-rate.T * (down + 1).astype(F32))).astype(BF16)
        leave = jnp.exp(-rate * (CHUNK - 1 - along).astype(F32))
        whole = jnp.exp(-rate * CHUNK)
        terms = scale * jnp.where(along == 0, 1.0, leave * jnp.exp(-rate))
        toeplitz = []
        for g in range(groups):
            line = jnp.sum(terms[g * modes : (g + 1) * modes], 0, keepdims=True)
            top = pltpu.roll(jnp.broadcast_to(line, (8, CHUNK)), 0, 1, stride=1, stride_axis=0)
            parts = [top] + [pltpu.roll(top, 8 * k, 1) for k in range(1, CHUNK // 8)]
            toeplitz.append(jnp.concatenate(parts, 0).astype(BF16))
        inside = group_mask(modes, size)
        state = left_state(states_ref, flags_ref, rate, lanes, modes, size, count) if carried else None
        taps = tap_rows(taps_ref, 0, lanes)
        skip = skip_ref[:, lanes]
        lane_group = iota((CHUNK, LANES), 1) // size
        for chunk in range(chunks):
            start = chunk * CHUNK
            mixed = mixed_ref[start : start + CHUNK, lanes]
            same = same_ref[chunk]
            left = [t * same for t in toeplitz]
            right = [jnp.where(lane_group == g, mixed, jnp.zeros_like(mixed)) for g in range(groups)]
            if state is not None:
                left.append(entry * keep_ref[chunk])
                right.append(state.astype(BF16))
            longer = jnp.dot(jnp.concatenate(left, 1), jnp.concatenate(right, 0), preferred_element_type=F32)
            if chunk + 1 < chunks:
                fresh = jnp.dot((leave * tail_ref[chunk]).astype(BF16), mixed, preferred_element_type=F32)
                held = flags_ref[2 + chunk] == 1
                fresh = jnp.where(inside, fresh, 0.0)
                state = fresh if state is None else jnp.where(held, whole * state, 0.0) + fresh
            body = longer + skip * mixed.astype(F32)
            for half in range(start, start + CHUNK, SPAN):
                gate = short_conv(extended(x_ref, halo_ref, 0, half, lanes), taps, lag_masks(mask_ref, half))
                inner = body[half - start : half - start + SPAN]
                summed = residual_ref[half : half + SPAN, lanes].astype(F32) + gate * inner
                if carried:
                    hand_over(out_ref, squares_ref, refs[5], summed, half, count // nblocks, lanes)
                else:
                    base_ref[half : half + SPAN, lanes] = summed
                    gate_ref[half : half + SPAN, lanes] = gate.astype(BF16)

    each_tile(width, tile)
    if carried:
        spare_ref[...] = out_ref[refs[5][nblocks]]


def add_kernel(
    modes, size, ndoc, nblocks,
    where_ref, lengths_ref, owner_ref,
    base_ref, gate_ref, rates_ref, residues_ref, states_ref,
    out_ref, spare_ref, squares_ref,
    keep_ref, flags_ref, slot_ref,
):
    count, width = base_ref.shape
    chunks = count // CHUNK

    @pl.when(pl.program_id(0) == 0)
    def _():
        where = where_ref[0]
        ends = running_ends(lengths_ref, ndoc)
        write_flags(flags_ref, ends, where, count, nblocks)
        write_slots(slot_ref, owner_ref, where, nblocks)
        squares_ref[...] = jnp.zeros_like(squares_ref)
        before = scalar_document(ends, where * count - 1)
        kept = jnp.int32(0)
        for end in reversed(ends):
            kept = jnp.where(end >= where * count, end - where * count, kept)
        kept = jnp.where(before < 0, 0, kept)
        keep_ref[...] = jnp.where(iota((count, LANES), 0) < kept, 1.0, 0.0).astype(F32)

    def tile(lanes):
        rate = tile_rates(rates_ref.at[0], lanes.start, size)
        scale = tile_rates(residues_ref.at[0], lanes.start, size) * jnp.sqrt(1.0 - jnp.exp(-2.0 * rate))
        down = iota((CHUNK, LANES), 0)
        entry = (scale.T * jnp.exp(-rate.T * (down + 1).astype(F32))).astype(BF16)
        whole = jnp.exp(-rate * CHUNK)
        state = left_state(states_ref, flags_ref, rate, lanes, modes, size, count)
        held = []
        for _ in range(chunks):
            held.append(state.astype(BF16))
            state = state * whole
        left = jnp.dot(entry, jnp.concatenate(held, 1), preferred_element_type=F32)
        for start in range(0, count, SPAN):
            low = start % CHUNK
            chunk = start // CHUNK
            carried = left[low : low + SPAN, chunk * LANES : (chunk + 1) * LANES] * keep_ref[start : start + SPAN, :]
            gate = gate_ref[start : start + SPAN, lanes].astype(F32)
            summed = base_ref[start : start + SPAN, lanes] + gate * carried
            hand_over(out_ref, squares_ref, slot_ref, summed, start, count // nblocks, lanes)

    each_tile(width, tile)
    spare_ref[...] = out_ref[slot_ref[nblocks]]


def norm_kernel(parts, where_ref, owner_ref, *refs):
    blocks, refs = refs[:parts], refs[parts:]
    spare_ref, gain_ref, out_ref = refs[:3]
    held, (done_ref, in_sems, out_sems) = refs[3 : 3 + parts], refs[3 + parts :]
    nblocks = blocks[0].shape[0]
    rows = out_ref.shape[0] // nblocks

    def fetch(part, i, source):
        return pltpu.make_async_copy(source, held[part].at[i], in_sems.at[part, i])

    for i in range(nblocks):
        ahead = where_ref[0] - owner_ref[i]
        source = jnp.where(ahead < 0, ahead + nblocks, ahead)
        second = is_second(owner_ref, nblocks, i)
        low = 0
        for part in range(parts):
            size = blocks[part].shape[1]

            @pl.when(second)
            def _(part=part, i=i, low=low, size=size):
                fetch(part, i, spare_ref.at[pl.ds(low, size)]).start()

            @pl.when(jnp.logical_not(second))
            def _(part=part, i=i, source=source):
                fetch(part, i, blocks[part].at[source]).start()

            low += size

    def store(i):
        here = pl.ds(i * rows, rows)
        return pltpu.make_async_copy(done_ref.at[here], out_ref.at[here], out_sems.at[i])

    for i in range(nblocks):
        for part in range(parts):
            fetch(part, i, blocks[part].at[0]).wait()
        halves = jnp.broadcast_to(held[-1][i, -ROOM:, :].astype(F32)[0:1], (8, LANES))
        scale = halves + pltpu.roll(halves, LANES - rows, 1)
        scale = jnp.broadcast_to(scale[0:1], (LANES, LANES)).T[:rows]
        tile = 0
        for part in range(parts):
            for low in range(0, held[part].shape[1] - (ROOM if part + 1 == parts else 0), rows):
                outs = slice(tile * LANES, (tile + 1) * LANES)
                value = held[part][i, low : low + rows, :].astype(F32)
                done_ref[i * rows : (i + 1) * rows, outs] = (value * scale * gain_ref[:, outs]).astype(BF16)
                tile += 1
        store(i).start()
    for i in range(nblocks):
        store(i).wait()


def params(limit=VMEM_LIMIT):
    return pltpu.CompilerParams(dimension_semantics=("arbitrary",), vmem_limit_bytes=limit)


def in_hbm(*arrays):
    return [pltpu.with_memory_space_constraint(array, pltpu.HBM) for array in arrays]


def in_vmem(array):
    return pltpu.with_memory_space_constraint(array, pltpu.VMEM)


def whole_array(rank):
    return lambda *_: (0,) * rank


def by_step(rates, wide, size):
    modes, groups = rates.shape
    held = wide // size
    return jnp.transpose(rates.reshape(modes, groups // held, held), (1, 0, 2))


def mix(scalars, x, halo, taps, rates, size, ndoc, copies):
    _, count, width = x.shape
    modes = rates.shape[0]
    wide = min(WIDE, width)
    deep = lambda t, *_: (0, 0, t)
    grid_spec = pltpu.PrefetchScalarGridSpec(
        num_scalar_prefetch=2,
        grid=(width // wide,),
        in_specs=[
            pl.BlockSpec((1, count, wide), lambda t, *_: (1, 0, t)),
            pl.BlockSpec((1, count, wide), lambda t, *_: (2, 0, t)),
            pl.BlockSpec((3, HALO, wide), deep),
            pl.BlockSpec((3, SHORT, wide), deep),
            pl.BlockSpec((1, modes, wide // size), lambda t, *_: (t, 0, 0)),
        ],
        out_specs=[
            pl.BlockSpec((count, wide), lambda t, *_: (0, t)),
            pl.BlockSpec((copies, modes, wide), deep),
        ],
        scratch_shapes=[
            pltpu.VMEM((count // SPAN, (NEAR - 1) * (SPAN + HALO), SPAN + 16), BF16),
            pltpu.VMEM((NEAR, count + 2 * HALO, LANES), F32),
            pltpu.VMEM((8, count), F32),
        ],
    )
    return pl.pallas_call(
        functools.partial(mix_kernel, modes, size, ndoc),
        grid_spec=grid_spec,
        out_shape=[pltpu.HBM((count, width), BF16), pltpu.HBM((copies, modes, width), BF16)],
        compiler_params=params(),
        cost_estimate=pl.CostEstimate(flops=60 * count * width, bytes_accessed=8 * count * width, transcendentals=count * width),
        name="mix",
    )(*scalars[:2], x, x, halo, taps, by_step(rates, wide, size))


def conv(low, share, room, scalars, x, halo, taps, mixed, rates, residues, skip, residual, states, size, ndoc, nblocks):
    _, count, width = x.shape
    modes = rates.shape[0]
    rows = count // nblocks
    wide = math.gcd(math.gcd(low, share), WIDE)
    first = low // wide
    carried = states is not None
    tile = lambda t, *_: (0, first + t)
    deep = lambda t, *_: (0, 0, first + t)
    step = pl.BlockSpec((1, modes, wide // size), lambda t, *_: (first + t, 0, 0))
    in_specs = [
        pl.BlockSpec((1, count, wide), deep),
        pl.BlockSpec((1, HALO, wide), deep),
        pl.BlockSpec((1, SHORT, wide), deep),
        pl.BlockSpec((count, wide), tile),
        step,
        step,
        pl.BlockSpec((1, wide), tile),
        pl.BlockSpec((count, wide), tile),
    ]
    operands = [x, halo, taps, mixed, by_step(rates, wide, size), by_step(residues, wide, size), skip, residual]
    scratch = [
        pltpu.VMEM((3, count + 2 * HALO, LANES), F32),
        pltpu.VMEM((count // CHUNK, CHUNK, CHUNK), BF16),
        pltpu.VMEM((count // CHUNK, CHUNK, LANES), BF16),
        pltpu.VMEM((count // CHUNK, LANES, CHUNK), F32),
        pltpu.SMEM((2 + count // CHUNK,), jnp.int32),
    ]
    if carried:
        in_specs.append(pl.BlockSpec((nblocks, modes, wide), deep))
        operands.append(states)
        scratch.append(pltpu.SMEM((nblocks + 1,), jnp.int32))
        out_specs, out_shape = handed(share, room, wide, count, nblocks)
    else:
        out_specs = [pl.BlockSpec((count, wide), lambda t, *_: (0, t))] * 2
        out_shape = [pltpu.VMEM((count, share), F32), pltpu.VMEM((count, share), BF16)]
    grid_spec = pltpu.PrefetchScalarGridSpec(
        num_scalar_prefetch=3, grid=(share // wide,), in_specs=in_specs, out_specs=out_specs, scratch_shapes=scratch
    )
    return pl.pallas_call(
        functools.partial(conv_kernel, modes, size, ndoc, nblocks, carried),
        grid_spec=grid_spec,
        out_shape=out_shape,
        compiler_params=params(VMEM_LIMIT if carried else VMEM_LIMIT_BESIDE),
        cost_estimate=pl.CostEstimate(
            flops=2 * 1152 * count * share, bytes_accessed=8 * count * share, transcendentals=count * share
        ),
        name="conv",
    )(*scalars, *in_hbm(*operands))


def handed(share, room, wide, count, nblocks):
    rows = count // nblocks
    specs = [
        pl.BlockSpec((nblocks, wide // LANES * rows, LANES), lambda t, *_: (0, t, 0)),
        pl.BlockSpec((wide // LANES * rows, LANES), lambda t, *_: (t, 0)),
        pl.BlockSpec((count, LANES), whole_array(2)),
    ]
    shapes = [
        pltpu.HBM((nblocks, share // LANES * rows + room, LANES), BF16),
        pltpu.HBM((share // LANES * rows, LANES), BF16),
        pltpu.HBM((count, LANES), F32),
    ]
    return specs, shapes


def add(scalars, base, gate, rates, residues, states, size, ndoc, nblocks):
    count, share = base.shape
    modes = rates.shape[0]
    wide = math.gcd(share, WIDE)
    tile = lambda t, *_: (0, t)
    step = pl.BlockSpec((1, modes, wide // size), lambda t, *_: (t, 0, 0))
    out_specs, out_shape = handed(share, 0, wide, count, nblocks)
    grid_spec = pltpu.PrefetchScalarGridSpec(
        num_scalar_prefetch=3,
        grid=(share // wide,),
        in_specs=[
            pl.BlockSpec((count, wide), tile),
            pl.BlockSpec((count, wide), tile),
            step,
            step,
            pl.BlockSpec((nblocks, modes, wide), lambda t, *_: (0, 0, t)),
        ],
        out_specs=out_specs,
        scratch_shapes=[
            pltpu.VMEM((count, LANES), F32),
            pltpu.SMEM((2 + count // CHUNK,), jnp.int32),
            pltpu.SMEM((nblocks + 1,), jnp.int32),
        ],
    )
    return pl.pallas_call(
        functools.partial(add_kernel, modes, size, ndoc, nblocks),
        grid_spec=grid_spec,
        out_shape=out_shape,
        compiler_params=params(VMEM_LIMIT_BESIDE),
        cost_estimate=pl.CostEstimate(flops=300 * count * share, bytes_accessed=8 * count * share, transcendentals=count * share),
        name="add",
    )(*scalars, in_vmem(base), in_vmem(gate), *in_hbm(by_step(rates, wide, size), by_step(residues, wide, size), states))


def norm(where, owner, blocks, spare, gain, count):
    width = gain.shape[1]
    nblocks = blocks[0].shape[0]
    smem, vmem, anywhere = (pl.BlockSpec(memory_space=space) for space in (pltpu.SMEM, pltpu.VMEM, pl.ANY))
    return pl.pallas_call(
        functools.partial(norm_kernel, len(blocks)),
        in_specs=[smem, smem] + [anywhere] * (len(blocks) + 1) + [vmem],
        out_specs=anywhere,
        out_shape=jax.ShapeDtypeStruct((count, width), BF16),
        scratch_shapes=[pltpu.VMEM(block.shape, BF16) for block in blocks]
        + [
            pltpu.VMEM((count, width), BF16),
            pltpu.SemaphoreType.DMA((len(blocks), nblocks)),
            pltpu.SemaphoreType.DMA((nblocks,)),
        ],
        compiler_params=pltpu.CompilerParams(vmem_limit_bytes=VMEM_LIMIT),
        cost_estimate=pl.CostEstimate(flops=3 * count * width, bytes_accessed=4 * count * width, transcendentals=0),
        name="norm",
    )(where, owner, *blocks, spare, gain)


def on_device(features, residual, short_taps, rates, residues, skip, gain, lengths, owner):
    count, _, width = features.shape
    size = width // rates.shape[0]
    ndoc = lengths.shape[0]
    nblocks = lax.axis_size("ctx")
    rows = count // nblocks
    where = lax.axis_index("ctx")
    x = jnp.transpose(features, (1, 0, 2))
    pairs = [(i, i + 1) for i in range(nblocks - 1)]
    halo = lax.ppermute(x[:, count - HALO :], "ctx", pairs)

    scalars = (where.reshape(1).astype(jnp.int32), lengths, owner)
    rates, residues = rates.T, residues.T

    table = owner.reshape(nblocks, nblocks)
    ids = jnp.arange(nblocks, dtype=jnp.int32)
    mine = lax.dynamic_index_in_dim(table, where, 0, keepdims=False)
    twice = jnp.any((mine[:, None] == mine[None, :]) & (ids[None, :] < ids[:, None]), 1)
    unused = nblocks * (nblocks - 1) // 2 - jnp.sum(jnp.where(twice, 0, mine))
    slots = jnp.where(twice, unused, mine).astype(jnp.int32)
    spare_shift = jnp.sum(jnp.where(twice, table[0], 0))

    def exchanged(value):
        return lax.all_to_all(value, "ctx", split_axis=0, concat_axis=0, tiled=True)

    first = width * SPLIT[0] // sum(SPLIT)
    second = width - first
    mixed, copies = mix(scalars, x, halo, short_taps, rates, size, ndoc, nblocks)
    states = exchanged(copies)
    shared = (scalars, x, halo, short_taps, mixed, rates, residues, skip.reshape(1, width), residual)
    base, gate = conv(0, first, 0, *shared, None, size, ndoc, nblocks)
    out, spare, squares = add(scalars, base, gate, rates, residues, states, size, ndoc, nblocks)
    block = exchanged(out)
    out, last_spare, last_squares = conv(first, second, ROOM, *shared, states, size, ndoc, nblocks)
    mean = lax.psum(jnp.sum(squares + last_squares, 1), "mp") / (width * lax.axis_size("mp"))
    inverse = lax.rsqrt(mean + EPS)
    high = lax.reduce_precision(inverse, 8, 7)
    halves = jnp.concatenate([high.reshape(nblocks, rows), (inverse - high).reshape(nblocks, rows)], 1)
    halves = jnp.pad(halves, ((0, 0), (0, LANES - 2 * rows)))
    in_slot = slots[None, :] == ids[:, None]
    by_slot = jnp.sum(jnp.where(in_slot[:, :, None], halves[None], 0.0), 1)
    by_slot = jnp.broadcast_to(by_slot.astype(BF16)[:, None], (nblocks, ROOM, LANES))
    spare_halves = jnp.sum(jnp.where(twice[:, None], halves, 0.0), 0).astype(BF16)
    out = lax.dynamic_update_slice(out, by_slot, (0, second // LANES * rows, 0))
    last_block = exchanged(out)
    spares = jnp.concatenate([spare, last_spare, jnp.broadcast_to(spare_halves[None], (ROOM, LANES))], 0)

    def moved(by):
        return lambda value: lax.ppermute(value, "ctx", [(s, (s + by) % nblocks) for s in range(nblocks)])

    spare = lax.switch(spare_shift, [lambda value: value] + [moved(d) for d in range(1, nblocks)], spares)
    return norm(scalars[0], owner, [block, last_block], spare, gain.reshape(1, width), count)


def solution(mesh):
    return jax.shard_map(
        on_device,
        mesh=mesh,
        in_specs=(
            P("ctx", None, "mp"),
            P("ctx", "mp"),
            P(None, None, "mp"),
            P("mp", None),
            P("mp", None),
            P("mp"),
            P("mp"),
            P(),
            P(),
        ),
        out_specs=P("ctx", "mp"),
        check_vma=False,
    )
```

```python
import functools
import math

import jax
import jax.numpy as jnp
from jax import lax
from jax.experimental import pallas as pl
from jax.experimental.pallas import tpu as pltpu
from jax.sharding import PartitionSpec as P

SHORT = 7
LANES = 128
CHUNK = 128
HALO = 8
EPS = 1e-06
SPLIT = (4, 4)
NEAR = 4
WIDE = 512
SPAN = 64
F32 = jnp.float32
BF16 = jnp.bfloat16
VMEM_LIMIT = 64 * 1024 * 1024
VMEM_LIMIT_BESIDE = 56 * 1024 * 1024


def iota(shape, dim):
    return lax.broadcasted_iota(jnp.int32, shape, dim)


def document(ends, positions):
    total = jnp.zeros(positions.shape, jnp.int32)
    for end in ends:
        total = total + (positions >= end).astype(jnp.int32)
    return total


def scalar_document(ends, position):
    total = jnp.int32(0)
    for end in ends:
        total = total + (position >= end).astype(jnp.int32)
    return jnp.where(position < 0, -1, total)


def running_ends(lengths_ref, ndoc):
    ends, total = [], jnp.int32(0)
    for j in range(ndoc):
        total = total + lengths_ref[j]
        ends.append(total)
    return ends


def write_lag_masks(mask_ref, ends, base, count):
    mask_ref[...] = jnp.ones_like(mask_ref)
    gap = jnp.zeros((1, LANES), F32)
    for end in ends:
        row = end - base + HALO

        @pl.when((row >= 0) & (row < count + HALO))
        def _(row=row):
            for lag in (1, 2, 3):
                for past in range(lag):
                    mask_ref[lag - 1, pl.ds(row + past, 1), :] = gap


def row_documents(ends, base, count):
    return document(ends, base + iota((8, count), 1)).astype(F32)


def is_second(owner_ref, nblocks, i):
    found = jnp.bool_(False)
    for j in range(i):
        found = found | (owner_ref[j] == owner_ref[i])
    return found


def write_slots(slot_ref, owner_ref, where, nblocks):
    unused = jnp.int32(nblocks * (nblocks - 1) // 2)
    seconds = [is_second(owner_ref, nblocks, i) for i in range(nblocks)]
    mine = [owner_ref[where * nblocks + i] for i in range(nblocks)]
    for i in range(nblocks):
        unused = unused - jnp.where(seconds[i], 0, mine[i])
    for i in range(nblocks):
        slot_ref[i] = jnp.where(seconds[i], unused, mine[i])
    slot_ref[nblocks] = unused


def step_rates(ref, origin, wide, size):
    first = origin + pl.program_id(0) * (wide // size)
    return pltpu.roll(ref[...], jnp.where(first == 0, 0, LANES - first), 1)


def tile_rates(rates, low, size):
    first = low // size
    columns = [rates[:, first + g : first + g + 1] for g in range(LANES // size)]
    return jnp.concatenate([jnp.broadcast_to(column, (column.shape[0], LANES)) for column in columns], 0)


def short_conv(ext, taps, masks):
    def back(value, lag):
        return pltpu.roll(value, lag, 0) * masks[lag - 1]

    one, two = back(ext, 1), back(ext, 2)
    far = ext * taps[6]
    middle = ext * taps[3] + one * taps[4] + two * taps[5] + back(far, 3)
    near = ext * taps[0] + one * taps[1] + two * taps[2] + back(middle, 3)
    return near[HALO:]


def extended(x_ref, halo_ref, which, start, lanes):
    rows = x_ref[0, start : start + SPAN, lanes].astype(F32)
    if start == 0:
        ahead = halo_ref[which, :, lanes].astype(F32)
    else:
        ahead = x_ref[0, start - 16 : start, lanes].astype(F32)[16 - HALO :]
    return jnp.concatenate([ahead, rows], 0)


def tap_rows(taps_ref, which, lanes):
    return [taps_ref[which, j : j + 1, lanes] for j in range(SHORT)]


def lag_masks(mask_ref, start):
    return [mask_ref[l, start : start + SPAN + HALO, :] for l in range(3)]


def group_mask(modes, size):
    return (iota((LANES, LANES), 0) // modes) == (iota((LANES, LANES), 1) // size)


def each_tile(width, body):
    for low in range(0, width, LANES):
        body(slice(low, low + LANES))


def write_shifts(shift_ref, mask_ref, ends, base, count):
    mask_ref[...] = jnp.ones_like(mask_ref)
    gap = jnp.zeros((1, LANES), F32)
    for end in ends:
        row = end - base + HALO

        @pl.when((row >= 0) & (row < count + HALO))
        def _(row=row):
            for lag in range(1, NEAR + 1):
                for past in range(lag):
                    mask_ref[lag - 1, pl.ds(row + past, 1), :] = gap

    reach = SPAN + HALO
    back = iota((reach, SPAN + 16), 0) + HALO - iota((reach, SPAN + 16), 1)
    for span in range(count // SPAN):
        moves = []
        for lag in range(1, NEAR):
            mask = mask_ref[lag - 1, span * SPAN : span * SPAN + reach, : SPAN + 16]
            moves.append(jnp.where(back == lag, mask, 0.0))
        shift_ref[span] = jnp.concatenate(moves, 0).astype(BF16)


def mix_kernel(
    modes, size, ndoc,
    where_ref, lengths_ref,
    key_ref, value_ref, halo_ref, taps_ref, rates_ref,
    mixed_ref, state_ref,
    shift_ref, mask_ref, tail_ref,
):
    _, count, width = key_ref.shape
    chunks = count // CHUNK
    reach = SPAN + HALO
    step = step_rates(rates_ref, 0, width, size)

    @pl.when(pl.program_id(0) == 0)
    def _():
        base = where_ref[0] * count
        ends = running_ends(lengths_ref, ndoc)
        write_shifts(shift_ref, mask_ref, ends, base, count)
        last = scalar_document(ends, base + count - 1).astype(F32)
        tail_ref[...] = jnp.where(row_documents(ends, base, count) == last, 1.0, 0.0).astype(F32)

    def window(x_ref, which, start, lanes):
        if start == 0:
            halo = halo_ref[which, :, lanes].astype(F32)
            ahead = jnp.concatenate([jnp.zeros((16 - HALO, LANES), F32), halo], 0).astype(BF16)
        else:
            ahead = x_ref[0, start - 16 : start, lanes]
        return jnp.concatenate([ahead, x_ref[0, start : start + SPAN, lanes]], 0)

    def finish(here, moved, taps, apart):
        rows = [here] + [moved[lag * reach : (lag + 1) * reach] for lag in range(NEAR - 1)]
        far = sum(rows[lag] * taps[NEAR + lag] for lag in range(SHORT - NEAR))
        far = pltpu.roll(far, NEAR, 0)[HALO:] * apart
        return far + sum(row[HALO:] * taps[lag] for lag, row in enumerate(rows))

    def tile(lanes):
        key_taps, value_taps = tap_rows(taps_ref, 1, lanes), tap_rows(taps_ref, 2, lanes)
        for start in range(0, count, SPAN):
            keys, values = window(key_ref, 1, start, lanes), window(value_ref, 2, start, lanes)
            moved = jnp.dot(shift_ref[start // SPAN], jnp.concatenate([keys, values], 1), preferred_element_type=F32)
            apart = mask_ref[NEAR - 1, HALO + start : HALO + start + SPAN, :]
            key = finish(keys.astype(F32)[16 - HALO :], moved[:, :LANES], key_taps, apart)
            value = finish(values.astype(F32)[16 - HALO :], moved[:, LANES:], value_taps, apart)
            mixed_ref[start : start + SPAN, lanes] = (key * value).astype(BF16)
        rate = tile_rates(step, lanes.start, size)
        leave = jnp.exp(-rate * (CHUNK - 1 - iota((LANES, CHUNK), 1)).astype(F32))
        whole = jnp.exp(-rate * CHUNK)
        spans = []
        for chunk in reversed(range(chunks)):
            tail = tail_ref[0:1, chunk * CHUNK : (chunk + 1) * CHUNK]
            spans.append((leave * tail).astype(BF16))
            leave = leave * whole
        full = jnp.dot(jnp.concatenate(spans[::-1], 1), mixed_ref[:, lanes], preferred_element_type=F32)
        full = jnp.where(group_mask(modes, size), full, 0.0)
        state = jnp.sum(full.reshape(LANES // modes, modes, LANES), 0).astype(BF16)
        for owner in range(state_ref.shape[0]):
            state_ref[owner, :, lanes] = state

    each_tile(width, tile)


def left_state(states_ref, flags_ref, rate, lanes, modes, size, count):
    inside = group_mask(modes, size)
    decay = jnp.exp(-rate * count)
    total = jnp.zeros((LANES, LANES), F32)
    for back in range(states_ref.shape[0] // 2, 0, -1):
        v = flags_ref[1] - back
        piece = jnp.concatenate([states_ref[jnp.maximum(v, 0), :, lanes].astype(F32)] * (LANES // modes), 0)
        total = jnp.where(inside & (v >= flags_ref[0]), piece + decay * total, 0.0)
    return total


def write_flags(flags_ref, ends, where, count, nblocks):
    before = scalar_document(ends, where * count - 1)
    first = jnp.int32(0)
    for v in range(nblocks):
        first = first + (scalar_document(ends, (v + 1) * count - 1) < before).astype(jnp.int32)
    flags_ref[0] = first
    flags_ref[1] = where
    for chunk in range(count // CHUNK):
        start = where * count + chunk * CHUNK
        held = scalar_document(ends, start - 1) == scalar_document(ends, start + CHUNK - 1)
        flags_ref[2 + chunk] = held.astype(jnp.int32)


def hand_over(out_ref, squares_ref, slot_ref, summed, start, rows, lanes):
    squares_ref[start : start + SPAN, :] += summed * summed
    rounded = summed.astype(BF16)
    for b in range(SPAN // rows):
        tile = lanes.start // LANES * rows
        out_ref[slot_ref[start // rows + b], tile : tile + rows, :] = rounded[b * rows : (b + 1) * rows]


def conv_kernel(modes, size, ndoc, nblocks, carried, origin, where_ref, lengths_ref, owner_ref, *refs):
    x_ref, halo_ref, taps_ref, mixed_ref, rates_ref, residues_ref, skip_ref, residual_ref = refs[:8]
    refs = refs[8:]
    if carried:
        states_ref, before_ref, out_ref, spare_ref, sums_ref = refs[:5]
        refs = refs[5:]
    else:
        base_ref, gate_ref = refs[:2]
        refs = refs[2:]
    mask_ref, same_ref, keep_ref, tail_ref, flags_ref = refs[:5]
    if carried:
        slot_ref, squares_ref = refs[5:]
    count, width = mixed_ref.shape
    chunks = count // CHUNK
    step = step_rates(rates_ref, origin, width, size)
    step_residues = step_rates(residues_ref, origin, width, size)

    @pl.when(pl.program_id(0) == 0)
    def _():
        where = where_ref[0]
        base = where * count
        ends = running_ends(lengths_ref, ndoc)
        write_lag_masks(mask_ref, ends, base, count)
        write_flags(flags_ref, ends, where, count, nblocks)
        if carried:
            write_slots(slot_ref, owner_ref, where, nblocks)
            squares_ref[...] = before_ref[...]
        documents = row_documents(ends, base, count)
        causal = iota((CHUNK, CHUNK), 1) <= iota((CHUNK, CHUNK), 0)
        for chunk in range(chunks):
            start = base + chunk * CHUNK
            there = jnp.broadcast_to(documents[0:1, chunk * CHUNK : (chunk + 1) * CHUNK], (CHUNK, CHUNK))
            here = there.T
            same_ref[chunk] = jnp.where((here == there) & causal, 1.0, 0.0).astype(BF16)
            before = scalar_document(ends, start - 1).astype(F32)
            keep_ref[chunk] = jnp.where(here == before, 1.0, 0.0).astype(BF16)
            last = scalar_document(ends, start + CHUNK - 1).astype(F32)
            tail_ref[chunk] = jnp.where(there == last, 1.0, 0.0).astype(F32)

    groups = LANES // modes

    def tile(lanes):
        rate = tile_rates(step, lanes.start, size)
        scale = tile_rates(step_residues, lanes.start, size) * jnp.sqrt(1.0 - jnp.exp(-2.0 * rate))
        down = iota((CHUNK, LANES), 0)
        along = iota((LANES, CHUNK), 1)
        entry = (scale.T * jnp.exp(-rate.T * (down + 1).astype(F32))).astype(BF16)
        leave = jnp.exp(-rate * (CHUNK - 1 - along).astype(F32))
        whole = jnp.exp(-rate * CHUNK)
        terms = scale * jnp.where(along == 0, 1.0, leave * jnp.exp(-rate))
        toeplitz = []
        for g in range(groups):
            line = jnp.sum(terms[g * modes : (g + 1) * modes], 0, keepdims=True)
            top = pltpu.roll(jnp.broadcast_to(line, (8, CHUNK)), 0, 1, stride=1, stride_axis=0)
            parts = [top] + [pltpu.roll(top, 8 * k, 1) for k in range(1, CHUNK // 8)]
            toeplitz.append(jnp.concatenate(parts, 0).astype(BF16))
        inside = group_mask(modes, size)
        state = left_state(states_ref, flags_ref, rate, lanes, modes, size, count) if carried else None
        taps = tap_rows(taps_ref, 0, lanes)
        skip = skip_ref[:, lanes]
        lane_group = iota((CHUNK, LANES), 1) // size
        for chunk in range(chunks):
            start = chunk * CHUNK
            mixed = mixed_ref[start : start + CHUNK, lanes]
            same = same_ref[chunk]
            left = [t * same for t in toeplitz]
            right = [jnp.where(lane_group == g, mixed, jnp.zeros_like(mixed)) for g in range(groups)]
            if state is not None:
                left.append(entry * keep_ref[chunk])
                right.append(state.astype(BF16))
            longer = jnp.dot(jnp.concatenate(left, 1), jnp.concatenate(right, 0), preferred_element_type=F32)
            if chunk + 1 < chunks:
                fresh = jnp.dot((leave * tail_ref[chunk]).astype(BF16), mixed, preferred_element_type=F32)
                held = flags_ref[2 + chunk] == 1
                fresh = jnp.where(inside, fresh, 0.0)
                state = fresh if state is None else jnp.where(held, whole * state, 0.0) + fresh
            body = longer + skip * mixed.astype(F32)
            for half in range(start, start + CHUNK, SPAN):
                gate = short_conv(extended(x_ref, halo_ref, 0, half, lanes), taps, lag_masks(mask_ref, half))
                inner = body[half - start : half - start + SPAN]
                summed = residual_ref[half : half + SPAN, lanes].astype(F32) + gate * inner
                if carried:
                    hand_over(out_ref, squares_ref, slot_ref, summed, half, count // nblocks, lanes)
                else:
                    base_ref[half : half + SPAN, lanes] = summed
                    gate_ref[half : half + SPAN, lanes] = gate.astype(BF16)

    each_tile(width, tile)
    if carried:
        spare_ref[...] = out_ref[slot_ref[nblocks]]

        @pl.when(pl.program_id(0) == pl.num_programs(0) - 1)
        def _():
            for start in range(0, count, LANES):
                rows = squares_ref[start : start + LANES, :].T
                sums_ref[:, start : start + LANES] = jnp.sum(rows, 0, keepdims=True)


def add_kernel(
    modes, size, ndoc, nblocks,
    where_ref, lengths_ref, owner_ref,
    base_ref, gate_ref, rates_ref, residues_ref, states_ref,
    out_ref, spare_ref, squares_ref,
    keep_ref, flags_ref, slot_ref,
):
    count, width = base_ref.shape
    chunks = count // CHUNK
    step = step_rates(rates_ref, 0, width, size)
    step_residues = step_rates(residues_ref, 0, width, size)

    @pl.when(pl.program_id(0) == 0)
    def _():
        where = where_ref[0]
        ends = running_ends(lengths_ref, ndoc)
        write_flags(flags_ref, ends, where, count, nblocks)
        write_slots(slot_ref, owner_ref, where, nblocks)
        squares_ref[...] = jnp.zeros_like(squares_ref)
        before = scalar_document(ends, where * count - 1)
        kept = jnp.int32(0)
        for end in reversed(ends):
            kept = jnp.where(end >= where * count, end - where * count, kept)
        kept = jnp.where(before < 0, 0, kept)
        keep_ref[...] = jnp.where(iota((count, LANES), 0) < kept, 1.0, 0.0).astype(F32)

    def tile(lanes):
        rate = tile_rates(step, lanes.start, size)
        scale = tile_rates(step_residues, lanes.start, size) * jnp.sqrt(1.0 - jnp.exp(-2.0 * rate))
        down = iota((CHUNK, LANES), 0)
        entry = (scale.T * jnp.exp(-rate.T * (down + 1).astype(F32))).astype(BF16)
        whole = jnp.exp(-rate * CHUNK)
        state = left_state(states_ref, flags_ref, rate, lanes, modes, size, count)
        held = []
        for _ in range(chunks):
            held.append(state.astype(BF16))
            state = state * whole
        left = jnp.dot(entry, jnp.concatenate(held, 1), preferred_element_type=F32)
        for start in range(0, count, SPAN):
            low = start % CHUNK
            chunk = start // CHUNK
            carried = left[low : low + SPAN, chunk * LANES : (chunk + 1) * LANES] * keep_ref[start : start + SPAN, :]
            gate = gate_ref[start : start + SPAN, lanes].astype(F32)
            summed = base_ref[start : start + SPAN, lanes] + gate * carried
            hand_over(out_ref, squares_ref, slot_ref, summed, start, count // nblocks, lanes)

    each_tile(width, tile)
    spare_ref[...] = out_ref[slot_ref[nblocks]]


def norm_kernel(parts, where_ref, owner_ref, *refs):
    blocks, refs = refs[:parts], refs[parts:]
    spare_ref, gain_ref, out_ref = refs[:3]
    held, (done_ref, in_sems, out_sems) = refs[3 : 3 + parts], refs[3 + parts :]
    nblocks = blocks[0].shape[0]
    rows = out_ref.shape[0] // nblocks
    room = sum(block.shape[1] for block in blocks) - out_ref.shape[1] // LANES * rows

    def fetch(part, i, source):
        return pltpu.make_async_copy(source, held[part].at[i], in_sems.at[part, i])

    for i in range(nblocks):
        ahead = where_ref[0] - owner_ref[i]
        source = jnp.where(ahead < 0, ahead + nblocks, ahead)
        second = is_second(owner_ref, nblocks, i)
        low = 0
        for part in range(parts):
            size = blocks[part].shape[1]

            @pl.when(second)
            def _(part=part, i=i, low=low, size=size):
                fetch(part, i, spare_ref.at[pl.ds(low, size)]).start()

            @pl.when(jnp.logical_not(second))
            def _(part=part, i=i, source=source):
                fetch(part, i, blocks[part].at[source]).start()

            low += size

    def store(i):
        here = pl.ds(i * rows, rows)
        return pltpu.make_async_copy(done_ref.at[here], out_ref.at[here], out_sems.at[i])

    for i in range(nblocks):
        for part in range(parts):
            fetch(part, i, blocks[part].at[0]).wait()
        start = held[-1].shape[1] - room + i // 16 * 16
        halves = held[-1][i, start : start + 16, :].astype(F32)[i % 16 : i % 16 + 1]
        halves = jnp.broadcast_to(halves, (8, LANES))
        scale = halves + pltpu.roll(halves, LANES - rows, 1)
        scale = jnp.broadcast_to(scale[0:1], (LANES, LANES)).T[:rows]
        tile = 0
        for part in range(parts):
            for low in range(0, held[part].shape[1] - (room if part + 1 == parts else 0), rows):
                outs = slice(tile * LANES, (tile + 1) * LANES)
                value = held[part][i, low : low + rows, :].astype(F32)
                done_ref[i * rows : (i + 1) * rows, outs] = (value * scale * gain_ref[:, outs]).astype(BF16)
                tile += 1
        store(i).start()
    for i in range(nblocks):
        store(i).wait()


def params(limit=VMEM_LIMIT):
    return pltpu.CompilerParams(dimension_semantics=("arbitrary",), vmem_limit_bytes=limit)


def in_hbm(*arrays):
    return [pltpu.with_memory_space_constraint(array, pltpu.HBM) for array in arrays]


def in_vmem(array):
    return pltpu.with_memory_space_constraint(array, pltpu.VMEM)


def whole_array(rank):
    return lambda *_: (0,) * rank


def mix(scalars, x, halo, taps, rates, size, ndoc, copies):
    _, count, width = x.shape
    modes = rates.shape[0]
    wide = min(WIDE, width)
    deep = lambda t, *_: (0, 0, t)
    grid_spec = pltpu.PrefetchScalarGridSpec(
        num_scalar_prefetch=2,
        grid=(width // wide,),
        in_specs=[
            pl.BlockSpec((1, count, wide), lambda t, *_: (1, 0, t)),
            pl.BlockSpec((1, count, wide), lambda t, *_: (2, 0, t)),
            pl.BlockSpec((3, HALO, wide), deep),
            pl.BlockSpec((3, SHORT, wide), deep),
            pl.BlockSpec(rates.shape, whole_array(2)),
        ],
        out_specs=[
            pl.BlockSpec((count, wide), lambda t, *_: (0, t)),
            pl.BlockSpec((copies, modes, wide), deep),
        ],
        scratch_shapes=[
            pltpu.VMEM((count // SPAN, (NEAR - 1) * (SPAN + HALO), SPAN + 16), BF16),
            pltpu.VMEM((NEAR, count + 2 * HALO, LANES), F32),
            pltpu.VMEM((8, count), F32),
        ],
    )
    return pl.pallas_call(
        functools.partial(mix_kernel, modes, size, ndoc),
        grid_spec=grid_spec,
        out_shape=[pltpu.HBM((count, width), BF16), pltpu.HBM((copies, modes, width), BF16)],
        compiler_params=params(),
        cost_estimate=pl.CostEstimate(flops=60 * count * width, bytes_accessed=8 * count * width, transcendentals=count * width),
        name="mix",
    )(*scalars[:2], x, x, halo, taps, rates)


def conv(low, share, room, scalars, x, halo, taps, mixed, rates, residues, skip, residual, carried, size, ndoc, nblocks):
    _, count, width = x.shape
    modes = rates.shape[0]
    wide = math.gcd(math.gcd(low, share), WIDE)
    first = low // wide
    tile = lambda t, *_: (0, first + t)
    deep = lambda t, *_: (0, 0, first + t)
    step = pl.BlockSpec(rates.shape, whole_array(2))
    in_specs = [
        pl.BlockSpec((1, count, wide), deep),
        pl.BlockSpec((1, HALO, wide), deep),
        pl.BlockSpec((1, SHORT, wide), deep),
        pl.BlockSpec((count, wide), tile),
        step,
        step,
        pl.BlockSpec((1, wide), tile),
        pl.BlockSpec((count, wide), tile),
    ]
    operands = [x, halo, taps, mixed, rates, residues, skip, residual]
    scratch = [
        pltpu.VMEM((3, count + 2 * HALO, LANES), F32),
        pltpu.VMEM((count // CHUNK, CHUNK, CHUNK), BF16),
        pltpu.VMEM((count // CHUNK, CHUNK, LANES), BF16),
        pltpu.VMEM((count // CHUNK, LANES, CHUNK), F32),
        pltpu.SMEM((2 + count // CHUNK,), jnp.int32),
    ]
    if carried:
        states, squares = carried
        in_specs += [pl.BlockSpec((nblocks, modes, wide), deep), pl.BlockSpec((count, LANES), whole_array(2))]
        operands += [states, squares]
        scratch += [pltpu.SMEM((nblocks + 1,), jnp.int32), pltpu.VMEM((count, LANES), F32)]
        out_specs, out_shape = handed(share, room, wide, count, nblocks)
        out_specs[2] = pl.BlockSpec((1, count), whole_array(2))
        out_shape[2] = jax.ShapeDtypeStruct((1, count), F32)
    else:
        out_specs = [pl.BlockSpec((count, wide), lambda t, *_: (0, t))] * 2
        out_shape = [pltpu.VMEM((count, share), F32), pltpu.VMEM((count, share), BF16)]
    grid_spec = pltpu.PrefetchScalarGridSpec(
        num_scalar_prefetch=3, grid=(share // wide,), in_specs=in_specs, out_specs=out_specs, scratch_shapes=scratch
    )
    return pl.pallas_call(
        functools.partial(conv_kernel, modes, size, ndoc, nblocks, bool(carried), low // size),
        grid_spec=grid_spec,
        out_shape=out_shape,
        compiler_params=params(VMEM_LIMIT if carried else VMEM_LIMIT_BESIDE),
        cost_estimate=pl.CostEstimate(
            flops=2 * 1152 * count * share, bytes_accessed=8 * count * share, transcendentals=count * share
        ),
        name="conv",
    )(*scalars, *in_hbm(*operands))


def handed(share, room, wide, count, nblocks):
    rows = count // nblocks
    specs = [
        pl.BlockSpec((nblocks, wide // LANES * rows, LANES), lambda t, *_: (0, t, 0)),
        pl.BlockSpec((wide // LANES * rows, LANES), lambda t, *_: (t, 0)),
        pl.BlockSpec((count, LANES), whole_array(2)),
    ]
    shapes = [
        pltpu.HBM((nblocks, share // LANES * rows + room, LANES), BF16),
        pltpu.HBM((share // LANES * rows, LANES), BF16),
        pltpu.HBM((count, LANES), F32),
    ]
    return specs, shapes


def add(scalars, base, gate, rates, residues, states, size, ndoc, nblocks):
    count, share = base.shape
    modes = rates.shape[0]
    wide = math.gcd(share, WIDE)
    tile = lambda t, *_: (0, t)
    step = pl.BlockSpec(rates.shape, whole_array(2))
    out_specs, out_shape = handed(share, 0, wide, count, nblocks)
    grid_spec = pltpu.PrefetchScalarGridSpec(
        num_scalar_prefetch=3,
        grid=(share // wide,),
        in_specs=[
            pl.BlockSpec((count, wide), tile),
            pl.BlockSpec((count, wide), tile),
            step,
            step,
            pl.BlockSpec((nblocks, modes, wide), lambda t, *_: (0, 0, t)),
        ],
        out_specs=out_specs,
        scratch_shapes=[
            pltpu.VMEM((count, LANES), F32),
            pltpu.SMEM((2 + count // CHUNK,), jnp.int32),
            pltpu.SMEM((nblocks + 1,), jnp.int32),
        ],
    )
    return pl.pallas_call(
        functools.partial(add_kernel, modes, size, ndoc, nblocks),
        grid_spec=grid_spec,
        out_shape=out_shape,
        compiler_params=params(VMEM_LIMIT_BESIDE),
        cost_estimate=pl.CostEstimate(flops=300 * count * share, bytes_accessed=8 * count * share, transcendentals=count * share),
        name="add",
    )(*scalars, in_vmem(base), in_vmem(gate), *in_hbm(rates, residues, states))


def norm(where, owner, blocks, spare, gain, count):
    width = gain.shape[1]
    nblocks = blocks[0].shape[0]
    smem, vmem, anywhere = (pl.BlockSpec(memory_space=space) for space in (pltpu.SMEM, pltpu.VMEM, pl.ANY))
    return pl.pallas_call(
        functools.partial(norm_kernel, len(blocks)),
        in_specs=[smem, smem] + [anywhere] * (len(blocks) + 1) + [vmem],
        out_specs=anywhere,
        out_shape=jax.ShapeDtypeStruct((count, width), BF16),
        scratch_shapes=[pltpu.VMEM(block.shape, BF16) for block in blocks]
        + [
            pltpu.VMEM((count, width), BF16),
            pltpu.SemaphoreType.DMA((len(blocks), nblocks)),
            pltpu.SemaphoreType.DMA((nblocks,)),
        ],
        compiler_params=pltpu.CompilerParams(vmem_limit_bytes=VMEM_LIMIT),
        cost_estimate=pl.CostEstimate(flops=3 * count * width, bytes_accessed=4 * count * width, transcendentals=0),
        name="norm",
    )(where, owner, *blocks, spare, gain)


def on_device(features, residual, short_taps, rates, residues, skip, gain, lengths, owner):
    count, _, width = features.shape
    size = width // rates.shape[0]
    ndoc = lengths.shape[0]
    nblocks = lax.axis_size("ctx")
    rows = count // nblocks
    where = lax.axis_index("ctx")
    x = jnp.transpose(features, (1, 0, 2))
    pairs = [(i, i + 1) for i in range(nblocks - 1)]
    halo = lax.ppermute(x[:, count - HALO :], "ctx", pairs)

    scalars = (where.reshape(1).astype(jnp.int32), lengths, owner)
    spread = ((0, 0), (0, LANES - rates.shape[0]))
    rates, residues = jnp.pad(rates.T, spread), jnp.pad(residues.T, spread)

    offsets = owner[:nblocks]
    ids = jnp.arange(nblocks, dtype=jnp.int32)
    twice = jnp.any((offsets[:, None] == offsets[None, :]) & (ids[None, :] < ids[:, None]), 1)
    spare_shift = jnp.sum(jnp.where(twice, offsets, 0))

    def exchanged(value):
        return lax.all_to_all(value, "ctx", split_axis=0, concat_axis=0, tiled=True)

    first = width * SPLIT[0] // sum(SPLIT)
    second = width - first
    mixed, copies = mix(scalars, x, halo, short_taps, rates, size, ndoc, nblocks)
    states = exchanged(copies)
    shared = (scalars, x, halo, short_taps, mixed, rates, residues, skip.reshape(1, width), residual)
    base, gate = conv(0, first, 0, *shared, (), size, ndoc, nblocks)
    out, spare, squares = add(scalars, base, gate, rates, residues, states, size, ndoc, nblocks)
    block = exchanged(out)
    room = -(-nblocks // 16) * 16
    out, last_spare, sums = conv(first, second, room, *shared, (states, squares), size, ndoc, nblocks)
    mean = lax.psum(sums, "mp") / (width * lax.axis_size("mp"))
    inverse = lax.rsqrt(mean + EPS)
    high = lax.reduce_precision(inverse, 8, 7)
    halves = jnp.concatenate([high.reshape(nblocks, rows), (inverse - high).reshape(nblocks, rows)], 1)
    halves = jnp.pad(halves, ((0, room - nblocks), (0, LANES - 2 * rows))).astype(BF16)
    table = jnp.broadcast_to(halves[None], (nblocks, room, LANES))
    out = lax.dynamic_update_slice(out, table, (0, second // LANES * rows, 0))
    last_block = exchanged(out)
    spares = jnp.concatenate([spare, last_spare, halves], 0)

    def moved(by):
        return lambda value: lax.ppermute(value, "ctx", [(s, (s + by) % nblocks) for s in range(nblocks)])

    spare = lax.switch(spare_shift, [lambda value: value] + [moved(d) for d in range(1, nblocks)], spares)
    return norm(scalars[0], owner, [block, last_block], spare, gain.reshape(1, width), count)


def solution(mesh):
    return jax.shard_map(
        on_device,
        mesh=mesh,
        in_specs=(
            P("ctx", None, "mp"),
            P("ctx", "mp"),
            P(None, None, "mp"),
            P("mp", None),
            P("mp", None),
            P("mp"),
            P("mp"),
            P(),
            P(),
        ),
        out_specs=P("ctx", "mp"),
        check_vma=False,
    )
```

```python
import functools
import math

import jax
import jax.numpy as jnp
from jax import lax
from jax.experimental import pallas as pl
from jax.experimental.pallas import tpu as pltpu
from jax.sharding import PartitionSpec as P

SHORT = 7
LANES = 128
CHUNK = 128
HALO = 8
EPS = 1e-06
SPLIT = (4, 4)
NEAR = 4
WIDE = 512
SPAN = 64
F32 = jnp.float32
BF16 = jnp.bfloat16
VMEM_LIMIT = 64 * 1024 * 1024
VMEM_LIMIT_BESIDE = 56 * 1024 * 1024


def iota(shape, dim):
    return lax.broadcasted_iota(jnp.int32, shape, dim)


def document(ends, positions):
    total = jnp.zeros(positions.shape, jnp.int32)
    for end in ends:
        total = total + (positions >= end).astype(jnp.int32)
    return total


def scalar_document(ends, position):
    total = jnp.int32(0)
    for end in ends:
        total = total + (position >= end).astype(jnp.int32)
    return jnp.where(position < 0, -1, total)


def running_ends(lengths_ref, ndoc):
    ends, total = [], jnp.int32(0)
    for j in range(ndoc):
        total = total + lengths_ref[j]
        ends.append(total)
    return ends


def write_lag_masks(mask_ref, ends, base, count):
    mask_ref[...] = jnp.ones_like(mask_ref)
    gap = jnp.zeros((1, LANES), F32)
    for end in ends:
        row = end - base + HALO

        @pl.when((row >= 0) & (row < count + HALO))
        def _(row=row):
            for lag in (1, 2, 3):
                for past in range(lag):
                    mask_ref[lag - 1, pl.ds(row + past, 1), :] = gap


def row_documents(ends, base, count):
    return document(ends, base + iota((8, count), 1)).astype(F32)


def is_second(owner_ref, nblocks, i):
    found = jnp.bool_(False)
    for j in range(i):
        found = found | (owner_ref[j] == owner_ref[i])
    return found


def write_slots(slot_ref, owner_ref, where, nblocks):
    unused = jnp.int32(nblocks * (nblocks - 1) // 2)
    seconds = [is_second(owner_ref, nblocks, i) for i in range(nblocks)]
    mine = [owner_ref[where * nblocks + i] for i in range(nblocks)]
    for i in range(nblocks):
        unused = unused - jnp.where(seconds[i], 0, mine[i])
    for i in range(nblocks):
        slot_ref[i] = jnp.where(seconds[i], unused, mine[i])
    slot_ref[nblocks] = unused


def step_rates(ref, origin, wide, size):
    first = origin + pl.program_id(0) * (wide // size)
    return pltpu.roll(ref[...], jnp.where(first == 0, 0, LANES - first), 1)


def tile_rates(rates, low, size):
    first = low // size
    columns = [rates[:, first + g : first + g + 1] for g in range(LANES // size)]
    return jnp.concatenate([jnp.broadcast_to(column, (column.shape[0], LANES)) for column in columns], 0)


def short_conv(ext, taps, masks):
    def back(value, lag):
        return pltpu.roll(value, lag, 0) * masks[lag - 1]

    one, two = back(ext, 1), back(ext, 2)
    far = ext * taps[6]
    middle = ext * taps[3] + one * taps[4] + two * taps[5] + back(far, 3)
    near = ext * taps[0] + one * taps[1] + two * taps[2] + back(middle, 3)
    return near[HALO:]


def extended(x_ref, halo_ref, which, start, lanes):
    rows = x_ref[0, start : start + SPAN, lanes].astype(F32)
    if start == 0:
        ahead = halo_ref[which, :, lanes].astype(F32)
    else:
        ahead = x_ref[0, start - 16 : start, lanes].astype(F32)[16 - HALO :]
    return jnp.concatenate([ahead, rows], 0)


def tap_rows(taps_ref, which, lanes):
    return [taps_ref[which, j : j + 1, lanes] for j in range(SHORT)]


def lag_masks(mask_ref, start):
    return [mask_ref[l, start : start + SPAN + HALO, :] for l in range(3)]


def group_mask(modes, size):
    return (iota((LANES, LANES), 0) // modes) == (iota((LANES, LANES), 1) // size)


def each_tile(width, body):
    for low in range(0, width, LANES):
        body(slice(low, low + LANES))


def write_shifts(shift_ref, mask_ref, ends, base, count):
    mask_ref[...] = jnp.ones_like(mask_ref)
    gap = jnp.zeros((1, LANES), F32)
    for end in ends:
        row = end - base + HALO

        @pl.when((row >= 0) & (row < count + HALO))
        def _(row=row):
            for lag in range(1, NEAR + 1):
                for past in range(lag):
                    mask_ref[lag - 1, pl.ds(row + past, 1), :] = gap

    reach = SPAN + HALO
    back = iota((reach, SPAN + 16), 0) + HALO - iota((reach, SPAN + 16), 1)
    for span in range(count // SPAN):
        moves = []
        for lag in range(1, NEAR):
            mask = mask_ref[lag - 1, span * SPAN : span * SPAN + reach, : SPAN + 16]
            moves.append(jnp.where(back == lag, mask, 0.0))
        shift_ref[span] = jnp.concatenate(moves, 0).astype(BF16)


def mix_kernel(
    modes, size, ndoc,
    where_ref, lengths_ref,
    x_ref, halo_ref, taps_ref, rates_ref,
    mixed_ref, state_ref,
    shift_ref, mask_ref, tail_ref, held_ref, sems,
):
    count, width = mixed_ref.shape
    chunks = count // CHUNK
    reach = SPAN + HALO
    step = step_rates(rates_ref, 0, width, size)
    turn = pl.program_id(0)
    slot = lax.rem(turn, 2)

    def fetches(turn):
        lanes = pl.ds(pl.multiple_of(turn * width, LANES), width)
        slot = lax.rem(turn, 2)
        return [
            pltpu.make_async_copy(x_ref.at[which, :, lanes], held_ref.at[slot, which - 1], sems.at[slot, which - 1])
            for which in (1, 2)
        ]

    @pl.when(turn == 0)
    def _():
        for copy in fetches(turn):
            copy.start()
        base = where_ref[0] * count
        ends = running_ends(lengths_ref, ndoc)
        write_shifts(shift_ref, mask_ref, ends, base, count)
        last = scalar_document(ends, base + count - 1).astype(F32)
        tail_ref[...] = jnp.where(row_documents(ends, base, count) == last, 1.0, 0.0).astype(F32)

    @pl.when(turn + 1 < pl.num_programs(0))
    def _():
        for copy in fetches(turn + 1):
            copy.start()

    for copy in fetches(turn):
        copy.wait()

    def window(which, start, lanes):
        if start == 0:
            halo = halo_ref[which, :, lanes].astype(F32)
            ahead = jnp.concatenate([jnp.zeros((16 - HALO, LANES), F32), halo], 0).astype(BF16)
        else:
            ahead = held_ref[slot, which - 1, start - 16 : start, lanes]
        return jnp.concatenate([ahead, held_ref[slot, which - 1, start : start + SPAN, lanes]], 0)

    def finish(here, moved, taps, apart):
        rows = [here] + [moved[lag * reach : (lag + 1) * reach] for lag in range(NEAR - 1)]
        far = sum(rows[lag] * taps[NEAR + lag] for lag in range(SHORT - NEAR))
        far = pltpu.roll(far, NEAR, 0)[HALO:] * apart
        return far + sum(row[HALO:] * taps[lag] for lag, row in enumerate(rows))

    def tile(lanes):
        key_taps, value_taps = tap_rows(taps_ref, 1, lanes), tap_rows(taps_ref, 2, lanes)
        for start in range(0, count, SPAN):
            keys, values = window(1, start, lanes), window(2, start, lanes)
            moved = jnp.dot(shift_ref[start // SPAN], jnp.concatenate([keys, values], 1), preferred_element_type=F32)
            apart = mask_ref[NEAR - 1, HALO + start : HALO + start + SPAN, :]
            key = finish(keys.astype(F32)[16 - HALO :], moved[:, :LANES], key_taps, apart)
            value = finish(values.astype(F32)[16 - HALO :], moved[:, LANES:], value_taps, apart)
            mixed_ref[start : start + SPAN, lanes] = (key * value).astype(BF16)
        rate = tile_rates(step, lanes.start, size)
        leave = jnp.exp(-rate * (CHUNK - 1 - iota((LANES, CHUNK), 1)).astype(F32))
        whole = jnp.exp(-rate * CHUNK)
        spans = []
        for chunk in reversed(range(chunks)):
            tail = tail_ref[0:1, chunk * CHUNK : (chunk + 1) * CHUNK]
            spans.append((leave * tail).astype(BF16))
            leave = leave * whole
        full = jnp.dot(jnp.concatenate(spans[::-1], 1), mixed_ref[:, lanes], preferred_element_type=F32)
        full = jnp.where(group_mask(modes, size), full, 0.0)
        state = jnp.sum(full.reshape(LANES // modes, modes, LANES), 0).astype(BF16)
        for owner in range(state_ref.shape[0]):
            state_ref[owner, :, lanes] = state

    each_tile(width, tile)


def left_state(states_ref, flags_ref, rate, lanes, modes, size, count):
    inside = group_mask(modes, size)
    decay = jnp.exp(-rate * count)
    total = jnp.zeros((LANES, LANES), F32)
    for back in range(states_ref.shape[0] // 2, 0, -1):
        v = flags_ref[1] - back
        piece = jnp.concatenate([states_ref[jnp.maximum(v, 0), :, lanes].astype(F32)] * (LANES // modes), 0)
        total = jnp.where(inside & (v >= flags_ref[0]), piece + decay * total, 0.0)
    return total


def write_flags(flags_ref, ends, where, count, nblocks):
    before = scalar_document(ends, where * count - 1)
    first = jnp.int32(0)
    for v in range(nblocks):
        first = first + (scalar_document(ends, (v + 1) * count - 1) < before).astype(jnp.int32)
    flags_ref[0] = first
    flags_ref[1] = where
    for chunk in range(count // CHUNK):
        start = where * count + chunk * CHUNK
        held = scalar_document(ends, start - 1) == scalar_document(ends, start + CHUNK - 1)
        flags_ref[2 + chunk] = held.astype(jnp.int32)


def hand_over(out_ref, squares_ref, slot_ref, summed, start, rows, lanes):
    squares_ref[start : start + SPAN, :] += summed * summed
    rounded = summed.astype(BF16)
    for b in range(SPAN // rows):
        tile = lanes.start // LANES * rows
        out_ref[slot_ref[start // rows + b], tile : tile + rows, :] = rounded[b * rows : (b + 1) * rows]


def conv_kernel(modes, size, ndoc, nblocks, carried, origin, where_ref, lengths_ref, owner_ref, *refs):
    x_ref, halo_ref, taps_ref, mixed_ref, rates_ref, residues_ref, skip_ref, residual_ref = refs[:8]
    refs = refs[8:]
    if carried:
        states_ref, before_ref, out_ref, spare_ref, sums_ref = refs[:5]
        refs = refs[5:]
    else:
        base_ref, gate_ref = refs[:2]
        refs = refs[2:]
    mask_ref, same_ref, keep_ref, tail_ref, flags_ref = refs[:5]
    if carried:
        slot_ref, squares_ref = refs[5:]
    count, width = mixed_ref.shape
    chunks = count // CHUNK
    step = step_rates(rates_ref, origin, width, size)
    step_residues = step_rates(residues_ref, origin, width, size)

    @pl.when(pl.program_id(0) == 0)
    def _():
        where = where_ref[0]
        base = where * count
        ends = running_ends(lengths_ref, ndoc)
        write_lag_masks(mask_ref, ends, base, count)
        write_flags(flags_ref, ends, where, count, nblocks)
        if carried:
            write_slots(slot_ref, owner_ref, where, nblocks)
            squares_ref[...] = before_ref[...]
        documents = row_documents(ends, base, count)
        causal = iota((CHUNK, CHUNK), 1) <= iota((CHUNK, CHUNK), 0)
        for chunk in range(chunks):
            start = base + chunk * CHUNK
            there = jnp.broadcast_to(documents[0:1, chunk * CHUNK : (chunk + 1) * CHUNK], (CHUNK, CHUNK))
            here = there.T
            same_ref[chunk] = jnp.where((here == there) & causal, 1.0, 0.0).astype(BF16)
            before = scalar_document(ends, start - 1).astype(F32)
            keep_ref[chunk] = jnp.where(here == before, 1.0, 0.0).astype(BF16)
            last = scalar_document(ends, start + CHUNK - 1).astype(F32)
            tail_ref[chunk] = jnp.where(there == last, 1.0, 0.0).astype(F32)

    groups = LANES // modes

    def tile(lanes):
        rate = tile_rates(step, lanes.start, size)
        scale = tile_rates(step_residues, lanes.start, size) * jnp.sqrt(1.0 - jnp.exp(-2.0 * rate))
        down = iota((CHUNK, LANES), 0)
        along = iota((LANES, CHUNK), 1)
        entry = (scale.T * jnp.exp(-rate.T * (down + 1).astype(F32))).astype(BF16)
        leave = jnp.exp(-rate * (CHUNK - 1 - along).astype(F32))
        whole = jnp.exp(-rate * CHUNK)
        terms = scale * jnp.where(along == 0, 1.0, leave * jnp.exp(-rate))
        toeplitz = []
        for g in range(groups):
            line = jnp.sum(terms[g * modes : (g + 1) * modes], 0, keepdims=True)
            top = pltpu.roll(jnp.broadcast_to(line, (8, CHUNK)), 0, 1, stride=1, stride_axis=0)
            parts = [top] + [pltpu.roll(top, 8 * k, 1) for k in range(1, CHUNK // 8)]
            toeplitz.append(jnp.concatenate(parts, 0).astype(BF16))
        inside = group_mask(modes, size)
        state = left_state(states_ref, flags_ref, rate, lanes, modes, size, count) if carried else None
        taps = tap_rows(taps_ref, 0, lanes)
        skip = skip_ref[:, lanes]
        lane_group = iota((CHUNK, LANES), 1) // size
        for chunk in range(chunks):
            start = chunk * CHUNK
            mixed = mixed_ref[start : start + CHUNK, lanes]
            same = same_ref[chunk]
            left = [t * same for t in toeplitz]
            right = [jnp.where(lane_group == g, mixed, jnp.zeros_like(mixed)) for g in range(groups)]
            if state is not None:
                left.append(entry * keep_ref[chunk])
                right.append(state.astype(BF16))
            longer = jnp.dot(jnp.concatenate(left, 1), jnp.concatenate(right, 0), preferred_element_type=F32)
            if chunk + 1 < chunks:
                fresh = jnp.dot((leave * tail_ref[chunk]).astype(BF16), mixed, preferred_element_type=F32)
                held = flags_ref[2 + chunk] == 1
                fresh = jnp.where(inside, fresh, 0.0)
                state = fresh if state is None else jnp.where(held, whole * state, 0.0) + fresh
            body = longer + skip * mixed.astype(F32)
            for half in range(start, start + CHUNK, SPAN):
                gate = short_conv(extended(x_ref, halo_ref, 0, half, lanes), taps, lag_masks(mask_ref, half))
                inner = body[half - start : half - start + SPAN]
                summed = residual_ref[half : half + SPAN, lanes].astype(F32) + gate * inner
                if carried:
                    hand_over(out_ref, squares_ref, slot_ref, summed, half, count // nblocks, lanes)
                else:
                    base_ref[half : half + SPAN, lanes] = summed
                    gate_ref[half : half + SPAN, lanes] = gate.astype(BF16)

    each_tile(width, tile)
    if carried:
        spare_ref[...] = out_ref[slot_ref[nblocks]]

        @pl.when(pl.program_id(0) == pl.num_programs(0) - 1)
        def _():
            for start in range(0, count, LANES):
                rows = squares_ref[start : start + LANES, :].T
                sums_ref[:, start : start + LANES] = jnp.sum(rows, 0, keepdims=True)


def add_kernel(
    modes, size, ndoc, nblocks,
    where_ref, lengths_ref, owner_ref,
    base_ref, gate_ref, rates_ref, residues_ref, states_ref,
    out_ref, spare_ref, squares_ref,
    keep_ref, flags_ref, slot_ref,
):
    count, width = base_ref.shape
    chunks = count // CHUNK
    step = step_rates(rates_ref, 0, width, size)
    step_residues = step_rates(residues_ref, 0, width, size)

    @pl.when(pl.program_id(0) == 0)
    def _():
        where = where_ref[0]
        ends = running_ends(lengths_ref, ndoc)
        write_flags(flags_ref, ends, where, count, nblocks)
        write_slots(slot_ref, owner_ref, where, nblocks)
        squares_ref[...] = jnp.zeros_like(squares_ref)
        before = scalar_document(ends, where * count - 1)
        kept = jnp.int32(0)
        for end in reversed(ends):
            kept = jnp.where(end >= where * count, end - where * count, kept)
        kept = jnp.where(before < 0, 0, kept)
        keep_ref[...] = jnp.where(iota((count, LANES), 0) < kept, 1.0, 0.0).astype(F32)

    def tile(lanes):
        rate = tile_rates(step, lanes.start, size)
        scale = tile_rates(step_residues, lanes.start, size) * jnp.sqrt(1.0 - jnp.exp(-2.0 * rate))
        down = iota((CHUNK, LANES), 0)
        entry = (scale.T * jnp.exp(-rate.T * (down + 1).astype(F32))).astype(BF16)
        whole = jnp.exp(-rate * CHUNK)
        state = left_state(states_ref, flags_ref, rate, lanes, modes, size, count)
        held = []
        for _ in range(chunks):
            held.append(state.astype(BF16))
            state = state * whole
        left = jnp.dot(entry, jnp.concatenate(held, 1), preferred_element_type=F32)
        for start in range(0, count, SPAN):
            low = start % CHUNK
            chunk = start // CHUNK
            carried = left[low : low + SPAN, chunk * LANES : (chunk + 1) * LANES] * keep_ref[start : start + SPAN, :]
            gate = gate_ref[start : start + SPAN, lanes].astype(F32)
            summed = base_ref[start : start + SPAN, lanes] + gate * carried
            hand_over(out_ref, squares_ref, slot_ref, summed, start, count // nblocks, lanes)

    each_tile(width, tile)
    spare_ref[...] = out_ref[slot_ref[nblocks]]


def norm_kernel(parts, where_ref, owner_ref, *refs):
    blocks, refs = refs[:parts], refs[parts:]
    spare_ref, gain_ref, out_ref = refs[:3]
    held, (done_ref, in_sems, out_sems) = refs[3 : 3 + parts], refs[3 + parts :]
    nblocks = blocks[0].shape[0]
    rows = out_ref.shape[0] // nblocks
    room = sum(block.shape[1] for block in blocks) - out_ref.shape[1] // LANES * rows

    def fetch(part, i, source):
        return pltpu.make_async_copy(source, held[part].at[i], in_sems.at[part, i])

    for i in range(nblocks):
        ahead = where_ref[0] - owner_ref[i]
        source = jnp.where(ahead < 0, ahead + nblocks, ahead)
        second = is_second(owner_ref, nblocks, i)
        low = 0
        for part in range(parts):
            size = blocks[part].shape[1]

            @pl.when(second)
            def _(part=part, i=i, low=low, size=size):
                fetch(part, i, spare_ref.at[pl.ds(low, size)]).start()

            @pl.when(jnp.logical_not(second))
            def _(part=part, i=i, source=source):
                fetch(part, i, blocks[part].at[source]).start()

            low += size

    def store(i):
        here = pl.ds(i * rows, rows)
        return pltpu.make_async_copy(done_ref.at[here], out_ref.at[here], out_sems.at[i])

    for i in range(nblocks):
        for part in range(parts):
            fetch(part, i, blocks[part].at[0]).wait()
        start = held[-1].shape[1] - room + i // 16 * 16
        halves = held[-1][i, start : start + 16, :].astype(F32)[i % 16 : i % 16 + 1]
        halves = jnp.broadcast_to(halves, (8, LANES))
        scale = halves + pltpu.roll(halves, LANES - rows, 1)
        scale = jnp.broadcast_to(scale[0:1], (LANES, LANES)).T[:rows]
        tile = 0
        for part in range(parts):
            for low in range(0, held[part].shape[1] - (room if part + 1 == parts else 0), rows):
                outs = slice(tile * LANES, (tile + 1) * LANES)
                value = held[part][i, low : low + rows, :].astype(F32)
                done_ref[i * rows : (i + 1) * rows, outs] = (value * scale * gain_ref[:, outs]).astype(BF16)
                tile += 1
        store(i).start()
    for i in range(nblocks):
        store(i).wait()


def params(limit=VMEM_LIMIT):
    return pltpu.CompilerParams(dimension_semantics=("arbitrary",), vmem_limit_bytes=limit)


def in_hbm(*arrays):
    return [pltpu.with_memory_space_constraint(array, pltpu.HBM) for array in arrays]


def in_vmem(array):
    return pltpu.with_memory_space_constraint(array, pltpu.VMEM)


def whole_array(rank):
    return lambda *_: (0,) * rank


def mix(scalars, x, halo, taps, rates, size, ndoc, copies):
    _, count, width = x.shape
    modes = rates.shape[0]
    wide = min(WIDE, width)
    deep = lambda t, *_: (0, 0, t)
    grid_spec = pltpu.PrefetchScalarGridSpec(
        num_scalar_prefetch=2,
        grid=(width // wide,),
        in_specs=[
            pl.BlockSpec(memory_space=pl.ANY),
            pl.BlockSpec((3, HALO, wide), deep),
            pl.BlockSpec((3, SHORT, wide), deep),
            pl.BlockSpec(rates.shape, whole_array(2)),
        ],
        out_specs=[
            pl.BlockSpec((count, wide), lambda t, *_: (0, t)),
            pl.BlockSpec((copies, modes, wide), deep),
        ],
        scratch_shapes=[
            pltpu.VMEM((count // SPAN, (NEAR - 1) * (SPAN + HALO), SPAN + 16), BF16),
            pltpu.VMEM((NEAR, count + 2 * HALO, LANES), F32),
            pltpu.VMEM((8, count), F32),
            pltpu.VMEM((2, 2, count, wide), BF16),
            pltpu.SemaphoreType.DMA((2, 2)),
        ],
    )
    return pl.pallas_call(
        functools.partial(mix_kernel, modes, size, ndoc),
        grid_spec=grid_spec,
        out_shape=[pltpu.HBM((count, width), BF16), pltpu.HBM((copies, modes, width), BF16)],
        compiler_params=params(),
        cost_estimate=pl.CostEstimate(flops=60 * count * width, bytes_accessed=8 * count * width, transcendentals=count * width),
        name="mix",
    )(*scalars[:2], x, halo, taps, rates)


def conv(low, share, room, scalars, x, halo, taps, mixed, rates, residues, skip, residual, carried, size, ndoc, nblocks):
    _, count, width = x.shape
    modes = rates.shape[0]
    wide = math.gcd(math.gcd(low, share), WIDE)
    first = low // wide
    tile = lambda t, *_: (0, first + t)
    deep = lambda t, *_: (0, 0, first + t)
    step = pl.BlockSpec(rates.shape, whole_array(2))
    in_specs = [
        pl.BlockSpec((1, count, wide), deep),
        pl.BlockSpec((1, HALO, wide), deep),
        pl.BlockSpec((1, SHORT, wide), deep),
        pl.BlockSpec((count, wide), tile),
        step,
        step,
        pl.BlockSpec((1, wide), tile),
        pl.BlockSpec((count, wide), tile),
    ]
    operands = [x, halo, taps, mixed, rates, residues, skip, residual]
    scratch = [
        pltpu.VMEM((3, count + 2 * HALO, LANES), F32),
        pltpu.VMEM((count // CHUNK, CHUNK, CHUNK), BF16),
        pltpu.VMEM((count // CHUNK, CHUNK, LANES), BF16),
        pltpu.VMEM((count // CHUNK, LANES, CHUNK), F32),
        pltpu.SMEM((2 + count // CHUNK,), jnp.int32),
    ]
    if carried:
        states, squares = carried
        in_specs += [pl.BlockSpec((nblocks, modes, wide), deep), pl.BlockSpec((count, LANES), whole_array(2))]
        operands += [states, squares]
        scratch += [pltpu.SMEM((nblocks + 1,), jnp.int32), pltpu.VMEM((count, LANES), F32)]
        out_specs, out_shape = handed(share, room, wide, count, nblocks)
        out_specs[2] = pl.BlockSpec((1, count), whole_array(2))
        out_shape[2] = jax.ShapeDtypeStruct((1, count), F32)
    else:
        out_specs = [pl.BlockSpec((count, wide), lambda t, *_: (0, t))] * 2
        out_shape = [pltpu.VMEM((count, share), F32), pltpu.VMEM((count, share), BF16)]
    grid_spec = pltpu.PrefetchScalarGridSpec(
        num_scalar_prefetch=3, grid=(share // wide,), in_specs=in_specs, out_specs=out_specs, scratch_shapes=scratch
    )
    return pl.pallas_call(
        functools.partial(conv_kernel, modes, size, ndoc, nblocks, bool(carried), low // size),
        grid_spec=grid_spec,
        out_shape=out_shape,
        compiler_params=params(VMEM_LIMIT if carried else VMEM_LIMIT_BESIDE),
        cost_estimate=pl.CostEstimate(
            flops=2 * 1152 * count * share, bytes_accessed=8 * count * share, transcendentals=count * share
        ),
        name="conv",
    )(*scalars, *in_hbm(*operands))


def handed(share, room, wide, count, nblocks):
    rows = count // nblocks
    specs = [
        pl.BlockSpec((nblocks, wide // LANES * rows, LANES), lambda t, *_: (0, t, 0)),
        pl.BlockSpec((wide // LANES * rows, LANES), lambda t, *_: (t, 0)),
        pl.BlockSpec((count, LANES), whole_array(2)),
    ]
    shapes = [
        pltpu.HBM((nblocks, share // LANES * rows + room, LANES), BF16),
        pltpu.HBM((share // LANES * rows, LANES), BF16),
        pltpu.HBM((count, LANES), F32),
    ]
    return specs, shapes


def add(scalars, base, gate, rates, residues, states, size, ndoc, nblocks):
    count, share = base.shape
    modes = rates.shape[0]
    wide = math.gcd(share, WIDE)
    tile = lambda t, *_: (0, t)
    step = pl.BlockSpec(rates.shape, whole_array(2))
    out_specs, out_shape = handed(share, 0, wide, count, nblocks)
    grid_spec = pltpu.PrefetchScalarGridSpec(
        num_scalar_prefetch=3,
        grid=(share // wide,),
        in_specs=[
            pl.BlockSpec((count, wide), tile),
            pl.BlockSpec((count, wide), tile),
            step,
            step,
            pl.BlockSpec((nblocks, modes, wide), lambda t, *_: (0, 0, t)),
        ],
        out_specs=out_specs,
        scratch_shapes=[
            pltpu.VMEM((count, LANES), F32),
            pltpu.SMEM((2 + count // CHUNK,), jnp.int32),
            pltpu.SMEM((nblocks + 1,), jnp.int32),
        ],
    )
    return pl.pallas_call(
        functools.partial(add_kernel, modes, size, ndoc, nblocks),
        grid_spec=grid_spec,
        out_shape=out_shape,
        compiler_params=params(VMEM_LIMIT_BESIDE),
        cost_estimate=pl.CostEstimate(flops=300 * count * share, bytes_accessed=8 * count * share, transcendentals=count * share),
        name="add",
    )(*scalars, in_vmem(base), in_vmem(gate), *in_hbm(rates, residues, states))


def norm(where, owner, blocks, spare, gain, count):
    width = gain.shape[1]
    nblocks = blocks[0].shape[0]
    smem, vmem, anywhere = (pl.BlockSpec(memory_space=space) for space in (pltpu.SMEM, pltpu.VMEM, pl.ANY))
    return pl.pallas_call(
        functools.partial(norm_kernel, len(blocks)),
        in_specs=[smem, smem] + [anywhere] * (len(blocks) + 1) + [vmem],
        out_specs=anywhere,
        out_shape=jax.ShapeDtypeStruct((count, width), BF16),
        scratch_shapes=[pltpu.VMEM(block.shape, BF16) for block in blocks]
        + [
            pltpu.VMEM((count, width), BF16),
            pltpu.SemaphoreType.DMA((len(blocks), nblocks)),
            pltpu.SemaphoreType.DMA((nblocks,)),
        ],
        compiler_params=pltpu.CompilerParams(vmem_limit_bytes=VMEM_LIMIT),
        cost_estimate=pl.CostEstimate(flops=3 * count * width, bytes_accessed=4 * count * width, transcendentals=0),
        name="norm",
    )(where, owner, *blocks, spare, gain)


def on_device(features, residual, short_taps, rates, residues, skip, gain, lengths, owner):
    count, _, width = features.shape
    size = width // rates.shape[0]
    ndoc = lengths.shape[0]
    nblocks = lax.axis_size("ctx")
    rows = count // nblocks
    where = lax.axis_index("ctx")
    x = jnp.transpose(features, (1, 0, 2))
    pairs = [(i, i + 1) for i in range(nblocks - 1)]
    halo = lax.ppermute(x[:, count - HALO :], "ctx", pairs)

    scalars = (where.reshape(1).astype(jnp.int32), lengths, owner)
    spread = ((0, 0), (0, LANES - rates.shape[0]))
    rates, residues = jnp.pad(rates.T, spread), jnp.pad(residues.T, spread)

    offsets = owner[:nblocks]
    ids = jnp.arange(nblocks, dtype=jnp.int32)
    twice = jnp.any((offsets[:, None] == offsets[None, :]) & (ids[None, :] < ids[:, None]), 1)
    spare_shift = jnp.sum(jnp.where(twice, offsets, 0))

    def exchanged(value):
        return lax.all_to_all(value, "ctx", split_axis=0, concat_axis=0, tiled=True)

    first = width * SPLIT[0] // sum(SPLIT)
    second = width - first
    mixed, copies = mix(scalars, x, halo, short_taps, rates, size, ndoc, nblocks)
    states = exchanged(copies)
    shared = (scalars, x, halo, short_taps, mixed, rates, residues, skip.reshape(1, width), residual)
    base, gate = conv(0, first, 0, *shared, (), size, ndoc, nblocks)
    out, spare, squares = add(scalars, base, gate, rates, residues, states, size, ndoc, nblocks)
    block = exchanged(out)
    room = -(-nblocks // 16) * 16
    out, last_spare, sums = conv(first, second, room, *shared, (states, squares), size, ndoc, nblocks)
    mean = lax.psum(sums, "mp") / (width * lax.axis_size("mp"))
    inverse = lax.rsqrt(mean + EPS)
    high = lax.reduce_precision(inverse, 8, 7)
    halves = jnp.concatenate([high.reshape(nblocks, rows), (inverse - high).reshape(nblocks, rows)], 1)
    halves = jnp.pad(halves, ((0, room - nblocks), (0, LANES - 2 * rows))).astype(BF16)
    table = jnp.broadcast_to(halves[None], (nblocks, room, LANES))
    out = lax.dynamic_update_slice(out, table, (0, second // LANES * rows, 0))
    spares = jnp.concatenate([spare, last_spare, halves], 0)
    out, spares, spare_shift = lax.optimization_barrier((out, spares, spare_shift))
    last_block = exchanged(out)

    def moved(by):
        return lambda value: lax.ppermute(value, "ctx", [(s, (s + by) % nblocks) for s in range(nblocks)])

    spare = lax.switch(spare_shift, [lambda value: value] + [moved(d) for d in range(1, nblocks)], spares)
    return norm(scalars[0], owner, [block, last_block], spare, gain.reshape(1, width), count)


def solution(mesh):
    return jax.shard_map(
        on_device,
        mesh=mesh,
        in_specs=(
            P("ctx", None, "mp"),
            P("ctx", "mp"),
            P(None, None, "mp"),
            P("mp", None),
            P("mp", None),
            P("mp"),
            P("mp"),
            P(),
            P(),
        ),
        out_specs=P("ctx", "mp"),
        check_vma=False,
    )
```

```python
import functools
import math

import jax
import jax.numpy as jnp
from jax import lax
from jax.experimental import pallas as pl
from jax.experimental.pallas import tpu as pltpu
from jax.sharding import PartitionSpec as P

SHORT = 7
LANES = 128
CHUNK = 128
HALO = 8
EPS = 1e-06
SPLIT = (4, 4)
NEAR = 4
WIDE = 512
SPAN = 64
F32 = jnp.float32
BF16 = jnp.bfloat16
VMEM_LIMIT = 64 * 1024 * 1024
VMEM_LIMIT_BESIDE = 56 * 1024 * 1024


def iota(shape, dim):
    return lax.broadcasted_iota(jnp.int32, shape, dim)


def document(ends, positions):
    total = jnp.zeros(positions.shape, jnp.int32)
    for end in ends:
        total = total + (positions >= end).astype(jnp.int32)
    return total


def scalar_document(ends, position):
    total = jnp.int32(0)
    for end in ends:
        total = total + (position >= end).astype(jnp.int32)
    return jnp.where(position < 0, -1, total)


def running_ends(lengths_ref, ndoc):
    ends, total = [], jnp.int32(0)
    for j in range(ndoc):
        total = total + lengths_ref[j]
        ends.append(total)
    return ends


def write_lag_masks(mask_ref, ends, base, count):
    mask_ref[...] = jnp.ones_like(mask_ref)
    gap = jnp.zeros((1, LANES), F32)
    for end in ends:
        row = end - base + HALO

        @pl.when((row >= 0) & (row < count + HALO))
        def _(row=row):
            for lag in (1, 2, 3):
                for past in range(lag):
                    mask_ref[lag - 1, pl.ds(row + past, 1), :] = gap


def row_documents(ends, base, count):
    return document(ends, base + iota((8, count), 1)).astype(F32)


def is_second(owner_ref, nblocks, i):
    found = jnp.bool_(False)
    for j in range(i):
        found = found | (owner_ref[j] == owner_ref[i])
    return found


def write_slots(slot_ref, owner_ref, where, nblocks):
    unused = jnp.int32(nblocks * (nblocks - 1) // 2)
    seconds = [is_second(owner_ref, nblocks, i) for i in range(nblocks)]
    mine = [owner_ref[where * nblocks + i] for i in range(nblocks)]
    for i in range(nblocks):
        unused = unused - jnp.where(seconds[i], 0, mine[i])
    for i in range(nblocks):
        slot_ref[i] = jnp.where(seconds[i], unused, mine[i])
    slot_ref[nblocks] = unused


def step_rates(ref, origin, wide, size):
    first = origin + pl.program_id(0) * (wide // size)
    return pltpu.roll(ref[...], jnp.where(first == 0, 0, LANES - first), 1)


def tile_rates(rates, low, size):
    first = low // size
    columns = [rates[:, first + g : first + g + 1] for g in range(LANES // size)]
    return jnp.concatenate([jnp.broadcast_to(column, (column.shape[0], LANES)) for column in columns], 0)


def short_conv(ext, taps, masks):
    def back(value, lag):
        return pltpu.roll(value, lag, 0) * masks[lag - 1]

    one, two = back(ext, 1), back(ext, 2)
    far = ext * taps[6]
    middle = ext * taps[3] + one * taps[4] + two * taps[5] + back(far, 3)
    near = ext * taps[0] + one * taps[1] + two * taps[2] + back(middle, 3)
    return near[HALO:]


def extended(x_ref, halo_ref, which, start, lanes):
    rows = x_ref[0, start : start + SPAN, lanes].astype(F32)
    if start == 0:
        ahead = halo_ref[which, :, lanes].astype(F32)
    else:
        ahead = x_ref[0, start - 16 : start, lanes].astype(F32)[16 - HALO :]
    return jnp.concatenate([ahead, rows], 0)


def tap_rows(taps_ref, which, lanes):
    return [taps_ref[which, j : j + 1, lanes] for j in range(SHORT)]


def lag_masks(mask_ref, start):
    return [mask_ref[l, start : start + SPAN + HALO, :] for l in range(3)]


def group_mask(modes, size):
    return (iota((LANES, LANES), 0) // modes) == (iota((LANES, LANES), 1) // size)


def each_tile(width, body):
    for low in range(0, width, LANES):
        body(slice(low, low + LANES))


def write_shifts(shift_ref, mask_ref, ends, base, count):
    mask_ref[...] = jnp.ones_like(mask_ref)
    gap = jnp.zeros((1, LANES), F32)
    for end in ends:
        row = end - base + HALO

        @pl.when((row >= 0) & (row < count + HALO))
        def _(row=row):
            for lag in range(1, NEAR + 1):
                for past in range(lag):
                    mask_ref[lag - 1, pl.ds(row + past, 1), :] = gap

    reach = SPAN + HALO
    back = iota((reach, SPAN + 16), 0) + HALO - iota((reach, SPAN + 16), 1)
    for span in range(count // SPAN):
        moves = []
        for lag in range(1, NEAR):
            mask = mask_ref[lag - 1, span * SPAN : span * SPAN + reach, : SPAN + 16]
            moves.append(jnp.where(back == lag, mask, 0.0))
        shift_ref[span] = jnp.concatenate(moves, 0).astype(BF16)


def mix_kernel(
    modes, size, ndoc,
    where_ref, lengths_ref,
    key_ref, value_ref, halo_ref, taps_ref, rates_ref,
    mixed_ref, state_ref,
    shift_ref, mask_ref, tail_ref,
):
    _, count, width = key_ref.shape
    chunks = count // CHUNK
    reach = SPAN + HALO
    step = step_rates(rates_ref, 0, width, size)

    @pl.when(pl.program_id(0) == 0)
    def _():
        base = where_ref[0] * count
        ends = running_ends(lengths_ref, ndoc)
        write_shifts(shift_ref, mask_ref, ends, base, count)
        last = scalar_document(ends, base + count - 1).astype(F32)
        tail_ref[...] = jnp.where(row_documents(ends, base, count) == last, 1.0, 0.0).astype(F32)

    def window(x_ref, which, start, lanes):
        if start == 0:
            halo = halo_ref[which, :, lanes].astype(F32)
            ahead = jnp.concatenate([jnp.zeros((16 - HALO, LANES), F32), halo], 0).astype(BF16)
        else:
            ahead = x_ref[0, start - 16 : start, lanes]
        return jnp.concatenate([ahead, x_ref[0, start : start + SPAN, lanes]], 0)

    def finish(here, moved, taps, apart):
        rows = [here] + [moved[lag * reach : (lag + 1) * reach] for lag in range(NEAR - 1)]
        far = sum(rows[lag] * taps[NEAR + lag] for lag in range(SHORT - NEAR))
        far = pltpu.roll(far, NEAR, 0)[HALO:] * apart
        return far + sum(row[HALO:] * taps[lag] for lag, row in enumerate(rows))

    def tile(lanes):
        key_taps, value_taps = tap_rows(taps_ref, 1, lanes), tap_rows(taps_ref, 2, lanes)
        for start in range(0, count, SPAN):
            keys, values = window(key_ref, 1, start, lanes), window(value_ref, 2, start, lanes)
            moved = jnp.dot(shift_ref[start // SPAN], jnp.concatenate([keys, values], 1), preferred_element_type=F32)
            apart = mask_ref[NEAR - 1, HALO + start : HALO + start + SPAN, :]
            key = finish(keys.astype(F32)[16 - HALO :], moved[:, :LANES], key_taps, apart)
            value = finish(values.astype(F32)[16 - HALO :], moved[:, LANES:], value_taps, apart)
            mixed_ref[start : start + SPAN, lanes] = (key * value).astype(BF16)
        rate = tile_rates(step, lanes.start, size)
        leave = jnp.exp(-rate * (CHUNK - 1 - iota((LANES, CHUNK), 1)).astype(F32))
        whole = jnp.exp(-rate * CHUNK)
        spans = []
        for chunk in reversed(range(chunks)):
            tail = tail_ref[0:1, chunk * CHUNK : (chunk + 1) * CHUNK]
            spans.append((leave * tail).astype(BF16))
            leave = leave * whole
        full = jnp.dot(jnp.concatenate(spans[::-1], 1), mixed_ref[:, lanes], preferred_element_type=F32)
        full = jnp.where(group_mask(modes, size), full, 0.0)
        state = jnp.sum(full.reshape(LANES // modes, modes, LANES), 0).astype(BF16)
        for owner in range(state_ref.shape[0]):
            state_ref[owner, :, lanes] = state

    each_tile(width, tile)


def left_state(states_ref, flags_ref, rate, lanes, modes, size, count):
    inside = group_mask(modes, size)
    decay = jnp.exp(-rate * count)
    total = jnp.zeros((LANES, LANES), F32)
    for back in range(states_ref.shape[0] // 2, 0, -1):
        v = flags_ref[1] - back
        piece = jnp.concatenate([states_ref[jnp.maximum(v, 0), :, lanes].astype(F32)] * (LANES // modes), 0)
        total = jnp.where(inside & (v >= flags_ref[0]), piece + decay * total, 0.0)
    return total


def write_flags(flags_ref, ends, where, count, nblocks):
    before = scalar_document(ends, where * count - 1)
    first = jnp.int32(0)
    for v in range(nblocks):
        first = first + (scalar_document(ends, (v + 1) * count - 1) < before).astype(jnp.int32)
    flags_ref[0] = first
    flags_ref[1] = where
    for chunk in range(count // CHUNK):
        start = where * count + chunk * CHUNK
        held = scalar_document(ends, start - 1) == scalar_document(ends, start + CHUNK - 1)
        flags_ref[2 + chunk] = held.astype(jnp.int32)


def hand_over(out_ref, squares_ref, slot_ref, summed, start, rows, lanes):
    squares_ref[start : start + SPAN, :] += summed * summed
    rounded = summed.astype(BF16)
    for b in range(SPAN // rows):
        tile = lanes.start // LANES * rows
        out_ref[slot_ref[start // rows + b], tile : tile + rows, :] = rounded[b * rows : (b + 1) * rows]


def conv_kernel(modes, size, ndoc, nblocks, carried, origin, where_ref, lengths_ref, owner_ref, *refs):
    x_ref, halo_ref, taps_ref, mixed_ref, rates_ref, residues_ref, skip_ref, residual_ref = refs[:8]
    refs = refs[8:]
    if carried:
        states_ref, before_ref, out_ref, spare_ref, sums_ref = refs[:5]
        refs = refs[5:]
    else:
        base_ref, gate_ref = refs[:2]
        refs = refs[2:]
    mask_ref, same_ref, keep_ref, tail_ref, flags_ref = refs[:5]
    if carried:
        slot_ref, squares_ref = refs[5:]
    count, width = mixed_ref.shape
    chunks = count // CHUNK
    step = step_rates(rates_ref, origin, width, size)
    step_residues = step_rates(residues_ref, origin, width, size)

    @pl.when(pl.program_id(0) == 0)
    def _():
        where = where_ref[0]
        base = where * count
        ends = running_ends(lengths_ref, ndoc)
        write_lag_masks(mask_ref, ends, base, count)
        write_flags(flags_ref, ends, where, count, nblocks)
        if carried:
            write_slots(slot_ref, owner_ref, where, nblocks)
            squares_ref[...] = before_ref[...]
        documents = row_documents(ends, base, count)
        causal = iota((CHUNK, CHUNK), 1) <= iota((CHUNK, CHUNK), 0)
        for chunk in range(chunks):
            start = base + chunk * CHUNK
            there = jnp.broadcast_to(documents[0:1, chunk * CHUNK : (chunk + 1) * CHUNK], (CHUNK, CHUNK))
            here = there.T
            same_ref[chunk] = jnp.where((here == there) & causal, 1.0, 0.0).astype(BF16)
            before = scalar_document(ends, start - 1).astype(F32)
            keep_ref[chunk] = jnp.where(here == before, 1.0, 0.0).astype(BF16)
            last = scalar_document(ends, start + CHUNK - 1).astype(F32)
            tail_ref[chunk] = jnp.where(there == last, 1.0, 0.0).astype(F32)

    groups = LANES // modes

    def tile(lanes):
        rate = tile_rates(step, lanes.start, size)
        scale = tile_rates(step_residues, lanes.start, size) * jnp.sqrt(1.0 - jnp.exp(-2.0 * rate))
        down = iota((CHUNK, LANES), 0)
        along = iota((LANES, CHUNK), 1)
        entry = (scale.T * jnp.exp(-rate.T * (down + 1).astype(F32))).astype(BF16)
        leave = jnp.exp(-rate * (CHUNK - 1 - along).astype(F32))
        whole = jnp.exp(-rate * CHUNK)
        terms = scale * jnp.where(along == 0, 1.0, leave * jnp.exp(-rate))
        toeplitz = []
        for g in range(groups):
            line = jnp.sum(terms[g * modes : (g + 1) * modes], 0, keepdims=True)
            top = pltpu.roll(jnp.broadcast_to(line, (8, CHUNK)), 0, 1, stride=1, stride_axis=0)
            parts = [top] + [pltpu.roll(top, 8 * k, 1) for k in range(1, CHUNK // 8)]
            toeplitz.append(jnp.concatenate(parts, 0).astype(BF16))
        inside = group_mask(modes, size)
        state = left_state(states_ref, flags_ref, rate, lanes, modes, size, count) if carried else None
        taps = tap_rows(taps_ref, 0, lanes)
        skip = skip_ref[:, lanes]
        lane_group = iota((CHUNK, LANES), 1) // size
        for chunk in range(chunks):
            start = chunk * CHUNK
            mixed = mixed_ref[start : start + CHUNK, lanes]
            same = same_ref[chunk]
            left = [t * same for t in toeplitz]
            right = [jnp.where(lane_group == g, mixed, jnp.zeros_like(mixed)) for g in range(groups)]
            if state is not None:
                left.append(entry * keep_ref[chunk])
                right.append(state.astype(BF16))
            longer = jnp.dot(jnp.concatenate(left, 1), jnp.concatenate(right, 0), preferred_element_type=F32)
            if chunk + 1 < chunks:
                fresh = jnp.dot((leave * tail_ref[chunk]).astype(BF16), mixed, preferred_element_type=F32)
                held = flags_ref[2 + chunk] == 1
                fresh = jnp.where(inside, fresh, 0.0)
                state = fresh if state is None else jnp.where(held, whole * state, 0.0) + fresh
            body = longer + skip * mixed.astype(F32)
            for half in range(start, start + CHUNK, SPAN):
                gate = short_conv(extended(x_ref, halo_ref, 0, half, lanes), taps, lag_masks(mask_ref, half))
                inner = body[half - start : half - start + SPAN]
                summed = residual_ref[half : half + SPAN, lanes].astype(F32) + gate * inner
                if carried:
                    hand_over(out_ref, squares_ref, slot_ref, summed, half, count // nblocks, lanes)
                else:
                    base_ref[half : half + SPAN, lanes] = summed
                    gate_ref[half : half + SPAN, lanes] = gate.astype(BF16)

    each_tile(width, tile)
    if carried:
        spare_ref[...] = out_ref[slot_ref[nblocks]]

        @pl.when(pl.program_id(0) == pl.num_programs(0) - 1)
        def _():
            for start in range(0, count, LANES):
                rows = squares_ref[start : start + LANES, :].T
                sums_ref[:, start : start + LANES] = jnp.sum(rows, 0, keepdims=True)


def add_kernel(
    modes, size, ndoc, nblocks,
    where_ref, lengths_ref, owner_ref,
    base_ref, gate_ref, rates_ref, residues_ref, states_ref,
    out_ref, spare_ref, squares_ref,
    keep_ref, flags_ref, slot_ref,
):
    count, width = base_ref.shape
    chunks = count // CHUNK
    step = step_rates(rates_ref, 0, width, size)
    step_residues = step_rates(residues_ref, 0, width, size)

    @pl.when(pl.program_id(0) == 0)
    def _():
        where = where_ref[0]
        ends = running_ends(lengths_ref, ndoc)
        write_flags(flags_ref, ends, where, count, nblocks)
        write_slots(slot_ref, owner_ref, where, nblocks)
        squares_ref[...] = jnp.zeros_like(squares_ref)
        before = scalar_document(ends, where * count - 1)
        kept = jnp.int32(0)
        for end in reversed(ends):
            kept = jnp.where(end >= where * count, end - where * count, kept)
        kept = jnp.where(before < 0, 0, kept)
        keep_ref[...] = jnp.where(iota((count, LANES), 0) < kept, 1.0, 0.0).astype(F32)

    def tile(lanes):
        rate = tile_rates(step, lanes.start, size)
        scale = tile_rates(step_residues, lanes.start, size) * jnp.sqrt(1.0 - jnp.exp(-2.0 * rate))
        down = iota((CHUNK, LANES), 0)
        entry = (scale.T * jnp.exp(-rate.T * (down + 1).astype(F32))).astype(BF16)
        whole = jnp.exp(-rate * CHUNK)
        state = left_state(states_ref, flags_ref, rate, lanes, modes, size, count)
        held = []
        for _ in range(chunks):
            held.append(state.astype(BF16))
            state = state * whole
        left = jnp.dot(entry, jnp.concatenate(held, 1), preferred_element_type=F32)
        for start in range(0, count, SPAN):
            low = start % CHUNK
            chunk = start // CHUNK
            carried = left[low : low + SPAN, chunk * LANES : (chunk + 1) * LANES] * keep_ref[start : start + SPAN, :]
            gate = gate_ref[start : start + SPAN, lanes].astype(F32)
            summed = base_ref[start : start + SPAN, lanes] + gate * carried
            hand_over(out_ref, squares_ref, slot_ref, summed, start, count // nblocks, lanes)

    each_tile(width, tile)
    spare_ref[...] = out_ref[slot_ref[nblocks]]


def norm_kernel(parts, where_ref, owner_ref, *refs):
    blocks, spares, refs = refs[:parts], refs[parts : 2 * parts], refs[2 * parts :]
    gain_ref, out_ref = refs[:2]
    held, (done_ref, in_sems, out_sems) = refs[2 : 2 + parts], refs[2 + parts :]
    nblocks = blocks[0].shape[0]
    rows = out_ref.shape[0] // nblocks
    room = sum(block.shape[1] for block in blocks) - out_ref.shape[1] // LANES * rows

    def fetch(part, i, source):
        return pltpu.make_async_copy(source, held[part].at[i], in_sems.at[part, i])

    for i in range(nblocks):
        ahead = where_ref[0] - owner_ref[i]
        source = jnp.where(ahead < 0, ahead + nblocks, ahead)
        second = is_second(owner_ref, nblocks, i)
        for part in range(parts):

            @pl.when(second)
            def _(part=part, i=i):
                fetch(part, i, spares[part]).start()

            @pl.when(jnp.logical_not(second))
            def _(part=part, i=i, source=source):
                fetch(part, i, blocks[part].at[source]).start()

    def store(i):
        here = pl.ds(i * rows, rows)
        return pltpu.make_async_copy(done_ref.at[here], out_ref.at[here], out_sems.at[i])

    for i in range(nblocks):
        for part in range(parts):
            fetch(part, i, blocks[part].at[0]).wait()
        start = held[-1].shape[1] - room + i // 16 * 16
        halves = held[-1][i, start : start + 16, :].astype(F32)[i % 16 : i % 16 + 1]
        halves = jnp.broadcast_to(halves, (8, LANES))
        scale = halves + pltpu.roll(halves, LANES - rows, 1)
        scale = jnp.broadcast_to(scale[0:1], (LANES, LANES)).T[:rows]
        tile = 0
        for part in range(parts):
            for low in range(0, held[part].shape[1] - (room if part + 1 == parts else 0), rows):
                outs = slice(tile * LANES, (tile + 1) * LANES)
                value = held[part][i, low : low + rows, :].astype(F32)
                done_ref[i * rows : (i + 1) * rows, outs] = (value * scale * gain_ref[:, outs]).astype(BF16)
                tile += 1
        store(i).start()
    for i in range(nblocks):
        store(i).wait()


def params(limit=VMEM_LIMIT):
    return pltpu.CompilerParams(dimension_semantics=("arbitrary",), vmem_limit_bytes=limit)


def in_hbm(*arrays):
    return [pltpu.with_memory_space_constraint(array, pltpu.HBM) for array in arrays]


def in_vmem(array):
    return pltpu.with_memory_space_constraint(array, pltpu.VMEM)


def whole_array(rank):
    return lambda *_: (0,) * rank


def mix(scalars, x, halo, taps, rates, size, ndoc, copies):
    _, count, width = x.shape
    modes = rates.shape[0]
    wide = min(WIDE, width)
    deep = lambda t, *_: (0, 0, t)
    grid_spec = pltpu.PrefetchScalarGridSpec(
        num_scalar_prefetch=2,
        grid=(width // wide,),
        in_specs=[
            pl.BlockSpec((1, count, wide), lambda t, *_: (1, 0, t)),
            pl.BlockSpec((1, count, wide), lambda t, *_: (2, 0, t)),
            pl.BlockSpec((3, HALO, wide), deep),
            pl.BlockSpec((3, SHORT, wide), deep),
            pl.BlockSpec(rates.shape, whole_array(2)),
        ],
        out_specs=[
            pl.BlockSpec((count, wide), lambda t, *_: (0, t)),
            pl.BlockSpec((copies, modes, wide), deep),
        ],
        scratch_shapes=[
            pltpu.VMEM((count // SPAN, (NEAR - 1) * (SPAN + HALO), SPAN + 16), BF16),
            pltpu.VMEM((NEAR, count + 2 * HALO, LANES), F32),
            pltpu.VMEM((8, count), F32),
        ],
    )
    return pl.pallas_call(
        functools.partial(mix_kernel, modes, size, ndoc),
        grid_spec=grid_spec,
        out_shape=[pltpu.HBM((count, width), BF16), pltpu.HBM((copies, modes, width), BF16)],
        compiler_params=params(),
        cost_estimate=pl.CostEstimate(flops=60 * count * width, bytes_accessed=8 * count * width, transcendentals=count * width),
        name="mix",
    )(*scalars[:2], x, x, halo, taps, rates)


def conv(low, share, room, scalars, x, halo, taps, mixed, rates, residues, skip, residual, carried, size, ndoc, nblocks):
    _, count, width = x.shape
    modes = rates.shape[0]
    wide = math.gcd(math.gcd(low, share), WIDE)
    first = low // wide
    tile = lambda t, *_: (0, first + t)
    deep = lambda t, *_: (0, 0, first + t)
    step = pl.BlockSpec(rates.shape, whole_array(2))
    in_specs = [
        pl.BlockSpec((1, count, wide), deep),
        pl.BlockSpec((1, HALO, wide), deep),
        pl.BlockSpec((1, SHORT, wide), deep),
        pl.BlockSpec((count, wide), tile),
        step,
        step,
        pl.BlockSpec((1, wide), tile),
        pl.BlockSpec((count, wide), tile),
    ]
    operands = [x, halo, taps, mixed, rates, residues, skip, residual]
    scratch = [
        pltpu.VMEM((3, count + 2 * HALO, LANES), F32),
        pltpu.VMEM((count // CHUNK, CHUNK, CHUNK), BF16),
        pltpu.VMEM((count // CHUNK, CHUNK, LANES), BF16),
        pltpu.VMEM((count // CHUNK, LANES, CHUNK), F32),
        pltpu.SMEM((2 + count // CHUNK,), jnp.int32),
    ]
    if carried:
        states, squares = carried
        in_specs += [pl.BlockSpec((nblocks, modes, wide), deep), pl.BlockSpec((count, LANES), whole_array(2))]
        operands += [states, squares]
        scratch += [pltpu.SMEM((nblocks + 1,), jnp.int32), pltpu.VMEM((count, LANES), F32)]
        out_specs, out_shape = handed(share, room, wide, count, nblocks)
        out_specs[2] = pl.BlockSpec((1, count), whole_array(2))
        out_shape[2] = jax.ShapeDtypeStruct((1, count), F32)
    else:
        out_specs = [pl.BlockSpec((count, wide), lambda t, *_: (0, t))] * 2
        out_shape = [pltpu.VMEM((count, share), F32), pltpu.VMEM((count, share), BF16)]
    grid_spec = pltpu.PrefetchScalarGridSpec(
        num_scalar_prefetch=3, grid=(share // wide,), in_specs=in_specs, out_specs=out_specs, scratch_shapes=scratch
    )
    return pl.pallas_call(
        functools.partial(conv_kernel, modes, size, ndoc, nblocks, bool(carried), low // size),
        grid_spec=grid_spec,
        out_shape=out_shape,
        compiler_params=params(VMEM_LIMIT if carried else VMEM_LIMIT_BESIDE),
        cost_estimate=pl.CostEstimate(
            flops=2 * 1152 * count * share, bytes_accessed=8 * count * share, transcendentals=count * share
        ),
        name="conv",
    )(*scalars, *in_hbm(*operands))


def handed(share, room, wide, count, nblocks):
    rows = count // nblocks
    specs = [
        pl.BlockSpec((nblocks, wide // LANES * rows, LANES), lambda t, *_: (0, t, 0)),
        pl.BlockSpec((wide // LANES * rows, LANES), lambda t, *_: (t, 0)),
        pl.BlockSpec((count, LANES), whole_array(2)),
    ]
    shapes = [
        pltpu.HBM((nblocks, share // LANES * rows + room, LANES), BF16),
        pltpu.HBM((share // LANES * rows, LANES), BF16),
        pltpu.HBM((count, LANES), F32),
    ]
    return specs, shapes


def add(scalars, base, gate, rates, residues, states, size, ndoc, nblocks):
    count, share = base.shape
    modes = rates.shape[0]
    wide = math.gcd(share, WIDE)
    tile = lambda t, *_: (0, t)
    step = pl.BlockSpec(rates.shape, whole_array(2))
    out_specs, out_shape = handed(share, 0, wide, count, nblocks)
    grid_spec = pltpu.PrefetchScalarGridSpec(
        num_scalar_prefetch=3,
        grid=(share // wide,),
        in_specs=[
            pl.BlockSpec((count, wide), tile),
            pl.BlockSpec((count, wide), tile),
            step,
            step,
            pl.BlockSpec((nblocks, modes, wide), lambda t, *_: (0, 0, t)),
        ],
        out_specs=out_specs,
        scratch_shapes=[
            pltpu.VMEM((count, LANES), F32),
            pltpu.SMEM((2 + count // CHUNK,), jnp.int32),
            pltpu.SMEM((nblocks + 1,), jnp.int32),
        ],
    )
    return pl.pallas_call(
        functools.partial(add_kernel, modes, size, ndoc, nblocks),
        grid_spec=grid_spec,
        out_shape=out_shape,
        compiler_params=params(VMEM_LIMIT_BESIDE),
        cost_estimate=pl.CostEstimate(flops=300 * count * share, bytes_accessed=8 * count * share, transcendentals=count * share),
        name="add",
    )(*scalars, in_vmem(base), in_vmem(gate), *in_hbm(rates, residues, states))


def norm(where, owner, blocks, spares, gain, count):
    width = gain.shape[1]
    nblocks = blocks[0].shape[0]
    smem, vmem, anywhere = (pl.BlockSpec(memory_space=space) for space in (pltpu.SMEM, pltpu.VMEM, pl.ANY))
    return pl.pallas_call(
        functools.partial(norm_kernel, len(blocks)),
        in_specs=[smem, smem] + [anywhere] * (2 * len(blocks)) + [vmem],
        out_specs=anywhere,
        out_shape=jax.ShapeDtypeStruct((count, width), BF16),
        scratch_shapes=[pltpu.VMEM(block.shape, BF16) for block in blocks]
        + [
            pltpu.VMEM((count, width), BF16),
            pltpu.SemaphoreType.DMA((len(blocks), nblocks)),
            pltpu.SemaphoreType.DMA((nblocks,)),
        ],
        compiler_params=pltpu.CompilerParams(vmem_limit_bytes=VMEM_LIMIT),
        cost_estimate=pl.CostEstimate(flops=3 * count * width, bytes_accessed=4 * count * width, transcendentals=0),
        name="norm",
    )(where, owner, *blocks, *spares, gain)


def on_device(features, residual, short_taps, rates, residues, skip, gain, lengths, owner):
    count, _, width = features.shape
    size = width // rates.shape[0]
    ndoc = lengths.shape[0]
    nblocks = lax.axis_size("ctx")
    rows = count // nblocks
    where = lax.axis_index("ctx")
    x = jnp.transpose(features, (1, 0, 2))
    pairs = [(i, i + 1) for i in range(nblocks - 1)]
    halo = lax.ppermute(x[:, count - HALO :], "ctx", pairs)

    scalars = (where.reshape(1).astype(jnp.int32), lengths, owner)
    spread = ((0, 0), (0, LANES - rates.shape[0]))
    rates, residues = jnp.pad(rates.T, spread), jnp.pad(residues.T, spread)

    offsets = owner[:nblocks]
    ids = jnp.arange(nblocks, dtype=jnp.int32)
    twice = jnp.any((offsets[:, None] == offsets[None, :]) & (ids[None, :] < ids[:, None]), 1)
    spare_shift = jnp.sum(jnp.where(twice, offsets, 0))

    def exchanged(value):
        return lax.all_to_all(value, "ctx", split_axis=0, concat_axis=0, tiled=True)

    first = width * SPLIT[0] // sum(SPLIT)
    second = width - first
    mixed, copies = mix(scalars, x, halo, short_taps, rates, size, ndoc, nblocks)
    states = exchanged(copies)
    shared = (scalars, x, halo, short_taps, mixed, rates, residues, skip.reshape(1, width), residual)
    base, gate = conv(0, first, 0, *shared, (), size, ndoc, nblocks)
    out, spare, squares = add(scalars, base, gate, rates, residues, states, size, ndoc, nblocks)
    block = exchanged(out)
    room = -(-nblocks // 16) * 16
    out, last_spare, sums = conv(first, second, room, *shared, (states, squares), size, ndoc, nblocks)
    mean = lax.psum(sums, "mp") / (width * lax.axis_size("mp"))
    inverse = lax.rsqrt(mean + EPS)
    high = lax.reduce_precision(inverse, 8, 7)
    halves = jnp.concatenate([high.reshape(nblocks, rows), (inverse - high).reshape(nblocks, rows)], 1)
    halves = jnp.pad(halves, ((0, room - nblocks), (0, LANES - 2 * rows))).astype(BF16)
    table = jnp.broadcast_to(halves[None], (nblocks, room, LANES))
    out = lax.dynamic_update_slice(out, table, (0, second // LANES * rows, 0))
    def moved(by):
        return lambda value: lax.ppermute(value, "ctx", [(s, (s + by) % nblocks) for s in range(nblocks)])

    def to_owner(value):
        return lax.switch(spare_shift, [lambda same: same] + [moved(d) for d in range(1, nblocks)], value)

    spare, _ = lax.optimization_barrier((spare, inverse))
    spare = to_owner(spare)
    last_spare = jnp.concatenate([last_spare, halves], 0)
    out, spare, last_spare = lax.optimization_barrier((out, spare, last_spare))
    last_block = exchanged(out)
    last_spare = to_owner(last_spare)
    return norm(scalars[0], owner, [block, last_block], [spare, last_spare], gain.reshape(1, width), count)


def solution(mesh):
    return jax.shard_map(
        on_device,
        mesh=mesh,
        in_specs=(
            P("ctx", None, "mp"),
            P("ctx", "mp"),
            P(None, None, "mp"),
            P("mp", None),
            P("mp", None),
            P("mp"),
            P("mp"),
            P(),
            P(),
        ),
        out_specs=P("ctx", "mp"),
        check_vma=False,
    )
```

```python
import functools
import math

import jax
import jax.numpy as jnp
from jax import lax
from jax.experimental import pallas as pl
from jax.experimental.pallas import tpu as pltpu
from jax.sharding import PartitionSpec as P

SHORT = 7
LANES = 128
CHUNK = 128
HALO = 8
EPS = 1e-06
SPLIT = (4, 4)
NEAR = 4
WIDE = 512
SPAN = 64
F32 = jnp.float32
BF16 = jnp.bfloat16
VMEM_LIMIT = 64 * 1024 * 1024
VMEM_LIMIT_BESIDE = 56 * 1024 * 1024


def iota(shape, dim):
    return lax.broadcasted_iota(jnp.int32, shape, dim)


def document(ends, positions):
    total = jnp.zeros(positions.shape, jnp.int32)
    for end in ends:
        total = total + (positions >= end).astype(jnp.int32)
    return total


def scalar_document(ends, position):
    total = jnp.int32(0)
    for end in ends:
        total = total + (position >= end).astype(jnp.int32)
    return jnp.where(position < 0, -1, total)


def running_ends(lengths_ref, ndoc):
    ends, total = [], jnp.int32(0)
    for j in range(ndoc):
        total = total + lengths_ref[j]
        ends.append(total)
    return ends


def write_lag_masks(mask_ref, ends, base, count):
    mask_ref[...] = jnp.ones_like(mask_ref)
    gap = jnp.zeros((1, LANES), F32)
    for end in ends:
        row = end - base + HALO

        @pl.when((row >= 0) & (row < count + HALO))
        def _(row=row):
            for lag in (1, 2, 3):
                for past in range(lag):
                    mask_ref[lag - 1, pl.ds(row + past, 1), :] = gap


def row_documents(ends, base, count):
    return document(ends, base + iota((8, count), 1)).astype(F32)


def is_second(owner_ref, nblocks, i):
    found = jnp.bool_(False)
    for j in range(i):
        found = found | (owner_ref[j] == owner_ref[i])
    return found


def write_slots(slot_ref, owner_ref, where, nblocks):
    unused = jnp.int32(nblocks * (nblocks - 1) // 2)
    seconds = [is_second(owner_ref, nblocks, i) for i in range(nblocks)]
    mine = [owner_ref[where * nblocks + i] for i in range(nblocks)]
    for i in range(nblocks):
        unused = unused - jnp.where(seconds[i], 0, mine[i])
    for i in range(nblocks):
        slot_ref[i] = jnp.where(seconds[i], unused, mine[i])
    slot_ref[nblocks] = unused


def step_rates(ref, origin, wide, size):
    first = origin + pl.program_id(0) * (wide // size)
    return pltpu.roll(ref[...], jnp.where(first == 0, 0, LANES - first), 1)


def tile_rates(rates, low, size):
    first = low // size
    columns = [rates[:, first + g : first + g + 1] for g in range(LANES // size)]
    return jnp.concatenate([jnp.broadcast_to(column, (column.shape[0], LANES)) for column in columns], 0)


def short_conv(ext, taps, masks):
    def back(value, lag):
        return pltpu.roll(value, lag, 0) * masks[lag - 1]

    one, two = back(ext, 1), back(ext, 2)
    far = ext * taps[6]
    middle = ext * taps[3] + one * taps[4] + two * taps[5] + back(far, 3)
    near = ext * taps[0] + one * taps[1] + two * taps[2] + back(middle, 3)
    return near[HALO:]


def extended(x_ref, halo_ref, which, start, lanes):
    rows = x_ref[0, start : start + SPAN, lanes].astype(F32)
    if start == 0:
        ahead = halo_ref[which, :, lanes].astype(F32)
    else:
        ahead = x_ref[0, start - 16 : start, lanes].astype(F32)[16 - HALO :]
    return jnp.concatenate([ahead, rows], 0)


def tap_rows(taps_ref, which, lanes):
    return [taps_ref[which, j : j + 1, lanes] for j in range(SHORT)]


def lag_masks(mask_ref, start):
    return [mask_ref[l, start : start + SPAN + HALO, :] for l in range(3)]


def group_mask(modes, size):
    return (iota((LANES, LANES), 0) // modes) == (iota((LANES, LANES), 1) // size)


def each_tile(width, body):
    for low in range(0, width, LANES):
        body(slice(low, low + LANES))


def write_shifts(shift_ref, mask_ref, ends, base, count):
    mask_ref[...] = jnp.ones_like(mask_ref)
    gap = jnp.zeros((1, LANES), F32)
    for end in ends:
        row = end - base + HALO

        @pl.when((row >= 0) & (row < count + HALO))
        def _(row=row):
            for lag in range(1, NEAR + 1):
                for past in range(lag):
                    mask_ref[lag - 1, pl.ds(row + past, 1), :] = gap

    reach = SPAN + HALO
    back = iota((reach, SPAN + 16), 0) + HALO - iota((reach, SPAN + 16), 1)
    for span in range(count // SPAN):
        moves = []
        for lag in range(1, NEAR):
            mask = mask_ref[lag - 1, span * SPAN : span * SPAN + reach, : SPAN + 16]
            moves.append(jnp.where(back == lag, mask, 0.0))
        shift_ref[span] = jnp.concatenate(moves, 0).astype(BF16)


def mix_kernel(
    modes, size, ndoc,
    where_ref, lengths_ref,
    key_ref, value_ref, halo_ref, taps_ref, rates_ref,
    mixed_ref, state_ref,
    shift_ref, mask_ref, tail_ref,
):
    _, count, width = key_ref.shape
    chunks = count // CHUNK
    reach = SPAN + HALO
    step = step_rates(rates_ref, 0, width, size)

    @pl.when(pl.program_id(0) == 0)
    def _():
        base = where_ref[0] * count
        ends = running_ends(lengths_ref, ndoc)
        write_shifts(shift_ref, mask_ref, ends, base, count)
        last = scalar_document(ends, base + count - 1).astype(F32)
        tail_ref[...] = jnp.where(row_documents(ends, base, count) == last, 1.0, 0.0).astype(F32)

    def window(x_ref, which, start, lanes):
        if start == 0:
            halo = halo_ref[which, :, lanes].astype(F32)
            ahead = jnp.concatenate([jnp.zeros((16 - HALO, LANES), F32), halo], 0).astype(BF16)
        else:
            ahead = x_ref[0, start - 16 : start, lanes]
        return jnp.concatenate([ahead, x_ref[0, start : start + SPAN, lanes]], 0)

    def finish(here, moved, taps, apart):
        rows = [here] + [moved[lag * reach : (lag + 1) * reach] for lag in range(NEAR - 1)]
        far = sum(rows[lag] * taps[NEAR + lag] for lag in range(SHORT - NEAR))
        far = pltpu.roll(far, NEAR, 0)[HALO:] * apart
        return far + sum(row[HALO:] * taps[lag] for lag, row in enumerate(rows))

    def tile(lanes):
        key_taps, value_taps = tap_rows(taps_ref, 1, lanes), tap_rows(taps_ref, 2, lanes)
        for start in range(0, count, SPAN):
            keys, values = window(key_ref, 1, start, lanes), window(value_ref, 2, start, lanes)
            moved = jnp.dot(shift_ref[start // SPAN], jnp.concatenate([keys, values], 1), preferred_element_type=F32)
            apart = mask_ref[NEAR - 1, HALO + start : HALO + start + SPAN, :]
            key = finish(keys.astype(F32)[16 - HALO :], moved[:, :LANES], key_taps, apart)
            value = finish(values.astype(F32)[16 - HALO :], moved[:, LANES:], value_taps, apart)
            mixed_ref[start : start + SPAN, lanes] = (key * value).astype(BF16)
        rate = tile_rates(step, lanes.start, size)
        leave = jnp.exp(-rate * (CHUNK - 1 - iota((LANES, CHUNK), 1)).astype(F32))
        whole = jnp.exp(-rate * CHUNK)
        spans = []
        for chunk in reversed(range(chunks)):
            tail = tail_ref[0:1, chunk * CHUNK : (chunk + 1) * CHUNK]
            spans.append((leave * tail).astype(BF16))
            leave = leave * whole
        full = jnp.dot(jnp.concatenate(spans[::-1], 1), mixed_ref[:, lanes], preferred_element_type=F32)
        full = jnp.where(group_mask(modes, size), full, 0.0)
        state = jnp.sum(full.reshape(LANES // modes, modes, LANES), 0).astype(BF16)
        for owner in range(state_ref.shape[0]):
            state_ref[owner, :, lanes] = state

    each_tile(width, tile)


def left_state(states_ref, flags_ref, rate, lanes, modes, size, count):
    inside = group_mask(modes, size)
    decay = jnp.exp(-rate * count)
    total = jnp.zeros((LANES, LANES), F32)
    for back in range(states_ref.shape[0] // 2, 0, -1):
        v = flags_ref[1] - back
        piece = jnp.concatenate([states_ref[jnp.maximum(v, 0), :, lanes].astype(F32)] * (LANES // modes), 0)
        total = jnp.where(inside & (v >= flags_ref[0]), piece + decay * total, 0.0)
    return total


def write_flags(flags_ref, ends, where, count, nblocks):
    before = scalar_document(ends, where * count - 1)
    first = jnp.int32(0)
    for v in range(nblocks):
        first = first + (scalar_document(ends, (v + 1) * count - 1) < before).astype(jnp.int32)
    flags_ref[0] = first
    flags_ref[1] = where
    for chunk in range(count // CHUNK):
        start = where * count + chunk * CHUNK
        held = scalar_document(ends, start - 1) == scalar_document(ends, start + CHUNK - 1)
        flags_ref[2 + chunk] = held.astype(jnp.int32)


def hand_over(out_ref, squares_ref, slot_ref, summed, start, rows, lanes):
    squares_ref[start : start + SPAN, :] += summed * summed
    rounded = summed.astype(BF16)
    for b in range(SPAN // rows):
        tile = lanes.start // LANES * rows
        out_ref[slot_ref[start // rows + b], tile : tile + rows, :] = rounded[b * rows : (b + 1) * rows]


def conv_kernel(modes, size, ndoc, nblocks, carried, origin, where_ref, lengths_ref, owner_ref, *refs):
    x_ref, halo_ref, taps_ref, mixed_ref, rates_ref, residues_ref, skip_ref, residual_ref = refs[:8]
    refs = refs[8:]
    if carried:
        states_ref, before_ref, out_ref, spare_ref, sums_ref = refs[:5]
        refs = refs[5:]
    else:
        base_ref, gate_ref = refs[:2]
        refs = refs[2:]
    mask_ref, same_ref, keep_ref, tail_ref, flags_ref = refs[:5]
    if carried:
        slot_ref, squares_ref = refs[5:]
    count, width = mixed_ref.shape
    chunks = count // CHUNK
    step = step_rates(rates_ref, origin, width, size)
    step_residues = step_rates(residues_ref, origin, width, size)

    @pl.when(pl.program_id(0) == 0)
    def _():
        where = where_ref[0]
        base = where * count
        ends = running_ends(lengths_ref, ndoc)
        write_lag_masks(mask_ref, ends, base, count)
        write_flags(flags_ref, ends, where, count, nblocks)
        if carried:
            write_slots(slot_ref, owner_ref, where, nblocks)
            squares_ref[...] = before_ref[...]
        documents = row_documents(ends, base, count)
        causal = iota((CHUNK, CHUNK), 1) <= iota((CHUNK, CHUNK), 0)
        for chunk in range(chunks):
            start = base + chunk * CHUNK
            there = jnp.broadcast_to(documents[0:1, chunk * CHUNK : (chunk + 1) * CHUNK], (CHUNK, CHUNK))
            here = there.T
            same_ref[chunk] = jnp.where((here == there) & causal, 1.0, 0.0).astype(BF16)
            before = scalar_document(ends, start - 1).astype(F32)
            keep_ref[chunk] = jnp.where(here == before, 1.0, 0.0).astype(BF16)
            last = scalar_document(ends, start + CHUNK - 1).astype(F32)
            tail_ref[chunk] = jnp.where(there == last, 1.0, 0.0).astype(F32)

    groups = LANES // modes

    def tile(lanes):
        rate = tile_rates(step, lanes.start, size)
        scale = tile_rates(step_residues, lanes.start, size) * jnp.sqrt(1.0 - jnp.exp(-2.0 * rate))
        down = iota((CHUNK, LANES), 0)
        along = iota((LANES, CHUNK), 1)
        entry = (scale.T * jnp.exp(-rate.T * (down + 1).astype(F32))).astype(BF16)
        leave = jnp.exp(-rate * (CHUNK - 1 - along).astype(F32))
        whole = jnp.exp(-rate * CHUNK)
        terms = scale * jnp.where(along == 0, 1.0, leave * jnp.exp(-rate))
        toeplitz = []
        for g in range(groups):
            line = jnp.sum(terms[g * modes : (g + 1) * modes], 0, keepdims=True)
            top = pltpu.roll(jnp.broadcast_to(line, (8, CHUNK)), 0, 1, stride=1, stride_axis=0)
            parts = [top] + [pltpu.roll(top, 8 * k, 1) for k in range(1, CHUNK // 8)]
            toeplitz.append(jnp.concatenate(parts, 0).astype(BF16))
        inside = group_mask(modes, size)
        state = left_state(states_ref, flags_ref, rate, lanes, modes, size, count) if carried else None
        taps = tap_rows(taps_ref, 0, lanes)
        skip = skip_ref[:, lanes]
        lane_group = iota((CHUNK, LANES), 1) // size
        for chunk in range(chunks):
            start = chunk * CHUNK
            mixed = mixed_ref[start : start + CHUNK, lanes]
            same = same_ref[chunk]
            left = [t * same for t in toeplitz]
            right = [jnp.where(lane_group == g, mixed, jnp.zeros_like(mixed)) for g in range(groups)]
            if state is not None:
                left.append(entry * keep_ref[chunk])
                right.append(state.astype(BF16))
            longer = jnp.dot(jnp.concatenate(left, 1), jnp.concatenate(right, 0), preferred_element_type=F32)
            if chunk + 1 < chunks:
                fresh = jnp.dot((leave * tail_ref[chunk]).astype(BF16), mixed, preferred_element_type=F32)
                held = flags_ref[2 + chunk] == 1
                fresh = jnp.where(inside, fresh, 0.0)
                state = fresh if state is None else jnp.where(held, whole * state, 0.0) + fresh
            body = longer + skip * mixed.astype(F32)
            for half in range(start, start + CHUNK, SPAN):
                gate = short_conv(extended(x_ref, halo_ref, 0, half, lanes), taps, lag_masks(mask_ref, half))
                inner = body[half - start : half - start + SPAN]
                summed = residual_ref[half : half + SPAN, lanes].astype(F32) + gate * inner
                if carried:
                    hand_over(out_ref, squares_ref, slot_ref, summed, half, count // nblocks, lanes)
                else:
                    base_ref[half : half + SPAN, lanes] = summed
                    gate_ref[half : half + SPAN, lanes] = gate.astype(BF16)

    each_tile(width, tile)
    if carried:
        spare_ref[...] = out_ref[slot_ref[nblocks]]

        @pl.when(pl.program_id(0) == pl.num_programs(0) - 1)
        def _():
            for start in range(0, count, LANES):
                rows = squares_ref[start : start + LANES, :].T
                sums_ref[:, start : start + LANES] = jnp.sum(rows, 0, keepdims=True)


def add_kernel(
    modes, size, ndoc, nblocks,
    where_ref, lengths_ref, owner_ref,
    base_ref, gate_ref, rates_ref, residues_ref, states_ref,
    out_ref, spare_ref, squares_ref,
    keep_ref, flags_ref, slot_ref,
):
    count, width = base_ref.shape
    chunks = count // CHUNK
    step = step_rates(rates_ref, 0, width, size)
    step_residues = step_rates(residues_ref, 0, width, size)

    @pl.when(pl.program_id(0) == 0)
    def _():
        where = where_ref[0]
        ends = running_ends(lengths_ref, ndoc)
        write_flags(flags_ref, ends, where, count, nblocks)
        write_slots(slot_ref, owner_ref, where, nblocks)
        squares_ref[...] = jnp.zeros_like(squares_ref)
        before = scalar_document(ends, where * count - 1)
        kept = jnp.int32(0)
        for end in reversed(ends):
            kept = jnp.where(end >= where * count, end - where * count, kept)
        kept = jnp.where(before < 0, 0, kept)
        keep_ref[...] = jnp.where(iota((count, LANES), 0) < kept, 1.0, 0.0).astype(F32)

    def tile(lanes):
        rate = tile_rates(step, lanes.start, size)
        scale = tile_rates(step_residues, lanes.start, size) * jnp.sqrt(1.0 - jnp.exp(-2.0 * rate))
        down = iota((CHUNK, LANES), 0)
        entry = (scale.T * jnp.exp(-rate.T * (down + 1).astype(F32))).astype(BF16)
        whole = jnp.exp(-rate * CHUNK)
        state = left_state(states_ref, flags_ref, rate, lanes, modes, size, count)
        held = []
        for _ in range(chunks):
            held.append(state.astype(BF16))
            state = state * whole
        left = jnp.dot(entry, jnp.concatenate(held, 1), preferred_element_type=F32)
        for start in range(0, count, SPAN):
            low = start % CHUNK
            chunk = start // CHUNK
            carried = left[low : low + SPAN, chunk * LANES : (chunk + 1) * LANES] * keep_ref[start : start + SPAN, :]
            gate = gate_ref[start : start + SPAN, lanes].astype(F32)
            summed = base_ref[start : start + SPAN, lanes] + gate * carried
            hand_over(out_ref, squares_ref, slot_ref, summed, start, count // nblocks, lanes)

    each_tile(width, tile)
    spare_ref[...] = out_ref[slot_ref[nblocks]]


def norm_kernel(parts, where_ref, owner_ref, *refs):
    blocks, refs = refs[:parts], refs[parts:]
    spare_ref, gain_ref, out_ref = refs[:3]
    held, (done_ref, in_sems, out_sems) = refs[3 : 3 + parts], refs[3 + parts :]
    nblocks = blocks[0].shape[0]
    rows = out_ref.shape[0] // nblocks
    room = sum(block.shape[1] for block in blocks) - out_ref.shape[1] // LANES * rows

    def fetch(part, i, source):
        return pltpu.make_async_copy(source, held[part].at[i], in_sems.at[part, i])

    for i in range(nblocks):
        ahead = where_ref[0] - owner_ref[i]
        source = jnp.where(ahead < 0, ahead + nblocks, ahead)
        second = is_second(owner_ref, nblocks, i)
        low = 0
        for part in range(parts):
            size = blocks[part].shape[1]

            @pl.when(second)
            def _(part=part, i=i, low=low, size=size):
                fetch(part, i, spare_ref.at[pl.ds(low, size)]).start()

            @pl.when(jnp.logical_not(second))
            def _(part=part, i=i, source=source):
                fetch(part, i, blocks[part].at[source]).start()

            low += size

    def store(i):
        here = pl.ds(i * rows, rows)
        return pltpu.make_async_copy(done_ref.at[here], out_ref.at[here], out_sems.at[i])

    for i in range(nblocks):
        for part in range(parts):
            fetch(part, i, blocks[part].at[0]).wait()
        start = held[-1].shape[1] - room + i // 16 * 16
        halves = held[-1][i, start : start + 16, :].astype(F32)[i % 16 : i % 16 + 1]
        halves = jnp.broadcast_to(halves, (8, LANES))
        scale = halves + pltpu.roll(halves, LANES - rows, 1)
        scale = jnp.broadcast_to(scale[0:1], (LANES, LANES)).T[:rows]
        tile = 0
        for part in range(parts):
            for low in range(0, held[part].shape[1] - (room if part + 1 == parts else 0), rows):
                outs = slice(tile * LANES, (tile + 1) * LANES)
                value = held[part][i, low : low + rows, :].astype(F32)
                done_ref[i * rows : (i + 1) * rows, outs] = (value * scale * gain_ref[:, outs]).astype(BF16)
                tile += 1
        store(i).start()
    for i in range(nblocks):
        store(i).wait()


def params(limit=VMEM_LIMIT):
    return pltpu.CompilerParams(dimension_semantics=("arbitrary",), vmem_limit_bytes=limit)


def in_hbm(*arrays):
    return [pltpu.with_memory_space_constraint(array, pltpu.HBM) for array in arrays]


def in_vmem(array):
    return pltpu.with_memory_space_constraint(array, pltpu.VMEM)


def whole_array(rank):
    return lambda *_: (0,) * rank


def mix(scalars, x, halo, taps, rates, size, ndoc, copies):
    _, count, width = x.shape
    modes = rates.shape[0]
    wide = min(WIDE, width)
    deep = lambda t, *_: (0, 0, t)
    grid_spec = pltpu.PrefetchScalarGridSpec(
        num_scalar_prefetch=2,
        grid=(width // wide,),
        in_specs=[
            pl.BlockSpec((1, count, wide), lambda t, *_: (1, 0, t)),
            pl.BlockSpec((1, count, wide), lambda t, *_: (2, 0, t)),
            pl.BlockSpec((3, HALO, wide), deep),
            pl.BlockSpec((3, SHORT, wide), deep),
            pl.BlockSpec(rates.shape, whole_array(2)),
        ],
        out_specs=[
            pl.BlockSpec((count, wide), lambda t, *_: (0, t)),
            pl.BlockSpec((copies, modes, wide), deep),
        ],
        scratch_shapes=[
            pltpu.VMEM((count // SPAN, (NEAR - 1) * (SPAN + HALO), SPAN + 16), BF16),
            pltpu.VMEM((NEAR, count + 2 * HALO, LANES), F32),
            pltpu.VMEM((8, count), F32),
        ],
    )
    return pl.pallas_call(
        functools.partial(mix_kernel, modes, size, ndoc),
        grid_spec=grid_spec,
        out_shape=[pltpu.HBM((count, width), BF16), pltpu.HBM((copies, modes, width), BF16)],
        compiler_params=params(),
        cost_estimate=pl.CostEstimate(flops=60 * count * width, bytes_accessed=8 * count * width, transcendentals=count * width),
        name="mix",
    )(*scalars[:2], x, x, halo, taps, rates)


def conv(low, share, room, scalars, x, halo, taps, mixed, rates, residues, skip, residual, carried, size, ndoc, nblocks):
    _, count, width = x.shape
    modes = rates.shape[0]
    wide = math.gcd(math.gcd(low, share), WIDE)
    first = low // wide
    tile = lambda t, *_: (0, first + t)
    deep = lambda t, *_: (0, 0, first + t)
    step = pl.BlockSpec(rates.shape, whole_array(2))
    in_specs = [
        pl.BlockSpec((1, count, wide), deep),
        pl.BlockSpec((1, HALO, wide), deep),
        pl.BlockSpec((1, SHORT, wide), deep),
        pl.BlockSpec((count, wide), tile),
        step,
        step,
        pl.BlockSpec((1, wide), tile),
        pl.BlockSpec((count, wide), tile),
    ]
    operands = [x, halo, taps, mixed, rates, residues, skip, residual]
    scratch = [
        pltpu.VMEM((3, count + 2 * HALO, LANES), F32),
        pltpu.VMEM((count // CHUNK, CHUNK, CHUNK), BF16),
        pltpu.VMEM((count // CHUNK, CHUNK, LANES), BF16),
        pltpu.VMEM((count // CHUNK, LANES, CHUNK), F32),
        pltpu.SMEM((2 + count // CHUNK,), jnp.int32),
    ]
    if carried:
        states, squares = carried
        in_specs += [pl.BlockSpec((nblocks, modes, wide), deep), pl.BlockSpec((count, LANES), whole_array(2))]
        operands += [states, squares]
        scratch += [pltpu.SMEM((nblocks + 1,), jnp.int32), pltpu.VMEM((count, LANES), F32)]
        out_specs, out_shape = handed(share, room, wide, count, nblocks)
        out_specs[2] = pl.BlockSpec((1, count), whole_array(2))
        out_shape[2] = jax.ShapeDtypeStruct((1, count), F32)
    else:
        out_specs = [pl.BlockSpec((count, wide), lambda t, *_: (0, t))] * 2
        out_shape = [pltpu.VMEM((count, share), F32), pltpu.VMEM((count, share), BF16)]
    grid_spec = pltpu.PrefetchScalarGridSpec(
        num_scalar_prefetch=3, grid=(share // wide,), in_specs=in_specs, out_specs=out_specs, scratch_shapes=scratch
    )
    return pl.pallas_call(
        functools.partial(conv_kernel, modes, size, ndoc, nblocks, bool(carried), low // size),
        grid_spec=grid_spec,
        out_shape=out_shape,
        compiler_params=params(VMEM_LIMIT if carried else VMEM_LIMIT_BESIDE),
        cost_estimate=pl.CostEstimate(
            flops=2 * 1152 * count * share, bytes_accessed=8 * count * share, transcendentals=count * share
        ),
        name="conv",
    )(*scalars, *in_hbm(*operands))


def handed(share, room, wide, count, nblocks):
    rows = count // nblocks
    specs = [
        pl.BlockSpec((nblocks, wide // LANES * rows, LANES), lambda t, *_: (0, t, 0)),
        pl.BlockSpec((wide // LANES * rows, LANES), lambda t, *_: (t, 0)),
        pl.BlockSpec((count, LANES), whole_array(2)),
    ]
    shapes = [
        pltpu.HBM((nblocks, share // LANES * rows + room, LANES), BF16),
        pltpu.HBM((share // LANES * rows, LANES), BF16),
        pltpu.HBM((count, LANES), F32),
    ]
    return specs, shapes


def add(scalars, base, gate, rates, residues, states, size, ndoc, nblocks):
    count, share = base.shape
    modes = rates.shape[0]
    wide = math.gcd(share, WIDE)
    tile = lambda t, *_: (0, t)
    step = pl.BlockSpec(rates.shape, whole_array(2))
    out_specs, out_shape = handed(share, 0, wide, count, nblocks)
    grid_spec = pltpu.PrefetchScalarGridSpec(
        num_scalar_prefetch=3,
        grid=(share // wide,),
        in_specs=[
            pl.BlockSpec((count, wide), tile),
            pl.BlockSpec((count, wide), tile),
            step,
            step,
            pl.BlockSpec((nblocks, modes, wide), lambda t, *_: (0, 0, t)),
        ],
        out_specs=out_specs,
        scratch_shapes=[
            pltpu.VMEM((count, LANES), F32),
            pltpu.SMEM((2 + count // CHUNK,), jnp.int32),
            pltpu.SMEM((nblocks + 1,), jnp.int32),
        ],
    )
    return pl.pallas_call(
        functools.partial(add_kernel, modes, size, ndoc, nblocks),
        grid_spec=grid_spec,
        out_shape=out_shape,
        compiler_params=params(VMEM_LIMIT_BESIDE),
        cost_estimate=pl.CostEstimate(flops=300 * count * share, bytes_accessed=8 * count * share, transcendentals=count * share),
        name="add",
    )(*scalars, in_vmem(base), in_vmem(gate), *in_hbm(rates, residues, states))


def norm(where, owner, blocks, spare, gain, count):
    width = gain.shape[1]
    nblocks = blocks[0].shape[0]
    smem, vmem, anywhere = (pl.BlockSpec(memory_space=space) for space in (pltpu.SMEM, pltpu.VMEM, pl.ANY))
    return pl.pallas_call(
        functools.partial(norm_kernel, len(blocks)),
        in_specs=[smem, smem] + [anywhere] * (len(blocks) + 1) + [vmem],
        out_specs=anywhere,
        out_shape=jax.ShapeDtypeStruct((count, width), BF16),
        scratch_shapes=[pltpu.VMEM(block.shape, BF16) for block in blocks]
        + [
            pltpu.VMEM((count, width), BF16),
            pltpu.SemaphoreType.DMA((len(blocks), nblocks)),
            pltpu.SemaphoreType.DMA((nblocks,)),
        ],
        compiler_params=pltpu.CompilerParams(vmem_limit_bytes=VMEM_LIMIT),
        cost_estimate=pl.CostEstimate(flops=3 * count * width, bytes_accessed=4 * count * width, transcendentals=0),
        name="norm",
    )(where, owner, *blocks, spare, gain)


def on_device(features, residual, short_taps, rates, residues, skip, gain, lengths, owner):
    count, _, width = features.shape
    size = width // rates.shape[0]
    ndoc = lengths.shape[0]
    nblocks = lax.axis_size("ctx")
    rows = count // nblocks
    where = lax.axis_index("ctx")
    x = jnp.transpose(features, (1, 0, 2))
    pairs = [(i, i + 1) for i in range(nblocks - 1)]
    halo = lax.ppermute(x[:, count - HALO :], "ctx", pairs)

    scalars = (where.reshape(1).astype(jnp.int32), lengths, owner)
    spread = ((0, 0), (0, LANES - rates.shape[0]))
    rates, residues = jnp.pad(rates.T, spread), jnp.pad(residues.T, spread)

    offsets = owner[:nblocks]
    ids = jnp.arange(nblocks, dtype=jnp.int32)
    twice = jnp.any((offsets[:, None] == offsets[None, :]) & (ids[None, :] < ids[:, None]), 1)
    spare_shift = jnp.sum(jnp.where(twice, offsets, 0))

    def exchanged(value):
        return lax.all_to_all(value, "ctx", split_axis=0, concat_axis=0, tiled=True)

    first = width * SPLIT[0] // sum(SPLIT)
    second = width - first
    mixed, copies = mix(scalars, x, halo, short_taps, rates, size, ndoc, nblocks)
    states = exchanged(copies)
    shared = (scalars, x, halo, short_taps, mixed, rates, residues, skip.reshape(1, width), residual)
    base, gate = conv(0, first, 0, *shared, (), size, ndoc, nblocks)
    out, spare, squares = add(scalars, base, gate, rates, residues, states, size, ndoc, nblocks)
    block = exchanged(out)
    room = -(-nblocks // 16) * 16
    out, last_spare, sums = conv(first, second, room, *shared, (states, squares), size, ndoc, nblocks)
    mean = lax.psum(sums, "mp") / (width * lax.axis_size("mp"))
    inverse = lax.rsqrt(mean + EPS)
    high = lax.reduce_precision(inverse, 8, 7)
    halves = jnp.concatenate([high.reshape(nblocks, rows), (inverse - high).reshape(nblocks, rows)], 1)
    halves = jnp.pad(halves, ((0, room - nblocks), (0, LANES - 2 * rows))).astype(BF16)
    table = jnp.broadcast_to(halves[None], (nblocks, room, LANES))
    out = lax.dynamic_update_slice(out, table, (0, second // LANES * rows, 0))
    spares = jnp.concatenate([spare, last_spare, halves], 0)
    out, spares, spare_shift = lax.optimization_barrier((out, spares, spare_shift))
    last_block = exchanged(out)

    def moved(by):
        return lambda value: lax.ppermute(value, "ctx", [(s, (s + by) % nblocks) for s in range(nblocks)])

    spare = lax.switch(spare_shift, [lambda value: value] + [moved(d) for d in range(1, nblocks)], spares)
    return norm(scalars[0], owner, [block, last_block], spare, gain.reshape(1, width), count)


def solution(mesh):
    return jax.shard_map(
        on_device,
        mesh=mesh,
        in_specs=(
            P("ctx", None, "mp"),
            P("ctx", "mp"),
            P(None, None, "mp"),
            P("mp", None),
            P("mp", None),
            P("mp"),
            P("mp"),
            P(),
            P(),
        ),
        out_specs=P("ctx", "mp"),
        check_vma=False,
    )
```

```python
import functools
import math

import jax
import jax.numpy as jnp
from jax import lax
from jax.experimental import pallas as pl
from jax.experimental.pallas import tpu as pltpu
from jax.sharding import PartitionSpec as P

SHORT = 7
LANES = 128
CHUNK = 128
HALO = 8
EPS = 1e-06
SPLIT = (4, 4)
NEAR = 4
WIDE = 512
SPAN = 64
F32 = jnp.float32
BF16 = jnp.bfloat16
VMEM_LIMIT = 64 * 1024 * 1024
VMEM_LIMIT_BESIDE = 56 * 1024 * 1024


def iota(shape, dim):
    return lax.broadcasted_iota(jnp.int32, shape, dim)


def document(ends, positions):
    total = jnp.zeros(positions.shape, jnp.int32)
    for end in ends:
        total = total + (positions >= end).astype(jnp.int32)
    return total


def scalar_document(ends, position):
    total = jnp.int32(0)
    for end in ends:
        total = total + (position >= end).astype(jnp.int32)
    return jnp.where(position < 0, -1, total)


def running_ends(lengths_ref, ndoc):
    ends, total = [], jnp.int32(0)
    for j in range(ndoc):
        total = total + lengths_ref[j]
        ends.append(total)
    return ends


def write_lag_masks(mask_ref, ends, base, count):
    mask_ref[...] = jnp.ones_like(mask_ref)
    gap = jnp.zeros((1, LANES), F32)
    for end in ends:
        row = end - base + HALO

        @pl.when((row >= 0) & (row < count + HALO))
        def _(row=row):
            for lag in (1, 2, 3):
                for past in range(lag):
                    mask_ref[lag - 1, pl.ds(row + past, 1), :] = gap


def row_documents(ends, base, count):
    return document(ends, base + iota((8, count), 1)).astype(F32)


def is_second(owner_ref, nblocks, i):
    found = jnp.bool_(False)
    for j in range(i):
        found = found | (owner_ref[j] == owner_ref[i])
    return found


def write_slots(slot_ref, owner_ref, where, nblocks):
    unused = jnp.int32(nblocks * (nblocks - 1) // 2)
    seconds = [is_second(owner_ref, nblocks, i) for i in range(nblocks)]
    mine = [owner_ref[where * nblocks + i] for i in range(nblocks)]
    for i in range(nblocks):
        unused = unused - jnp.where(seconds[i], 0, mine[i])
    for i in range(nblocks):
        slot_ref[i] = jnp.where(seconds[i], unused, mine[i])
    slot_ref[nblocks] = unused


def step_rates(ref, origin, wide, size):
    first = origin + pl.program_id(0) * (wide // size)
    return pltpu.roll(ref[...], jnp.where(first == 0, 0, LANES - first), 1)


def tile_rates(rates, low, size):
    first = low // size
    columns = [rates[:, first + g : first + g + 1] for g in range(LANES // size)]
    return jnp.concatenate([jnp.broadcast_to(column, (column.shape[0], LANES)) for column in columns], 0)


def short_conv(ext, taps, masks):
    def back(value, lag):
        return pltpu.roll(value, lag, 0) * masks[lag - 1]

    one, two = back(ext, 1), back(ext, 2)
    far = ext * taps[6]
    middle = ext * taps[3] + one * taps[4] + two * taps[5] + back(far, 3)
    near = ext * taps[0] + one * taps[1] + two * taps[2] + back(middle, 3)
    return near[HALO:]


def extended(x_ref, halo_ref, which, start, lanes):
    rows = x_ref[0, start : start + SPAN, lanes].astype(F32)
    if start == 0:
        ahead = halo_ref[which, :, lanes].astype(F32)
    else:
        ahead = x_ref[0, start - 16 : start, lanes].astype(F32)[16 - HALO :]
    return jnp.concatenate([ahead, rows], 0)


def tap_rows(taps_ref, which, lanes):
    return [taps_ref[which, j : j + 1, lanes] for j in range(SHORT)]


def lag_masks(mask_ref, start):
    return [mask_ref[l, start : start + SPAN + HALO, :] for l in range(3)]


def group_mask(modes, size):
    return (iota((LANES, LANES), 0) // modes) == (iota((LANES, LANES), 1) // size)


def each_tile(width, body):
    for low in range(0, width, LANES):
        body(slice(low, low + LANES))


def write_shifts(shift_ref, mask_ref, ends, base, count):
    mask_ref[...] = jnp.ones_like(mask_ref)
    gap = jnp.zeros((1, LANES), F32)
    for end in ends:
        row = end - base + HALO

        @pl.when((row >= 0) & (row < count + HALO))
        def _(row=row):
            for lag in range(1, NEAR + 1):
                for past in range(lag):
                    mask_ref[lag - 1, pl.ds(row + past, 1), :] = gap

    reach = SPAN + HALO
    back = iota((reach, SPAN + 16), 0) + HALO - iota((reach, SPAN + 16), 1)
    for span in range(count // SPAN):
        moves = []
        for lag in range(1, NEAR):
            mask = mask_ref[lag - 1, span * SPAN : span * SPAN + reach, : SPAN + 16]
            moves.append(jnp.where(back == lag, mask, 0.0))
        shift_ref[span] = jnp.concatenate(moves, 0).astype(BF16)


def mix_kernel(
    modes, size, ndoc,
    where_ref, lengths_ref,
    key_ref, value_ref, halo_ref, taps_ref, rates_ref,
    mixed_ref, state_ref,
    shift_ref, mask_ref, tail_ref,
):
    _, count, width = key_ref.shape
    chunks = count // CHUNK
    reach = SPAN + HALO
    step = step_rates(rates_ref, 0, width, size)

    @pl.when(pl.program_id(0) == 0)
    def _():
        base = where_ref[0] * count
        ends = running_ends(lengths_ref, ndoc)
        write_shifts(shift_ref, mask_ref, ends, base, count)
        last = scalar_document(ends, base + count - 1).astype(F32)
        tail_ref[...] = jnp.where(row_documents(ends, base, count) == last, 1.0, 0.0).astype(F32)

    def window(x_ref, which, start, lanes):
        if start == 0:
            halo = halo_ref[which, :, lanes].astype(F32)
            ahead = jnp.concatenate([jnp.zeros((16 - HALO, LANES), F32), halo], 0).astype(BF16)
        else:
            ahead = x_ref[0, start - 16 : start, lanes]
        return jnp.concatenate([ahead, x_ref[0, start : start + SPAN, lanes]], 0)

    def finish(here, moved, taps, apart):
        rows = [here] + [moved[lag * reach : (lag + 1) * reach] for lag in range(NEAR - 1)]
        far = sum(rows[lag] * taps[NEAR + lag] for lag in range(SHORT - NEAR))
        far = pltpu.roll(far, NEAR, 0)[HALO:] * apart
        return far + sum(row[HALO:] * taps[lag] for lag, row in enumerate(rows))

    def tile(lanes):
        key_taps, value_taps = tap_rows(taps_ref, 1, lanes), tap_rows(taps_ref, 2, lanes)
        for start in range(0, count, SPAN):
            keys, values = window(key_ref, 1, start, lanes), window(value_ref, 2, start, lanes)
            moved = jnp.dot(shift_ref[start // SPAN], jnp.concatenate([keys, values], 1), preferred_element_type=F32)
            apart = mask_ref[NEAR - 1, HALO + start : HALO + start + SPAN, :]
            key = finish(keys.astype(F32)[16 - HALO :], moved[:, :LANES], key_taps, apart)
            value = finish(values.astype(F32)[16 - HALO :], moved[:, LANES:], value_taps, apart)
            mixed_ref[start : start + SPAN, lanes] = (key * value).astype(BF16)
        rate = tile_rates(step, lanes.start, size)
        leave = jnp.exp(-rate * (CHUNK - 1 - iota((LANES, CHUNK), 1)).astype(F32))
        whole = jnp.exp(-rate * CHUNK)
        spans = []
        for chunk in reversed(range(chunks)):
            tail = tail_ref[0:1, chunk * CHUNK : (chunk + 1) * CHUNK]
            spans.append((leave * tail).astype(BF16))
            leave = leave * whole
        full = jnp.dot(jnp.concatenate(spans[::-1], 1), mixed_ref[:, lanes], preferred_element_type=F32)
        full = jnp.where(group_mask(modes, size), full, 0.0)
        state = jnp.sum(full.reshape(LANES // modes, modes, LANES), 0).astype(BF16)
        for owner in range(state_ref.shape[0]):
            state_ref[owner, :, lanes] = state

    each_tile(width, tile)


def left_state(states_ref, flags_ref, rate, lanes, modes, size, count):
    inside = group_mask(modes, size)
    decay = jnp.exp(-rate * count)
    total = jnp.zeros((LANES, LANES), F32)
    for back in range(states_ref.shape[0] // 2, 0, -1):
        v = flags_ref[1] - back
        piece = jnp.concatenate([states_ref[jnp.maximum(v, 0), :, lanes].astype(F32)] * (LANES // modes), 0)
        total = jnp.where(inside & (v >= flags_ref[0]), piece + decay * total, 0.0)
    return total


def write_flags(flags_ref, ends, where, count, nblocks):
    before = scalar_document(ends, where * count - 1)
    first = jnp.int32(0)
    for v in range(nblocks):
        first = first + (scalar_document(ends, (v + 1) * count - 1) < before).astype(jnp.int32)
    flags_ref[0] = first
    flags_ref[1] = where
    for chunk in range(count // CHUNK):
        start = where * count + chunk * CHUNK
        held = scalar_document(ends, start - 1) == scalar_document(ends, start + CHUNK - 1)
        flags_ref[2 + chunk] = held.astype(jnp.int32)


def hand_over(out_ref, squares_ref, slot_ref, summed, start, rows, lanes):
    squares_ref[start : start + SPAN, :] += summed * summed
    rounded = summed.astype(BF16)
    for b in range(SPAN // rows):
        tile = lanes.start // LANES * rows
        out_ref[slot_ref[start // rows + b], tile : tile + rows, :] = rounded[b * rows : (b + 1) * rows]


def conv_kernel(modes, size, ndoc, nblocks, carried, origin, where_ref, lengths_ref, owner_ref, *refs):
    x_ref, halo_ref, taps_ref, mixed_ref, rates_ref, residues_ref, skip_ref, residual_ref = refs[:8]
    refs = refs[8:]
    if carried:
        states_ref, before_ref, out_ref, spare_ref, sums_ref = refs[:5]
        refs = refs[5:]
    else:
        base_ref, gate_ref = refs[:2]
        refs = refs[2:]
    mask_ref, same_ref, keep_ref, tail_ref, flags_ref = refs[:5]
    if carried:
        slot_ref, squares_ref = refs[5:]
    count, width = mixed_ref.shape
    chunks = count // CHUNK
    step = step_rates(rates_ref, origin, width, size)
    step_residues = step_rates(residues_ref, origin, width, size)

    @pl.when(pl.program_id(0) == 0)
    def _():
        where = where_ref[0]
        base = where * count
        ends = running_ends(lengths_ref, ndoc)
        write_lag_masks(mask_ref, ends, base, count)
        write_flags(flags_ref, ends, where, count, nblocks)
        if carried:
            write_slots(slot_ref, owner_ref, where, nblocks)
            squares_ref[...] = before_ref[...]
        documents = row_documents(ends, base, count)
        causal = iota((CHUNK, CHUNK), 1) <= iota((CHUNK, CHUNK), 0)
        for chunk in range(chunks):
            start = base + chunk * CHUNK
            there = jnp.broadcast_to(documents[0:1, chunk * CHUNK : (chunk + 1) * CHUNK], (CHUNK, CHUNK))
            here = there.T
            same_ref[chunk] = jnp.where((here == there) & causal, 1.0, 0.0).astype(BF16)
            before = scalar_document(ends, start - 1).astype(F32)
            keep_ref[chunk] = jnp.where(here == before, 1.0, 0.0).astype(BF16)
            last = scalar_document(ends, start + CHUNK - 1).astype(F32)
            tail_ref[chunk] = jnp.where(there == last, 1.0, 0.0).astype(F32)

    groups = LANES // modes

    def tile(lanes):
        rate = tile_rates(step, lanes.start, size)
        scale = tile_rates(step_residues, lanes.start, size) * jnp.sqrt(1.0 - jnp.exp(-2.0 * rate))
        down = iota((CHUNK, LANES), 0)
        along = iota((LANES, CHUNK), 1)
        entry = (scale.T * jnp.exp(-rate.T * (down + 1).astype(F32))).astype(BF16)
        leave = jnp.exp(-rate * (CHUNK - 1 - along).astype(F32))
        whole = jnp.exp(-rate * CHUNK)
        terms = scale * jnp.where(along == 0, 1.0, leave * jnp.exp(-rate))
        toeplitz = []
        for g in range(groups):
            line = jnp.sum(terms[g * modes : (g + 1) * modes], 0, keepdims=True)
            top = pltpu.roll(jnp.broadcast_to(line, (8, CHUNK)), 0, 1, stride=1, stride_axis=0)
            parts = [top] + [pltpu.roll(top, 8 * k, 1) for k in range(1, CHUNK // 8)]
            toeplitz.append(jnp.concatenate(parts, 0).astype(BF16))
        inside = group_mask(modes, size)
        state = left_state(states_ref, flags_ref, rate, lanes, modes, size, count) if carried else None
        taps = tap_rows(taps_ref, 0, lanes)
        skip = skip_ref[:, lanes]
        lane_group = iota((CHUNK, LANES), 1) // size
        for chunk in range(chunks):
            start = chunk * CHUNK
            mixed = mixed_ref[start : start + CHUNK, lanes]
            same = same_ref[chunk]
            left = [t * same for t in toeplitz]
            right = [jnp.where(lane_group == g, mixed, jnp.zeros_like(mixed)) for g in range(groups)]
            if state is not None:
                left.append(entry * keep_ref[chunk])
                right.append(state.astype(BF16))
            longer = jnp.dot(jnp.concatenate(left, 1), jnp.concatenate(right, 0), preferred_element_type=F32)
            if chunk + 1 < chunks:
                fresh = jnp.dot((leave * tail_ref[chunk]).astype(BF16), mixed, preferred_element_type=F32)
                held = flags_ref[2 + chunk] == 1
                fresh = jnp.where(inside, fresh, 0.0)
                state = fresh if state is None else jnp.where(held, whole * state, 0.0) + fresh
            body = longer + skip * mixed.astype(F32)
            for half in range(start, start + CHUNK, SPAN):
                gate = short_conv(extended(x_ref, halo_ref, 0, half, lanes), taps, lag_masks(mask_ref, half))
                inner = body[half - start : half - start + SPAN]
                summed = residual_ref[half : half + SPAN, lanes].astype(F32) + gate * inner
                if carried:
                    hand_over(out_ref, squares_ref, slot_ref, summed, half, count // nblocks, lanes)
                else:
                    base_ref[half : half + SPAN, lanes] = summed
                    gate_ref[half : half + SPAN, lanes] = gate.astype(BF16)

    each_tile(width, tile)
    if carried:
        spare_ref[...] = out_ref[slot_ref[nblocks]]

        @pl.when(pl.program_id(0) == pl.num_programs(0) - 1)
        def _():
            for start in range(0, count, LANES):
                rows = squares_ref[start : start + LANES, :].T
                sums_ref[:, start : start + LANES] = jnp.sum(rows, 0, keepdims=True)


def add_kernel(
    modes, size, ndoc, nblocks,
    where_ref, lengths_ref, owner_ref,
    base_ref, gate_ref, rates_ref, residues_ref, states_ref,
    out_ref, spare_ref, squares_ref,
    keep_ref, flags_ref, slot_ref,
):
    count, width = base_ref.shape
    chunks = count // CHUNK
    step = step_rates(rates_ref, 0, width, size)
    step_residues = step_rates(residues_ref, 0, width, size)

    @pl.when(pl.program_id(0) == 0)
    def _():
        where = where_ref[0]
        ends = running_ends(lengths_ref, ndoc)
        write_flags(flags_ref, ends, where, count, nblocks)
        write_slots(slot_ref, owner_ref, where, nblocks)
        squares_ref[...] = jnp.zeros_like(squares_ref)
        before = scalar_document(ends, where * count - 1)
        kept = jnp.int32(0)
        for end in reversed(ends):
            kept = jnp.where(end >= where * count, end - where * count, kept)
        kept = jnp.where(before < 0, 0, kept)
        keep_ref[...] = jnp.where(iota((count, LANES), 0) < kept, 1.0, 0.0).astype(F32)

    def tile(lanes):
        rate = tile_rates(step, lanes.start, size)
        scale = tile_rates(step_residues, lanes.start, size) * jnp.sqrt(1.0 - jnp.exp(-2.0 * rate))
        down = iota((CHUNK, LANES), 0)
        entry = (scale.T * jnp.exp(-rate.T * (down + 1).astype(F32))).astype(BF16)
        whole = jnp.exp(-rate * CHUNK)
        state = left_state(states_ref, flags_ref, rate, lanes, modes, size, count)
        held = []
        for _ in range(chunks):
            held.append(state.astype(BF16))
            state = state * whole
        left = jnp.dot(entry, jnp.concatenate(held, 1), preferred_element_type=F32)
        for start in range(0, count, SPAN):
            low = start % CHUNK
            chunk = start // CHUNK
            carried = left[low : low + SPAN, chunk * LANES : (chunk + 1) * LANES] * keep_ref[start : start + SPAN, :]
            gate = gate_ref[start : start + SPAN, lanes].astype(F32)
            summed = base_ref[start : start + SPAN, lanes] + gate * carried
            hand_over(out_ref, squares_ref, slot_ref, summed, start, count // nblocks, lanes)

    each_tile(width, tile)
    spare_ref[...] = out_ref[slot_ref[nblocks]]


def norm_kernel(parts, where_ref, owner_ref, *refs):
    blocks, refs = refs[:parts], refs[parts:]
    spare_ref, gain_ref, out_ref = refs[:3]
    held, (done_ref, in_sems, out_sems) = refs[3 : 3 + parts], refs[3 + parts :]
    nblocks = blocks[0].shape[0]
    rows = out_ref.shape[0] // nblocks
    room = sum(block.shape[1] for block in blocks) - out_ref.shape[1] // LANES * rows

    def fetch(part, i, source):
        return pltpu.make_async_copy(source, held[part].at[i], in_sems.at[part, i])

    for i in range(nblocks):
        ahead = where_ref[0] - owner_ref[i]
        source = jnp.where(ahead < 0, ahead + nblocks, ahead)
        second = is_second(owner_ref, nblocks, i)
        low = 0
        for part in range(parts):
            size = blocks[part].shape[1]

            @pl.when(second)
            def _(part=part, i=i, low=low, size=size):
                fetch(part, i, spare_ref.at[pl.ds(low, size)]).start()

            @pl.when(jnp.logical_not(second))
            def _(part=part, i=i, source=source):
                fetch(part, i, blocks[part].at[source]).start()

            low += size

    def store(i):
        here = pl.ds(i * rows, rows)
        return pltpu.make_async_copy(done_ref.at[here], out_ref.at[here], out_sems.at[i])

    for i in range(nblocks):
        for part in range(parts):
            fetch(part, i, blocks[part].at[0]).wait()
        start = held[-1].shape[1] - room + i // 16 * 16
        halves = held[-1][i, start : start + 16, :].astype(F32)[i % 16 : i % 16 + 1]
        halves = jnp.broadcast_to(halves, (8, LANES))
        scale = halves + pltpu.roll(halves, LANES - rows, 1)
        scale = jnp.broadcast_to(scale[0:1], (LANES, LANES)).T[:rows]
        tile = 0
        for part in range(parts):
            for low in range(0, held[part].shape[1] - (room if part + 1 == parts else 0), rows):
                outs = slice(tile * LANES, (tile + 1) * LANES)
                value = held[part][i, low : low + rows, :].astype(F32)
                done_ref[i * rows : (i + 1) * rows, outs] = (value * scale * gain_ref[:, outs]).astype(BF16)
                tile += 1
        store(i).start()
    for i in range(nblocks):
        store(i).wait()


def params(limit=VMEM_LIMIT):
    return pltpu.CompilerParams(dimension_semantics=("arbitrary",), vmem_limit_bytes=limit)


def in_hbm(*arrays):
    return [pltpu.with_memory_space_constraint(array, pltpu.HBM) for array in arrays]


def in_vmem(array):
    return pltpu.with_memory_space_constraint(array, pltpu.VMEM)


def whole_array(rank):
    return lambda *_: (0,) * rank


def mix(scalars, x, halo, taps, rates, size, ndoc, copies):
    _, count, width = x.shape
    modes = rates.shape[0]
    wide = min(WIDE, width)
    deep = lambda t, *_: (0, 0, t)
    grid_spec = pltpu.PrefetchScalarGridSpec(
        num_scalar_prefetch=2,
        grid=(width // wide,),
        in_specs=[
            pl.BlockSpec((1, count, wide), lambda t, *_: (1, 0, t)),
            pl.BlockSpec((1, count, wide), lambda t, *_: (2, 0, t)),
            pl.BlockSpec((3, HALO, wide), deep),
            pl.BlockSpec((3, SHORT, wide), deep),
            pl.BlockSpec(rates.shape, whole_array(2)),
        ],
        out_specs=[
            pl.BlockSpec((count, wide), lambda t, *_: (0, t)),
            pl.BlockSpec((copies, modes, wide), deep),
        ],
        scratch_shapes=[
            pltpu.VMEM((count // SPAN, (NEAR - 1) * (SPAN + HALO), SPAN + 16), BF16),
            pltpu.VMEM((NEAR, count + 2 * HALO, LANES), F32),
            pltpu.VMEM((8, count), F32),
        ],
    )
    return pl.pallas_call(
        functools.partial(mix_kernel, modes, size, ndoc),
        grid_spec=grid_spec,
        out_shape=[pltpu.HBM((count, width), BF16), pltpu.HBM((copies, modes, width), BF16)],
        compiler_params=params(),
        cost_estimate=pl.CostEstimate(flops=60 * count * width, bytes_accessed=8 * count * width, transcendentals=count * width),
        name="mix",
    )(*scalars[:2], x, x, halo, taps, rates)


def conv(low, share, room, scalars, x, halo, taps, mixed, rates, residues, skip, residual, carried, size, ndoc, nblocks):
    _, count, width = x.shape
    modes = rates.shape[0]
    wide = math.gcd(math.gcd(low, share), WIDE)
    first = low // wide
    tile = lambda t, *_: (0, first + t)
    deep = lambda t, *_: (0, 0, first + t)
    step = pl.BlockSpec(rates.shape, whole_array(2))
    in_specs = [
        pl.BlockSpec((1, count, wide), deep),
        pl.BlockSpec((1, HALO, wide), deep),
        pl.BlockSpec((1, SHORT, wide), deep),
        pl.BlockSpec((count, wide), tile),
        step,
        step,
        pl.BlockSpec((1, wide), tile),
        pl.BlockSpec((count, wide), tile),
    ]
    operands = [x, halo, taps, mixed, rates, residues, skip, residual]
    scratch = [
        pltpu.VMEM((3, count + 2 * HALO, LANES), F32),
        pltpu.VMEM((count // CHUNK, CHUNK, CHUNK), BF16),
        pltpu.VMEM((count // CHUNK, CHUNK, LANES), BF16),
        pltpu.VMEM((count // CHUNK, LANES, CHUNK), F32),
        pltpu.SMEM((2 + count // CHUNK,), jnp.int32),
    ]
    if carried:
        states, squares = carried
        in_specs += [pl.BlockSpec((nblocks, modes, wide), deep), pl.BlockSpec((count, LANES), whole_array(2))]
        operands += [states, squares]
        scratch += [pltpu.SMEM((nblocks + 1,), jnp.int32), pltpu.VMEM((count, LANES), F32)]
        out_specs, out_shape = handed(share, room, wide, count, nblocks)
        out_specs[2] = pl.BlockSpec((1, count), whole_array(2))
        out_shape[2] = jax.ShapeDtypeStruct((1, count), F32)
    else:
        out_specs = [pl.BlockSpec((count, wide), lambda t, *_: (0, t))] * 2
        out_shape = [pltpu.VMEM((count, share), F32), pltpu.VMEM((count, share), BF16)]
    grid_spec = pltpu.PrefetchScalarGridSpec(
        num_scalar_prefetch=3, grid=(share // wide,), in_specs=in_specs, out_specs=out_specs, scratch_shapes=scratch
    )
    return pl.pallas_call(
        functools.partial(conv_kernel, modes, size, ndoc, nblocks, bool(carried), low // size),
        grid_spec=grid_spec,
        out_shape=out_shape,
        compiler_params=params(VMEM_LIMIT if carried else VMEM_LIMIT_BESIDE),
        cost_estimate=pl.CostEstimate(
            flops=2 * 1152 * count * share, bytes_accessed=8 * count * share, transcendentals=count * share
        ),
        name="conv",
    )(*scalars, *in_hbm(*operands))


def handed(share, room, wide, count, nblocks):
    rows = count // nblocks
    specs = [
        pl.BlockSpec((nblocks, wide // LANES * rows, LANES), lambda t, *_: (0, t, 0)),
        pl.BlockSpec((wide // LANES * rows, LANES), lambda t, *_: (t, 0)),
        pl.BlockSpec((count, LANES), whole_array(2)),
    ]
    shapes = [
        pltpu.HBM((nblocks, share // LANES * rows + room, LANES), BF16),
        pltpu.HBM((share // LANES * rows, LANES), BF16),
        pltpu.HBM((count, LANES), F32),
    ]
    return specs, shapes


def add(scalars, base, gate, rates, residues, states, size, ndoc, nblocks):
    count, share = base.shape
    modes = rates.shape[0]
    wide = math.gcd(share, WIDE)
    tile = lambda t, *_: (0, t)
    step = pl.BlockSpec(rates.shape, whole_array(2))
    out_specs, out_shape = handed(share, 0, wide, count, nblocks)
    grid_spec = pltpu.PrefetchScalarGridSpec(
        num_scalar_prefetch=3,
        grid=(share // wide,),
        in_specs=[
            pl.BlockSpec((count, wide), tile),
            pl.BlockSpec((count, wide), tile),
            step,
            step,
            pl.BlockSpec((nblocks, modes, wide), lambda t, *_: (0, 0, t)),
        ],
        out_specs=out_specs,
        scratch_shapes=[
            pltpu.VMEM((count, LANES), F32),
            pltpu.SMEM((2 + count // CHUNK,), jnp.int32),
            pltpu.SMEM((nblocks + 1,), jnp.int32),
        ],
    )
    return pl.pallas_call(
        functools.partial(add_kernel, modes, size, ndoc, nblocks),
        grid_spec=grid_spec,
        out_shape=out_shape,
        compiler_params=params(VMEM_LIMIT_BESIDE),
        cost_estimate=pl.CostEstimate(flops=300 * count * share, bytes_accessed=8 * count * share, transcendentals=count * share),
        name="add",
    )(*scalars, in_vmem(base), in_vmem(gate), *in_hbm(rates, residues, states))


def norm(where, owner, blocks, spare, gain, count):
    width = gain.shape[1]
    nblocks = blocks[0].shape[0]
    smem, vmem, anywhere = (pl.BlockSpec(memory_space=space) for space in (pltpu.SMEM, pltpu.VMEM, pl.ANY))
    return pl.pallas_call(
        functools.partial(norm_kernel, len(blocks)),
        in_specs=[smem, smem] + [anywhere] * (len(blocks) + 1) + [vmem],
        out_specs=anywhere,
        out_shape=jax.ShapeDtypeStruct((count, width), BF16),
        scratch_shapes=[pltpu.VMEM(block.shape, BF16) for block in blocks]
        + [
            pltpu.VMEM((count, width), BF16),
            pltpu.SemaphoreType.DMA((len(blocks), nblocks)),
            pltpu.SemaphoreType.DMA((nblocks,)),
        ],
        compiler_params=pltpu.CompilerParams(vmem_limit_bytes=24 * 1024 * 1024),
        cost_estimate=pl.CostEstimate(flops=3 * count * width, bytes_accessed=4 * count * width, transcendentals=0),
        name="norm",
    )(where, owner, *in_hbm(*blocks), spare, gain)


def on_device(features, residual, short_taps, rates, residues, skip, gain, lengths, owner):
    count, _, width = features.shape
    size = width // rates.shape[0]
    ndoc = lengths.shape[0]
    nblocks = lax.axis_size("ctx")
    rows = count // nblocks
    where = lax.axis_index("ctx")
    x = jnp.transpose(features, (1, 0, 2))
    pairs = [(i, i + 1) for i in range(nblocks - 1)]
    halo = lax.ppermute(x[:, count - HALO :], "ctx", pairs)

    scalars = (where.reshape(1).astype(jnp.int32), lengths, owner)
    spread = ((0, 0), (0, LANES - rates.shape[0]))
    rates, residues = jnp.pad(rates.T, spread), jnp.pad(residues.T, spread)

    offsets = owner[:nblocks]
    ids = jnp.arange(nblocks, dtype=jnp.int32)
    twice = jnp.any((offsets[:, None] == offsets[None, :]) & (ids[None, :] < ids[:, None]), 1)
    spare_shift = jnp.sum(jnp.where(twice, offsets, 0))

    def exchanged(value):
        return lax.all_to_all(value, "ctx", split_axis=0, concat_axis=0, tiled=True)

    first = width * SPLIT[0] // sum(SPLIT)
    second = width - first
    mixed, copies = mix(scalars, x, halo, short_taps, rates, size, ndoc, nblocks)
    states = exchanged(copies)
    shared = (scalars, x, halo, short_taps, mixed, rates, residues, skip.reshape(1, width), residual)
    base, gate = conv(0, first, 0, *shared, (), size, ndoc, nblocks)
    out, spare, squares = add(scalars, base, gate, rates, residues, states, size, ndoc, nblocks)
    block = exchanged(out)
    room = -(-nblocks // 16) * 16
    out, last_spare, sums = conv(first, second, room, *shared, (states, squares), size, ndoc, nblocks)
    mean = lax.psum(sums, "mp") / (width * lax.axis_size("mp"))
    inverse = lax.rsqrt(mean + EPS)
    high = lax.reduce_precision(inverse, 8, 7)
    halves = jnp.concatenate([high.reshape(nblocks, rows), (inverse - high).reshape(nblocks, rows)], 1)
    halves = jnp.pad(halves, ((0, room - nblocks), (0, LANES - 2 * rows))).astype(BF16)
    table = jnp.broadcast_to(halves[None], (nblocks, room, LANES))
    out = lax.dynamic_update_slice(out, table, (0, second // LANES * rows, 0))
    spares = jnp.concatenate([spare, last_spare, halves], 0)
    out, spares, spare_shift = lax.optimization_barrier((out, spares, spare_shift))
    last_block = exchanged(out)

    def moved(by):
        return lambda value: lax.ppermute(value, "ctx", [(s, (s + by) % nblocks) for s in range(nblocks)])

    spare = lax.switch(spare_shift, [lambda value: value] + [moved(d) for d in range(1, nblocks)], spares)
    return norm(scalars[0], owner, [block, last_block], spare, gain.reshape(1, width), count)


def solution(mesh):
    return jax.shard_map(
        on_device,
        mesh=mesh,
        in_specs=(
            P("ctx", None, "mp"),
            P("ctx", "mp"),
            P(None, None, "mp"),
            P("mp", None),
            P("mp", None),
            P("mp"),
            P("mp"),
            P(),
            P(),
        ),
        out_specs=P("ctx", "mp"),
        check_vma=False,
    )
```

```python
import functools
import math

import jax
import jax.numpy as jnp
from jax import lax
from jax.experimental import pallas as pl
from jax.experimental.pallas import tpu as pltpu
from jax.sharding import PartitionSpec as P

SHORT = 7
LANES = 128
CHUNK = 128
HALO = 8
EPS = 1e-06
SPLIT = (4, 4)
NEAR = 4
WIDE = 512
SPAN = 64
F32 = jnp.float32
BF16 = jnp.bfloat16
VMEM_LIMIT = 64 * 1024 * 1024
VMEM_LIMIT_BESIDE = 56 * 1024 * 1024


def iota(shape, dim):
    return lax.broadcasted_iota(jnp.int32, shape, dim)


def document(ends, positions):
    total = jnp.zeros(positions.shape, jnp.int32)
    for end in ends:
        total = total + (positions >= end).astype(jnp.int32)
    return total


def scalar_document(ends, position):
    total = jnp.int32(0)
    for end in ends:
        total = total + (position >= end).astype(jnp.int32)
    return jnp.where(position < 0, -1, total)


def running_ends(lengths_ref, ndoc):
    ends, total = [], jnp.int32(0)
    for j in range(ndoc):
        total = total + lengths_ref[j]
        ends.append(total)
    return ends


def write_lag_masks(mask_ref, ends, base, count):
    mask_ref[...] = jnp.ones_like(mask_ref)
    gap = jnp.zeros((1, LANES), F32)
    for end in ends:
        row = end - base + HALO

        @pl.when((row >= 0) & (row < count + HALO))
        def _(row=row):
            for lag in (1, 2, 3):
                for past in range(lag):
                    mask_ref[lag - 1, pl.ds(row + past, 1), :] = gap


def row_documents(ends, base, count):
    return document(ends, base + iota((8, count), 1)).astype(F32)


def is_second(owner_ref, nblocks, i):
    found = jnp.bool_(False)
    for j in range(i):
        found = found | (owner_ref[j] == owner_ref[i])
    return found


def write_slots(slot_ref, owner_ref, where, nblocks):
    unused = jnp.int32(nblocks * (nblocks - 1) // 2)
    seconds = [is_second(owner_ref, nblocks, i) for i in range(nblocks)]
    mine = [owner_ref[where * nblocks + i] for i in range(nblocks)]
    for i in range(nblocks):
        unused = unused - jnp.where(seconds[i], 0, mine[i])
    for i in range(nblocks):
        slot_ref[i] = jnp.where(seconds[i], unused, mine[i])
    slot_ref[nblocks] = unused


def step_rates(ref, origin, wide, size):
    first = origin + pl.program_id(0) * (wide // size)
    return pltpu.roll(ref[...], jnp.where(first == 0, 0, LANES - first), 1)


def tile_rates(rates, low, size):
    first = low // size
    columns = [rates[:, first + g : first + g + 1] for g in range(LANES // size)]
    return jnp.concatenate([jnp.broadcast_to(column, (column.shape[0], LANES)) for column in columns], 0)


def short_conv(ext, taps, masks):
    def back(value, lag):
        return pltpu.roll(value, lag, 0) * masks[lag - 1]

    one, two = back(ext, 1), back(ext, 2)
    far = ext * taps[6]
    middle = ext * taps[3] + one * taps[4] + two * taps[5] + back(far, 3)
    near = ext * taps[0] + one * taps[1] + two * taps[2] + back(middle, 3)
    return near[HALO:]


def extended(x_ref, halo_ref, which, start, lanes):
    rows = x_ref[0, start : start + SPAN, lanes].astype(F32)
    if start == 0:
        ahead = halo_ref[which, :, lanes].astype(F32)
    else:
        ahead = x_ref[0, start - 16 : start, lanes].astype(F32)[16 - HALO :]
    return jnp.concatenate([ahead, rows], 0)


def tap_rows(taps_ref, which, lanes):
    return [taps_ref[which, j : j + 1, lanes] for j in range(SHORT)]


def lag_masks(mask_ref, start):
    return [mask_ref[l, start : start + SPAN + HALO, :] for l in range(3)]


def group_mask(modes, size):
    return (iota((LANES, LANES), 0) // modes) == (iota((LANES, LANES), 1) // size)


def each_tile(width, body):
    for low in range(0, width, LANES):
        body(slice(low, low + LANES))


def write_shifts(shift_ref, mask_ref, ends, base, count):
    mask_ref[...] = jnp.ones_like(mask_ref)
    gap = jnp.zeros((1, LANES), F32)
    for end in ends:
        row = end - base + HALO

        @pl.when((row >= 0) & (row < count + HALO))
        def _(row=row):
            for lag in range(1, NEAR + 1):
                for past in range(lag):
                    mask_ref[lag - 1, pl.ds(row + past, 1), :] = gap

    reach = SPAN + HALO
    back = iota((reach, SPAN + 16), 0) + HALO - iota((reach, SPAN + 16), 1)
    for span in range(count // SPAN):
        moves = []
        for lag in range(1, NEAR):
            mask = mask_ref[lag - 1, span * SPAN : span * SPAN + reach, : SPAN + 16]
            moves.append(jnp.where(back == lag, mask, 0.0))
        shift_ref[span] = jnp.concatenate(moves, 0).astype(BF16)


def mix_kernel(
    modes, size, ndoc,
    where_ref, lengths_ref,
    key_ref, value_ref, halo_ref, taps_ref, rates_ref,
    mixed_ref, state_ref,
    shift_ref, mask_ref, tail_ref,
):
    _, count, width = key_ref.shape
    chunks = count // CHUNK
    reach = SPAN + HALO
    step = step_rates(rates_ref, 0, width, size)

    @pl.when(pl.program_id(0) == 0)
    def _():
        base = where_ref[0] * count
        ends = running_ends(lengths_ref, ndoc)
        write_shifts(shift_ref, mask_ref, ends, base, count)
        last = scalar_document(ends, base + count - 1).astype(F32)
        tail_ref[...] = jnp.where(row_documents(ends, base, count) == last, 1.0, 0.0).astype(F32)

    def window(x_ref, which, start, lanes):
        if start == 0:
            halo = halo_ref[which, :, lanes].astype(F32)
            ahead = jnp.concatenate([jnp.zeros((16 - HALO, LANES), F32), halo], 0).astype(BF16)
        else:
            ahead = x_ref[0, start - 16 : start, lanes]
        return jnp.concatenate([ahead, x_ref[0, start : start + SPAN, lanes]], 0)

    def finish(here, moved, taps, apart):
        rows = [here] + [moved[lag * reach : (lag + 1) * reach] for lag in range(NEAR - 1)]
        far = sum(rows[lag] * taps[NEAR + lag] for lag in range(SHORT - NEAR))
        far = pltpu.roll(far, NEAR, 0)[HALO:] * apart
        return far + sum(row[HALO:] * taps[lag] for lag, row in enumerate(rows))

    def tile(lanes):
        key_taps, value_taps = tap_rows(taps_ref, 1, lanes), tap_rows(taps_ref, 2, lanes)
        for start in range(0, count, SPAN):
            keys, values = window(key_ref, 1, start, lanes), window(value_ref, 2, start, lanes)
            moved = jnp.dot(shift_ref[start // SPAN], jnp.concatenate([keys, values], 1), preferred_element_type=F32)
            apart = mask_ref[NEAR - 1, HALO + start : HALO + start + SPAN, :]
            key = finish(keys.astype(F32)[16 - HALO :], moved[:, :LANES], key_taps, apart)
            value = finish(values.astype(F32)[16 - HALO :], moved[:, LANES:], value_taps, apart)
            mixed_ref[start : start + SPAN, lanes] = (key * value).astype(BF16)
        rate = tile_rates(step, lanes.start, size)
        leave = jnp.exp(-rate * (CHUNK - 1 - iota((LANES, CHUNK), 1)).astype(F32))
        whole = jnp.exp(-rate * CHUNK)
        spans = []
        for chunk in reversed(range(chunks)):
            tail = tail_ref[0:1, chunk * CHUNK : (chunk + 1) * CHUNK]
            spans.append((leave * tail).astype(BF16))
            leave = leave * whole
        full = jnp.dot(jnp.concatenate(spans[::-1], 1), mixed_ref[:, lanes], preferred_element_type=F32)
        full = jnp.where(group_mask(modes, size), full, 0.0)
        state = jnp.sum(full.reshape(LANES // modes, modes, LANES), 0).astype(BF16)
        for owner in range(state_ref.shape[0]):
            state_ref[owner, :, lanes] = state

    each_tile(width, tile)


def left_state(states_ref, flags_ref, rate, lanes, modes, size, count):
    inside = group_mask(modes, size)
    decay = jnp.exp(-rate * count)
    total = jnp.zeros((LANES, LANES), F32)
    for back in range(states_ref.shape[0] // 2, 0, -1):
        v = flags_ref[1] - back
        piece = jnp.concatenate([states_ref[jnp.maximum(v, 0), :, lanes].astype(F32)] * (LANES // modes), 0)
        total = jnp.where(inside & (v >= flags_ref[0]), piece + decay * total, 0.0)
    return total


def write_flags(flags_ref, ends, where, count, nblocks):
    before = scalar_document(ends, where * count - 1)
    first = jnp.int32(0)
    for v in range(nblocks):
        first = first + (scalar_document(ends, (v + 1) * count - 1) < before).astype(jnp.int32)
    flags_ref[0] = first
    flags_ref[1] = where
    for chunk in range(count // CHUNK):
        start = where * count + chunk * CHUNK
        held = scalar_document(ends, start - 1) == scalar_document(ends, start + CHUNK - 1)
        flags_ref[2 + chunk] = held.astype(jnp.int32)


def hand_over(out_ref, squares_ref, slot_ref, summed, start, rows, lanes):
    squares_ref[start : start + SPAN, :] += summed * summed
    rounded = summed.astype(BF16)
    for b in range(SPAN // rows):
        tile = lanes.start // LANES * rows
        out_ref[slot_ref[start // rows + b], tile : tile + rows, :] = rounded[b * rows : (b + 1) * rows]


def conv_kernel(modes, size, ndoc, nblocks, carried, origin, where_ref, lengths_ref, owner_ref, *refs):
    x_ref, halo_ref, taps_ref, mixed_ref, rates_ref, residues_ref, skip_ref, residual_ref = refs[:8]
    refs = refs[8:]
    if carried:
        states_ref, before_ref, out_ref, spare_ref, sums_ref = refs[:5]
        refs = refs[5:]
    else:
        base_ref, gate_ref = refs[:2]
        refs = refs[2:]
    mask_ref, same_ref, keep_ref, tail_ref, flags_ref = refs[:5]
    if carried:
        slot_ref, squares_ref = refs[5:]
    count, width = mixed_ref.shape
    chunks = count // CHUNK
    step = step_rates(rates_ref, origin, width, size)
    step_residues = step_rates(residues_ref, origin, width, size)

    @pl.when(pl.program_id(0) == 0)
    def _():
        where = where_ref[0]
        base = where * count
        ends = running_ends(lengths_ref, ndoc)
        write_lag_masks(mask_ref, ends, base, count)
        write_flags(flags_ref, ends, where, count, nblocks)
        if carried:
            write_slots(slot_ref, owner_ref, where, nblocks)
            squares_ref[...] = before_ref[...]
        documents = row_documents(ends, base, count)
        causal = iota((CHUNK, CHUNK), 1) <= iota((CHUNK, CHUNK), 0)
        for chunk in range(chunks):
            start = base + chunk * CHUNK
            there = jnp.broadcast_to(documents[0:1, chunk * CHUNK : (chunk + 1) * CHUNK], (CHUNK, CHUNK))
            here = there.T
            same_ref[chunk] = jnp.where((here == there) & causal, 1.0, 0.0).astype(BF16)
            before = scalar_document(ends, start - 1).astype(F32)
            keep_ref[chunk] = jnp.where(here == before, 1.0, 0.0).astype(BF16)
            last = scalar_document(ends, start + CHUNK - 1).astype(F32)
            tail_ref[chunk] = jnp.where(there == last, 1.0, 0.0).astype(F32)

    groups = LANES // modes

    def tile(lanes):
        rate = tile_rates(step, lanes.start, size)
        scale = tile_rates(step_residues, lanes.start, size) * jnp.sqrt(1.0 - jnp.exp(-2.0 * rate))
        down = iota((CHUNK, LANES), 0)
        along = iota((LANES, CHUNK), 1)
        entry = (scale.T * jnp.exp(-rate.T * (down + 1).astype(F32))).astype(BF16)
        leave = jnp.exp(-rate * (CHUNK - 1 - along).astype(F32))
        whole = jnp.exp(-rate * CHUNK)
        terms = scale * jnp.where(along == 0, 1.0, leave * jnp.exp(-rate))
        toeplitz = []
        for g in range(groups):
            line = jnp.sum(terms[g * modes : (g + 1) * modes], 0, keepdims=True)
            top = pltpu.roll(jnp.broadcast_to(line, (8, CHUNK)), 0, 1, stride=1, stride_axis=0)
            parts = [top] + [pltpu.roll(top, 8 * k, 1) for k in range(1, CHUNK // 8)]
            toeplitz.append(jnp.concatenate(parts, 0).astype(BF16))
        inside = group_mask(modes, size)
        state = left_state(states_ref, flags_ref, rate, lanes, modes, size, count) if carried else None
        taps = tap_rows(taps_ref, 0, lanes)
        skip = skip_ref[:, lanes]
        lane_group = iota((CHUNK, LANES), 1) // size
        for chunk in range(chunks):
            start = chunk * CHUNK
            mixed = mixed_ref[start : start + CHUNK, lanes]
            same = same_ref[chunk]
            left = [t * same for t in toeplitz]
            right = [jnp.where(lane_group == g, mixed, jnp.zeros_like(mixed)) for g in range(groups)]
            if state is not None:
                left.append(entry * keep_ref[chunk])
                right.append(state.astype(BF16))
            longer = jnp.dot(jnp.concatenate(left, 1), jnp.concatenate(right, 0), preferred_element_type=F32)
            if chunk + 1 < chunks:
                fresh = jnp.dot((leave * tail_ref[chunk]).astype(BF16), mixed, preferred_element_type=F32)
                held = flags_ref[2 + chunk] == 1
                fresh = jnp.where(inside, fresh, 0.0)
                state = fresh if state is None else jnp.where(held, whole * state, 0.0) + fresh
            body = longer + skip * mixed.astype(F32)
            for half in range(start, start + CHUNK, SPAN):
                gate = short_conv(extended(x_ref, halo_ref, 0, half, lanes), taps, lag_masks(mask_ref, half))
                inner = body[half - start : half - start + SPAN]
                summed = residual_ref[half : half + SPAN, lanes].astype(F32) + gate * inner
                if carried:
                    hand_over(out_ref, squares_ref, slot_ref, summed, half, count // nblocks, lanes)
                else:
                    base_ref[half : half + SPAN, lanes] = summed
                    gate_ref[half : half + SPAN, lanes] = gate.astype(BF16)

    each_tile(width, tile)
    if carried:
        spare_ref[...] = out_ref[slot_ref[nblocks]]

        @pl.when(pl.program_id(0) == pl.num_programs(0) - 1)
        def _():
            for start in range(0, count, LANES):
                rows = squares_ref[start : start + LANES, :].T
                sums_ref[:, start : start + LANES] = jnp.sum(rows, 0, keepdims=True)


def add_kernel(
    modes, size, ndoc, nblocks,
    where_ref, lengths_ref, owner_ref,
    base_ref, gate_ref, rates_ref, residues_ref, states_ref,
    out_ref, spare_ref, squares_ref,
    keep_ref, flags_ref, slot_ref,
):
    count, width = base_ref.shape
    chunks = count // CHUNK
    step = step_rates(rates_ref, 0, width, size)
    step_residues = step_rates(residues_ref, 0, width, size)

    @pl.when(pl.program_id(0) == 0)
    def _():
        where = where_ref[0]
        ends = running_ends(lengths_ref, ndoc)
        write_flags(flags_ref, ends, where, count, nblocks)
        write_slots(slot_ref, owner_ref, where, nblocks)
        squares_ref[...] = jnp.zeros_like(squares_ref)
        before = scalar_document(ends, where * count - 1)
        kept = jnp.int32(0)
        for end in reversed(ends):
            kept = jnp.where(end >= where * count, end - where * count, kept)
        kept = jnp.where(before < 0, 0, kept)
        keep_ref[...] = jnp.where(iota((count, LANES), 0) < kept, 1.0, 0.0).astype(F32)

    def tile(lanes):
        rate = tile_rates(step, lanes.start, size)
        scale = tile_rates(step_residues, lanes.start, size) * jnp.sqrt(1.0 - jnp.exp(-2.0 * rate))
        down = iota((CHUNK, LANES), 0)
        entry = (scale.T * jnp.exp(-rate.T * (down + 1).astype(F32))).astype(BF16)
        whole = jnp.exp(-rate * CHUNK)
        state = left_state(states_ref, flags_ref, rate, lanes, modes, size, count)
        held = []
        for _ in range(chunks):
            held.append(state.astype(BF16))
            state = state * whole
        left = jnp.dot(entry, jnp.concatenate(held, 1), preferred_element_type=F32)
        for start in range(0, count, SPAN):
            low = start % CHUNK
            chunk = start // CHUNK
            carried = left[low : low + SPAN, chunk * LANES : (chunk + 1) * LANES] * keep_ref[start : start + SPAN, :]
            gate = gate_ref[start : start + SPAN, lanes].astype(F32)
            summed = base_ref[start : start + SPAN, lanes] + gate * carried
            hand_over(out_ref, squares_ref, slot_ref, summed, start, count // nblocks, lanes)

    each_tile(width, tile)
    spare_ref[...] = out_ref[slot_ref[nblocks]]


def norm_kernel(parts, where_ref, owner_ref, *refs):
    blocks, refs = refs[:parts], refs[parts:]
    spare_ref, gain_ref, out_ref = refs[:3]
    held, (done_ref, in_sems, out_sems) = refs[3 : 3 + parts], refs[3 + parts :]
    nblocks = blocks[0].shape[0]
    rows = out_ref.shape[0] // nblocks
    room = sum(block.shape[1] for block in blocks) - out_ref.shape[1] // LANES * rows

    def fetch(part, i, source):
        return pltpu.make_async_copy(source, held[part].at[i], in_sems.at[part, i])

    for i in range(nblocks):
        ahead = where_ref[0] - owner_ref[i]
        source = jnp.where(ahead < 0, ahead + nblocks, ahead)
        second = is_second(owner_ref, nblocks, i)
        low = 0
        for part in range(parts):
            size = blocks[part].shape[1]

            @pl.when(second)
            def _(part=part, i=i, low=low, size=size):
                fetch(part, i, spare_ref.at[pl.ds(low, size)]).start()

            @pl.when(jnp.logical_not(second))
            def _(part=part, i=i, source=source):
                fetch(part, i, blocks[part].at[source]).start()

            low += size

    def store(i):
        here = pl.ds(i * rows, rows)
        return pltpu.make_async_copy(done_ref.at[here], out_ref.at[here], out_sems.at[i])

    for i in range(nblocks):
        for part in range(parts):
            fetch(part, i, blocks[part].at[0]).wait()
        start = held[-1].shape[1] - room + i // 16 * 16
        halves = held[-1][i, start : start + 16, :].astype(F32)[i % 16 : i % 16 + 1]
        halves = jnp.broadcast_to(halves, (8, LANES))
        scale = halves + pltpu.roll(halves, LANES - rows, 1)
        scale = jnp.broadcast_to(scale[0:1], (LANES, LANES)).T[:rows]
        tile = 0
        for part in range(parts):
            for low in range(0, held[part].shape[1] - (room if part + 1 == parts else 0), rows):
                outs = slice(tile * LANES, (tile + 1) * LANES)
                value = held[part][i, low : low + rows, :].astype(F32)
                done_ref[i * rows : (i + 1) * rows, outs] = (value * scale * gain_ref[:, outs]).astype(BF16)
                tile += 1
        store(i).start()
    for i in range(nblocks):
        store(i).wait()


def params(limit=VMEM_LIMIT):
    return pltpu.CompilerParams(dimension_semantics=("arbitrary",), vmem_limit_bytes=limit)


def in_hbm(*arrays):
    return [pltpu.with_memory_space_constraint(array, pltpu.HBM) for array in arrays]


def in_vmem(array):
    return pltpu.with_memory_space_constraint(array, pltpu.VMEM)


def whole_array(rank):
    return lambda *_: (0,) * rank


def mix(scalars, x, halo, taps, rates, size, ndoc, copies):
    _, count, width = x.shape
    modes = rates.shape[0]
    wide = min(WIDE, width)
    deep = lambda t, *_: (0, 0, t)
    grid_spec = pltpu.PrefetchScalarGridSpec(
        num_scalar_prefetch=2,
        grid=(width // wide,),
        in_specs=[
            pl.BlockSpec((1, count, wide), lambda t, *_: (1, 0, t)),
            pl.BlockSpec((1, count, wide), lambda t, *_: (2, 0, t)),
            pl.BlockSpec((3, HALO, wide), deep),
            pl.BlockSpec((3, SHORT, wide), deep),
            pl.BlockSpec(rates.shape, whole_array(2)),
        ],
        out_specs=[
            pl.BlockSpec((count, wide), lambda t, *_: (0, t)),
            pl.BlockSpec((copies, modes, wide), deep),
        ],
        scratch_shapes=[
            pltpu.VMEM((count // SPAN, (NEAR - 1) * (SPAN + HALO), SPAN + 16), BF16),
            pltpu.VMEM((NEAR, count + 2 * HALO, LANES), F32),
            pltpu.VMEM((8, count), F32),
        ],
    )
    return pl.pallas_call(
        functools.partial(mix_kernel, modes, size, ndoc),
        grid_spec=grid_spec,
        out_shape=[pltpu.HBM((count, width), BF16), pltpu.HBM((copies, modes, width), BF16)],
        compiler_params=params(),
        cost_estimate=pl.CostEstimate(flops=60 * count * width, bytes_accessed=8 * count * width, transcendentals=count * width),
        name="mix",
    )(*scalars[:2], x, x, halo, taps, rates)


def conv(low, share, room, scalars, x, halo, taps, mixed, rates, residues, skip, residual, carried, size, ndoc, nblocks):
    _, count, width = x.shape
    modes = rates.shape[0]
    wide = math.gcd(math.gcd(low, share), WIDE)
    first = low // wide
    tile = lambda t, *_: (0, first + t)
    deep = lambda t, *_: (0, 0, first + t)
    step = pl.BlockSpec(rates.shape, whole_array(2))
    in_specs = [
        pl.BlockSpec((1, count, wide), deep),
        pl.BlockSpec((1, HALO, wide), deep),
        pl.BlockSpec((1, SHORT, wide), deep),
        pl.BlockSpec((count, wide), tile),
        step,
        step,
        pl.BlockSpec((1, wide), tile),
        pl.BlockSpec((count, wide), tile),
    ]
    operands = [x, halo, taps, mixed, rates, residues, skip, residual]
    scratch = [
        pltpu.VMEM((3, count + 2 * HALO, LANES), F32),
        pltpu.VMEM((count // CHUNK, CHUNK, CHUNK), BF16),
        pltpu.VMEM((count // CHUNK, CHUNK, LANES), BF16),
        pltpu.VMEM((count // CHUNK, LANES, CHUNK), F32),
        pltpu.SMEM((2 + count // CHUNK,), jnp.int32),
    ]
    if carried:
        states, squares = carried
        in_specs += [pl.BlockSpec((nblocks, modes, wide), deep), pl.BlockSpec((count, LANES), whole_array(2))]
        operands += [states, squares]
        scratch += [pltpu.SMEM((nblocks + 1,), jnp.int32), pltpu.VMEM((count, LANES), F32)]
        out_specs, out_shape = handed(share, room, wide, count, nblocks)
        out_specs[2] = pl.BlockSpec((1, count), whole_array(2))
        out_shape[2] = jax.ShapeDtypeStruct((1, count), F32)
    else:
        out_specs = [pl.BlockSpec((count, wide), lambda t, *_: (0, t))] * 2
        out_shape = [pltpu.VMEM((count, share), F32), pltpu.VMEM((count, share), BF16)]
    grid_spec = pltpu.PrefetchScalarGridSpec(
        num_scalar_prefetch=3, grid=(share // wide,), in_specs=in_specs, out_specs=out_specs, scratch_shapes=scratch
    )
    return pl.pallas_call(
        functools.partial(conv_kernel, modes, size, ndoc, nblocks, bool(carried), low // size),
        grid_spec=grid_spec,
        out_shape=out_shape,
        compiler_params=params(VMEM_LIMIT if carried else VMEM_LIMIT_BESIDE),
        cost_estimate=pl.CostEstimate(
            flops=2 * 1152 * count * share, bytes_accessed=8 * count * share, transcendentals=count * share
        ),
        name="conv",
    )(*scalars, *in_hbm(*operands))


def handed(share, room, wide, count, nblocks):
    rows = count // nblocks
    specs = [
        pl.BlockSpec((nblocks, wide // LANES * rows, LANES), lambda t, *_: (0, t, 0)),
        pl.BlockSpec((wide // LANES * rows, LANES), lambda t, *_: (t, 0)),
        pl.BlockSpec((count, LANES), whole_array(2)),
    ]
    shapes = [
        pltpu.HBM((nblocks, share // LANES * rows + room, LANES), BF16),
        pltpu.HBM((share // LANES * rows, LANES), BF16),
        pltpu.HBM((count, LANES), F32),
    ]
    return specs, shapes


def add(scalars, base, gate, rates, residues, states, size, ndoc, nblocks):
    count, share = base.shape
    modes = rates.shape[0]
    wide = math.gcd(share, 2 * WIDE)
    tile = lambda t, *_: (0, t)
    step = pl.BlockSpec(rates.shape, whole_array(2))
    out_specs, out_shape = handed(share, 0, wide, count, nblocks)
    grid_spec = pltpu.PrefetchScalarGridSpec(
        num_scalar_prefetch=3,
        grid=(share // wide,),
        in_specs=[
            pl.BlockSpec((count, wide), tile),
            pl.BlockSpec((count, wide), tile),
            step,
            step,
            pl.BlockSpec((nblocks, modes, wide), lambda t, *_: (0, 0, t)),
        ],
        out_specs=out_specs,
        scratch_shapes=[
            pltpu.VMEM((count, LANES), F32),
            pltpu.SMEM((2 + count // CHUNK,), jnp.int32),
            pltpu.SMEM((nblocks + 1,), jnp.int32),
        ],
    )
    return pl.pallas_call(
        functools.partial(add_kernel, modes, size, ndoc, nblocks),
        grid_spec=grid_spec,
        out_shape=out_shape,
        compiler_params=params(VMEM_LIMIT_BESIDE),
        cost_estimate=pl.CostEstimate(flops=300 * count * share, bytes_accessed=8 * count * share, transcendentals=count * share),
        name="add",
    )(*scalars, in_vmem(base), in_vmem(gate), *in_hbm(rates, residues, states))


def norm(where, owner, blocks, spare, gain, count):
    width = gain.shape[1]
    nblocks = blocks[0].shape[0]
    smem, vmem, anywhere = (pl.BlockSpec(memory_space=space) for space in (pltpu.SMEM, pltpu.VMEM, pl.ANY))
    return pl.pallas_call(
        functools.partial(norm_kernel, len(blocks)),
        in_specs=[smem, smem] + [anywhere] * (len(blocks) + 1) + [vmem],
        out_specs=anywhere,
        out_shape=jax.ShapeDtypeStruct((count, width), BF16),
        scratch_shapes=[pltpu.VMEM(block.shape, BF16) for block in blocks]
        + [
            pltpu.VMEM((count, width), BF16),
            pltpu.SemaphoreType.DMA((len(blocks), nblocks)),
            pltpu.SemaphoreType.DMA((nblocks,)),
        ],
        compiler_params=pltpu.CompilerParams(vmem_limit_bytes=VMEM_LIMIT),
        cost_estimate=pl.CostEstimate(flops=3 * count * width, bytes_accessed=4 * count * width, transcendentals=0),
        name="norm",
    )(where, owner, *blocks, spare, gain)


def on_device(features, residual, short_taps, rates, residues, skip, gain, lengths, owner):
    count, _, width = features.shape
    size = width // rates.shape[0]
    ndoc = lengths.shape[0]
    nblocks = lax.axis_size("ctx")
    rows = count // nblocks
    where = lax.axis_index("ctx")
    x = jnp.transpose(features, (1, 0, 2))
    pairs = [(i, i + 1) for i in range(nblocks - 1)]
    halo = lax.ppermute(x[:, count - HALO :], "ctx", pairs)

    scalars = (where.reshape(1).astype(jnp.int32), lengths, owner)
    spread = ((0, 0), (0, LANES - rates.shape[0]))
    rates, residues = jnp.pad(rates.T, spread), jnp.pad(residues.T, spread)

    offsets = owner[:nblocks]
    ids = jnp.arange(nblocks, dtype=jnp.int32)
    twice = jnp.any((offsets[:, None] == offsets[None, :]) & (ids[None, :] < ids[:, None]), 1)
    spare_shift = jnp.sum(jnp.where(twice, offsets, 0))

    def exchanged(value):
        return lax.all_to_all(value, "ctx", split_axis=0, concat_axis=0, tiled=True)

    first = width * SPLIT[0] // sum(SPLIT)
    second = width - first
    mixed, copies = mix(scalars, x, halo, short_taps, rates, size, ndoc, nblocks)
    states = exchanged(copies)
    shared = (scalars, x, halo, short_taps, mixed, rates, residues, skip.reshape(1, width), residual)
    base, gate = conv(0, first, 0, *shared, (), size, ndoc, nblocks)
    out, spare, squares = add(scalars, base, gate, rates, residues, states, size, ndoc, nblocks)
    block = exchanged(out)
    room = -(-nblocks // 16) * 16
    out, last_spare, sums = conv(first, second, room, *shared, (states, squares), size, ndoc, nblocks)
    mean = lax.psum(sums, "mp") / (width * lax.axis_size("mp"))
    inverse = lax.rsqrt(mean + EPS)
    high = lax.reduce_precision(inverse, 8, 7)
    halves = jnp.concatenate([high.reshape(nblocks, rows), (inverse - high).reshape(nblocks, rows)], 1)
    halves = jnp.pad(halves, ((0, room - nblocks), (0, LANES - 2 * rows))).astype(BF16)
    table = jnp.broadcast_to(halves[None], (nblocks, room, LANES))
    out = lax.dynamic_update_slice(out, table, (0, second // LANES * rows, 0))
    last_block = exchanged(out)
    spares = jnp.concatenate([spare, last_spare, halves], 0)

    def moved(by):
        return lambda value: lax.ppermute(value, "ctx", [(s, (s + by) % nblocks) for s in range(nblocks)])

    spare = lax.switch(spare_shift, [lambda value: value] + [moved(d) for d in range(1, nblocks)], spares)
    return norm(scalars[0], owner, [block, last_block], spare, gain.reshape(1, width), count)


def solution(mesh):
    return jax.shard_map(
        on_device,
        mesh=mesh,
        in_specs=(
            P("ctx", None, "mp"),
            P("ctx", "mp"),
            P(None, None, "mp"),
            P("mp", None),
            P("mp", None),
            P("mp"),
            P("mp"),
            P(),
            P(),
        ),
        out_specs=P("ctx", "mp"),
        check_vma=False,
    )
```
